128 devices in a mesh: dp: 64 (over y, z_lo, x, core), mp: 2 (over z_hi).
Axes of the slice: x: 4, y: 4, z: 4 (z_hi: 2, z_lo: 2; z = z_hi * 2 + z_lo), core: 2. Of those that a mesh axis runs over, the one named last changes fastest.
Arguments:
- tokens: bfloat16 [8192, 2560], P('dp'), may hold values from -6 to 6
- attn_gain: bfloat16 [2560], P('dp'), may hold values from 0.099609375 to 1.8984375
- query_weight: bfloat16 [2560, 2560], P('dp', 'mp'), may hold values from -0.125 to 0.125
- kv_weight: bfloat16 [2560, 512], P('dp'), may hold values from -0.125 to 0.125
- out_weight: bfloat16 [2560, 2560], P('mp', 'dp'), may hold values from -0.625 to 0.625
- mlp_gain: bfloat16 [2560], P('dp'), may hold values from 0.099609375 to 1.8984375
- gate_weight: bfloat16 [2560, 7680], P('dp', 'mp'), may hold values from -0.125 to 0.125
- up_weight: bfloat16 [2560, 7680], P('dp', 'mp'), may hold values from -0.125 to 0.125
- down_weight: bfloat16 [7680, 2560], P('mp', 'dp'), may hold values from -0.0625 to 0.0625
- cotangent: bfloat16 [8192, 2560], P('dp'), may hold values from -16 to 16
Outputs:
- block_out: bfloat16 [8192, 2560], P('dp')
- tokens_grad: bfloat16 [8192, 2560], P('dp')
- attn_gain_grad: float32 [2560], P('dp')
- query_weight_grad: float32 [2560, 2560], P('dp', 'mp')
- kv_weight_grad: float32 [2560, 512], P('dp')
- out_weight_grad: float32 [2560, 2560], P('mp', 'dp')
- mlp_gain_grad: float32 [2560], P('dp')
- gate_weight_grad: float32 [2560, 7680], P('dp', 'mp')
- up_weight_grad: float32 [2560, 7680], P('dp', 'mp')
- down_weight_grad: float32 [7680, 2560], P('mp', 'dp')
The draws below stay inside these ranges and needn't reach their ends.
All inputs are finite; a program needn't handle non-finite values.
Results may differ from the reference program's by a relative error of at most 0.017.
Values may be sent and summed in bfloat16 or wider, within the bound.
A program may use at most 448 MiB of HBM per device.

```python
import math
import jax
import jax.numpy as jnp
from jax import lax

D = 2560
HEADS = 10
HEAD_DIM = 256
FF = 7680
WINDOW = 2048
SEQ_LEN = 128
ROT = 128
SEQS = 64
TOKENS = 8192


def strengthened(drawn, rng, source, target, shards_of, factor):
    owner, partner = [(jnp.arange(drawn.shape[dim]) // (drawn.shape[dim] // shards_of)).reshape([-1 if axis == dim else 1 for axis in range(drawn.ndim)]) for dim in (source, target)]
    chosen = jax.random.permutation(rng, shards_of)[partner]
    strong = (owner == chosen) | (owner == (partner + shards_of // 2) % shards_of)
    return jnp.where(strong, factor * drawn, drawn)


def block_levels(key, extent, cuts, least, top_value):
    loudness = 1.0
    for dim, shards_of in cuts:
        heights = jax.random.uniform(jax.random.fold_in(jax.random.fold_in(key, 6), dim), (shards_of,), jnp.float32, least / len(cuts), top_value / len(cuts))
        loudness = loudness * jnp.repeat(jnp.exp(heights), extent[dim] // shards_of).reshape((-1,) + (1,) * (len(extent) - 1 - dim))
    return loudness


def normal_values(rng, extent, spread, bound, shards=(), kind=jnp.bfloat16):
    level = block_levels(rng, extent, shards, -0.22, 0.18) if shards else 1.0
    drawn = jax.random.normal(rng, extent, jnp.float32) * spread * level
    return jnp.minimum(jnp.maximum(drawn, -bound), bound).astype(kind)


def noise_with(rng, dims, spread, most, pieces, heavy, kind=jnp.bfloat16):
    values = spread * jax.random.normal(rng, dims, jnp.float32)
    if pieces:
        values = values * block_levels(rng, dims, pieces, -0.22, 0.18)
    return jnp.clip(strengthened(values, jax.random.fold_in(rng, 3), *heavy), -most, most).astype(kind)


def setup_inputs(seed: int = 0) -> dict:
    key_list = jax.random.split(jax.random.key(seed), 11)
    tokens = normal_values(key_list[0], (TOKENS, D), 1.0, 6.0, ((0, 64),))
    attn_gain = jnp.clip(1.0 + 0.18 * jax.random.normal(key_list[1], (D,), jnp.float32), 0.099609375, 1.8984375).astype(jnp.bfloat16)
    query_weight = normal_values(key_list[2], (D, HEADS * HEAD_DIM), D ** -0.5, 0.125, ((0, 64), (1, 2)))
    kv_weight = normal_values(key_list[3], (D, 2 * HEAD_DIM), D ** -0.5, 0.125, ((0, 64),))
    out_weight = normal_values(key_list[4], (HEADS * HEAD_DIM, D), (HEADS * HEAD_DIM // 32) ** -0.5, 0.625, ((0, 2), (1, 64)))
    mlp_gain = jnp.clip(1.0 + 0.18 * jax.random.normal(key_list[5], (D,), jnp.float32), 0.099609375, 1.8984375).astype(jnp.bfloat16)
    gate_weight = normal_values(key_list[6], (D, FF), D ** -0.5, 0.125, ((0, 64), (1, 2)))
    up_weight = normal_values(key_list[7], (D, FF), D ** -0.5, 0.125, ((0, 64), (1, 2)))
    down_weight = normal_values(key_list[8], (FF, D), FF ** -0.5, 0.0625, ((0, 2), (1, 64)))
    cotangent = noise_with(key_list[9], (TOKENS, D), 1.0, 16.0, ((0, 64),), (0, 1, 64, 4.0))
    return {"tokens": tokens, "attn_gain": attn_gain, "query_weight": query_weight, "kv_weight": kv_weight, "out_weight": out_weight, "mlp_gain": mlp_gain, "gate_weight": gate_weight, "up_weight": up_weight, "down_weight": down_weight, "cotangent": cotangent}


@jax.custom_vjp
def low(v):
    return lax.optimization_barrier(v.astype(jnp.bfloat16)).astype(jnp.float32)

@jax.custom_vjp
def low_back(v):
    return v

def low_keep(v):
    return (low(v), None)

def low_pass(kept, grad):
    return (grad,)

def back_keep(v):
    return (v, None)

def back_low(kept, grad):
    return (low(grad),)
low.defvjp(low_keep, low_pass)
low_back.defvjp(back_keep, back_low)
norm_eps = 1e-06

def matmul_high(left, right):
    return jnp.einsum('...i,ij->...j', left, right, precision=lax.Precision.HIGHEST)

def rms_norm(values, gain_row):
    return values * lax.rsqrt(lax.optimization_barrier(jnp.mean(values * values, axis=-1, keepdims=True)) + norm_eps) * gain_row

def tables():
    half_rot = ROT // 2
    rates = jnp.exp(jnp.arange(half_rot, dtype=jnp.float32) * (-2.0 * math.log(10000.0) / ROT))
    angles = jnp.arange(SEQ_LEN, dtype=jnp.float32)[:, None] * rates[None, :]
    return (jnp.cos(angles), jnp.sin(angles))

def rotate(field, cosine, sine):
    half_rot = ROT // 2
    first = field[..., :half_rot]
    second = field[..., half_rot:ROT]
    return jnp.concatenate([first * cosine - second * sine, second * cosine + first * sine, field[..., ROT:]], axis=-1)

def residual_block(x_in, gain_one, w_query, w_kv, w_out, gain_two, w_gate, w_up, w_down):
    groups = x_in.shape[0]
    cosine, sine = tables()
    positions = jnp.arange(SEQ_LEN)
    keep_mask = (positions[:, None] >= positions[None, :]) & (positions[:, None] - positions[None, :] < WINDOW)
    xn_one = low(rms_norm(x_in, gain_one))
    q_pre = low_back(matmul_high(xn_one, w_query))
    kv_pre = low_back(matmul_high(xn_one, w_kv))
    queries = low(rotate(q_pre.reshape(groups, SEQ_LEN, HEADS, HEAD_DIM), cosine[:, None, :], sine[:, None, :]))
    key_rot = low(rotate(kv_pre[..., :HEAD_DIM], cosine, sine))
    value_rows = low(kv_pre[..., HEAD_DIM:])
    scores = low_back(jnp.einsum('gqhd,gkd->ghqk', queries, key_rot, precision=lax.Precision.HIGHEST) * HEAD_DIM ** (-0.5))
    scores = jnp.where(keep_mask, scores, -1e+30)
    row_max = lax.optimization_barrier(jnp.max(scores, axis=-1, keepdims=True))
    weights = jnp.exp(scores - row_max)
    attn_probs = low(weights / lax.optimization_barrier(jnp.sum(weights, axis=-1, keepdims=True)))
    mixed_heads = jnp.einsum('ghqk,gkd->gqhd', attn_probs, value_rows, precision=lax.Precision.HIGHEST)
    mixed_heads = low(low_back(mixed_heads.reshape(groups, SEQ_LEN, HEADS * HEAD_DIM)))
    attn_branch = low_back(matmul_high(mixed_heads, w_out))
    x_mid = x_in + attn_branch
    xn_two = low(rms_norm(x_mid, gain_two))
    gate_pre = low_back(matmul_high(xn_two, w_gate))
    up_pre = low_back(matmul_high(xn_two, w_up))
    hidden = low(jax.nn.gelu(gate_pre) * up_pre)
    return x_mid + matmul_high(hidden, w_down)

def reference(tokens, attn_gain, query_weight, kv_weight, out_weight, mlp_gain, gate_weight, up_weight, down_weight, cotangent):
    weights_f32 = tuple((w.astype(jnp.float32) for w in (attn_gain, query_weight, kv_weight, out_weight, mlp_gain, gate_weight, up_weight, down_weight)))
    group_size = math.gcd(SEQS, max(1, 4096 // SEQ_LEN))
    group_count = SEQS // group_size
    inputs = tokens.astype(jnp.float32).reshape(group_count, group_size, SEQ_LEN, D)
    grads_in = cotangent.astype(jnp.float32).reshape(group_count, group_size, SEQ_LEN, D)

    def per_group(grad_sums, group_item):
        x_group, ct_group = group_item
        result, pull = jax.vjp(residual_block, x_group, *weights_f32)
        pulled = pull(ct_group)
        grad_sums = tuple((total + part for total, part in zip(grad_sums, pulled[1:])))
        return (grad_sums, (result.astype(jnp.bfloat16), pulled[0].astype(jnp.bfloat16)))
    zero_sums = tuple((jnp.zeros_like(w) for w in weights_f32))
    grad_sums, (results, input_grads) = lax.scan(per_group, zero_sums, (inputs, grads_in))
    return (results.reshape(TOKENS, D), input_grads.reshape(TOKENS, D), grad_sums[0], grad_sums[1], grad_sums[2], grad_sums[3], grad_sums[4], grad_sums[5], grad_sums[6], grad_sums[7])
```

```python
import math

import jax
import jax.numpy as jnp
from jax import lax
from jax.experimental import pallas as pl
from jax.experimental.pallas import tpu as pltpu
from jax.sharding import Mesh
from jax.sharding import PartitionSpec as P

HEAD_DIM = 256
WINDOW = 2048
SEQ_LEN = 128
ROT = 128
AXES = ("y", "zl", "x", "c", "zh")
PLANE = ("y", "x")
GROUP = ("zl", "c")
OWNERS = ("y", "x", "zl", "c")
MESH = pl.DeviceIdType.MESH

norm_eps = 1e-06


def permuted(v):
    n = v.shape[0]
    return v.reshape(n, 4, 2, 4, 80).transpose(0, 1, 3, 2, 4).reshape(n, 2560)


def restored(v):
    n = v.shape[0]
    return v.reshape(n, 4, 4, 2, 80).transpose(0, 1, 3, 2, 4).reshape(n, 2560)


def greet(peers):
    barrier = pltpu.get_barrier_semaphore()
    for peer in peers:
        pl.semaphore_signal(barrier, inc=1, device_id=peer, device_id_type=MESH)
    pl.semaphore_wait(barrier, len(peers))


def remote(src, dst, send, recv, peer):
    return pltpu.make_async_remote_copy(
        src_ref=src, dst_ref=dst, send_sem=send, recv_sem=recv, device_id=peer, device_id_type=MESH
    )


def gather_kernel(x_ref, o_ref, local_sem, send, recv):
    zl, c, zh = lax.axis_index("zl"), lax.axis_index("c"), lax.axis_index("zh")
    half = x_ref.shape[0] // 2
    core = {"c": 1 - c}
    chips = [{"zl": 1 - zl, "zh": k} for k in range(2)]
    greet([core, *chips])
    mine, other = zl * 2 + c, (1 - zl) * 2 + c
    part = pl.ds(pl.multiple_of(zh * half, half), half)
    away = [
        remote(x_ref.at[part], o_ref.at[mine, part], send.at[k], recv.at[zh], chips[k])
        for k in range(2)
    ]
    for copy in away:
        copy.start()
    keep = pltpu.make_async_copy(x_ref, o_ref.at[mine], local_sem)
    keep.start()
    across = remote(x_ref, o_ref.at[mine], send.at[2], recv.at[2], core)
    across.start()
    passed = []
    for k in range(2):
        rows = pl.ds(k * half, half)
        arrived = remote(x_ref.at[rows], o_ref.at[other, rows], send.at[k], recv.at[k], chips[k])
        arrived.wait_recv()
        on = remote(o_ref.at[other, rows], o_ref.at[other, rows], send.at[3 + k], recv.at[3 + k], core)
        on.start()
        passed.append(on)
    for copy in away:
        copy.wait_send()
    across.wait()
    for copy in passed:
        copy.wait()
    keep.wait()


def token_gather(x, cid):
    return pl.pallas_call(
        gather_kernel,
        out_shape=jax.ShapeDtypeStruct((4, *x.shape), x.dtype),
        in_specs=[pl.BlockSpec(memory_space=pltpu.VMEM)],
        out_specs=pl.BlockSpec(memory_space=pltpu.VMEM),
        scratch_shapes=[
            pltpu.SemaphoreType.DMA,
            pltpu.SemaphoreType.DMA((5,)),
            pltpu.SemaphoreType.DMA((5,)),
        ],
        compiler_params=pltpu.CompilerParams(
            collective_id=cid, has_side_effects=True, vmem_limit_bytes=32 * 2**20
        ),
    )(x)


def sum_kernel(p_ref, o_ref, from_core, other, from_chips, own, own_low, from_far, send, recv):
    zl, c, zh = lax.axis_index("zl"), lax.axis_index("c"), lax.axis_index("zh")
    rows = p_ref.shape[1]
    half = rows // 2
    core, far = {"c": 1 - c}, {"zh": 1 - zh}
    chips = [{"zl": 1 - zl, "zh": k} for k in range(2)]
    greet([core, far, *chips])
    order = [1 - zl, zl]
    cores = [
        remote(p_ref.at[z * 2 + 1 - c], from_core.at[i], send.at[i], recv.at[i], core)
        for i, z in enumerate(order)
    ]
    for copy in cores:
        copy.start()
    step = 16
    cores[0].wait_recv()
    aways = []
    for k in range(2):

        @pl.loop(0, half // step)
        def _(j, k=k):
            at = pl.ds(pl.multiple_of(k * half + j * step, step), step)
            total = p_ref[(1 - zl) * 2 + c, at].astype(jnp.float32) + from_core[0, at].astype(jnp.float32)
            other[at] = total.astype(jnp.bfloat16)

        away = remote(
            other.at[pl.ds(k * half, half)], from_chips.at[zh], send.at[2 + k], recv.at[2 + zh], chips[k]
        )
        away.start()
        aways.append(away)
    cores[1].wait_recv()
    fars = []
    for k in range(2):
        piece = (1 - zh) if k == 0 else zh
        if k == 1:
            for i in range(2):
                remote(
                    other.at[pl.ds(0, half)], from_chips.at[i], send.at[2 + i], recv.at[2 + i], chips[i]
                ).wait_recv()

        @pl.loop(0, half // step)
        def _(j, k=k, piece=piece):
            at = pl.ds(pl.multiple_of(piece * half + j * step, step), step)
            total = p_ref[zl * 2 + c, at].astype(jnp.float32) + from_core[1, at].astype(jnp.float32)
            if k == 1:
                here = pl.ds(pl.multiple_of(j * step, step), step)
                total += from_chips[0, here].astype(jnp.float32) + from_chips[1, here].astype(jnp.float32)
            own[at] = total.astype(jnp.bfloat16)

        at = pl.ds(pl.multiple_of(piece * half, half), half)
        copy = remote(own.at[at], from_far.at[at], send.at[4 + k], recv.at[4 + k], far)
        copy.start()
        fars.append(copy)
    for k in range(2):
        fars[k].wait_recv()
        piece = zh if k == 0 else (1 - zh)

        @pl.loop(0, half // step)
        def _(j, piece=piece):
            at = pl.ds(pl.multiple_of(piece * half + j * step, step), step)
            o_ref[at] = own[at].astype(jnp.float32) + from_far[at].astype(jnp.float32)

    for copy in (*cores, *aways, *fars):
        copy.wait_send()


def token_sum(p, cid):
    rows, width = p.shape[1:]
    low = jnp.bfloat16
    return pl.pallas_call(
        sum_kernel,
        out_shape=jax.ShapeDtypeStruct((rows, width), jnp.float32),
        in_specs=[pl.BlockSpec(memory_space=pltpu.VMEM)],
        out_specs=pl.BlockSpec(memory_space=pltpu.VMEM),
        scratch_shapes=[
            pltpu.VMEM((2, rows, width), low),
            pltpu.VMEM((rows, width), low),
            pltpu.VMEM((2, rows // 2, width), low),
            pltpu.VMEM((rows, width), low),
            pltpu.VMEM((rows, width), low),
            pltpu.VMEM((rows, width), low),
            pltpu.SemaphoreType.DMA((6,)),
            pltpu.SemaphoreType.DMA((6,)),
        ],
        compiler_params=pltpu.CompilerParams(
            collective_id=cid, has_side_effects=True, vmem_limit_bytes=32 * 2**20
        ),
    )(p)


def pair_kernel(p_ref, o_ref, landed, send, recv):
    far = {"zh": 1 - lax.axis_index("zh")}
    rows = p_ref.shape[0]
    greet([far])
    copy = remote(p_ref, landed, send, recv, far)
    copy.start()
    copy.wait()
    step = 16

    @pl.loop(0, rows // step)
    def _(j):
        at = pl.ds(pl.multiple_of(j * step, step), step)
        o_ref[at] = p_ref[at].astype(jnp.float32) + landed[at].astype(jnp.float32)


def pair_sum(p, cid):
    return pl.pallas_call(
        pair_kernel,
        out_shape=jax.ShapeDtypeStruct(p.shape, jnp.float32),
        in_specs=[pl.BlockSpec(memory_space=pltpu.VMEM)],
        out_specs=pl.BlockSpec(memory_space=pltpu.VMEM),
        scratch_shapes=[
            pltpu.VMEM(p.shape, p.dtype),
            pltpu.SemaphoreType.DMA,
            pltpu.SemaphoreType.DMA,
        ],
        compiler_params=pltpu.CompilerParams(
            collective_id=cid, has_side_effects=True, vmem_limit_bytes=32 * 2**20
        ),
    )(p)


def ring_of(axis, at):
    return {axis: lax.rem(at + 3, 4)}, {axis: lax.rem(at + 1, 4)}


def block_rows(row, column, start=0, size=160):
    return pl.ds(pl.multiple_of((row * 4 + column) * 160 + start, 16), size)


def exchange_kernel(*refs):
    n = (len(refs) - 3) // 2
    ins, outs, (here, send, recv) = refs[:n], refs[n : 2 * n], refs[2 * n :]
    zl, c = lax.axis_index("zl"), lax.axis_index("c")
    mine = zl * 2 + c
    peers = [({"zl": 1 - zl, "c": k}, (1 - zl) * 2 + k) for k in range(2)]
    peers.append(({"c": 1 - c}, zl * 2 + 1 - c))
    greet([p for p, _ in peers])
    copies = []
    for i in range(n):
        for k, (peer, block) in enumerate(peers):
            slot = i * 3 + k
            landing = i * 3 + (c if k < 2 else 2)
            copies.append(
                remote(ins[i].at[block], outs[i].at[mine], send.at[slot], recv.at[landing], peer)
            )
            copies[-1].start()
    keeps = [pltpu.make_async_copy(ins[i].at[mine], outs[i].at[mine], here.at[i]) for i in range(n)]
    for keep in keeps:
        keep.start()
    for keep in keeps:
        keep.wait()
    for i in range(n):
        for k, (peer, block) in enumerate(peers):
            remote(
                ins[i].at[block], outs[i].at[block], send.at[i * 3 + k], recv.at[i * 3 + k], peer
            ).wait_recv()
    for copy in copies:
        copy.wait_send()


def group_exchange(arrays, cid):
    n = len(arrays)
    return pl.pallas_call(
        exchange_kernel,
        out_shape=[jax.ShapeDtypeStruct(a.shape, a.dtype) for a in arrays],
        in_specs=[pl.BlockSpec(memory_space=pl.ANY)] * n,
        out_specs=[pl.BlockSpec(memory_space=pl.ANY)] * n,
        scratch_shapes=[
            pltpu.SemaphoreType.DMA((n,)),
            pltpu.SemaphoreType.DMA((3 * n,)),
            pltpu.SemaphoreType.DMA((3 * n,)),
        ],
        compiler_params=pltpu.CompilerParams(collective_id=cid, has_side_effects=True),
    )(*arrays)


ATTN, FEED = 768, 512


def plane_gather_kernel(in_ref, dy_ref, a_ref, f_ref, o_ref, here, send, recv, csend, crecv, dsend, drecv):
    y, x, c = lax.axis_index("y"), lax.axis_index("x"), lax.axis_index("c")
    zl, zh = lax.axis_index("zl"), lax.axis_index("zh")
    core = {"c": 1 - c}
    chips = [{"zl": 1 - zl, "zh": k} for k in range(2)]
    greet([*ring_of("x", x), *ring_of("y", y), core, *chips])

    half = dy_ref.shape[0] // 2
    mine, other = zl * 2 + c, (1 - zl) * 2 + c
    part = pl.ds(pl.multiple_of(zh * half, half), half)
    dy_copies = [
        remote(dy_ref.at[part], o_ref.at[mine, part], dsend.at[k], drecv.at[zh], chips[k])
        for k in range(2)
    ]
    dy_copies.append(remote(dy_ref, o_ref.at[mine], dsend.at[2], drecv.at[2], core))
    for copy in dy_copies:
        copy.start()
    keeps = [pltpu.make_async_copy(dy_ref, o_ref.at[mine], here.at[0])]

    def spot(h, kind, start=0, size=160):
        def at(i1, i2):
            row, column = (i2, i1) if h == 0 else (i1, i2)
            rows = block_rows(row, column, start, size)
            if kind == 0:
                return a_ref.at[rows, pl.ds(pl.multiple_of((c * 2 + h) * ATTN, 128), ATTN)]
            return f_ref.at[rows, pl.ds(h * FEED, FEED)]

        return at

    def own(h, kind, start=0, size=160):
        columns = pl.ds(0, ATTN) if kind == 0 else pl.ds(ATTN, FEED)
        return in_ref.at[h, pl.ds(start, size), columns]

    pieces = [(h, kind) for kind in range(2) for h in range(2)]
    for n, (h, kind) in enumerate(pieces):
        i1, i2 = (x, y) if h == 0 else (y, x)
        keeps.append(
            pltpu.make_async_copy(own(h, kind), spot(h, kind)(i1, i2), here.at[1 + n])
        )
    for keep in keeps:
        keep.start()
    started = []

    def go(src, dst, n, ring, slot, peer):
        k = (n * 5 + ring) * 4 + slot
        copy = remote(src, dst, send.at[k], recv.at[k], peer)
        copy.start()
        started.append(copy)

    def arrived(dst, n, ring, slot):
        k = (n * 5 + ring) * 4 + slot
        remote(dst, dst, send.at[k], recv.at[k], core).wait_recv()

    crossed = []

    def cross(n, ref):
        if pieces[n][1] == 0:
            k = len(crossed)
            copy = remote(ref, ref, csend.at[k], crecv.at[k], core)
            copy.start()
            crossed.append(copy)

    def cross_own(n, src, dst):
        if pieces[n][1] == 0:
            k = len(crossed)
            copy = remote(src, dst, csend.at[k], crecv.at[k], core)
            copy.start()
            crossed.append(copy)

    def around(h):
        if h == 0:
            return x, ring_of("x", x), y, ring_of("y", y)
        return y, ring_of("y", y), x, ring_of("x", x)

    def shift(i, by):
        return lax.rem(i + by, 4)

    for n, (h, kind) in enumerate(pieces):
        i1, (back1, ahead1), i2, (back2, ahead2) = around(h)
        place = spot(h, kind)(i1, i2)
        go(own(h, kind), place, n, 0, 0, ahead1)
        go(own(h, kind), place, n, 0, 1, back1)
    for n, (h, kind) in enumerate(pieces):
        i1, (back1, ahead1), i2, (back2, ahead2) = around(h)
        place = spot(h, kind)(i1, i2)
        go(own(h, kind), place, n, 1, 0, ahead2)
        go(own(h, kind), place, n, 1, 1, back2)
        cross_own(n, own(h, kind), place)
    for n, (h, kind) in enumerate(pieces):
        i1, (back1, ahead1), i2, (back2, ahead2) = around(h)
        left, right = spot(h, kind)(shift(i1, 3), i2), spot(h, kind)(shift(i1, 1), i2)
        arrived(left, n, 0, 0)
        low_half = spot(h, kind, 0, 80)(shift(i1, 3), i2)
        go(low_half, low_half, n, 0, 2, ahead1)
        arrived(right, n, 0, 1)
        high_half = spot(h, kind, 80, 80)(shift(i1, 1), i2)
        go(high_half, high_half, n, 0, 3, back1)
        for ring, ref in ((2, left), (3, right)):
            go(ref, ref, n, ring, 0, ahead2)
            go(ref, ref, n, ring, 1, back2)
            cross(n, ref)
    for n, (h, kind) in enumerate(pieces):
        i1, (back1, ahead1), i2, (back2, ahead2) = around(h)
        far = shift(i1, 2)
        arrived(spot(h, kind, 0, 80)(far, i2), n, 0, 2)
        arrived(spot(h, kind, 80, 80)(far, i2), n, 0, 3)
        ref = spot(h, kind)(far, i2)
        go(ref, ref, n, 4, 0, ahead2)
        go(ref, ref, n, 4, 1, back2)
        cross(n, ref)
    firsts = ((1, 0), (2, 3), (3, 1), (4, 2))
    for ring, by in firsts:
        for n, (h, kind) in enumerate(pieces):
            i1, (back1, ahead1), i2, (back2, ahead2) = around(h)
            j = shift(i1, by)
            left, right = spot(h, kind)(j, shift(i2, 3)), spot(h, kind)(j, shift(i2, 1))
            arrived(left, n, ring, 0)
            low_half = spot(h, kind, 0, 80)(j, shift(i2, 3))
            go(low_half, low_half, n, ring, 2, ahead2)
            cross(n, left)
            arrived(right, n, ring, 1)
            high_half = spot(h, kind, 80, 80)(j, shift(i2, 1))
            go(high_half, high_half, n, ring, 3, back2)
            cross(n, right)
    passed = []
    for k in range(2):
        rows = pl.ds(k * half, half)
        remote(dy_ref.at[rows], o_ref.at[other, rows], dsend.at[k], drecv.at[k], chips[k]).wait_recv()
        on = remote(o_ref.at[other, rows], o_ref.at[other, rows], dsend.at[3 + k], drecv.at[3 + k], core)
        on.start()
        passed.append(on)
    for ring, by in firsts:
        for n, (h, kind) in enumerate(pieces):
            i1, (back1, ahead1), i2, (back2, ahead2) = around(h)
            j, far = shift(i1, by), shift(i2, 2)
            arrived(spot(h, kind, 0, 80)(j, far), n, ring, 2)
            arrived(spot(h, kind, 80, 80)(j, far), n, ring, 3)
            cross(n, spot(h, kind)(j, far))
    for copy in crossed:
        copy.wait()
    for copy in passed:
        copy.wait()
    dy_copies[2].wait()
    for copy in (*started, *dy_copies[:2]):
        copy.wait_send()
    for keep in keeps:
        keep.wait()


def plane_gather(own, dy, cid):
    return pl.pallas_call(
        plane_gather_kernel,
        out_shape=[
            jax.ShapeDtypeStruct((2560, 4 * ATTN), own.dtype),
            jax.ShapeDtypeStruct((2560, 2 * FEED), own.dtype),
            jax.ShapeDtypeStruct((4, *dy.shape), dy.dtype),
        ],
        in_specs=[pl.BlockSpec(memory_space=pl.ANY)] * 2,
        out_specs=[pl.BlockSpec(memory_space=pl.ANY)] * 3,
        scratch_shapes=[
            pltpu.SemaphoreType.DMA((5,)),
            pltpu.SemaphoreType.DMA((80,)),
            pltpu.SemaphoreType.DMA((80,)),
            pltpu.SemaphoreType.DMA((32,)),
            pltpu.SemaphoreType.DMA((32,)),
            pltpu.SemaphoreType.DMA((5,)),
            pltpu.SemaphoreType.DMA((5,)),
        ],
        compiler_params=pltpu.CompilerParams(collective_id=cid, has_side_effects=True),
    )(own, dy)


WIDE = ATTN + FEED
SEGMENTS = ((0, 0, 256), (256, 256, 512), (WIDE, 768, 768))


def plane_sum_kernel(
    a_ref, o_ref, f_ref, attn_ref, feed_ref,
    sums, from_core, via, main, from_chip, attn_low, feed_low,
    here, csend, crecv, send, recv, esend, erecv,
):
    y, x, c, zl = (lax.axis_index(k) for k in ("y", "x", "c", "zl"))
    core, chip = {"c": 1 - c}, {"zl": 1 - zl}
    greet([*ring_of("x", x), *ring_of("y", y), core, chip])
    step = 16
    f32, low = jnp.float32, jnp.bfloat16

    def shift(i, by):
        return lax.rem(i + by, 4)

    order = (2, 1, 3, 0)

    def chunk(q):
        return pl.ds(pl.multiple_of(shift(y, order[q]) * 640, 640), 640)

    def load(q, side, remote_side):
        rows = chunk(q)
        if side == 0:
            parts = [a_ref.at[rows, pl.ds(0, 256)], a_ref.at[rows, pl.ds(256, 512)], a_ref.at[rows, pl.ds(768, 768)]]
        else:
            parts = [a_ref.at[rows, pl.ds(1536, 256)], o_ref.at[rows, pl.ds(0, 512)], o_ref.at[rows, pl.ds(512, 768)]]
        out = []
        for s, (at, landing, width) in enumerate(SEGMENTS):
            k = q * 3 + s
            if remote_side:
                out.append(
                    remote(parts[s], from_core.at[rows, pl.ds(landing, width)], csend.at[k], crecv.at[k], core)
                )
            else:
                out.append(pltpu.make_async_copy(parts[s], sums.at[rows, pl.ds(at, width)], here.at[k]))
        return out

    def feed_load(q):
        rows = chunk(q)
        return [
            pltpu.make_async_copy(
                f_ref.at[rows, pl.ds(h * FEED, FEED)],
                sums.at[rows, pl.ds(h * WIDE + ATTN, FEED)],
                here.at[12 + q * 2 + h],
            )
            for h in range(2)
        ]

    for side in range(2):

        @pl.when(c == side)
        def _(side=side):
            for q in range(4):
                for copy in load(q, 1 - side, True):
                    copy.start()
                for copy in load(q, side, False):
                    copy.start()

    for q in range(4):
        for copy in feed_load(q):
            copy.start()

    def columns(h):
        return pl.ds(h * WIDE, WIDE)

    def rows_at(h, i1, i2, start=0, size=160):
        row, column = (i2, i1) if h == 0 else (i1, i2)
        return block_rows(row, column, start, size)

    def around(h):
        if h == 0:
            return x, ring_of("x", x), y, ring_of("y", y)
        return y, ring_of("y", y), x, ring_of("x", x)

    def add(h, first, size, terms):
        @pl.loop(0, size // step)
        def _(i):
            at = pl.ds(pl.multiple_of(first + i * step, step), step)
            total = sums[at, columns(h)].astype(f32)
            for ref, index, start in terms:
                total += ref[(*index, pl.ds(pl.multiple_of(start + i * step, step), step))].astype(f32)
            sums[at, columns(h)] = total.astype(low)

    started = []

    def go(h, ring, slot, src, dst, peer):
        k = (h * 5 + ring) * 4 + slot
        copy = remote(src, dst, send.at[k], recv.at[k], peer)
        copy.start()
        started.append(copy)

    def arrived(h, ring, slot, dst):
        k = (h * 5 + ring) * 4 + slot
        remote(dst, dst, send.at[k], recv.at[k], core).wait_recv()

    def first_row(h, i1, i2):
        row, column = (i2, i1) if h == 0 else (i1, i2)
        return (row * 4 + column) * 160

    def out_via(h, ring, place, at, ring_peers):
        back, ahead = ring_peers
        far = shift(at, 2)
        go(h, ring, 0, sums.at[place(far, 0, 80), columns(h)], via.at[h, ring, 0], ahead)
        go(h, ring, 1, sums.at[place(far, 80, 80), columns(h)], via.at[h, ring, 1], back)

    def out_main(h, ring, place, first, at, ring_peers):
        back, ahead = ring_peers
        arrived(h, ring, 0, via.at[h, ring, 0])
        add(h, first(shift(at, 1)), 80, [(via, (h, ring, 0), 0)])
        go(h, ring, 2, sums.at[place(shift(at, 1), 0, 160), columns(h)], main.at[h, ring, 0], ahead)
        arrived(h, ring, 1, via.at[h, ring, 1])
        add(h, first(shift(at, 3)) + 80, 80, [(via, (h, ring, 1), 0)])
        go(h, ring, 3, sums.at[place(shift(at, 3), 0, 160), columns(h)], main.at[h, ring, 1], back)

    def take(h, ring, first, at):
        arrived(h, ring, 2, main.at[h, ring, 0])
        arrived(h, ring, 3, main.at[h, ring, 1])
        add(h, first(at), 160, [(main, (h, ring, 0), 0), (main, (h, ring, 1), 0)])

    def along_second(h, j):
        i1, _, i2, peers = around(h)
        fixed = shift(i1, order[j])
        return (
            lambda k, start, size: rows_at(h, fixed, k, start, size),
            lambda k: first_row(h, fixed, k),
            i2,
            peers,
        )

    def along_first(h):
        i1, peers, i2, _ = around(h)
        return (
            lambda k, start, size: rows_at(h, k, i2, start, size),
            lambda k: first_row(h, k, i2),
            i1,
            peers,
        )

    for q in range(4):
        for copy in load(q, 0, False):
            copy.wait()
        for copy in feed_load(q):
            copy.wait()
        for copy in load(q, 0, True):
            copy.wait_recv()
        top = shift(y, order[q]) * 640

        @pl.loop(0, 640 // step)
        def _(i, top=top):
            at = pl.ds(pl.multiple_of(top + i * step, step), step)
            for place, landing, width in SEGMENTS:
                total = sums[at, pl.ds(place, width)].astype(f32) + from_core[
                    at, pl.ds(landing, width)
                ].astype(f32)
                sums[at, pl.ds(place, width)] = total.astype(low)

        if q == 0:
            for j in range(4):
                place, first, at, peers = along_second(0, j)
                out_via(0, j, place, at, peers)
        place, first, at, peers = along_second(1, q)
        out_via(1, q, place, at, peers)
        if q > 0:
            place, first, at, peers = along_second(1, q - 1)
            out_main(1, q - 1, place, first, at, peers)
    for j in range(4):
        place, first, at, peers = along_second(0, j)
        out_main(0, j, place, first, at, peers)
        if j == 0:
            place, first, at, peers = along_second(1, 3)
            out_main(1, 3, place, first, at, peers)
    for j in range(4):
        for h in (1, 0):
            place, first, at, peers = along_second(h, j)
            take(h, j, first, at)
            if j == 0:
                place, first, at, peers = along_first(h)
                out_via(h, 4, place, at, peers)
    for h in (1, 0):
        place, first, at, peers = along_first(h)
        out_main(h, 4, place, first, at, peers)
    for h in (1, 0):
        place, first, at, peers = along_first(h)
        take(h, 4, first, at)
    home = (y * 4 + x) * 160
    theirs = pl.ds(pl.multiple_of(home + (1 - zl) * 80, 16), 80)
    away = remote(sums.at[theirs], from_chip, esend.at[0], erecv.at[0], chip)
    away.start()
    away.wait()

    @pl.loop(0, 80 // step)
    def _(i):
        here_at = pl.ds(pl.multiple_of(home + zl * 80 + i * step, step), step)
        at = pl.ds(pl.multiple_of(i * step, step), step)
        for h in range(2):
            a = pl.ds(h * WIDE, ATTN)
            attn_low[at, pl.ds(h * ATTN, ATTN)] = sums[here_at, a].astype(f32) + from_chip[at, a].astype(f32)
            f = pl.ds(h * WIDE + ATTN, FEED)
            feed_low[0, at, pl.ds(h * FEED, FEED)] = sums[here_at, f].astype(f32)
            feed_low[1, at, pl.ds(h * FEED, FEED)] = from_chip[at, f].astype(f32)

    ours = pl.ds(pl.multiple_of(c * 40, 8), 40)
    for_core = pl.ds(pl.multiple_of((1 - c) * 40, 8), 40)
    half = pl.ds(pl.multiple_of(c * 2 * ATTN, 128), 2 * ATTN)
    last = [remote(attn_low.at[for_core], attn_ref.at[:, half], esend.at[1], erecv.at[1], core)]
    keep = [pltpu.make_async_copy(attn_low.at[ours], attn_ref.at[:, half], here.at[0])]
    for k, source in enumerate((zl * 2 + c, (1 - zl) * 2 + c)):
        last.append(
            remote(feed_low.at[k, for_core], feed_ref.at[source], esend.at[2 + k], erecv.at[2 + k], core)
        )
        keep.append(pltpu.make_async_copy(feed_low.at[k, ours], feed_ref.at[source], here.at[1 + k]))
    for copy in (*last, *keep):
        copy.start()
    for copy in (*last, *keep):
        copy.wait()
    for copy in started:
        copy.wait_send()
    for q in range(4):
        for copy in load(q, 0, True):
            copy.wait_send()


def plane_sum(a, o, f, cid):
    low, dma = jnp.bfloat16, pltpu.SemaphoreType.DMA
    return pl.pallas_call(
        plane_sum_kernel,
        out_shape=[
            jax.ShapeDtypeStruct((40, 4 * ATTN), jnp.float32),
            jax.ShapeDtypeStruct((4, 40, 2 * FEED), jnp.float32),
        ],
        in_specs=[pl.BlockSpec(memory_space=pl.ANY)] * 3,
        out_specs=[pl.BlockSpec(memory_space=pltpu.VMEM)] * 2,
        scratch_shapes=[
            pltpu.VMEM((2560, 2 * WIDE), low),
            pltpu.VMEM((2560, 2 * ATTN), low),
            pltpu.VMEM((2, 5, 2, 80, WIDE), low),
            pltpu.VMEM((2, 5, 2, 160, WIDE), low),
            pltpu.VMEM((80, 2 * WIDE), low),
            pltpu.VMEM((80, 2 * ATTN), jnp.float32),
            pltpu.VMEM((2, 80, 2 * FEED), jnp.float32),
            dma((20,)),
            dma((12,)),
            dma((12,)),
            dma((40,)),
            dma((40,)),
            dma((4,)),
            dma((4,)),
        ],
        compiler_params=pltpu.CompilerParams(
            collective_id=cid, has_side_effects=True, vmem_limit_bytes=48 * 2**20
        ),
    )(a, o, f)


def rms_norm(values, gain_row):
    return (
        values * lax.rsqrt(jnp.mean(values * values, axis=-1, keepdims=True) + norm_eps) * gain_row
    )


def geglu(gate_part, up_part):
    return jax.nn.gelu(gate_part) * up_part


def tables():
    half_rot = ROT // 2
    rates = jnp.exp(jnp.arange(half_rot, dtype=jnp.float32) * (-2.0 * math.log(10000.0) / ROT))
    angles = jnp.arange(SEQ_LEN, dtype=jnp.float32)[:, None] * rates[None, :]
    return (jnp.cos(angles), jnp.sin(angles))


def rotate(field, cosine, sine):
    half_rot = ROT // 2
    first = field[..., :half_rot]
    second = field[..., half_rot:ROT]
    return jnp.concatenate(
        [first * cosine - second * sine, second * cosine + first * sine, field[..., ROT:]], axis=-1
    )


def contract(left, right, left_dim, right_dim):
    return lax.dot_general(
        left, right, (((left_dim,), (right_dim,)), ((), ())), preferred_element_type=jnp.float32
    )


def padded(weight):
    return jnp.pad(weight.reshape(40, 4, 960), ((0, 0), (0, 0), (0, 64)))


def scattered(value):
    return lax.psum_scatter(value.astype(jnp.bfloat16), PLANE, scatter_dimension=0, tiled=True)


def joined(slices):
    return slices[:, :, :960].transpose(1, 0, 2).reshape(40, 3840).astype(jnp.float32)


def local(
    tokens,
    attn_gain,
    query_weight,
    kv_weight,
    out_weight,
    mlp_gain,
    gate_weight,
    up_weight,
    down_weight,
    cotangent,
):
    low = jnp.bfloat16
    rows = tokens.shape[0]
    seqs = rows // SEQ_LEN
    heads_here = query_weight.shape[1] // HEAD_DIM
    wide = heads_here * HEAD_DIM
    scale = HEAD_DIM ** (-0.5)
    cosine, sine = tables()
    positions = jnp.arange(SEQ_LEN)
    keep_mask = (positions[:, None] >= positions[None, :]) & (
        positions[:, None] - positions[None, :] < WINDOW
    )
    attn = jnp.concatenate([query_weight, kv_weight, out_weight.T], axis=1)
    attn = attn.reshape(40, 2, 2, ATTN).transpose(1, 2, 0, 3)
    attn = jnp.broadcast_to(attn, (2, *attn.shape)).reshape(4, 2, 40, ATTN)
    gains = jnp.stack([attn_gain, mlp_gain], axis=1)[:, None, :]
    gains = jnp.pad(jnp.broadcast_to(gains, (40, 4, 2)), ((0, 0), (0, 0), (960, 62)))
    down = (padded(down_weight.T) + gains).reshape(40, 4, 2, FEED).transpose(1, 2, 0, 3)
    first = jnp.concatenate([attn, down], axis=3).reshape(4, 80, WIDE)
    second = jnp.stack([padded(gate_weight), padded(up_weight)], axis=0)
    second = second.transpose(2, 0, 1, 3).reshape(4, 80, 2 * FEED)
    first, second = group_exchange([first, second], 5)
    first = first.reshape(4, 2, 40, WIDE).transpose(1, 0, 2, 3).reshape(2, 160, WIDE)
    second = second.reshape(4, 2, 40, 2 * FEED).transpose(0, 2, 1, 3).reshape(160, 4 * FEED)
    w_gate_up = lax.all_gather(second, PLANE, axis=0, tiled=True)
    dy_here = permuted(cotangent)
    w_attn, w_down_t, dy = plane_gather(first, dy_here, 6)
    dy = dy.reshape(4 * rows, -1)
    w_query, w_kv, w_out_t = (
        w_attn[:, :wide],
        w_attn[:, wide : wide + 2 * HEAD_DIM],
        w_attn[:, wide + 2 * HEAD_DIM :],
    )
    chosen = jnp.zeros((16, 2 * FEED), low).at[0, 960].set(1).at[1, 961].set(1)
    gain_rows = contract(chosen[:, 896:], w_down_t[:, 896:], 1, 1)
    gain_one, gain_two = gain_rows[0], gain_rows[1]

    x_in = permuted(tokens).astype(jnp.float32)
    xn_one = rms_norm(x_in, gain_one).astype(low)
    q_pre = jnp.dot(xn_one, w_query, preferred_element_type=jnp.float32)
    kv_pre = jnp.dot(xn_one, w_kv, preferred_element_type=jnp.float32)
    queries = rotate(
        q_pre.reshape(seqs, SEQ_LEN, heads_here, HEAD_DIM), cosine[:, None, :], sine[:, None, :]
    ).astype(low)
    key_rot = rotate(kv_pre[:, :HEAD_DIM].reshape(seqs, SEQ_LEN, HEAD_DIM), cosine, sine).astype(low)
    value_rows = kv_pre[:, HEAD_DIM:].reshape(seqs, SEQ_LEN, HEAD_DIM).astype(low)

    def score_rows():
        raw = (
            jnp.einsum("sqhd,skd->shqk", queries, key_rot, preferred_element_type=jnp.float32)
            * scale
        )
        return jnp.where(keep_mask, raw, -1e30)

    scores = score_rows()
    row_max = jnp.max(scores, axis=-1, keepdims=True)
    log_total = row_max + jnp.log(jnp.sum(jnp.exp(scores - row_max), axis=-1, keepdims=True))
    attn_probs = jnp.exp(scores - log_total).astype(low)
    mixed_heads = jnp.einsum(
        "shqk,skd->sqhd", attn_probs, value_rows, preferred_element_type=jnp.float32
    )
    mixed_heads = mixed_heads.reshape(rows, wide).astype(low)
    x_mid = x_in + pair_sum(contract(mixed_heads, w_out_t, 1, 1).astype(low), 1)

    xn_two = rms_norm(x_mid, gain_two).astype(low)
    xn_all = token_gather(xn_two, 2).reshape(4 * rows, -1)
    gate_up = jnp.dot(xn_all, w_gate_up, preferred_element_type=jnp.float32)
    gate_pre, up_pre = gate_up[:, : 2 * FEED], gate_up[:, 2 * FEED :]
    hidden = geglu(gate_pre, up_pre).astype(low)
    down_part = contract(hidden, w_down_t, 1, 1).astype(low)
    d_down_t = contract(dy, hidden, 0, 0)
    d_hidden = jnp.dot(dy, w_down_t, preferred_element_type=jnp.float32)
    geglu_pull = jax.vjp(geglu, gate_pre, up_pre)[1]
    d_gate_pre, d_up_pre = geglu_pull(d_hidden)
    d_gate_low = d_gate_pre.astype(low)
    d_up_low = d_up_pre.astype(low)
    d_xn_two_part = contract(jnp.concatenate([d_gate_low, d_up_low], axis=1), w_gate_up, 1, 1)
    d_xn_two = token_sum(d_xn_two_part.astype(low).reshape(4, rows, -1), 3)
    down_branch = token_sum(down_part.reshape(4, rows, -1), 3)
    block_out = restored((x_mid + down_branch).astype(low))
    d_gate_w = contract(xn_all, d_gate_low, 0, 0)
    sent = jnp.stack([scattered(d_down_t), scattered(d_gate_w)], axis=0)

    norm_two_pull = jax.vjp(rms_norm, x_mid, gain_two)[1]
    d_mid_norm, d_gain_two = norm_two_pull(d_xn_two)
    d_mid = dy_here.astype(jnp.float32) + d_mid_norm
    d_mid_low = d_mid.astype(low)
    d_out_t = contract(d_mid_low, mixed_heads, 0, 0)
    d_mixed = (
        jnp.dot(d_mid_low, w_out_t, preferred_element_type=jnp.float32)
        .astype(low)
        .reshape(seqs, SEQ_LEN, heads_here, HEAD_DIM)
    )
    soft_rows = jnp.exp(score_rows() - log_total)
    d_probs = jnp.einsum("sqhd,skd->shqk", d_mixed, value_rows, preferred_element_type=jnp.float32)
    d_scores = (
        soft_rows * (d_probs - jnp.sum(soft_rows * d_probs, axis=-1, keepdims=True))
    ).astype(low)
    d_queries = (
        jnp.einsum("shqk,skd->sqhd", d_scores, key_rot, preferred_element_type=jnp.float32) * scale
    )
    d_keys = (
        jnp.einsum("shqk,sqhd->skd", d_scores, queries, preferred_element_type=jnp.float32) * scale
    )
    d_values = jnp.einsum("shqk,sqhd->skd", attn_probs, d_mixed, preferred_element_type=jnp.float32)
    d_q_pre = (
        rotate(d_queries, cosine[:, None, :], -sine[:, None, :]).reshape(rows, wide).astype(low)
    )
    d_k_pre = rotate(d_keys, cosine, -sine).reshape(rows, HEAD_DIM)
    d_kv_part = jnp.concatenate([d_k_pre, d_values.reshape(rows, HEAD_DIM)], axis=-1)
    d_xn_one_part = contract(d_q_pre, w_query, 1, 1)
    sums = pair_sum(jnp.concatenate([d_xn_one_part.astype(low), d_kv_part.astype(low)], axis=1), 4)
    d_xn_one_q, d_kv_low = sums[:, : x_in.shape[1]], sums[:, x_in.shape[1] :].astype(low)
    d_q_kv_w = contract(xn_one, jnp.concatenate([d_q_pre, d_kv_low], axis=1), 0, 0).astype(low)
    d_xn_one = d_xn_one_q + contract(d_kv_low, w_kv, 1, 1)
    norm_one_pull = jax.vjp(rms_norm, x_in, gain_one)[1]
    d_in_norm, d_gain_one = norm_one_pull(d_xn_one)
    tokens_grad = restored((d_mid + d_in_norm).astype(low))
    d_gains = jnp.pad(jnp.stack([d_gain_one, d_gain_two], axis=0).astype(low), ((0, 14), (0, 0)))
    d_up_w = contract(
        jnp.concatenate([xn_all, d_gains], axis=0),
        jnp.concatenate([d_up_low, chosen], axis=0),
        0,
        0,
    ).astype(low)
    attn_out, up_out = plane_sum(d_q_kv_w, d_out_t.astype(low), d_up_w, 7)
    sent = sent.reshape(2, 4, 40, 2 * FEED).transpose(1, 0, 2, 3).reshape(4, 80, 2 * FEED)
    sent = group_exchange([sent], 8)[0].reshape(4, 2, 40, 2 * FEED)
    gain_out = up_out[:, :, 960:962].sum(axis=0)
    return (
        block_out,
        tokens_grad,
        gain_out[:, 0],
        attn_out[:, :wide],
        attn_out[:, wide : wide + 2 * HEAD_DIM],
        attn_out[:, wide + 2 * HEAD_DIM :].T,
        gain_out[:, 1],
        joined(sent[:, 1]),
        joined(up_out),
        joined(sent[:, 0]).T,
    )


def solution(mesh):
    fine = Mesh(mesh.devices.reshape(4, 2, 4, 2, 2), AXES)
    dp = ("y", "zl", "x", "c")
    in_specs = (
        P(dp, None),
        P(dp),
        P(dp, "zh"),
        P(dp, None),
        P("zh", dp),
        P(dp),
        P(dp, "zh"),
        P(dp, "zh"),
        P("zh", dp),
        P(dp, None),
    )
    out_specs = (
        P(dp, None),
        P(dp, None),
        P(dp),
        P(dp, "zh"),
        P(dp, None),
        P("zh", dp),
        P(dp),
        P(dp, "zh"),
        P(dp, "zh"),
        P("zh", dp),
    )
    return jax.shard_map(local, mesh=fine, in_specs=in_specs, out_specs=out_specs, check_vma=False)
```

```python
import math

import jax
import jax.numpy as jnp
import numpy as np
from jax import lax
from jax.experimental import pallas as pl
from jax.experimental.pallas import tpu as pltpu
from jax.sharding import Mesh
from jax.sharding import PartitionSpec as P

HEAD_DIM = 256
WINDOW = 2048
SEQ_LEN = 128
ROT = 128
AXES = ("y", "zl", "x", "c", "zh")
PLANE = ("y", "x")
GROUP = ("zl", "c")
OWNERS = ("y", "x", "zl", "c")
MESH = pl.DeviceIdType.MESH

norm_eps = 1e-06


def feature_order():
    place = np.arange(640).reshape(2, 4, 80).transpose(1, 0, 2).reshape(640)
    return (np.arange(640)[:, None] == place[None, :]).astype(np.float32)


def reorder(src, order, dst, back):
    for k in range(4):
        group = pl.ds(k * 640, 640)
        dst[:, group] = lax.dot_general(
            src[:, group],
            order[...],
            (((1,), (1 if back else 0,)), ((), ())),
            preferred_element_type=jnp.float32,
        ).astype(dst.dtype)


def greet(peers):
    barrier = pltpu.get_barrier_semaphore()
    for peer in peers:
        pl.semaphore_signal(barrier, inc=1, device_id=peer, device_id_type=MESH)
    pl.semaphore_wait(barrier, len(peers))


def remote(src, dst, send, recv, peer):
    return pltpu.make_async_remote_copy(
        src_ref=src, dst_ref=dst, send_sem=send, recv_sem=recv, device_id=peer, device_id_type=MESH
    )


def sum_kernel(p_ref, o_ref, from_core, other, from_chips, own, own_low, from_far, send, recv):
    zl, c, zh = lax.axis_index("zl"), lax.axis_index("c"), lax.axis_index("zh")
    rows = p_ref.shape[1]
    half = rows // 2
    core, far = {"c": 1 - c}, {"zh": 1 - zh}
    chips = [{"zl": 1 - zl, "zh": k} for k in range(2)]
    greet([core, far, *chips])
    order = [1 - zl, zl]
    cores = [
        remote(p_ref.at[z * 2 + 1 - c], from_core.at[i], send.at[i], recv.at[i], core)
        for i, z in enumerate(order)
    ]
    for copy in cores:
        copy.start()
    step = 16
    cores[0].wait_recv()
    aways = []
    for k in range(2):

        @pl.loop(0, half // step)
        def _(j, k=k):
            at = pl.ds(pl.multiple_of(k * half + j * step, step), step)
            total = p_ref[(1 - zl) * 2 + c, at].astype(jnp.float32) + from_core[0, at].astype(jnp.float32)
            other[at] = total.astype(jnp.bfloat16)

        away = remote(
            other.at[pl.ds(k * half, half)], from_chips.at[zh], send.at[2 + k], recv.at[2 + zh], chips[k]
        )
        away.start()
        aways.append(away)
    cores[1].wait_recv()
    fars = []
    for k in range(2):
        piece = (1 - zh) if k == 0 else zh
        if k == 1:
            for i in range(2):
                remote(
                    other.at[pl.ds(0, half)], from_chips.at[i], send.at[2 + i], recv.at[2 + i], chips[i]
                ).wait_recv()

        @pl.loop(0, half // step)
        def _(j, k=k, piece=piece):
            at = pl.ds(pl.multiple_of(piece * half + j * step, step), step)
            total = p_ref[zl * 2 + c, at].astype(jnp.float32) + from_core[1, at].astype(jnp.float32)
            if k == 1:
                here = pl.ds(pl.multiple_of(j * step, step), step)
                total += from_chips[0, here].astype(jnp.float32) + from_chips[1, here].astype(jnp.float32)
            own[at] = total.astype(jnp.bfloat16)

        at = pl.ds(pl.multiple_of(piece * half, half), half)
        copy = remote(own.at[at], from_far.at[at], send.at[4 + k], recv.at[4 + k], far)
        copy.start()
        fars.append(copy)
    for k in range(2):
        fars[k].wait_recv()
        piece = zh if k == 0 else (1 - zh)

        @pl.loop(0, half // step)
        def _(j, piece=piece):
            at = pl.ds(pl.multiple_of(piece * half + j * step, step), step)
            o_ref[at] = own[at].astype(jnp.float32) + from_far[at].astype(jnp.float32)

    for copy in (*cores, *aways, *fars):
        copy.wait_send()


def token_sum(p, cid):
    rows, width = p.shape[1:]
    low = jnp.bfloat16
    return pl.pallas_call(
        sum_kernel,
        out_shape=jax.ShapeDtypeStruct((rows, width), jnp.float32),
        in_specs=[pl.BlockSpec(memory_space=pltpu.VMEM)],
        out_specs=pl.BlockSpec(memory_space=pltpu.VMEM),
        scratch_shapes=[
            pltpu.VMEM((2, rows, width), low),
            pltpu.VMEM((rows, width), low),
            pltpu.VMEM((2, rows // 2, width), low),
            pltpu.VMEM((rows, width), low),
            pltpu.VMEM((rows, width), low),
            pltpu.VMEM((rows, width), low),
            pltpu.SemaphoreType.DMA((6,)),
            pltpu.SemaphoreType.DMA((6,)),
        ],
        compiler_params=pltpu.CompilerParams(
            collective_id=cid, has_side_effects=True, vmem_limit_bytes=32 * 2**20
        ),
    )(p)


def pair_kernel(p_ref, o_ref, landed, send, recv):
    far = {"zh": 1 - lax.axis_index("zh")}
    rows = p_ref.shape[0]
    greet([far])
    copy = remote(p_ref, landed, send, recv, far)
    copy.start()
    copy.wait()
    step = 16

    @pl.loop(0, rows // step)
    def _(j):
        at = pl.ds(pl.multiple_of(j * step, step), step)
        o_ref[at] = p_ref[at].astype(jnp.float32) + landed[at].astype(jnp.float32)


def pair_sum(p, cid):
    return pl.pallas_call(
        pair_kernel,
        out_shape=jax.ShapeDtypeStruct(p.shape, jnp.float32),
        in_specs=[pl.BlockSpec(memory_space=pltpu.VMEM)],
        out_specs=pl.BlockSpec(memory_space=pltpu.VMEM),
        scratch_shapes=[
            pltpu.VMEM(p.shape, p.dtype),
            pltpu.SemaphoreType.DMA,
            pltpu.SemaphoreType.DMA,
        ],
        compiler_params=pltpu.CompilerParams(
            collective_id=cid, has_side_effects=True, vmem_limit_bytes=32 * 2**20
        ),
    )(p)


def ring_of(axis, at):
    return {axis: lax.rem(at + 3, 4)}, {axis: lax.rem(at + 1, 4)}


def block_rows(row, column, start=0, size=160):
    return pl.ds(pl.multiple_of((row * 4 + column) * 160 + start, 16), size)


def send_blocks(ins, outs, here, send, recv):
    zl, c = lax.axis_index("zl"), lax.axis_index("c")
    mine = zl * 2 + c
    peers = [({"zl": 1 - zl, "c": k}, (1 - zl) * 2 + k) for k in range(2)]
    peers.append(({"c": 1 - c}, zl * 2 + 1 - c))
    n = len(ins)
    copies, keeps = [], []
    for i in range(n):
        for k, (peer, block) in enumerate(peers):
            landing = i * 3 + (c if k < 2 else 2)
            copy = remote(ins[i].at[block], outs[i].at[mine], send.at[i * 3 + k], recv.at[landing], peer)
            copy.start()
            copies.append(copy)
    for i in range(n):
        keep = pltpu.make_async_copy(ins[i].at[mine], outs[i].at[mine], here.at[i])
        keep.start()
        keeps.append(keep)

    def finish():
        for keep in keeps:
            keep.wait()
        for i in range(n):
            for k, (peer, block) in enumerate(peers):
                remote(
                    ins[i].at[block], outs[i].at[block], send.at[i * 3 + k], recv.at[i * 3 + k], peer
                ).wait_recv()
        for copy in copies:
            copy.wait_send()

    return finish


def group_peers():
    zl, c = lax.axis_index("zl"), lax.axis_index("c")
    return [{"c": 1 - c}, {"zl": 1 - zl, "c": 0}, {"zl": 1 - zl, "c": 1}]


def exchange_kernel(
    a_ref, g_ref, s_ref, tok_ref, cot_ref, order_ref, ao_ref, go_ref, so_ref, x_ref, dy_ref, here, send, recv
):
    greet(group_peers())
    finish = send_blocks([a_ref, g_ref, s_ref], [ao_ref, go_ref, so_ref], here, send, recv)
    reorder(tok_ref, order_ref, x_ref, False)
    reorder(cot_ref, order_ref, dy_ref, False)
    finish()


def group_exchange(arrays, tokens, cotangent, order, cid):
    n = len(arrays)
    like = lambda a, kind: jax.ShapeDtypeStruct(a.shape, kind)
    anywhere, vmem = pl.BlockSpec(memory_space=pl.ANY), pl.BlockSpec(memory_space=pltpu.VMEM)
    return pl.pallas_call(
        exchange_kernel,
        out_shape=[
            *(like(a, a.dtype) for a in arrays),
            like(tokens, jnp.float32),
            like(cotangent, jnp.bfloat16),
        ],
        in_specs=[anywhere] * n + [vmem] * 3,
        out_specs=[anywhere] * n + [vmem] * 2,
        scratch_shapes=[
            pltpu.SemaphoreType.DMA((n,)),
            pltpu.SemaphoreType.DMA((3 * n,)),
            pltpu.SemaphoreType.DMA((3 * n,)),
        ],
        compiler_params=pltpu.CompilerParams(
            collective_id=cid, has_side_effects=True, vmem_limit_bytes=32 * 2**20
        ),
    )(*arrays, tokens, cotangent, order)


ATTN, FEED = 768, 512
WIDE = ATTN + FEED


def shift(i, by):
    return lax.rem(i + by, 4)


def around(h, y, x):
    if h == 0:
        return x, ring_of("x", x), y, ring_of("y", y)
    return y, ring_of("y", y), x, ring_of("x", x)


class Piece:
    def __init__(self, h, source, target, columns, rows=160):
        self.h, self.source, self.target, self.columns, self.rows = h, source, target, columns, rows

    def own(self):
        return self.source

    def at(self, i1, i2, part=None):
        row, column = (i2, i1) if self.h == 0 else (i1, i2)
        size = self.rows if part is None else self.rows // 2
        first = (row * 4 + column) * self.rows + (0 if part is None else part * size)
        return self.target.at[pl.ds(pl.multiple_of(first, 16), size), self.columns]


def gather_steps(y, x, pieces, send, recv, cross):
    started = []

    def go(src, dst, n, ring, slot, peer):
        k = (n * 5 + ring) * 4 + slot
        copy = remote(src, dst, send.at[k], recv.at[k], peer)
        copy.start()
        started.append(copy)

    def arrived(dst, n, ring, slot):
        k = (n * 5 + ring) * 4 + slot
        remote(dst, dst, send.at[k], recv.at[k], {"c": 1 - lax.axis_index("c")}).wait_recv()

    each = [(n, p, *around(p.h, y, x)) for n, p in enumerate(pieces)]
    firsts = ((1, 0), (2, 3), (3, 1), (4, 2))

    def own_blocks():
        for n, p, i1, (back1, ahead1), i2, _ in each:
            go(p.own(), p.at(i1, i2), n, 0, 0, ahead1)
            go(p.own(), p.at(i1, i2), n, 0, 1, back1)
        for n, p, i1, _, i2, (back2, ahead2) in each:
            go(p.own(), p.at(i1, i2), n, 1, 0, ahead2)
            go(p.own(), p.at(i1, i2), n, 1, 1, back2)
            cross(n, p.own(), p.at(i1, i2))

    def first_axis():
        for n, p, i1, (back1, ahead1), i2, (back2, ahead2) in each:
            left, right = p.at(shift(i1, 3), i2), p.at(shift(i1, 1), i2)
            arrived(left, n, 0, 0)
            low = p.at(shift(i1, 3), i2, 0)
            go(low, low, n, 0, 2, ahead1)
            arrived(right, n, 0, 1)
            high = p.at(shift(i1, 1), i2, 1)
            go(high, high, n, 0, 3, back1)
            for ring, ref in ((2, left), (3, right)):
                go(ref, ref, n, ring, 0, ahead2)
                go(ref, ref, n, ring, 1, back2)
                cross(n, ref, ref)
        for n, p, i1, _, i2, (back2, ahead2) in each:
            far = shift(i1, 2)
            arrived(p.at(far, i2, 0), n, 0, 2)
            arrived(p.at(far, i2, 1), n, 0, 3)
            ref = p.at(far, i2)
            go(ref, ref, n, 4, 0, ahead2)
            go(ref, ref, n, 4, 1, back2)
            cross(n, ref, ref)

    def second_axis():
        for ring, by in firsts:
            for n, p, i1, _, i2, (back2, ahead2) in each:
                j = shift(i1, by)
                left, right = p.at(j, shift(i2, 3)), p.at(j, shift(i2, 1))
                arrived(left, n, ring, 0)
                low = p.at(j, shift(i2, 3), 0)
                go(low, low, n, ring, 2, ahead2)
                cross(n, left, left)
                arrived(right, n, ring, 1)
                high = p.at(j, shift(i2, 1), 1)
                go(high, high, n, ring, 3, back2)
                cross(n, right, right)

    def last():
        for ring, by in firsts:
            for n, p, i1, _, i2, _ in each:
                j, far = shift(i1, by), shift(i2, 2)
                arrived(p.at(j, far, 0), n, ring, 2)
                arrived(p.at(j, far, 1), n, ring, 3)
                cross(n, p.at(j, far), p.at(j, far))
        for copy in started:
            copy.wait_send()

    return own_blocks, first_axis, second_axis, last


def attention_gather_kernel(
    in_ref, g_ref, dy_ref, d_ref, a_ref, o_ref, go_ref, all_ref, do_ref,
    here, send, recv, csend, crecv, dsend, drecv, xhere, xsend, xrecv,
):
    y, x, c = lax.axis_index("y"), lax.axis_index("x"), lax.axis_index("c")
    zl, zh = lax.axis_index("zl"), lax.axis_index("zh")
    core = {"c": 1 - c}
    chips = [{"zl": 1 - zl, "zh": k} for k in range(2)]
    greet([*ring_of("x", x), *ring_of("y", y), core, *chips, {"zl": 1 - zl, "c": 1 - c}])
    whole = pl.ds(0, 160)

    for side in range(2):

        @pl.when(c == side)
        def _(side=side):
            sources = [
                in_ref.at[0, whole, pl.ds(0, 256)],
                in_ref.at[0, whole, pl.ds(256, 512)],
                in_ref.at[1, whole, pl.ds(0, 768)],
                g_ref,
            ]
            if side == 0:
                targets = [(a_ref, 0, 256), (a_ref, 256, 512), (a_ref, 768, 768)]
            else:
                targets = [(a_ref, 1536, 256), (o_ref, 0, 512), (o_ref, 512, 768)]
            targets.append((go_ref, 0, 128))
            pieces = [
                Piece(h, source, ref, pl.ds(first, width), rows)
                for h, source, (ref, first, width), rows in zip((0, 0, 1, 0), sources, targets, (160, 160, 160, 64))
            ]
            crossed = []

            def cross(n, src, dst):
                if n < 3:
                    k = len(crossed)
                    copy = remote(src, dst, csend.at[k], crecv.at[k], core)
                    copy.start()
                    crossed.append(copy)

            own_blocks, first_axis, second_axis, last = gather_steps(y, x, pieces, send, recv, cross)
            own_blocks()
            keeps = []
            for n, p in enumerate(pieces):
                i1, _, i2, _ = around(p.h, y, x)
                keeps.append(pltpu.make_async_copy(p.own(), p.at(i1, i2), here.at[n]))
                keeps[-1].start()
            finish = send_blocks([d_ref], [do_ref], xhere, xsend, xrecv)
            half = dy_ref.shape[0] // 2
            mine, other = zl * 2 + c, (1 - zl) * 2 + c
            part = pl.ds(pl.multiple_of(zh * half, half), half)
            away = [
                remote(dy_ref.at[part], all_ref.at[mine, part], dsend.at[k], drecv.at[zh], chips[k])
                for k in range(2)
            ]
            across = remote(dy_ref, all_ref.at[mine], dsend.at[2], drecv.at[2], core)
            for copy in (*away, across):
                copy.start()
            keeps.append(pltpu.make_async_copy(dy_ref, all_ref.at[mine], here.at[4]))
            keeps[-1].start()
            first_axis()
            second_axis()
            passed = []
            for k in range(2):
                rows = pl.ds(k * half, half)
                there = all_ref.at[other, rows]
                remote(dy_ref.at[rows], there, dsend.at[k], drecv.at[k], chips[k]).wait_recv()
                passed.append(remote(there, there, dsend.at[3 + k], drecv.at[3 + k], core))
                passed[-1].start()
            last()
            for copy in (*crossed, *passed, across):
                copy.wait()
            for copy in away:
                copy.wait_send()
            for keep in keeps:
                keep.wait()
            finish()


def attention_gather(own, gains, dy, down, cid):
    kind, dma = jnp.bfloat16, pltpu.SemaphoreType.DMA
    return pl.pallas_call(
        attention_gather_kernel,
        out_shape=[
            jax.ShapeDtypeStruct((2560, 1792), kind),
            jax.ShapeDtypeStruct((2560, 1280), kind),
            jax.ShapeDtypeStruct((1024, 128), kind),
            jax.ShapeDtypeStruct((4, *dy.shape), kind),
            jax.ShapeDtypeStruct(down.shape, kind),
        ],
        in_specs=[pl.BlockSpec(memory_space=pl.ANY)] * 4,
        out_specs=[pl.BlockSpec(memory_space=pl.ANY)] * 5,
        scratch_shapes=[
            dma((5,)),
            dma((80,)),
            dma((80,)),
            dma((48,)),
            dma((48,)),
            dma((5,)),
            dma((5,)),
            dma((1,)),
            dma((3,)),
            dma((3,)),
        ],
        compiler_params=pltpu.CompilerParams(collective_id=cid, has_side_effects=True),
    )(own, gains, dy, down)


def middle_kernel(
    p_ref, x_ref, g_ref, d_ref, mid_ref, all_ref, w_ref, landed, here, psend, precv, gsend, grecv, send, recv
):
    y, x, c = lax.axis_index("y"), lax.axis_index("x"), lax.axis_index("c")
    zl, zh = lax.axis_index("zl"), lax.axis_index("zh")
    core, far = {"c": 1 - c}, {"zh": 1 - zh}
    chips = [{"zl": 1 - zl, "zh": k} for k in range(2)]
    greet([*ring_of("x", x), *ring_of("y", y), core, far, *chips])
    half, step = p_ref.shape[0] // 2, 16
    mine, other = zl * 2 + c, (1 - zl) * 2 + c
    parts = [pl.ds(pl.multiple_of(k * half, half), half) for k in (1 - zh, zh)]
    pair = [
        remote(p_ref.at[part], landed.at[part], psend.at[k], precv.at[k], far)
        for k, part in enumerate(parts)
    ]
    for copy in pair:
        copy.start()
    pieces = [
        Piece(h, d_ref.at[h, pl.ds(0, 160)], w_ref, pl.ds(h * FEED, FEED)) for h in range(2)
    ]
    own_blocks, first_axis, second_axis, last = gather_steps(
        y, x, pieces, send, recv, lambda n, src, dst: None
    )
    own_blocks()
    keeps = []
    for n, p in enumerate(pieces):
        i1, _, i2, _ = around(p.h, y, x)
        keeps.append(pltpu.make_async_copy(p.own(), p.at(i1, i2), here.at[n]))
        keeps[-1].start()
    away, across = [], []
    for k in range(2):
        part = parts[1 - k]
        pair[k].wait_recv()
        first = (zh if k == 0 else 1 - zh) * half

        @pl.loop(0, half // step)
        def _(i, first=first):
            at = pl.ds(pl.multiple_of(first + i * step, step), step)
            branch = p_ref[at].astype(jnp.float32) + landed[at].astype(jnp.float32)
            v = x_ref[at] + branch
            mid_ref[at] = v
            r = lax.rsqrt(jnp.mean(v * v, axis=-1, keepdims=True) + norm_eps)
            all_ref[mine, at] = (v * r * g_ref[...]).astype(jnp.bfloat16)

        rows = all_ref.at[mine, part]
        if k == 0:
            for i in range(2):
                away.append(remote(rows, rows, gsend.at[i], grecv.at[zh], chips[i]))
                away[-1].start()
        across.append(remote(rows, rows, gsend.at[2 + k], grecv.at[2 + k], core))
        across[-1].start()
        if k == 0:
            first_axis()
    second_axis()
    passed = []
    for k in range(2):
        there = all_ref.at[other, pl.ds(k * half, half)]
        remote(there, there, gsend.at[k], grecv.at[k], chips[k]).wait_recv()
        passed.append(remote(there, there, gsend.at[4 + k], grecv.at[4 + k], core))
        passed[-1].start()
    last()
    for copy in (*across, *passed):
        copy.wait()
    for copy in (*away, *pair):
        copy.wait_send()
    for keep in keeps:
        keep.wait()


def middle(p, x, gain, down, cid):
    dma = pltpu.SemaphoreType.DMA
    anywhere, vmem = pl.BlockSpec(memory_space=pl.ANY), pl.BlockSpec(memory_space=pltpu.VMEM)
    return pl.pallas_call(
        middle_kernel,
        out_shape=[
            jax.ShapeDtypeStruct(x.shape, jnp.float32),
            jax.ShapeDtypeStruct((4, *x.shape), jnp.bfloat16),
            jax.ShapeDtypeStruct((2560, 2 * FEED), jnp.bfloat16),
        ],
        in_specs=[vmem, vmem, vmem, anywhere],
        out_specs=[vmem, vmem, anywhere],
        scratch_shapes=[
            pltpu.VMEM(p.shape, p.dtype),
            dma((2,)),
            dma((2,)),
            dma((2,)),
            dma((6,)),
            dma((6,)),
            dma((40,)),
            dma((40,)),
        ],
        compiler_params=pltpu.CompilerParams(
            collective_id=cid, has_side_effects=True, vmem_limit_bytes=32 * 2**20
        ),
    )(p, x, gain, down)


SEGMENTS = ((0, 0, 256), (256, 256, 512), (WIDE, 768, 768))


def plane_sum_kernel(
    a_ref, o_ref, f_ref, s_ref, p_ref, t_ref, x_ref, mid_ref, dmid_ref, g_ref, order_ref,
    attn_ref, feed_ref, so_ref, block_ref, grad_ref,
    sums, from_core, via, main, from_chip, attn_low, feed_low, gains,
    t_core, t_other, t_chips, t_own, t_far, landed, block_low, grad_low,
    here, csend, crecv, send, recv, esend, erecv, tsend, trecv, shere, ssend, srecv,
):
    y, x, c, zl, zh = (lax.axis_index(k) for k in ("y", "x", "c", "zl", "zh"))
    core, chip, far_peer = {"c": 1 - c}, {"zl": 1 - zl}, {"zh": 1 - zh}
    diagonal = {"zl": 1 - zl, "zh": 1 - zh}
    chips = [{"zl": 1 - zl, "zh": k} for k in range(2)]
    greet(
        [
            *ring_of("x", x), *ring_of("y", y), core, chip, far_peer, diagonal,
            {"zl": 1 - zl, "c": 1 - c},
        ]
    )
    step = 16
    f32, low = jnp.float32, jnp.bfloat16

    order = (2, 1, 3, 0)

    def chunk(q):
        return pl.ds(pl.multiple_of(shift(y, order[q]) * 640, 640), 640)

    def load(q, side, remote_side):
        rows = chunk(q)
        if side == 0:
            parts = [a_ref.at[rows, pl.ds(0, 256)], a_ref.at[rows, pl.ds(256, 512)], a_ref.at[rows, pl.ds(768, 768)]]
        else:
            parts = [a_ref.at[rows, pl.ds(1536, 256)], o_ref.at[rows, pl.ds(0, 512)], o_ref.at[rows, pl.ds(512, 768)]]
        out = []
        for s, (at, landing, width) in enumerate(SEGMENTS):
            k = q * 3 + s
            if remote_side:
                out.append(
                    remote(parts[s], from_core.at[rows, pl.ds(landing, width)], csend.at[k], crecv.at[k], core)
                )
            else:
                out.append(pltpu.make_async_copy(parts[s], sums.at[rows, pl.ds(at, width)], here.at[k]))
        return out

    def feed_load(q):
        rows = chunk(q)
        return [
            pltpu.make_async_copy(
                f_ref.at[rows, pl.ds(h * FEED, FEED)],
                sums.at[rows, pl.ds(h * WIDE + ATTN, FEED)],
                here.at[12 + q * 2 + h],
            )
            for h in range(2)
        ]

    for side in range(2):

        @pl.when(c == side)
        def _(side=side):
            for q in range(4):
                for copy in load(q, 1 - side, True):
                    copy.start()
                for copy in load(q, side, False):
                    copy.start()

    for q in range(4):
        for copy in feed_load(q):
            copy.start()
    finish = send_blocks([s_ref], [so_ref], shere, ssend, srecv)
    pair = remote(t_ref, landed, tsend.at[6], trecv.at[6], far_peer)
    pair.start()
    tokens = p_ref.shape[1]
    half = tokens // 2
    t_cores = [
        remote(p_ref.at[z * 2 + 1 - c], t_core.at[i], tsend.at[i], trecv.at[i], core)
        for i, z in enumerate((1 - zl, zl))
    ]
    for copy in t_cores:
        copy.start()
    t_sent = []

    def tokens_to_chips():
        t_cores[0].wait_recv()

        @pl.loop(0, tokens // step)
        def _(i):
            at = pl.ds(pl.multiple_of(i * step, step), step)
            total = p_ref[(1 - zl) * 2 + c, at].astype(f32) + t_core[0, at].astype(f32)
            t_other[at] = total.astype(low)

        for k in range(2):
            t_sent.append(
                remote(t_other.at[pl.ds(k * half, half)], t_chips.at[zh], tsend.at[2 + k], trecv.at[2 + zh], chips[k])
            )
            t_sent[-1].start()

    def tokens_to_far(k):
        piece = (1 - zh) if k == 0 else zh
        if k == 0:
            t_cores[1].wait_recv()
        else:
            for i in range(2):
                remote(
                    t_other.at[pl.ds(0, half)], t_chips.at[i], tsend.at[2 + i], trecv.at[2 + i], chips[i]
                ).wait_recv()

        @pl.loop(0, half // step)
        def _(i):
            at = pl.ds(pl.multiple_of(piece * half + i * step, step), step)
            total = p_ref[zl * 2 + c, at].astype(f32) + t_core[1, at].astype(f32)
            if k == 1:
                there = pl.ds(pl.multiple_of(i * step, step), step)
                total += t_chips[0, there].astype(f32) + t_chips[1, there].astype(f32)
            t_own[at] = total.astype(low)

        at = pl.ds(pl.multiple_of(piece * half, half), half)
        t_sent.append(remote(t_own.at[at], t_far.at[at], tsend.at[4 + k], trecv.at[4 + k], far_peer))
        t_sent[-1].start()

    def tokens_gradient():
        pair.wait_recv()

        @pl.loop(0, tokens // step)
        def _(i):
            at = pl.ds(pl.multiple_of(i * step, step), step)
            d = (t_ref[at].astype(f32) + landed[at].astype(f32)) * g_ref[...]
            v = x_ref[at]
            r = lax.rsqrt(jnp.mean(v * v, axis=-1, keepdims=True) + norm_eps)
            n = v * r
            d = r * (d - n * jnp.mean(d * n, axis=-1, keepdims=True))
            grad_low[at] = (dmid_ref[at] + d).astype(low)

        reorder(grad_low, order_ref, grad_ref, True)

    def tokens_output():
        for k in range(2):
            t_sent[2 + k].wait_recv()

        @pl.loop(0, tokens // step)
        def _(i):
            at = pl.ds(pl.multiple_of(i * step, step), step)
            branch = t_own[at].astype(f32) + t_far[at].astype(f32)
            block_low[at] = (mid_ref[at] + branch).astype(low)

        reorder(block_low, order_ref, block_ref, True)

    def columns(h):
        return pl.ds(h * WIDE, WIDE)

    def rows_at(h, i1, i2, start=0, size=160):
        row, column = (i2, i1) if h == 0 else (i1, i2)
        return block_rows(row, column, start, size)

    def add(h, first, size, terms):
        @pl.loop(0, size // step)
        def _(i):
            at = pl.ds(pl.multiple_of(first + i * step, step), step)
            total = sums[at, columns(h)].astype(f32)
            for ref, index, start in terms:
                total += ref[(*index, pl.ds(pl.multiple_of(start + i * step, step), step))].astype(f32)
            sums[at, columns(h)] = total.astype(low)

    started = []

    def go(h, ring, slot, src, dst, peer):
        k = (h * 5 + ring) * 4 + slot
        copy = remote(src, dst, send.at[k], recv.at[k], peer)
        copy.start()
        started.append(copy)

    def arrived(h, ring, slot, dst):
        k = (h * 5 + ring) * 4 + slot
        remote(dst, dst, send.at[k], recv.at[k], core).wait_recv()

    def first_row(h, i1, i2):
        row, column = (i2, i1) if h == 0 else (i1, i2)
        return (row * 4 + column) * 160

    def out_via(h, ring, place, at, ring_peers):
        back, ahead = ring_peers
        far = shift(at, 2)
        go(h, ring, 0, sums.at[place(far, 0, 80), columns(h)], via.at[h, ring, 0], ahead)
        go(h, ring, 1, sums.at[place(far, 80, 80), columns(h)], via.at[h, ring, 1], back)

    def out_main(h, ring, place, first, at, ring_peers):
        back, ahead = ring_peers
        arrived(h, ring, 0, via.at[h, ring, 0])
        add(h, first(shift(at, 1)), 80, [(via, (h, ring, 0), 0)])
        go(h, ring, 2, sums.at[place(shift(at, 1), 0, 160), columns(h)], main.at[h, ring, 0], ahead)
        arrived(h, ring, 1, via.at[h, ring, 1])
        add(h, first(shift(at, 3)) + 80, 80, [(via, (h, ring, 1), 0)])
        go(h, ring, 3, sums.at[place(shift(at, 3), 0, 160), columns(h)], main.at[h, ring, 1], back)

    def take(h, ring, first, at):
        arrived(h, ring, 2, main.at[h, ring, 0])
        arrived(h, ring, 3, main.at[h, ring, 1])
        add(h, first(at), 160, [(main, (h, ring, 0), 0), (main, (h, ring, 1), 0)])

    def along_second(h, j):
        i1, _, i2, peers = around(h, y, x)
        fixed = shift(i1, order[j])
        return (
            lambda k, start, size: rows_at(h, fixed, k, start, size),
            lambda k: first_row(h, fixed, k),
            i2,
            peers,
        )

    def along_first(h):
        i1, peers, i2, _ = around(h, y, x)
        return (
            lambda k, start, size: rows_at(h, k, i2, start, size),
            lambda k: first_row(h, k, i2),
            i1,
            peers,
        )

    for q in range(4):
        for copy in load(q, 0, False):
            copy.wait()
        for copy in feed_load(q):
            copy.wait()
        for copy in load(q, 0, True):
            copy.wait_recv()
        top = shift(y, order[q]) * 640

        @pl.loop(0, 640 // step)
        def _(i, top=top):
            at = pl.ds(pl.multiple_of(top + i * step, step), step)
            for place, landing, width in SEGMENTS:
                total = sums[at, pl.ds(place, width)].astype(f32) + from_core[
                    at, pl.ds(landing, width)
                ].astype(f32)
                sums[at, pl.ds(place, width)] = total.astype(low)

        if q == 0:
            for j in range(4):
                place, first, at, peers = along_second(0, j)
                out_via(0, j, place, at, peers)
        place, first, at, peers = along_second(1, q)
        out_via(1, q, place, at, peers)
        if q > 0:
            place, first, at, peers = along_second(1, q - 1)
            out_main(1, q - 1, place, first, at, peers)
        if q == 1:
            tokens_to_chips()
        if q == 2:
            tokens_to_far(0)
    for j in range(4):
        place, first, at, peers = along_second(0, j)
        out_main(0, j, place, first, at, peers)
        if j == 0:
            place, first, at, peers = along_second(1, 3)
            out_main(1, 3, place, first, at, peers)
        if j == 1:
            tokens_to_far(1)
        if j == 3:
            tokens_gradient()
    for j in range(4):
        for h in (1, 0):
            place, first, at, peers = along_second(h, j)
            take(h, j, first, at)
            if j == 0:
                place, first, at, peers = along_first(h)
                out_via(h, 4, place, at, peers)
    for h in (1, 0):
        place, first, at, peers = along_first(h)
        out_main(h, 4, place, first, at, peers)
    tokens_output()
    for h in (1, 0):
        place, first, at, peers = along_first(h)
        take(h, 4, first, at)
    home = (y * 4 + x) * 160
    theirs = pl.ds(pl.multiple_of(home + (1 - zl) * 80, 16), 80)
    yours = pl.ds(pl.multiple_of(home + zl * 80, 16), 80)
    tile = pl.ds(2 * WIDE - 128, 128)
    away = [
        remote(sums.at[theirs], from_chip, esend.at[0], erecv.at[0], chip),
        remote(sums.at[yours, tile], gains.at[0], esend.at[4], erecv.at[4], far_peer),
        remote(sums.at[theirs, tile], gains.at[1], esend.at[5], erecv.at[5], diagonal),
    ]
    for copy in away:
        copy.start()
    finish()
    for copy in away:
        copy.wait()
    is_gain = lax.broadcasted_iota(jnp.int32, (step, 128), 1) >= 64

    @pl.loop(0, 80 // step)
    def _(i):
        here_at = pl.ds(pl.multiple_of(home + zl * 80 + i * step, step), step)
        at = pl.ds(pl.multiple_of(i * step, step), step)
        for h in range(2):
            a = pl.ds(h * WIDE, ATTN)
            attn_low[at, pl.ds(h * ATTN, ATTN)] = sums[here_at, a].astype(f32) + from_chip[at, a].astype(f32)
            f = pl.ds(h * WIDE + ATTN, FEED)
            feed_low[0, at, pl.ds(h * FEED, FEED)] = sums[here_at, f].astype(f32)
            feed_low[1, at, pl.ds(h * FEED, FEED)] = from_chip[at, f].astype(f32)
        end = pl.ds(2 * FEED - 128, 128)
        for k in range(2):
            v = feed_low[k, at, end]
            feed_low[k, at, end] = jnp.where(is_gain, v + gains[k, at].astype(f32), v)

    ours = pl.ds(pl.multiple_of(c * 40, 8), 40)
    for_core = pl.ds(pl.multiple_of((1 - c) * 40, 8), 40)
    half = pl.ds(pl.multiple_of(c * 2 * ATTN, 128), 2 * ATTN)
    last = [remote(attn_low.at[for_core], attn_ref.at[:, half], esend.at[1], erecv.at[1], core)]
    keep = [pltpu.make_async_copy(attn_low.at[ours], attn_ref.at[:, half], here.at[0])]
    for k, source in enumerate((zl * 2 + c, (1 - zl) * 2 + c)):
        last.append(
            remote(feed_low.at[k, for_core], feed_ref.at[source], esend.at[2 + k], erecv.at[2 + k], core)
        )
        keep.append(pltpu.make_async_copy(feed_low.at[k, ours], feed_ref.at[source], here.at[1 + k]))
    for copy in (*last, *keep):
        copy.start()
    for copy in (*last, *keep):
        copy.wait()
    for copy in (*started, pair, *t_cores, *t_sent):
        copy.wait_send()
    for q in range(4):
        for copy in load(q, 0, True):
            copy.wait_send()


def plane_sum(a, o, f, sent, down, d_xn, x, mid, d_mid, gain, order, cid):
    low, dma, f32 = jnp.bfloat16, pltpu.SemaphoreType.DMA, jnp.float32
    rows, width = x.shape
    anywhere, vmem = pl.BlockSpec(memory_space=pl.ANY), pl.BlockSpec(memory_space=pltpu.VMEM)
    return pl.pallas_call(
        plane_sum_kernel,
        out_shape=[
            jax.ShapeDtypeStruct((40, 4 * ATTN), f32),
            jax.ShapeDtypeStruct((4, 40, 2 * FEED), f32),
            jax.ShapeDtypeStruct(sent.shape, low),
            jax.ShapeDtypeStruct(x.shape, low),
            jax.ShapeDtypeStruct(x.shape, low),
        ],
        in_specs=[anywhere] * 4 + [vmem] * 7,
        out_specs=[vmem, vmem, anywhere, vmem, vmem],
        scratch_shapes=[
            pltpu.VMEM((2560, 2 * WIDE), low),
            pltpu.VMEM((2560, 2 * ATTN), low),
            pltpu.VMEM((2, 5, 2, 80, WIDE), low),
            pltpu.VMEM((2, 5, 2, 160, WIDE), low),
            pltpu.VMEM((80, 2 * WIDE), low),
            pltpu.VMEM((80, 2 * ATTN), f32),
            pltpu.VMEM((2, 80, 2 * FEED), f32),
            pltpu.VMEM((2, 80, 128), low),
            pltpu.VMEM((2, rows, width), low),
            pltpu.VMEM((rows, width), low),
            pltpu.VMEM((2, rows // 2, width), low),
            pltpu.VMEM((rows, width), low),
            pltpu.VMEM((rows, width), low),
            pltpu.VMEM((rows, width), low),
            pltpu.VMEM((rows, width), low),
            pltpu.VMEM((rows, width), low),
            dma((20,)),
            dma((12,)),
            dma((12,)),
            dma((40,)),
            dma((40,)),
            dma((6,)),
            dma((6,)),
            dma((7,)),
            dma((7,)),
            dma((1,)),
            dma((3,)),
            dma((3,)),
        ],
        compiler_params=pltpu.CompilerParams(
            collective_id=cid, has_side_effects=True, vmem_limit_bytes=56 * 2**20
        ),
    )(a, o, f, sent, down, d_xn, x, mid, d_mid, gain, order)


def grads_kernel(l_ref, r_ref, o_ref):
    o_ref[...] = lax.dot_general(
        l_ref[0], r_ref[0], (((0,), (0,)), ((), ())), preferred_element_type=jnp.float32
    ).astype(o_ref.dtype)


def pair_of_grads(left, right):
    n, depth, rows = left.shape
    columns, tile = right.shape[2], 256
    per = columns // tile
    return pl.pallas_call(
        grads_kernel,
        grid=(n, per),
        out_shape=jax.ShapeDtypeStruct((rows, n * columns), jnp.bfloat16),
        in_specs=[
            pl.BlockSpec((1, depth, rows), lambda b, j: (b, 0, 0)),
            pl.BlockSpec((1, depth, tile), lambda b, j: (b, 0, j)),
        ],
        out_specs=pl.BlockSpec((rows, tile), lambda b, j: (0, b * per + j)),
        compiler_params=pltpu.CompilerParams(vmem_limit_bytes=40 * 2**20),
        cost_estimate=pl.CostEstimate(
            flops=2 * n * depth * rows * columns,
            bytes_accessed=2 * n * (depth * rows + depth * columns + rows * columns),
            transcendentals=0,
        ),
    )(left, right)


def rms_norm(values, gain_row):
    return (
        values * lax.rsqrt(jnp.mean(values * values, axis=-1, keepdims=True) + norm_eps) * gain_row
    )


def geglu(gate_part, up_part):
    return jax.nn.gelu(gate_part) * up_part


def tables():
    half_rot = ROT // 2
    rates = jnp.exp(jnp.arange(half_rot, dtype=jnp.float32) * (-2.0 * math.log(10000.0) / ROT))
    angles = jnp.arange(SEQ_LEN, dtype=jnp.float32)[:, None] * rates[None, :]
    return (jnp.cos(angles), jnp.sin(angles))


def rotate(field, cosine, sine):
    half_rot = ROT // 2
    first = field[..., :half_rot]
    second = field[..., half_rot:ROT]
    return jnp.concatenate(
        [first * cosine - second * sine, second * cosine + first * sine, field[..., ROT:]], axis=-1
    )


def contract(left, right, left_dim, right_dim):
    return lax.dot_general(
        left, right, (((left_dim,), (right_dim,)), ((), ())), preferred_element_type=jnp.float32
    )


def padded(weight):
    return jnp.pad(weight.reshape(40, 4, 960), ((0, 0), (0, 0), (0, 64)))


def joined(slices):
    return slices[:, :, :960].transpose(1, 0, 2).reshape(40, 3840).astype(jnp.float32)


def local(
    tokens,
    attn_gain,
    query_weight,
    kv_weight,
    out_weight,
    mlp_gain,
    gate_weight,
    up_weight,
    down_weight,
    cotangent,
):
    low = jnp.bfloat16
    rows = tokens.shape[0]
    seqs = rows // SEQ_LEN
    heads_here = query_weight.shape[1] // HEAD_DIM
    wide = heads_here * HEAD_DIM
    scale = HEAD_DIM ** (-0.5)
    cosine, sine = tables()
    positions = jnp.arange(SEQ_LEN)
    keep_mask = (positions[:, None] >= positions[None, :]) & (
        positions[:, None] - positions[None, :] < WINDOW
    )
    attn = jnp.concatenate([query_weight, kv_weight, out_weight.T], axis=1)
    attn = attn.reshape(40, 2, 2, ATTN).transpose(1, 2, 0, 3)
    attn = jnp.broadcast_to(attn, (2, *attn.shape)).reshape(4, 2, 40, ATTN)
    first = attn.reshape(4, 80, ATTN)
    gains = jnp.pad(jnp.stack([attn_gain, mlp_gain], axis=0), ((0, 14), (0, 88)))
    gains = jnp.broadcast_to(gains, (4, 16, 128))
    down = padded(down_weight.T).reshape(40, 4, 2, FEED).transpose(1, 2, 0, 3).reshape(4, 80, FEED)
    second = jnp.stack([padded(gate_weight), padded(up_weight)], axis=0)
    second = second.transpose(2, 0, 1, 3).reshape(4, 80, 2 * FEED)
    order = jnp.asarray(feature_order(), low)
    first, gains, second, x_in, dy_here = group_exchange(
        [first, gains, second], tokens, cotangent, order, 5
    )
    second = second.reshape(4, 2, 40, 2 * FEED).transpose(0, 2, 1, 3).reshape(160, 4 * FEED)
    w_gate_up = lax.all_gather(second, PLANE, axis=0, tiled=True)
    first = first.reshape(4, 2, 40, ATTN).transpose(1, 0, 2, 3).reshape(2, 160, ATTN)
    w_q_kv, w_out_t, gains, dy, down = attention_gather(first, gains.reshape(64, 128), dy_here, down, 6)
    gains = gains.reshape(64, 16, 128)[:, :2, :40].transpose(1, 0, 2).reshape(2, 2560).astype(jnp.float32)
    down = down.reshape(4, 2, 40, FEED).transpose(1, 0, 2, 3).reshape(2, 160, FEED)
    dy = dy.reshape(4 * rows, -1)
    gain_one, gain_two = gains[0], gains[1]

    xn_one = rms_norm(x_in, gain_one).astype(low)
    q_kv_pre = jnp.dot(xn_one, w_q_kv, preferred_element_type=jnp.float32)
    q_pre, kv_pre = q_kv_pre[:, :wide], q_kv_pre[:, wide:]
    queries = rotate(
        q_pre.reshape(seqs, SEQ_LEN, heads_here, HEAD_DIM), cosine[:, None, :], sine[:, None, :]
    ).astype(low)
    key_rot = rotate(kv_pre[:, :HEAD_DIM].reshape(seqs, SEQ_LEN, HEAD_DIM), cosine, sine).astype(low)
    value_rows = kv_pre[:, HEAD_DIM:].reshape(seqs, SEQ_LEN, HEAD_DIM).astype(low)

    def score_rows():
        raw = (
            jnp.einsum("sqhd,skd->shqk", queries, key_rot, preferred_element_type=jnp.float32)
            * scale
        )
        return jnp.where(keep_mask, raw, -1e30)

    scores = score_rows()
    row_max = jnp.max(scores, axis=-1, keepdims=True)
    log_total = row_max + jnp.log(jnp.sum(jnp.exp(scores - row_max), axis=-1, keepdims=True))
    attn_probs = jnp.exp(scores - log_total).astype(low)
    mixed_heads = jnp.einsum(
        "shqk,skd->sqhd", attn_probs, value_rows, preferred_element_type=jnp.float32
    )
    mixed_heads = mixed_heads.reshape(rows, wide).astype(low)
    attn_part = contract(mixed_heads, w_out_t, 1, 1).astype(low)
    x_mid, xn_all, w_down_t = middle(attn_part, x_in, gain_two[None, :], down, 2)
    xn_all = xn_all.reshape(4 * rows, -1)
    gate_up = jnp.dot(xn_all, w_gate_up, preferred_element_type=jnp.float32)
    gate_pre, up_pre = gate_up[:, : 2 * FEED], gate_up[:, 2 * FEED :]
    hidden = geglu(gate_pre, up_pre).astype(low)
    down_part = contract(hidden, w_down_t, 1, 1).astype(low)
    d_hidden = jnp.dot(dy, w_down_t, preferred_element_type=jnp.float32)
    geglu_pull = jax.vjp(geglu, gate_pre, up_pre)[1]
    d_gate_pre, d_up_pre = geglu_pull(d_hidden)
    d_gate_low = d_gate_pre.astype(low)
    d_up_low = d_up_pre.astype(low)
    d_xn_two_part = contract(jnp.concatenate([d_gate_low, d_up_low], axis=1), w_gate_up, 1, 1)
    d_xn_two = token_sum(d_xn_two_part.astype(low).reshape(4, rows, -1), 3)
    sent = pair_of_grads(jnp.stack([dy, xn_all]), jnp.stack([hidden, d_gate_low]))
    sent = lax.psum_scatter(sent, PLANE, scatter_dimension=0, tiled=True)
    sent = sent.reshape(4, 40, 2, 2 * FEED).transpose(0, 2, 1, 3).reshape(4, 80, 2 * FEED)

    norm_two_pull = jax.vjp(rms_norm, x_mid, gain_two)[1]
    d_mid_norm, d_gain_two = norm_two_pull(d_xn_two)
    d_mid = dy_here.astype(jnp.float32) + d_mid_norm
    d_mid_low = d_mid.astype(low)
    d_out_t = contract(d_mid_low, mixed_heads, 0, 0)
    d_mixed = (
        jnp.dot(d_mid_low, w_out_t, preferred_element_type=jnp.float32)
        .astype(low)
        .reshape(seqs, SEQ_LEN, heads_here, HEAD_DIM)
    )
    soft_rows = jnp.exp(score_rows() - log_total)
    d_probs = jnp.einsum("sqhd,skd->shqk", d_mixed, value_rows, preferred_element_type=jnp.float32)
    d_scores = (
        soft_rows * (d_probs - jnp.sum(soft_rows * d_probs, axis=-1, keepdims=True))
    ).astype(low)
    d_queries = (
        jnp.einsum("shqk,skd->sqhd", d_scores, key_rot, preferred_element_type=jnp.float32) * scale
    )
    d_keys = (
        jnp.einsum("shqk,sqhd->skd", d_scores, queries, preferred_element_type=jnp.float32) * scale
    )
    d_values = jnp.einsum("shqk,sqhd->skd", attn_probs, d_mixed, preferred_element_type=jnp.float32)
    d_q_pre = (
        rotate(d_queries, cosine[:, None, :], -sine[:, None, :]).reshape(rows, wide).astype(low)
    )
    d_k_pre = rotate(d_keys, cosine, -sine).reshape(rows, HEAD_DIM)
    d_kv_part = jnp.concatenate([d_k_pre, d_values.reshape(rows, HEAD_DIM)], axis=-1)
    d_kv_low = pair_sum(d_kv_part.astype(low), 4).astype(low)
    d_q_kv_w = contract(xn_one, jnp.concatenate([d_q_pre, d_kv_low], axis=1), 0, 0).astype(low)
    d_xn_one = contract(jnp.concatenate([d_q_pre, d_kv_low * 0.5], axis=1), w_q_kv, 1, 1)
    norm_one_pull = jax.vjp(lambda g: rms_norm(x_in, g), gain_one)[1]
    d_gain_one = norm_one_pull(d_xn_one)[0]
    d_gains = jnp.pad(jnp.stack([d_gain_one, 0.5 * d_gain_two], axis=0).astype(low), ((0, 14), (0, 0)))
    chosen = jnp.asarray(np.eye(16, 2 * FEED, 960) * (np.arange(16) < 2)[:, None], low)
    d_up_w = contract(
        jnp.concatenate([xn_all, d_gains], axis=0),
        jnp.concatenate([d_up_low, chosen], axis=0),
        0,
        0,
    ).astype(low)
    attn_out, up_out, sent, block_out, tokens_grad = plane_sum(
        d_q_kv_w,
        d_out_t.astype(low),
        d_up_w,
        sent,
        down_part.reshape(4, rows, -1),
        d_xn_one.astype(low),
        x_in,
        x_mid,
        d_mid,
        gain_one[None, :],
        order,
        7,
    )
    sent = sent.reshape(4, 2, 40, 2 * FEED)
    gain_out = up_out[:, :, 960:962].sum(axis=0)
    return (
        block_out,
        tokens_grad,
        gain_out[:, 0],
        attn_out[:, :wide],
        attn_out[:, wide : wide + 2 * HEAD_DIM],
        attn_out[:, wide + 2 * HEAD_DIM :].T,
        gain_out[:, 1],
        joined(sent[:, 1]),
        joined(up_out),
        joined(sent[:, 0]).T,
    )


def solution(mesh):
    fine = Mesh(mesh.devices.reshape(4, 2, 4, 2, 2), AXES)
    dp = ("y", "zl", "x", "c")
    in_specs = (
        P(dp, None),
        P(dp),
        P(dp, "zh"),
        P(dp, None),
        P("zh", dp),
        P(dp),
        P(dp, "zh"),
        P(dp, "zh"),
        P("zh", dp),
        P(dp, None),
    )
    out_specs = (
        P(dp, None),
        P(dp, None),
        P(dp),
        P(dp, "zh"),
        P(dp, None),
        P("zh", dp),
        P(dp),
        P(dp, "zh"),
        P(dp, "zh"),
        P("zh", dp),
    )
    return jax.shard_map(local, mesh=fine, in_specs=in_specs, out_specs=out_specs, check_vma=False)
```

```python
import math

import jax
import jax.numpy as jnp
import numpy as np
from jax import lax
from jax.experimental import pallas as pl
from jax.experimental.pallas import tpu as pltpu
from jax.sharding import Mesh
from jax.sharding import PartitionSpec as P

HEAD_DIM = 256
WINDOW = 2048
SEQ_LEN = 128
ROT = 128
AXES = ("y", "zl", "x", "c", "zh")
PLANE = ("y", "x")
GROUP = ("zl", "c")
OWNERS = ("y", "x", "zl", "c")
MESH = pl.DeviceIdType.MESH

norm_eps = 1e-06


def feature_order():
    place = np.arange(640).reshape(2, 4, 80).transpose(1, 0, 2).reshape(640)
    return (np.arange(640)[:, None] == place[None, :]).astype(np.float32)


def reorder(src, order, dst, back):
    for k in range(4):
        group = pl.ds(k * 640, 640)
        dst[:, group] = lax.dot_general(
            src[:, group],
            order[...],
            (((1,), (1 if back else 0,)), ((), ())),
            preferred_element_type=jnp.float32,
        ).astype(dst.dtype)


def greet(peers):
    barrier = pltpu.get_barrier_semaphore()
    for peer in peers:
        pl.semaphore_signal(barrier, inc=1, device_id=peer, device_id_type=MESH)
    pl.semaphore_wait(barrier, len(peers))


def remote(src, dst, send, recv, peer):
    return pltpu.make_async_remote_copy(
        src_ref=src, dst_ref=dst, send_sem=send, recv_sem=recv, device_id=peer, device_id_type=MESH
    )


def sum_kernel(p_ref, o_ref, from_core, other, from_chips, own, own_low, from_far, send, recv):
    zl, c, zh = lax.axis_index("zl"), lax.axis_index("c"), lax.axis_index("zh")
    rows = p_ref.shape[1]
    half = rows // 2
    core, far = {"c": 1 - c}, {"zh": 1 - zh}
    chips = [{"zl": 1 - zl, "zh": k} for k in range(2)]
    greet([core, far, *chips])
    order = [1 - zl, zl]
    cores = [
        remote(p_ref.at[z * 2 + 1 - c], from_core.at[i], send.at[i], recv.at[i], core)
        for i, z in enumerate(order)
    ]
    for copy in cores:
        copy.start()
    step = 16
    cores[0].wait_recv()
    aways = []
    for k in range(2):

        @pl.loop(0, half // step)
        def _(j, k=k):
            at = pl.ds(pl.multiple_of(k * half + j * step, step), step)
            total = p_ref[(1 - zl) * 2 + c, at].astype(jnp.float32) + from_core[0, at].astype(jnp.float32)
            other[at] = total.astype(jnp.bfloat16)

        away = remote(
            other.at[pl.ds(k * half, half)], from_chips.at[zh], send.at[2 + k], recv.at[2 + zh], chips[k]
        )
        away.start()
        aways.append(away)
    cores[1].wait_recv()
    fars = []
    for k in range(2):
        piece = (1 - zh) if k == 0 else zh
        if k == 1:
            for i in range(2):
                remote(
                    other.at[pl.ds(0, half)], from_chips.at[i], send.at[2 + i], recv.at[2 + i], chips[i]
                ).wait_recv()

        @pl.loop(0, half // step)
        def _(j, k=k, piece=piece):
            at = pl.ds(pl.multiple_of(piece * half + j * step, step), step)
            total = p_ref[zl * 2 + c, at].astype(jnp.float32) + from_core[1, at].astype(jnp.float32)
            if k == 1:
                here = pl.ds(pl.multiple_of(j * step, step), step)
                total += from_chips[0, here].astype(jnp.float32) + from_chips[1, here].astype(jnp.float32)
            own[at] = total.astype(jnp.bfloat16)

        at = pl.ds(pl.multiple_of(piece * half, half), half)
        copy = remote(own.at[at], from_far.at[at], send.at[4 + k], recv.at[4 + k], far)
        copy.start()
        fars.append(copy)
    for k in range(2):
        fars[k].wait_recv()
        piece = zh if k == 0 else (1 - zh)

        @pl.loop(0, half // step)
        def _(j, piece=piece):
            at = pl.ds(pl.multiple_of(piece * half + j * step, step), step)
            o_ref[at] = own[at].astype(jnp.float32) + from_far[at].astype(jnp.float32)

    for copy in (*cores, *aways, *fars):
        copy.wait_send()


def token_sum(p, cid):
    rows, width = p.shape[1:]
    low = jnp.bfloat16
    return pl.pallas_call(
        sum_kernel,
        out_shape=jax.ShapeDtypeStruct((rows, width), jnp.float32),
        in_specs=[pl.BlockSpec(memory_space=pltpu.VMEM)],
        out_specs=pl.BlockSpec(memory_space=pltpu.VMEM),
        scratch_shapes=[
            pltpu.VMEM((2, rows, width), low),
            pltpu.VMEM((rows, width), low),
            pltpu.VMEM((2, rows // 2, width), low),
            pltpu.VMEM((rows, width), low),
            pltpu.VMEM((rows, width), low),
            pltpu.VMEM((rows, width), low),
            pltpu.SemaphoreType.DMA((6,)),
            pltpu.SemaphoreType.DMA((6,)),
        ],
        compiler_params=pltpu.CompilerParams(
            collective_id=cid, has_side_effects=True, vmem_limit_bytes=32 * 2**20
        ),
    )(p)


def pair_kernel(p_ref, o_ref, landed, send, recv):
    far = {"zh": 1 - lax.axis_index("zh")}
    rows = p_ref.shape[0]
    greet([far])
    copy = remote(p_ref, landed, send, recv, far)
    copy.start()
    copy.wait()
    step = 16

    @pl.loop(0, rows // step)
    def _(j):
        at = pl.ds(pl.multiple_of(j * step, step), step)
        o_ref[at] = p_ref[at].astype(jnp.float32) + landed[at].astype(jnp.float32)


def pair_sum(p, cid):
    return pl.pallas_call(
        pair_kernel,
        out_shape=jax.ShapeDtypeStruct(p.shape, jnp.float32),
        in_specs=[pl.BlockSpec(memory_space=pltpu.VMEM)],
        out_specs=pl.BlockSpec(memory_space=pltpu.VMEM),
        scratch_shapes=[
            pltpu.VMEM(p.shape, p.dtype),
            pltpu.SemaphoreType.DMA,
            pltpu.SemaphoreType.DMA,
        ],
        compiler_params=pltpu.CompilerParams(
            collective_id=cid, has_side_effects=True, vmem_limit_bytes=32 * 2**20
        ),
    )(p)


def ring_of(axis, at):
    return {axis: lax.rem(at + 3, 4)}, {axis: lax.rem(at + 1, 4)}


def send_blocks(ins, outs, here, send, recv):
    zl, c = lax.axis_index("zl"), lax.axis_index("c")
    mine = zl * 2 + c
    peers = [({"zl": 1 - zl, "c": k}, (1 - zl) * 2 + k) for k in range(2)]
    peers.append(({"c": 1 - c}, zl * 2 + 1 - c))
    n = len(ins)
    copies, keeps = [], []
    for i in range(n):
        for k, (peer, block) in enumerate(peers):
            landing = i * 3 + (c if k < 2 else 2)
            copy = remote(ins[i].at[block], outs[i].at[mine], send.at[i * 3 + k], recv.at[landing], peer)
            copy.start()
            copies.append(copy)
    for i in range(n):
        keep = pltpu.make_async_copy(ins[i].at[mine], outs[i].at[mine], here.at[i])
        keep.start()
        keeps.append(keep)

    def finish():
        for keep in keeps:
            keep.wait()
        for i in range(n):
            for k, (peer, block) in enumerate(peers):
                remote(
                    ins[i].at[block], outs[i].at[block], send.at[i * 3 + k], recv.at[i * 3 + k], peer
                ).wait_recv()
        for copy in copies:
            copy.wait_send()

    return finish


def group_peers():
    zl, c = lax.axis_index("zl"), lax.axis_index("c")
    return [{"c": 1 - c}, {"zl": 1 - zl, "c": 0}, {"zl": 1 - zl, "c": 1}]


def exchange_kernel(
    a_ref, g_ref, s_ref, tok_ref, cot_ref, order_ref, ao_ref, go_ref, so_ref, x_ref, dy_ref, here, send, recv
):
    greet(group_peers())
    finish = send_blocks([a_ref, g_ref, s_ref], [ao_ref, go_ref, so_ref], here, send, recv)
    reorder(tok_ref, order_ref, x_ref, False)
    reorder(cot_ref, order_ref, dy_ref, False)
    finish()


def group_exchange(arrays, tokens, cotangent, order, cid):
    n = len(arrays)
    like = lambda a, kind: jax.ShapeDtypeStruct(a.shape, kind)
    anywhere, vmem = pl.BlockSpec(memory_space=pl.ANY), pl.BlockSpec(memory_space=pltpu.VMEM)
    return pl.pallas_call(
        exchange_kernel,
        out_shape=[
            *(like(a, a.dtype) for a in arrays),
            like(tokens, jnp.float32),
            like(cotangent, jnp.bfloat16),
        ],
        in_specs=[anywhere] * n + [vmem] * 3,
        out_specs=[anywhere] * n + [vmem] * 2,
        scratch_shapes=[
            pltpu.SemaphoreType.DMA((n,)),
            pltpu.SemaphoreType.DMA((3 * n,)),
            pltpu.SemaphoreType.DMA((3 * n,)),
        ],
        compiler_params=pltpu.CompilerParams(
            collective_id=cid, has_side_effects=True, vmem_limit_bytes=32 * 2**20
        ),
    )(*arrays, tokens, cotangent, order)


ATTN, FEED = 768, 512
WIDE = ATTN + FEED


def shift(i, by):
    return lax.rem(i + by, 4)


def around(h, y, x):
    if h == 0:
        return x, ring_of("x", x), y, ring_of("y", y)
    return y, ring_of("y", y), x, ring_of("x", x)


class Piece:
    def __init__(self, h, source, target, columns, rows=160):
        self.h, self.source, self.target, self.columns, self.rows = h, source, target, columns, rows

    def own(self):
        return self.source

    def at(self, i1, i2, part=None):
        row, column = (i2, i1) if self.h == 0 else (i1, i2)
        size = self.rows if part is None else self.rows // 2
        first = (row * 4 + column) * self.rows + (0 if part is None else part * size)
        return self.target.at[pl.ds(pl.multiple_of(first, 16), size), self.columns]


def gather_steps(y, x, pieces, send, recv, cross):
    started = []

    def go(src, dst, n, ring, slot, peer):
        k = (n * 5 + ring) * 4 + slot
        copy = remote(src, dst, send.at[k], recv.at[k], peer)
        copy.start()
        started.append(copy)

    def arrived(dst, n, ring, slot):
        k = (n * 5 + ring) * 4 + slot
        remote(dst, dst, send.at[k], recv.at[k], {"c": 1 - lax.axis_index("c")}).wait_recv()

    each = [(n, p, *around(p.h, y, x)) for n, p in enumerate(pieces)]
    firsts = ((1, 0), (2, 3), (3, 1), (4, 2))

    def own_blocks():
        for n, p, i1, (back1, ahead1), i2, _ in each:
            go(p.own(), p.at(i1, i2), n, 0, 0, ahead1)
            go(p.own(), p.at(i1, i2), n, 0, 1, back1)
        for n, p, i1, _, i2, (back2, ahead2) in each:
            go(p.own(), p.at(i1, i2), n, 1, 0, ahead2)
            go(p.own(), p.at(i1, i2), n, 1, 1, back2)
            cross(n, p.own(), p.at(i1, i2))

    def first_axis():
        for n, p, i1, (back1, ahead1), i2, (back2, ahead2) in each:
            left, right = p.at(shift(i1, 3), i2), p.at(shift(i1, 1), i2)
            arrived(left, n, 0, 0)
            low = p.at(shift(i1, 3), i2, 0)
            go(low, low, n, 0, 2, ahead1)
            arrived(right, n, 0, 1)
            high = p.at(shift(i1, 1), i2, 1)
            go(high, high, n, 0, 3, back1)
            for ring, ref in ((2, left), (3, right)):
                go(ref, ref, n, ring, 0, ahead2)
                go(ref, ref, n, ring, 1, back2)
                cross(n, ref, ref)
        for n, p, i1, _, i2, (back2, ahead2) in each:
            far = shift(i1, 2)
            arrived(p.at(far, i2, 0), n, 0, 2)
            arrived(p.at(far, i2, 1), n, 0, 3)
            ref = p.at(far, i2)
            go(ref, ref, n, 4, 0, ahead2)
            go(ref, ref, n, 4, 1, back2)
            cross(n, ref, ref)

    def second_axis():
        for ring, by in firsts:
            for n, p, i1, _, i2, (back2, ahead2) in each:
                j = shift(i1, by)
                left, right = p.at(j, shift(i2, 3)), p.at(j, shift(i2, 1))
                arrived(left, n, ring, 0)
                low = p.at(j, shift(i2, 3), 0)
                go(low, low, n, ring, 2, ahead2)
                cross(n, left, left)
                arrived(right, n, ring, 1)
                high = p.at(j, shift(i2, 1), 1)
                go(high, high, n, ring, 3, back2)
                cross(n, right, right)

    def last():
        for ring, by in firsts:
            for n, p, i1, _, i2, _ in each:
                j, far = shift(i1, by), shift(i2, 2)
                arrived(p.at(j, far, 0), n, ring, 2)
                arrived(p.at(j, far, 1), n, ring, 3)
                cross(n, p.at(j, far), p.at(j, far))
        for copy in started:
            copy.wait_send()

    return own_blocks, first_axis, second_axis, last


def attention_gather_kernel(
    in_ref, g_ref, dy_ref, d_ref, a_ref, o_ref, go_ref, all_ref, do_ref,
    here, send, recv, csend, crecv, dsend, drecv, xhere, xsend, xrecv,
):
    y, x, c = lax.axis_index("y"), lax.axis_index("x"), lax.axis_index("c")
    zl, zh = lax.axis_index("zl"), lax.axis_index("zh")
    core = {"c": 1 - c}
    chips = [{"zl": 1 - zl, "zh": k} for k in range(2)]
    greet([*ring_of("x", x), *ring_of("y", y), core, *chips, {"zl": 1 - zl, "c": 1 - c}])
    whole = pl.ds(0, 160)

    for side in range(2):

        @pl.when(c == side)
        def _(side=side):
            sources = [
                in_ref.at[0, whole, pl.ds(0, 256)],
                in_ref.at[0, whole, pl.ds(256, 512)],
                in_ref.at[1, whole, pl.ds(0, 768)],
                g_ref,
            ]
            if side == 0:
                targets = [(a_ref, 0, 256), (a_ref, 256, 512), (a_ref, 768, 768)]
            else:
                targets = [(a_ref, 1536, 256), (o_ref, 0, 512), (o_ref, 512, 768)]
            targets.append((go_ref, 0, 128))
            pieces = [
                Piece(h, source, ref, pl.ds(first, width), rows)
                for h, source, (ref, first, width), rows in zip((0, 0, 1, 0), sources, targets, (160, 160, 160, 64))
            ]
            crossed = []

            def cross(n, src, dst):
                if n < 3:
                    k = len(crossed)
                    copy = remote(src, dst, csend.at[k], crecv.at[k], core)
                    copy.start()
                    crossed.append(copy)

            own_blocks, first_axis, second_axis, last = gather_steps(y, x, pieces, send, recv, cross)
            own_blocks()
            keeps = []
            for n, p in enumerate(pieces):
                i1, _, i2, _ = around(p.h, y, x)
                keeps.append(pltpu.make_async_copy(p.own(), p.at(i1, i2), here.at[n]))
                keeps[-1].start()
            finish = send_blocks([d_ref], [do_ref], xhere, xsend, xrecv)
            half = dy_ref.shape[0] // 2
            mine, other = zl * 2 + c, (1 - zl) * 2 + c
            part = pl.ds(pl.multiple_of(zh * half, half), half)
            away = [
                remote(dy_ref.at[part], all_ref.at[mine, part], dsend.at[k], drecv.at[zh], chips[k])
                for k in range(2)
            ]
            across = remote(dy_ref, all_ref.at[mine], dsend.at[2], drecv.at[2], core)
            for copy in (*away, across):
                copy.start()
            keeps.append(pltpu.make_async_copy(dy_ref, all_ref.at[mine], here.at[4]))
            keeps[-1].start()
            first_axis()
            second_axis()
            passed = []
            for k in range(2):
                rows = pl.ds(k * half, half)
                there = all_ref.at[other, rows]
                remote(dy_ref.at[rows], there, dsend.at[k], drecv.at[k], chips[k]).wait_recv()
                passed.append(remote(there, there, dsend.at[3 + k], drecv.at[3 + k], core))
                passed[-1].start()
            last()
            for copy in (*crossed, *passed, across):
                copy.wait()
            for copy in away:
                copy.wait_send()
            for keep in keeps:
                keep.wait()
            finish()


def attention_gather(own, gains, dy, down, cid):
    kind, dma = jnp.bfloat16, pltpu.SemaphoreType.DMA
    return pl.pallas_call(
        attention_gather_kernel,
        out_shape=[
            jax.ShapeDtypeStruct((2560, 1792), kind),
            jax.ShapeDtypeStruct((2560, 1280), kind),
            jax.ShapeDtypeStruct((1024, 128), kind),
            jax.ShapeDtypeStruct((4, *dy.shape), kind),
            jax.ShapeDtypeStruct(down.shape, kind),
        ],
        in_specs=[pl.BlockSpec(memory_space=pl.ANY)] * 4,
        out_specs=[pl.BlockSpec(memory_space=pl.ANY)] * 5,
        scratch_shapes=[
            dma((5,)),
            dma((80,)),
            dma((80,)),
            dma((48,)),
            dma((48,)),
            dma((5,)),
            dma((5,)),
            dma((1,)),
            dma((3,)),
            dma((3,)),
        ],
        compiler_params=pltpu.CompilerParams(collective_id=cid, has_side_effects=True),
    )(own, gains, dy, down)


def middle_kernel(
    p_ref, x_ref, g_ref, d_ref, mid_ref, all_ref, w_ref, landed, here, psend, precv, gsend, grecv, send, recv
):
    y, x, c = lax.axis_index("y"), lax.axis_index("x"), lax.axis_index("c")
    zl, zh = lax.axis_index("zl"), lax.axis_index("zh")
    core, far = {"c": 1 - c}, {"zh": 1 - zh}
    chips = [{"zl": 1 - zl, "zh": k} for k in range(2)]
    greet([*ring_of("x", x), *ring_of("y", y), core, far, *chips])
    half, step = p_ref.shape[0] // 2, 16
    mine, other = zl * 2 + c, (1 - zl) * 2 + c
    parts = [pl.ds(pl.multiple_of(k * half, half), half) for k in (1 - zh, zh)]
    pair = [
        remote(p_ref.at[part], landed.at[part], psend.at[k], precv.at[k], far)
        for k, part in enumerate(parts)
    ]
    for copy in pair:
        copy.start()
    pieces = [
        Piece(h, d_ref.at[h, pl.ds(0, 160)], w_ref, pl.ds(h * FEED, FEED)) for h in range(2)
    ]
    own_blocks, first_axis, second_axis, last = gather_steps(
        y, x, pieces, send, recv, lambda n, src, dst: None
    )
    own_blocks()
    keeps = []
    for n, p in enumerate(pieces):
        i1, _, i2, _ = around(p.h, y, x)
        keeps.append(pltpu.make_async_copy(p.own(), p.at(i1, i2), here.at[n]))
        keeps[-1].start()
    away, across = [], []
    for k in range(2):
        part = parts[1 - k]
        pair[k].wait_recv()
        first = (zh if k == 0 else 1 - zh) * half

        @pl.loop(0, half // step)
        def _(i, first=first):
            at = pl.ds(pl.multiple_of(first + i * step, step), step)
            branch = p_ref[at].astype(jnp.float32) + landed[at].astype(jnp.float32)
            v = x_ref[at] + branch
            mid_ref[at] = v
            r = lax.rsqrt(jnp.mean(v * v, axis=-1, keepdims=True) + norm_eps)
            all_ref[mine, at] = (v * r * g_ref[...]).astype(jnp.bfloat16)

        rows = all_ref.at[mine, part]
        if k == 0:
            for i in range(2):
                away.append(remote(rows, rows, gsend.at[i], grecv.at[zh], chips[i]))
                away[-1].start()
        across.append(remote(rows, rows, gsend.at[2 + k], grecv.at[2 + k], core))
        across[-1].start()
        if k == 0:
            first_axis()
    second_axis()
    passed = []
    for k in range(2):
        there = all_ref.at[other, pl.ds(k * half, half)]
        remote(there, there, gsend.at[k], grecv.at[k], chips[k]).wait_recv()
        passed.append(remote(there, there, gsend.at[4 + k], grecv.at[4 + k], core))
        passed[-1].start()
    last()
    for copy in (*across, *passed):
        copy.wait()
    for copy in (*away, *pair):
        copy.wait_send()
    for keep in keeps:
        keep.wait()


def middle(p, x, gain, down, cid):
    dma = pltpu.SemaphoreType.DMA
    anywhere, vmem = pl.BlockSpec(memory_space=pl.ANY), pl.BlockSpec(memory_space=pltpu.VMEM)
    return pl.pallas_call(
        middle_kernel,
        out_shape=[
            jax.ShapeDtypeStruct(x.shape, jnp.float32),
            jax.ShapeDtypeStruct((4, *x.shape), jnp.bfloat16),
            jax.ShapeDtypeStruct((2560, 2 * FEED), jnp.bfloat16),
        ],
        in_specs=[vmem, vmem, vmem, anywhere],
        out_specs=[vmem, vmem, anywhere],
        scratch_shapes=[
            pltpu.VMEM(p.shape, p.dtype),
            dma((2,)),
            dma((2,)),
            dma((2,)),
            dma((6,)),
            dma((6,)),
            dma((40,)),
            dma((40,)),
        ],
        compiler_params=pltpu.CompilerParams(
            collective_id=cid, has_side_effects=True, vmem_limit_bytes=32 * 2**20
        ),
    )(p, x, gain, down)


def finish_kernel(s_ref, down_ref, gate_ref, up_ref, landed, here, send, recv):
    greet(group_peers())
    send_blocks([s_ref], [landed], here, send, recv)()
    for t in range(4):
        v = landed[t].astype(jnp.float32)
        for k, out in enumerate((down_ref, gate_ref, up_ref)):
            for h in range(2):
                width = min(FEED, 960 - h * FEED)
                first = t * 960 + h * FEED
                out[:, first : first + width] = v[(2 * k + h) * 40 : (2 * k + h + 1) * 40, :width]


def finish(sent, cid):
    dma = pltpu.SemaphoreType.DMA
    vmem = pl.BlockSpec(memory_space=pltpu.VMEM)
    return pl.pallas_call(
        finish_kernel,
        out_shape=[jax.ShapeDtypeStruct((40, 3840), jnp.float32)] * 3,
        in_specs=[pl.BlockSpec(memory_space=pl.ANY)],
        out_specs=[vmem] * 3,
        scratch_shapes=[pltpu.VMEM(sent.shape, sent.dtype), dma((1,)), dma((3,)), dma((3,))],
        compiler_params=pltpu.CompilerParams(
            collective_id=cid, has_side_effects=True, vmem_limit_bytes=32 * 2**20
        ),
    )(sent)


class SumPiece:
    def __init__(self, h, sums, columns, via, main, sems, rows=160):
        self.h, self.sums, self.columns, self.via, self.main, self.sems, self.rows = (
            h, sums, columns, via, main, sems, rows,
        )

    def first(self, i1, i2, part=0):
        row, column = (i2, i1) if self.h == 0 else (i1, i2)
        return (row * 4 + column) * self.rows + part * (self.rows // 2)

    def at(self, i1, i2, part=None):
        size = self.rows if part is None else self.rows // 2
        return self.sums.at[pl.ds(pl.multiple_of(self.first(i1, i2, part or 0), 16), size), self.columns]


def plane_sum_kernel(
    xn_ref, dq_ref, dl_ref, m_ref, gi_ref, p_ref, t_ref, x_ref, mid_ref, dmid_ref, g_ref, order_ref,
    attn_ref, go_ref, block_ref, grad_ref,
    left, right, left_o, right_o, sums, via, main, gsums, gvia, gmain, from_chip, attn_low, gfar, gsum, gall,
    t_core, t_other, t_chips, t_own, t_far, landed, block_low, grad_low,
    here, csend, crecv, send, recv, esend, erecv, tsend, trecv, shere, ssend, srecv,
):
    y, x, c, zl, zh = (lax.axis_index(k) for k in ("y", "x", "c", "zl", "zh"))
    core, chip, far_peer = {"c": 1 - c}, {"zl": 1 - zl}, {"zh": 1 - zh}
    chips = [{"zl": 1 - zl, "zh": k} for k in range(2)]
    greet(
        [*ring_of("x", x), *ring_of("y", y), core, *chips, far_peer, {"zl": 1 - zl, "c": 1 - c}]
    )
    step = 16
    f32, low = jnp.float32, jnp.bfloat16
    order = (2, 1, 3, 0)
    tokens = p_ref.shape[1]
    half = tokens // 2

    inputs = [(xn_ref, left), (dq_ref, right), (dl_ref, left_o), (m_ref, right_o)]
    mine, theirs_at = pl.ds(0, tokens), pl.ds(tokens, tokens)
    shared = [
        remote(src, dst.at[theirs_at], csend.at[k], crecv.at[k], core) for k, (src, dst) in enumerate(inputs)
    ]
    kept = [pltpu.make_async_copy(src, dst.at[mine], here.at[k]) for k, (src, dst) in enumerate(inputs)]
    kept.append(pltpu.make_async_copy(gi_ref, gsums, here.at[4]))
    for copy in (*shared, *kept):
        copy.start()
    t_cores = [
        remote(p_ref.at[z * 2 + 1 - c], t_core.at[i], tsend.at[i], trecv.at[i], core)
        for i, z in enumerate((1 - zl, zl))
    ]
    for copy in t_cores:
        copy.start()
    pair = remote(t_ref, landed, tsend.at[6], trecv.at[6], far_peer)
    pair.start()
    t_sent = []

    def tokens_to_chips():
        t_cores[0].wait_recv()

        @pl.loop(0, tokens // step)
        def _(i):
            at = pl.ds(pl.multiple_of(i * step, step), step)
            total = p_ref[(1 - zl) * 2 + c, at].astype(f32) + t_core[0, at].astype(f32)
            t_other[at] = total.astype(low)

        for k in range(2):
            t_sent.append(
                remote(t_other.at[pl.ds(k * half, half)], t_chips.at[zh], tsend.at[2 + k], trecv.at[2 + zh], chips[k])
            )
            t_sent[-1].start()

    def tokens_to_far(k):
        piece = (1 - zh) if k == 0 else zh
        if k == 0:
            t_cores[1].wait_recv()
        else:
            for i in range(2):
                remote(
                    t_other.at[pl.ds(0, half)], t_chips.at[i], tsend.at[2 + i], trecv.at[2 + i], chips[i]
                ).wait_recv()

        @pl.loop(0, half // step)
        def _(i):
            at = pl.ds(pl.multiple_of(piece * half + i * step, step), step)
            total = p_ref[zl * 2 + c, at].astype(f32) + t_core[1, at].astype(f32)
            if k == 1:
                there = pl.ds(pl.multiple_of(i * step, step), step)
                total += t_chips[0, there].astype(f32) + t_chips[1, there].astype(f32)
            t_own[at] = total.astype(low)

        at = pl.ds(pl.multiple_of(piece * half, half), half)
        t_sent.append(remote(t_own.at[at], t_far.at[at], tsend.at[4 + k], trecv.at[4 + k], far_peer))
        t_sent[-1].start()

    def tokens_gradient():
        pair.wait_recv()

        @pl.loop(0, tokens // step)
        def _(i):
            at = pl.ds(pl.multiple_of(i * step, step), step)
            d = (t_ref[at].astype(f32) + landed[at].astype(f32)) * g_ref[...]
            v = x_ref[at]
            r = lax.rsqrt(jnp.mean(v * v, axis=-1, keepdims=True) + norm_eps)
            n = v * r
            d = r * (d - n * jnp.mean(d * n, axis=-1, keepdims=True))
            grad_low[at] = (dmid_ref[at] + d).astype(low)

        reorder(grad_low, order_ref, grad_ref, True)

    def tokens_output():
        for k in range(2):
            t_sent[2 + k].wait_recv()

        @pl.loop(0, tokens // step)
        def _(i):
            at = pl.ds(pl.multiple_of(i * step, step), step)
            branch = t_own[at].astype(f32) + t_far[at].astype(f32)
            block_low[at] = (mid_ref[at] + branch).astype(low)

        reorder(block_low, order_ref, block_ref, True)

    def products(q):
        top = shift(y, order[q]) * 640
        for side in range(2):

            @pl.when(c == side)
            def _(side=side):
                if side == 0:
                    parts = [(left, right, 0, 0, 768), (left, right, 768, 768, 768)]
                else:
                    parts = [
                        (left, right, 1536, 0, 256),
                        (left_o, right_o, 0, 256, 512),
                        (left_o, right_o, 512, 768, 768),
                    ]

                @pl.loop(0, 5)
                def _(i):
                    at = pl.ds(pl.multiple_of(top + i * 128, 128), 128)
                    for lhs, rhs, source, target, width in parts:
                        sums[at, pl.ds(target, width)] = lax.dot_general(
                            lhs[:, at],
                            rhs[:, pl.ds(source, width)],
                            (((0,), (0,)), ((), ())),
                            preferred_element_type=f32,
                        ).astype(low)

    pieces = [
        SumPiece(h, sums, pl.ds(h * ATTN, ATTN), via.at[h], main.at[h], h * 20) for h in range(2)
    ]
    pieces.append(SumPiece(0, gsums, pl.ds(0, 128), gvia, gmain, 40, 64))

    def add(p, first, size, terms):
        @pl.loop(0, size // step)
        def _(i):
            at = pl.ds(pl.multiple_of(first + i * step, step), step)
            total = p.sums[at, p.columns].astype(f32)
            for ref, index, start in terms:
                total += ref[(*index, pl.ds(pl.multiple_of(start + i * step, step), step))].astype(f32)
            p.sums[at, p.columns] = total.astype(low)

    started = []

    def go(p, ring, slot, src, dst, peer):
        k = p.sems + ring * 4 + slot
        copy = remote(src, dst, send.at[k], recv.at[k], peer)
        copy.start()
        started.append(copy)

    def arrived(p, ring, slot, dst):
        k = p.sems + ring * 4 + slot
        remote(dst, dst, send.at[k], recv.at[k], core).wait_recv()

    def line(p, j):
        i1, peers1, i2, peers2 = around(p.h, y, x)
        if j == 4:
            return lambda k: (k, i2), i1, peers1
        fixed = shift(i1, order[j])
        return lambda k: (fixed, k), i2, peers2

    def out_via(p, ring):
        place, at, (back, ahead) = line(p, ring)
        far = place(shift(at, 2))
        go(p, ring, 0, p.at(*far, 0), p.via.at[ring, 0], ahead)
        go(p, ring, 1, p.at(*far, 1), p.via.at[ring, 1], back)

    def out_main(p, ring):
        place, at, (back, ahead) = line(p, ring)
        small = p.rows // 2
        arrived(p, ring, 0, p.via.at[ring, 0])
        add(p, p.first(*place(shift(at, 1)), 0), small, [(p.via, (ring, 0), 0)])
        go(p, ring, 2, p.at(*place(shift(at, 1))), p.main.at[ring, 0], ahead)
        arrived(p, ring, 1, p.via.at[ring, 1])
        add(p, p.first(*place(shift(at, 3)), 1), small, [(p.via, (ring, 1), 0)])
        go(p, ring, 3, p.at(*place(shift(at, 3))), p.main.at[ring, 1], back)

    def take(p, ring):
        place, at, _ = line(p, ring)
        arrived(p, ring, 2, p.main.at[ring, 0])
        arrived(p, ring, 3, p.main.at[ring, 1])
        add(p, p.first(*place(at)), p.rows, [(p.main, (ring, 0), 0), (p.main, (ring, 1), 0)])

    y_first, x_first, gain = pieces
    for copy in kept:
        copy.wait()
    for copy in shared:
        copy.wait_recv()
    for q in range(4):
        products(q)
        if q == 0:
            for j in range(4):
                out_via(y_first, j)
                out_via(gain, j)
        out_via(x_first, q)
        if q > 0:
            out_main(x_first, q - 1)
    tokens_to_chips()
    for j in range(4):
        out_main(y_first, j)
        out_main(gain, j)
        if j == 0:
            out_main(x_first, 3)
            tokens_to_far(0)
    for j in range(4):
        for p in (x_first, y_first, gain):
            take(p, j)
            if j == 0:
                out_via(p, 4)
        if j == 0:
            tokens_to_far(1)
    tokens_gradient()
    for p in (x_first, y_first, gain):
        out_main(p, 4)
    tokens_output()
    for p in (gain, x_first, y_first):
        take(p, 4)
    home = (y * 4 + x) * 160
    ghome = pl.ds(pl.multiple_of((y * 4 + x) * 64, 16), 64)
    theirs = pl.ds(pl.multiple_of(home + (1 - zl) * 80, 16), 80)
    across = remote(gsums.at[ghome], gfar, esend.at[0], erecv.at[0], far_peer)
    across.start()
    away = remote(sums.at[theirs], from_chip, esend.at[1], erecv.at[1], chip)
    away.start()
    across.wait()
    both = gsums[ghome].astype(f32) + gfar[...].astype(f32)
    for t in range(4):
        gsum[t] = both[t * 16 : (t + 1) * 16].astype(low)
    finish_gains = send_blocks([gsum], [gall], shere, ssend, srecv)
    away.wait()

    @pl.loop(0, 80 // step)
    def _(i):
        here_at = pl.ds(pl.multiple_of(home + zl * 80 + i * step, step), step)
        at = pl.ds(pl.multiple_of(i * step, step), step)
        attn_low[at] = sums[here_at].astype(f32) + from_chip[at].astype(f32)

    ours = pl.ds(pl.multiple_of(c * 40, 8), 40)
    for_core = pl.ds(pl.multiple_of((1 - c) * 40, 8), 40)
    columns = pl.ds(pl.multiple_of(c * 2 * ATTN, 128), 2 * ATTN)
    last = remote(attn_low.at[for_core], attn_ref.at[:, columns], esend.at[2], erecv.at[2], core)
    keep = pltpu.make_async_copy(attn_low.at[ours], attn_ref.at[:, columns], here.at[0])
    last.start()
    keep.start()
    finish_gains()
    go_ref[...] = (
        gall[0].astype(f32) + gall[1].astype(f32) + gall[2].astype(f32) + gall[3].astype(f32)
    )
    last.wait()
    keep.wait()
    for copy in (*started, *shared, pair, *t_cores, *t_sent):
        copy.wait_send()


def plane_sum(xn, d_q_kv, d_low, mixed, gains, down, d_xn, x, mid, d_mid, gain, order, cid):
    low, dma, f32 = jnp.bfloat16, pltpu.SemaphoreType.DMA, jnp.float32
    rows, width = x.shape
    vmem = pl.BlockSpec(memory_space=pltpu.VMEM)
    return pl.pallas_call(
        plane_sum_kernel,
        out_shape=[
            jax.ShapeDtypeStruct((40, 4 * ATTN), f32),
            jax.ShapeDtypeStruct((16, 128), f32),
            jax.ShapeDtypeStruct(x.shape, low),
            jax.ShapeDtypeStruct(x.shape, low),
        ],
        in_specs=[vmem] * 12,
        out_specs=[vmem] * 4,
        scratch_shapes=[
            pltpu.VMEM((2 * rows, width), low),
            pltpu.VMEM((2 * rows, d_q_kv.shape[1]), low),
            pltpu.VMEM((2 * rows, width), low),
            pltpu.VMEM((2 * rows, mixed.shape[1]), low),
            pltpu.VMEM((2560, 2 * ATTN), low),
            pltpu.VMEM((2, 5, 2, 80, ATTN), low),
            pltpu.VMEM((2, 5, 2, 160, ATTN), low),
            pltpu.VMEM((1024, 128), low),
            pltpu.VMEM((5, 2, 32, 128), low),
            pltpu.VMEM((5, 2, 64, 128), low),
            pltpu.VMEM((80, 2 * ATTN), low),
            pltpu.VMEM((80, 2 * ATTN), f32),
            pltpu.VMEM((64, 128), low),
            pltpu.VMEM((4, 16, 128), low),
            pltpu.VMEM((4, 16, 128), low),
            pltpu.VMEM((2, rows, width), low),
            pltpu.VMEM((rows, width), low),
            pltpu.VMEM((2, rows // 2, width), low),
            pltpu.VMEM((rows, width), low),
            pltpu.VMEM((rows, width), low),
            pltpu.VMEM((rows, width), low),
            pltpu.VMEM((rows, width), low),
            pltpu.VMEM((rows, width), low),
            dma((5,)),
            dma((4,)),
            dma((4,)),
            dma((60,)),
            dma((60,)),
            dma((3,)),
            dma((3,)),
            dma((7,)),
            dma((7,)),
            dma((1,)),
            dma((3,)),
            dma((3,)),
        ],
        compiler_params=pltpu.CompilerParams(
            collective_id=cid, has_side_effects=True, vmem_limit_bytes=52 * 2**20
        ),
    )(xn, d_q_kv, d_low, mixed, gains, down, d_xn, x, mid, d_mid, gain, order)


def grads_kernel(dy_ref, xn_ref, h_ref, d_ref, o_ref):
    def product(left, right):
        o_ref[...] = lax.dot_general(
            left[...], right[...], (((0,), (0,)), ((), ())), preferred_element_type=jnp.float32
        ).astype(o_ref.dtype)

    pl.when(pl.program_id(0) < 4)(lambda: product(dy_ref, h_ref))
    pl.when(pl.program_id(0) >= 4)(lambda: product(xn_ref, d_ref))


def feed_grads(dy, xn, hidden, d_gate_up):
    depth, rows = dy.shape
    tile = 256
    return pl.pallas_call(
        grads_kernel,
        grid=(12,),
        out_shape=jax.ShapeDtypeStruct((rows, 12 * tile), jnp.bfloat16),
        in_specs=[
            pl.BlockSpec((depth, rows), lambda j: (0, 0)),
            pl.BlockSpec((depth, rows), lambda j: (0, 0)),
            pl.BlockSpec((depth, tile), lambda j: (0, jnp.minimum(j, 3))),
            pl.BlockSpec((depth, tile), lambda j: (0, jnp.maximum(j - 4, 0))),
        ],
        out_specs=pl.BlockSpec((rows, tile), lambda j: (0, j)),
        compiler_params=pltpu.CompilerParams(vmem_limit_bytes=40 * 2**20),
        cost_estimate=pl.CostEstimate(
            flops=2 * depth * rows * 12 * tile,
            bytes_accessed=4 * depth * rows + 2 * rows * 12 * tile,
            transcendentals=0,
        ),
    )(dy, xn, hidden, d_gate_up)


def rms_norm(values, gain_row):
    return (
        values * lax.rsqrt(jnp.mean(values * values, axis=-1, keepdims=True) + norm_eps) * gain_row
    )


def geglu(gate_part, up_part):
    return jax.nn.gelu(gate_part) * up_part


def tables():
    half_rot = ROT // 2
    rates = jnp.exp(jnp.arange(half_rot, dtype=jnp.float32) * (-2.0 * math.log(10000.0) / ROT))
    angles = jnp.arange(SEQ_LEN, dtype=jnp.float32)[:, None] * rates[None, :]
    return (jnp.cos(angles), jnp.sin(angles))


def rotate(field, cosine, sine):
    half_rot = ROT // 2
    first = field[..., :half_rot]
    second = field[..., half_rot:ROT]
    return jnp.concatenate(
        [first * cosine - second * sine, second * cosine + first * sine, field[..., ROT:]], axis=-1
    )


def contract(left, right, left_dim, right_dim):
    return lax.dot_general(
        left, right, (((left_dim,), (right_dim,)), ((), ())), preferred_element_type=jnp.float32
    )


def padded(weight):
    return jnp.pad(weight.reshape(40, 4, 960), ((0, 0), (0, 0), (0, 64)))


def local(
    tokens,
    attn_gain,
    query_weight,
    kv_weight,
    out_weight,
    mlp_gain,
    gate_weight,
    up_weight,
    down_weight,
    cotangent,
):
    low = jnp.bfloat16
    rows = tokens.shape[0]
    seqs = rows // SEQ_LEN
    heads_here = query_weight.shape[1] // HEAD_DIM
    wide = heads_here * HEAD_DIM
    scale = HEAD_DIM ** (-0.5)
    cosine, sine = tables()
    positions = jnp.arange(SEQ_LEN)
    keep_mask = (positions[:, None] >= positions[None, :]) & (
        positions[:, None] - positions[None, :] < WINDOW
    )
    attn = jnp.concatenate([query_weight, kv_weight, out_weight.T], axis=1)
    attn = attn.reshape(40, 2, 2, ATTN).transpose(1, 2, 0, 3)
    attn = jnp.broadcast_to(attn, (2, *attn.shape)).reshape(4, 2, 40, ATTN)
    first = attn.reshape(4, 80, ATTN)
    gains = jnp.pad(jnp.stack([attn_gain, mlp_gain], axis=0), ((0, 14), (0, 88)))
    gains = jnp.broadcast_to(gains, (4, 16, 128))
    down = padded(down_weight.T).reshape(40, 4, 2, FEED).transpose(1, 2, 0, 3).reshape(4, 80, FEED)
    second = jnp.stack([padded(gate_weight), padded(up_weight)], axis=0)
    second = second.transpose(2, 0, 1, 3).reshape(4, 80, 2 * FEED)
    order = jnp.asarray(feature_order(), low)
    first, gains, second, x_in, dy_here = group_exchange(
        [first, gains, second], tokens, cotangent, order, 5
    )
    second = second.reshape(4, 2, 40, 2 * FEED).transpose(0, 2, 1, 3).reshape(160, 4 * FEED)
    w_gate_up = lax.all_gather(second, PLANE, axis=0, tiled=True)
    first = first.reshape(4, 2, 40, ATTN).transpose(1, 0, 2, 3).reshape(2, 160, ATTN)
    w_q_kv, w_out_t, gains, dy, down = attention_gather(first, gains.reshape(64, 128), dy_here, down, 6)
    gains = gains.reshape(64, 16, 128)[:, :2, :40].transpose(1, 0, 2).reshape(2, 2560).astype(jnp.float32)
    down = down.reshape(4, 2, 40, FEED).transpose(1, 0, 2, 3).reshape(2, 160, FEED)
    dy = dy.reshape(4 * rows, -1)
    gain_one, gain_two = gains[0], gains[1]

    xn_one = rms_norm(x_in, gain_one).astype(low)
    q_kv_pre = jnp.dot(xn_one, w_q_kv, preferred_element_type=jnp.float32)
    q_pre, kv_pre = q_kv_pre[:, :wide], q_kv_pre[:, wide:]
    queries = rotate(
        q_pre.reshape(seqs, SEQ_LEN, heads_here, HEAD_DIM), cosine[:, None, :], sine[:, None, :]
    ).astype(low)
    key_rot = rotate(kv_pre[:, :HEAD_DIM].reshape(seqs, SEQ_LEN, HEAD_DIM), cosine, sine).astype(low)
    value_rows = kv_pre[:, HEAD_DIM:].reshape(seqs, SEQ_LEN, HEAD_DIM).astype(low)

    def score_rows():
        raw = (
            jnp.einsum("sqhd,skd->shqk", queries, key_rot, preferred_element_type=jnp.float32)
            * scale
        )
        return jnp.where(keep_mask, raw, -1e30)

    scores = score_rows()
    row_max = jnp.max(scores, axis=-1, keepdims=True)
    log_total = row_max + jnp.log(jnp.sum(jnp.exp(scores - row_max), axis=-1, keepdims=True))
    attn_probs = jnp.exp(scores - log_total).astype(low)
    mixed_heads = jnp.einsum(
        "shqk,skd->sqhd", attn_probs, value_rows, preferred_element_type=jnp.float32
    )
    mixed_heads = mixed_heads.reshape(rows, wide).astype(low)
    attn_part = contract(mixed_heads, w_out_t, 1, 1).astype(low)
    x_mid, xn_all, w_down_t = middle(attn_part, x_in, gain_two[None, :], down, 2)
    xn_all = xn_all.reshape(4 * rows, -1)
    gate_up = jnp.dot(xn_all, w_gate_up, preferred_element_type=jnp.float32)
    gate_pre, up_pre = gate_up[:, : 2 * FEED], gate_up[:, 2 * FEED :]
    hidden = geglu(gate_pre, up_pre).astype(low)
    down_part = contract(hidden, w_down_t, 1, 1).astype(low)
    d_hidden = jnp.dot(dy, w_down_t, preferred_element_type=jnp.float32)
    geglu_pull = jax.vjp(geglu, gate_pre, up_pre)[1]
    d_gate_pre, d_up_pre = geglu_pull(d_hidden)
    d_gate_low = d_gate_pre.astype(low)
    d_up_low = d_up_pre.astype(low)
    d_gate_up = jnp.concatenate([d_gate_low, d_up_low], axis=1)
    sent = feed_grads(dy, xn_all, hidden, d_gate_up)
    sent = lax.psum_scatter(sent, PLANE, scatter_dimension=0, tiled=True)
    sent = sent.reshape(4, 40, 3, 2, FEED).transpose(0, 2, 3, 1, 4).reshape(4, 240, FEED)
    d_xn_two_part = contract(d_gate_up, w_gate_up, 1, 1)
    d_xn_two = token_sum(d_xn_two_part.astype(low).reshape(4, rows, -1), 3)

    norm_two_pull = jax.vjp(rms_norm, x_mid, gain_two)[1]
    d_mid_norm, d_gain_two = norm_two_pull(d_xn_two)
    d_mid = dy_here.astype(jnp.float32) + d_mid_norm
    d_mid_low = d_mid.astype(low)
    d_mixed = (
        jnp.dot(d_mid_low, w_out_t, preferred_element_type=jnp.float32)
        .astype(low)
        .reshape(seqs, SEQ_LEN, heads_here, HEAD_DIM)
    )
    soft_rows = jnp.exp(score_rows() - log_total)
    d_probs = jnp.einsum("sqhd,skd->shqk", d_mixed, value_rows, preferred_element_type=jnp.float32)
    d_scores = (
        soft_rows * (d_probs - jnp.sum(soft_rows * d_probs, axis=-1, keepdims=True))
    ).astype(low)
    d_queries = (
        jnp.einsum("shqk,skd->sqhd", d_scores, key_rot, preferred_element_type=jnp.float32) * scale
    )
    d_keys = (
        jnp.einsum("shqk,sqhd->skd", d_scores, queries, preferred_element_type=jnp.float32) * scale
    )
    d_values = jnp.einsum("shqk,sqhd->skd", attn_probs, d_mixed, preferred_element_type=jnp.float32)
    d_q_pre = (
        rotate(d_queries, cosine[:, None, :], -sine[:, None, :]).reshape(rows, wide).astype(low)
    )
    d_k_pre = rotate(d_keys, cosine, -sine).reshape(rows, HEAD_DIM)
    d_kv_part = jnp.concatenate([d_k_pre, d_values.reshape(rows, HEAD_DIM)], axis=-1)
    d_kv_low = pair_sum(d_kv_part.astype(low), 4).astype(low)
    d_xn_one = contract(jnp.concatenate([d_q_pre, d_kv_low * 0.5], axis=1), w_q_kv, 1, 1)
    norm_one_pull = jax.vjp(lambda g: rms_norm(x_in, g), gain_one)[1]
    d_gain_one = norm_one_pull(d_xn_one)[0]
    d_gains = jnp.stack([d_gain_one, 0.5 * d_gain_two], axis=0).astype(low)
    d_gains = d_gains.reshape(2, 64, 40).transpose(1, 0, 2)
    d_gains = jnp.pad(d_gains, ((0, 0), (0, 14), (0, 88))).reshape(1024, 128)
    attn_out, gain_out, block_out, tokens_grad = plane_sum(
        xn_one,
        jnp.concatenate([d_q_pre, d_kv_low], axis=1),
        d_mid_low,
        mixed_heads,
        d_gains,
        down_part.reshape(4, rows, -1),
        d_xn_one.astype(low),
        x_in,
        x_mid,
        d_mid,
        gain_one[None, :],
        order,
        7,
    )
    down_out, gate_out, up_out = finish(sent, 8)
    return (
        block_out,
        tokens_grad,
        gain_out[0, :40],
        attn_out[:, :wide],
        attn_out[:, wide : wide + 2 * HEAD_DIM],
        attn_out[:, wide + 2 * HEAD_DIM :].T,
        gain_out[1, :40],
        gate_out,
        up_out,
        down_out.T,
    )


def solution(mesh):
    fine = Mesh(mesh.devices.reshape(4, 2, 4, 2, 2), AXES)
    dp = ("y", "zl", "x", "c")
    in_specs = (
        P(dp, None),
        P(dp),
        P(dp, "zh"),
        P(dp, None),
        P("zh", dp),
        P(dp),
        P(dp, "zh"),
        P(dp, "zh"),
        P("zh", dp),
        P(dp, None),
    )
    out_specs = (
        P(dp, None),
        P(dp, None),
        P(dp),
        P(dp, "zh"),
        P(dp, None),
        P("zh", dp),
        P(dp),
        P(dp, "zh"),
        P(dp, "zh"),
        P("zh", dp),
    )
    return jax.shard_map(local, mesh=fine, in_specs=in_specs, out_specs=out_specs, check_vma=False)
```

```python
import math

import jax
import jax.numpy as jnp
import numpy as np
from jax import lax
from jax.experimental import pallas as pl
from jax.experimental.pallas import tpu as pltpu
from jax.sharding import Mesh
from jax.sharding import PartitionSpec as P

HEAD_DIM = 256
WINDOW = 2048
SEQ_LEN = 128
ROT = 128
AXES = ("y", "zl", "x", "c", "zh")
PLANE = ("y", "x")
GROUP = ("zl", "c")
OWNERS = ("y", "x", "zl", "c")
MESH = pl.DeviceIdType.MESH

norm_eps = 1e-06


def feature_order():
    place = np.arange(640).reshape(2, 4, 80).transpose(1, 0, 2).reshape(640)
    return (np.arange(640)[:, None] == place[None, :]).astype(np.float32)


def reorder(src, order, dst, back):
    for k in range(4):
        group = pl.ds(k * 640, 640)
        dst[:, group] = lax.dot_general(
            src[:, group],
            order[...],
            (((1,), (1 if back else 0,)), ((), ())),
            preferred_element_type=jnp.float32,
        ).astype(dst.dtype)


def greet(peers):
    barrier = pltpu.get_barrier_semaphore()
    for peer in peers:
        pl.semaphore_signal(barrier, inc=1, device_id=peer, device_id_type=MESH)
    pl.semaphore_wait(barrier, len(peers))


def remote(src, dst, send, recv, peer):
    return pltpu.make_async_remote_copy(
        src_ref=src, dst_ref=dst, send_sem=send, recv_sem=recv, device_id=peer, device_id_type=MESH
    )


def fetch(pairs, sems):
    copies = [pltpu.make_async_copy(src, dst, sems.at[k]) for k, (src, dst) in enumerate(pairs)]
    for copy in copies:
        copy.start()
    return copies


def buffers(*arrays):
    return [pltpu.VMEM(a.shape, a.dtype) for a in arrays]


HBM = pl.BlockSpec(memory_space=pltpu.HBM)


def ring_of(axis, at):
    return {axis: lax.rem(at + 3, 4)}, {axis: lax.rem(at + 1, 4)}


def send_blocks(ins, outs, here, send, recv):
    zl, c = lax.axis_index("zl"), lax.axis_index("c")
    mine = zl * 2 + c
    peers = [({"zl": 1 - zl, "c": k}, (1 - zl) * 2 + k) for k in range(2)]
    peers.append(({"c": 1 - c}, zl * 2 + 1 - c))
    n = len(ins)
    copies, keeps = [], []
    for i in range(n):
        for k, (peer, block) in enumerate(peers):
            landing = i * 3 + (c if k < 2 else 2)
            copy = remote(ins[i].at[block], outs[i].at[mine], send.at[i * 3 + k], recv.at[landing], peer)
            copy.start()
            copies.append(copy)
    for i in range(n):
        keep = pltpu.make_async_copy(ins[i].at[mine], outs[i].at[mine], here.at[i])
        keep.start()
        keeps.append(keep)

    def finish():
        for keep in keeps:
            keep.wait()
        for i in range(n):
            for k, (peer, block) in enumerate(peers):
                remote(
                    ins[i].at[block], outs[i].at[block], send.at[i * 3 + k], recv.at[i * 3 + k], peer
                ).wait_recv()
        for copy in copies:
            copy.wait_send()

    return finish


def group_peers():
    zl, c = lax.axis_index("zl"), lax.axis_index("c")
    return [{"c": 1 - c}, {"zl": 1 - zl, "c": 0}, {"zl": 1 - zl, "c": 1}]


def exchange_kernel(
    a_ref, g_ref, s_ref, tok_ref, cot_ref, order_ref,
    ao_out, go_ref, so_out, x_out, dy_out,
    al, sl, ao_ref, so_ref, x_ref, dy_ref, here, send, recv, out_sem
):
    greet(group_peers())
    finish = send_blocks([a_ref, g_ref, s_ref], [al, go_ref, sl], here, send, recv)
    reorder(tok_ref, order_ref, x_ref, False)
    reorder(cot_ref, order_ref, dy_ref, False)
    puts = fetch([(x_ref, x_out), (dy_ref, dy_out)], out_sem)
    finish()
    f32, low = jnp.float32, jnp.bfloat16
    for h in range(2):
        parts = [al[t].astype(f32)[h * 40 : (h + 1) * 40] for t in range(4)]
        ao_ref[h] = jnp.concatenate(parts, axis=0).astype(low)
    for k in range(2):
        parts = [sl[t].astype(f32) for t in (2 * k, 2 * k + 1)]
        parts = [jnp.concatenate([v[:40], v[40:]], axis=1) for v in parts]
        so_ref[pl.ds(k * 80, 80)] = jnp.concatenate(parts, axis=0).astype(low)
    last = fetch([(ao_ref, ao_out), (so_ref, so_out)], out_sem.at[pl.ds(2, 2)])
    for put in (*puts, *last):
        put.wait()


def group_exchange(attn, gains, second, tokens, cotangent, order, cid):
    low, dma = jnp.bfloat16, pltpu.SemaphoreType.DMA
    anywhere, vmem = pl.BlockSpec(memory_space=pl.ANY), pl.BlockSpec(memory_space=pltpu.VMEM)
    shapes = [
            jax.ShapeDtypeStruct((2, 160, attn.shape[2]), low),
            jax.ShapeDtypeStruct(gains.shape, low),
            jax.ShapeDtypeStruct((160, 2 * second.shape[2]), low),
            jax.ShapeDtypeStruct(tokens.shape, jnp.float32),
            jax.ShapeDtypeStruct(cotangent.shape, low),
        ]
    return pl.pallas_call(
        exchange_kernel,
        out_shape=shapes,
        in_specs=[anywhere] * 3 + [vmem] * 3,
        out_specs=[HBM] * 5,
        scratch_shapes=[
            pltpu.VMEM(attn.shape, low),
            pltpu.VMEM(second.shape, low),
            *buffers(shapes[0], *shapes[2:]),
            dma((3,)),
            dma((9,)),
            dma((9,)),
            dma((4,)),
        ],
        compiler_params=pltpu.CompilerParams(
            collective_id=cid, has_side_effects=True, vmem_limit_bytes=60 * 2**20
        ),
    )(attn, gains, second, tokens, cotangent, order)


ATTN, FEED = 768, 512
WIDE = ATTN + FEED


def shift(i, by):
    return lax.rem(i + by, 4)


def around(h, y, x):
    if h == 0:
        return x, ring_of("x", x), y, ring_of("y", y)
    return y, ring_of("y", y), x, ring_of("x", x)


class Piece:
    def __init__(self, h, source, target, columns, rows=160):
        self.h, self.source, self.target, self.columns, self.rows = h, source, target, columns, rows

    def own(self):
        return self.source

    def at(self, i1, i2, part=None):
        row, column = (i2, i1) if self.h == 0 else (i1, i2)
        size = self.rows if part is None else self.rows // 2
        first = (row * 4 + column) * self.rows + (0 if part is None else part * size)
        return self.target.at[pl.ds(pl.multiple_of(first, 16), size), self.columns]


def gather_steps(y, x, pieces, send, recv, cross):
    started = []

    def go(src, dst, n, ring, slot, peer):
        k = (n * 5 + ring) * 4 + slot
        copy = remote(src, dst, send.at[k], recv.at[k], peer)
        copy.start()
        started.append(copy)

    def arrived(dst, n, ring, slot):
        k = (n * 5 + ring) * 4 + slot
        remote(dst, dst, send.at[k], recv.at[k], {"c": 1 - lax.axis_index("c")}).wait_recv()

    each = [(n, p, *around(p.h, y, x)) for n, p in enumerate(pieces)]
    firsts = ((1, 0), (2, 3), (3, 1), (4, 2))

    def own_blocks():
        for n, p, i1, (back1, ahead1), i2, _ in each:
            go(p.own(), p.at(i1, i2), n, 0, 0, ahead1)
            go(p.own(), p.at(i1, i2), n, 0, 1, back1)
        for n, p, i1, _, i2, (back2, ahead2) in each:
            go(p.own(), p.at(i1, i2), n, 1, 0, ahead2)
            go(p.own(), p.at(i1, i2), n, 1, 1, back2)
            cross(n, p.own(), p.at(i1, i2))

    def first_axis():
        for n, p, i1, (back1, ahead1), i2, (back2, ahead2) in each:
            left, right = p.at(shift(i1, 3), i2), p.at(shift(i1, 1), i2)
            arrived(left, n, 0, 0)
            low = p.at(shift(i1, 3), i2, 0)
            go(low, low, n, 0, 2, ahead1)
            arrived(right, n, 0, 1)
            high = p.at(shift(i1, 1), i2, 1)
            go(high, high, n, 0, 3, back1)
            for ring, ref in ((2, left), (3, right)):
                go(ref, ref, n, ring, 0, ahead2)
                go(ref, ref, n, ring, 1, back2)
                cross(n, ref, ref)
        for n, p, i1, _, i2, (back2, ahead2) in each:
            far = shift(i1, 2)
            arrived(p.at(far, i2, 0), n, 0, 2)
            arrived(p.at(far, i2, 1), n, 0, 3)
            ref = p.at(far, i2)
            go(ref, ref, n, 4, 0, ahead2)
            go(ref, ref, n, 4, 1, back2)
            cross(n, ref, ref)

    def second_axis():
        for ring, by in firsts:
            for n, p, i1, _, i2, (back2, ahead2) in each:
                j = shift(i1, by)
                left, right = p.at(j, shift(i2, 3)), p.at(j, shift(i2, 1))
                arrived(left, n, ring, 0)
                low = p.at(j, shift(i2, 3), 0)
                go(low, low, n, ring, 2, ahead2)
                cross(n, left, left)
                arrived(right, n, ring, 1)
                high = p.at(j, shift(i2, 1), 1)
                go(high, high, n, ring, 3, back2)
                cross(n, right, right)

    def last():
        for ring, by in firsts:
            for n, p, i1, _, i2, _ in each:
                j, far = shift(i1, by), shift(i2, 2)
                arrived(p.at(j, far, 0), n, ring, 2)
                arrived(p.at(j, far, 1), n, ring, 3)
                cross(n, p.at(j, far), p.at(j, far))
        for copy in started:
            copy.wait_send()

    return own_blocks, first_axis, second_axis, last


def attention_gather_kernel(
    in_ref, g_ref, dy_ref, d_ref, a_ref, o_ref, go_ref, all_ref, do_out,
    dl, do_ref, do_sem, here, send, recv, csend, crecv, dsend, drecv, xhere, xsend, xrecv,
):
    y, x, c = lax.axis_index("y"), lax.axis_index("x"), lax.axis_index("c")
    zl, zh = lax.axis_index("zl"), lax.axis_index("zh")
    core = {"c": 1 - c}
    chips = [{"zl": 1 - zl, "zh": k} for k in range(2)]
    greet([*ring_of("x", x), *ring_of("y", y), core, *chips, {"zl": 1 - zl, "c": 1 - c}])
    whole = pl.ds(0, 160)

    for side in range(2):

        @pl.when(c == side)
        def _(side=side):
            sources = [
                in_ref.at[0, whole, pl.ds(0, 256)],
                in_ref.at[0, whole, pl.ds(256, 512)],
                in_ref.at[1, whole, pl.ds(0, 768)],
                g_ref,
            ]
            if side == 0:
                targets = [(a_ref, 0, 256), (a_ref, 256, 512), (a_ref, 768, 768)]
            else:
                targets = [(a_ref, 1536, 256), (o_ref, 0, 512), (o_ref, 512, 768)]
            targets.append((go_ref, 0, 128))
            pieces = [
                Piece(h, source, ref, pl.ds(first, width), rows)
                for h, source, (ref, first, width), rows in zip((0, 0, 1, 0), sources, targets, (160, 160, 160, 64))
            ]
            crossed = []

            def cross(n, src, dst):
                if n < 3:
                    k = len(crossed)
                    copy = remote(src, dst, csend.at[k], crecv.at[k], core)
                    copy.start()
                    crossed.append(copy)

            own_blocks, first_axis, second_axis, last = gather_steps(y, x, pieces, send, recv, cross)
            own_blocks()
            keeps = []
            for n, p in enumerate(pieces):
                i1, _, i2, _ = around(p.h, y, x)
                keeps.append(pltpu.make_async_copy(p.own(), p.at(i1, i2), here.at[n]))
                keeps[-1].start()
            finish = send_blocks([d_ref], [dl], xhere, xsend, xrecv)
            half = dy_ref.shape[0] // 2
            mine, other = zl * 2 + c, (1 - zl) * 2 + c
            part = pl.ds(pl.multiple_of(zh * half, half), half)
            away = [
                remote(dy_ref.at[part], all_ref.at[mine, part], dsend.at[k], drecv.at[zh], chips[k])
                for k in range(2)
            ]
            across = remote(dy_ref, all_ref.at[mine], dsend.at[2], drecv.at[2], core)
            for copy in (*away, across):
                copy.start()
            keeps.append(pltpu.make_async_copy(dy_ref, all_ref.at[mine], here.at[4]))
            keeps[-1].start()
            first_axis()
            finish()
            for h in range(2):
                parts = [dl[t].astype(jnp.float32)[h * 40 : (h + 1) * 40] for t in range(4)]
                do_ref[h] = jnp.concatenate(parts, axis=0).astype(jnp.bfloat16)
            puts = fetch([(do_ref, do_out)], do_sem)
            second_axis()
            passed = []
            for k in range(2):
                rows = pl.ds(k * half, half)
                there = all_ref.at[other, rows]
                remote(dy_ref.at[rows], there, dsend.at[k], drecv.at[k], chips[k]).wait_recv()
                passed.append(remote(there, there, dsend.at[3 + k], drecv.at[3 + k], core))
                passed[-1].start()
            last()
            for copy in (*crossed, *passed, across):
                copy.wait()
            for copy in away:
                copy.wait_send()
            for keep in (*keeps, *puts):
                keep.wait()


def attention_gather(own, gains, dy, down, cid):
    kind, dma = jnp.bfloat16, pltpu.SemaphoreType.DMA
    return pl.pallas_call(
        attention_gather_kernel,
        out_shape=[
            jax.ShapeDtypeStruct((2560, 1792), kind),
            jax.ShapeDtypeStruct((2560, 1280), kind),
            jax.ShapeDtypeStruct((1024, 128), kind),
            jax.ShapeDtypeStruct((4, *dy.shape), kind),
            jax.ShapeDtypeStruct((2, 160, down.shape[2]), kind),
        ],
        in_specs=[HBM] * 4,
        out_specs=[HBM] * 5,
        scratch_shapes=[
            pltpu.VMEM(down.shape, kind),
            pltpu.VMEM((2, 160, down.shape[2]), kind),
            dma((1,)),
            dma((5,)),
            dma((80,)),
            dma((80,)),
            dma((48,)),
            dma((48,)),
            dma((5,)),
            dma((5,)),
            dma((1,)),
            dma((3,)),
            dma((3,)),
        ],
        compiler_params=pltpu.CompilerParams(collective_id=cid, has_side_effects=True),
    )(own, gains, dy, down)


def middle_kernel(
    x_in, g1_ref, g2_ref, cos_ref, sin_ref, wq_ref, wo_ref, d_ref,
    mid_out, all_out, w_ref, xn_out, mixed_out, q_out, kv_out, soft_out,
    x_ref, mid_ref, all_ref, xn_ref, mixed_ref, q_ref, kv_ref, soft_ref, in_sem, out_sem,
    wq, wo, p_ref, landed, here, wsem, psend, precv, gsend, grecv, send, recv, csend, crecv,
):
    y, x, c = lax.axis_index("y"), lax.axis_index("x"), lax.axis_index("c")
    zl, zh = lax.axis_index("zl"), lax.axis_index("zh")
    core, far = {"c": 1 - c}, {"zh": 1 - zh}
    chips = [{"zl": 1 - zl, "zh": k} for k in range(2)]
    f32, low = jnp.float32, jnp.bfloat16
    heads = soft_ref.shape[0]
    get_x = fetch([(x_in, x_ref)], in_sem)[0]
    loads = []
    for k in range(heads + 2):
        columns = pl.ds(k * HEAD_DIM, HEAD_DIM)
        loads.append(pltpu.make_async_copy(wq_ref.at[:, columns], wq.at[:, columns], wsem.at[k]))
    for k in range(5):
        some = pl.ds(k * 512, 512)
        loads.append(pltpu.make_async_copy(wo_ref.at[some], wo.at[some], wsem.at[heads + 2 + k]))
    for k in (heads, heads + 1, *range(heads), *range(heads + 2, heads + 7)):
        loads[k].start()
    greet([*ring_of("x", x), *ring_of("y", y), core, far, *chips])
    pieces = [
        Piece(h, d_ref.at[h, pl.ds(0, 160)], w_ref, pl.ds(h * FEED, FEED)) for h in range(2)
    ]
    own_blocks, first_axis, second_axis, last = gather_steps(
        y, x, pieces, send, recv, lambda n, src, dst: None
    )
    own_blocks()
    keeps = []
    for n, p in enumerate(pieces):
        i1, _, i2, _ = around(p.h, y, x)
        keeps.append(pltpu.make_async_copy(p.own(), p.at(i1, i2), here.at[n]))
        keeps[-1].start()
    half, step = x_ref.shape[0] // 2, 16
    get_x.wait()

    @pl.loop(0, 2 * half // step)
    def _(i):
        at = pl.ds(pl.multiple_of(i * step, step), step)
        v = x_ref[at]
        r = lax.rsqrt(jnp.mean(v * v, axis=-1, keepdims=True) + norm_eps)
        xn_ref[c, at] = (v * r * g1_ref[...]).astype(low)

    shared = [remote(xn_ref.at[c], xn_ref.at[c], csend.at[0], crecv.at[0], core)]
    shared[0].start()

    def projected(k):
        loads[k].wait()
        return jnp.dot(xn_ref[c], wq[:, k * HEAD_DIM : (k + 1) * HEAD_DIM], preferred_element_type=f32)

    def rotated(u):
        turn = u[:, :ROT]
        turn = turn * cos_ref[...] + pltpu.roll(turn, ROT // 2, 1) * sin_ref[...]
        return jnp.concatenate([turn, u[:, ROT:]], axis=1).astype(low)

    kv_ref[:, :HEAD_DIM] = rotated(projected(heads))
    kv_ref[:, HEAD_DIM:] = projected(heads + 1).astype(low)
    rows = lax.broadcasted_iota(jnp.int32, (SEQ_LEN, SEQ_LEN), 0)
    behind = rows - lax.broadcasted_iota(jnp.int32, (SEQ_LEN, SEQ_LEN), 1)
    keep_mask = (behind >= 0) & (behind < WINDOW)
    for h in range(heads):
        columns = pl.ds(h * HEAD_DIM, HEAD_DIM)
        q = rotated(projected(h))
        q_ref[:, columns] = q
        scores = lax.dot_general(
            q, kv_ref[:, :HEAD_DIM], (((1,), (1,)), ((), ())), preferred_element_type=f32
        )
        scores = jnp.where(keep_mask, scores * HEAD_DIM**-0.5, -1e30)
        top = jnp.max(scores, axis=-1, keepdims=True)
        total = top + jnp.log(jnp.sum(jnp.exp(scores - top), axis=-1, keepdims=True))
        soft = jnp.exp(scores - total)
        soft_ref[h] = soft
        mixed_ref[c, :, columns] = jnp.dot(
            soft.astype(low), kv_ref[:, HEAD_DIM:], preferred_element_type=f32
        ).astype(low)
    shared.append(remote(mixed_ref.at[c], mixed_ref.at[c], csend.at[1], crecv.at[1], core))
    shared[1].start()
    puts = fetch([(q_ref, q_out), (kv_ref, kv_out), (soft_ref, soft_out)], out_sem)
    for k in range(5):
        loads[heads + 2 + k].wait()
        some = pl.ds(k * 512, 512)
        p_ref[:, some] = lax.dot_general(
            mixed_ref[c], wo[some], (((1,), (1,)), ((), ())), preferred_element_type=f32
        ).astype(low)
    mine, other = zl * 2 + c, (1 - zl) * 2 + c
    parts = [pl.ds(pl.multiple_of(k * half, half), half) for k in (1 - zh, zh)]
    pair = [
        remote(p_ref.at[part], landed.at[part], psend.at[k], precv.at[k], far)
        for k, part in enumerate(parts)
    ]
    for copy in pair:
        copy.start()
    first_axis()
    away, across = [], []
    for k in range(2):
        part = parts[1 - k]
        pair[k].wait_recv()
        first = (zh if k == 0 else 1 - zh) * half

        @pl.loop(0, half // step)
        def _(i, first=first):
            at = pl.ds(pl.multiple_of(first + i * step, step), step)
            branch = p_ref[at].astype(f32) + landed[at].astype(f32)
            v = x_ref[at] + branch
            mid_ref[at] = v
            r = lax.rsqrt(jnp.mean(v * v, axis=-1, keepdims=True) + norm_eps)
            all_ref[mine, at] = (v * r * g2_ref[...]).astype(low)

        ready = all_ref.at[mine, part]
        if k == 0:
            for i in range(2):
                away.append(remote(ready, ready, gsend.at[i], grecv.at[zh], chips[i]))
                away[-1].start()
        across.append(remote(ready, ready, gsend.at[2 + k], grecv.at[2 + k], core))
        across[-1].start()
        if k == 0:
            second_axis()
    passed = []
    for k in range(2):
        there = all_ref.at[other, pl.ds(k * half, half)]
        remote(there, there, gsend.at[k], grecv.at[k], chips[k]).wait_recv()
        passed.append(remote(there, there, gsend.at[4 + k], grecv.at[4 + k], core))
        passed[-1].start()
    last()
    for copy in (*across, *passed, *shared):
        copy.wait()
    puts += fetch(
        [(mid_ref, mid_out), (all_ref, all_out), (xn_ref, xn_out), (mixed_ref, mixed_out)],
        out_sem.at[pl.ds(3, 4)],
    )
    for copy in (*away, *pair):
        copy.wait_send()
    for keep in (*keeps, *puts):
        keep.wait()


def middle(x, gain_one, gain_two, cosine, sine, w_q_kv, w_out_t, down, cid):
    dma, f32, low = pltpu.SemaphoreType.DMA, jnp.float32, jnp.bfloat16
    vmem = pl.BlockSpec(memory_space=pltpu.VMEM)
    rows, width = x.shape
    wide = w_out_t.shape[1]
    heads = wide // HEAD_DIM
    shapes = [
        jax.ShapeDtypeStruct(x.shape, f32),
        jax.ShapeDtypeStruct((4, *x.shape), low),
        jax.ShapeDtypeStruct((2560, 2 * FEED), low),
        jax.ShapeDtypeStruct((2, rows, width), low),
        jax.ShapeDtypeStruct((2, rows, wide), low),
        jax.ShapeDtypeStruct((rows, wide), low),
        jax.ShapeDtypeStruct((rows, 2 * HEAD_DIM), low),
        jax.ShapeDtypeStruct((heads, rows, rows), f32),
    ]
    return pl.pallas_call(
        middle_kernel,
        out_shape=shapes,
        in_specs=[HBM] + [vmem] * 4 + [HBM] * 3,
        out_specs=[HBM] * 8,
        scratch_shapes=[
            *buffers(x, *shapes[:2], *shapes[3:]),
            dma((1,)),
            dma((7,)),
            pltpu.VMEM(w_q_kv.shape, low),
            pltpu.VMEM(w_out_t.shape, low),
            pltpu.VMEM(x.shape, low),
            pltpu.VMEM(x.shape, low),
            dma((2,)),
            dma((heads + 7,)),
            dma((2,)),
            dma((2,)),
            dma((6,)),
            dma((6,)),
            dma((40,)),
            dma((40,)),
            dma((2,)),
            dma((2,)),
        ],
        compiler_params=pltpu.CompilerParams(
            collective_id=cid, has_side_effects=True, vmem_limit_bytes=60 * 2**20
        ),
    )(x, gain_one, gain_two, cosine, sine, w_q_kv, w_out_t, down)


def finish_kernel(s_in, down_ref, gate_ref, up_ref, s_ref, in_sem, blocks, landed, here, send, recv):
    get = fetch([(s_in, s_ref)], in_sem)[0]
    greet(group_peers())
    get.wait()
    wide = s_ref.shape[1] // 2
    for t in range(4):
        first = t * 40 // 16 * 16
        size = (t * 40 + 40 + 15) // 16 * 16 - first
        v = s_ref[pl.ds(first, size)].astype(jnp.float32)[t * 40 - first : t * 40 - first + 40]
        blocks[t] = jnp.concatenate([v[:, :wide], v[:, wide:]], axis=0).astype(jnp.bfloat16)
    send_blocks([blocks], [landed], here, send, recv)()
    for t in range(4):
        v = landed[t].astype(jnp.float32)
        v = jnp.concatenate([v[:40], v[40:]], axis=1)
        for k, out in enumerate((down_ref, gate_ref, up_ref)):
            out[:, t * 960 : (t + 1) * 960] = v[:, k * 2 * FEED : k * 2 * FEED + 960]


def finish(sent, cid):
    dma = pltpu.SemaphoreType.DMA
    vmem = pl.BlockSpec(memory_space=pltpu.VMEM)
    buffer = pltpu.VMEM((4, 80, sent.shape[1] // 2), sent.dtype)
    return pl.pallas_call(
        finish_kernel,
        out_shape=[jax.ShapeDtypeStruct((40, 3840), jnp.float32)] * 3,
        in_specs=[HBM],
        out_specs=[vmem] * 3,
        scratch_shapes=[*buffers(sent), dma((1,)), buffer, buffer, dma((1,)), dma((3,)), dma((3,))],
        compiler_params=pltpu.CompilerParams(
            collective_id=cid, has_side_effects=True, vmem_limit_bytes=60 * 2**20
        ),
    )(sent)


class SumPiece:
    def __init__(self, h, sums, columns, via, main, sems, rows=160):
        self.h, self.sums, self.columns, self.via, self.main, self.sems, self.rows = (
            h, sums, columns, via, main, sems, rows,
        )

    def first(self, i1, i2, part=0):
        row, column = (i2, i1) if self.h == 0 else (i1, i2)
        return (row * 4 + column) * self.rows + part * (self.rows // 2)

    def at(self, i1, i2, part=None):
        size = self.rows if part is None else self.rows // 2
        return self.sums.at[pl.ds(pl.multiple_of(self.first(i1, i2, part or 0), 16), size), self.columns]


ORDER = (
    "P0", "yv0", "yv1", "yv2", "xv0", "P1", "xv1", "P2", "xv2", "P3", "yxm0", "yxv3", "Tc", "yxm1",
    "T0", "xyt0", "xyv4", "xym2", "gv0", "gv1", "gv2", "gv3", "xyt1", "T1", "xym3", "xyt2", "gm0",
    "gm1", "gm2", "gm3", "xym4", "xyt3", "gt0", "gt1", "gt2", "gt3", "gv4", "Tg", "gm4", "xyt4",
    "gt4", "To",
)


def plane_sum_kernel(
    left_in, dq_ref, dl_ref, right_in, gi_ref, p_in, t_in, x_in, mid_in, dmid_in, g_ref, order_in,
    attn_ref, go_ref, block_ref, grad_ref,
    left, right_o, p_ref, t_ref, x_ref, mid_ref, dmid_ref, order_ref, in_sem,
    right, left_o, sums, via, main, gsums, gvia, gmain, from_chip, attn_low, gfar, gsum, gall,
    t_core, t_other, t_chips, t_own, t_far, landed, block_low, grad_low,
    here, csend, crecv, send, recv, esend, erecv, tsend, trecv, shere, ssend, srecv,
):
    y, x, c, zl, zh = (lax.axis_index(k) for k in ("y", "x", "c", "zl", "zh"))
    core, chip, far_peer = {"c": 1 - c}, {"zl": 1 - zl}, {"zh": 1 - zh}
    chips = [{"zl": 1 - zl, "zh": k} for k in range(2)]
    get_p, get_t, get_left, get_right, *gets = fetch(
        [
            (p_in, p_ref), (t_in, t_ref), (left_in, left), (right_in, right_o), (x_in, x_ref),
            (mid_in, mid_ref), (dmid_in, dmid_ref), (order_in, order_ref),
        ],
        in_sem,
    )
    greet(
        [*ring_of("x", x), *ring_of("y", y), core, *chips, far_peer, {"zl": 1 - zl, "c": 1 - c}]
    )
    step = 16
    f32, low = jnp.float32, jnp.bfloat16
    order = (2, 1, 3, 0)
    tokens = p_ref.shape[1]
    half = tokens // 2

    inputs = [(dq_ref, right), (dl_ref, left_o)]
    mine = pl.ds(pl.multiple_of(c * tokens, tokens), tokens)
    shared = [
        remote(src, dst.at[mine], csend.at[k], crecv.at[k], core) for k, (src, dst) in enumerate(inputs)
    ]
    kept = [pltpu.make_async_copy(src, dst.at[mine], here.at[k]) for k, (src, dst) in enumerate(inputs)]
    kept.append(pltpu.make_async_copy(gi_ref, gsums, here.at[2]))
    for copy in (*shared, *kept):
        copy.start()
    t_cores = [
        remote(p_ref.at[z * 2 + 1 - c], t_core.at[i], tsend.at[i], trecv.at[i], core)
        for i, z in enumerate((1 - zl, zl))
    ]
    get_p.wait()
    for copy in t_cores:
        copy.start()
    get_t.wait()
    pair = remote(t_ref, landed, tsend.at[6], trecv.at[6], far_peer)
    pair.start()
    t_sent = []

    def tokens_to_chips():
        t_cores[0].wait_recv()

        @pl.loop(0, tokens // step)
        def _(i):
            at = pl.ds(pl.multiple_of(i * step, step), step)
            total = p_ref[(1 - zl) * 2 + c, at].astype(f32) + t_core[0, at].astype(f32)
            t_other[at] = total.astype(low)

        for k in range(2):
            t_sent.append(
                remote(t_other.at[pl.ds(k * half, half)], t_chips.at[zh], tsend.at[2 + k], trecv.at[2 + zh], chips[k])
            )
            t_sent[-1].start()

    def tokens_to_far(k):
        piece = (1 - zh) if k == 0 else zh
        if k == 0:
            t_cores[1].wait_recv()
        else:
            for i in range(2):
                remote(
                    t_other.at[pl.ds(0, half)], t_chips.at[i], tsend.at[2 + i], trecv.at[2 + i], chips[i]
                ).wait_recv()

        @pl.loop(0, half // step)
        def _(i):
            at = pl.ds(pl.multiple_of(piece * half + i * step, step), step)
            total = p_ref[zl * 2 + c, at].astype(f32) + t_core[1, at].astype(f32)
            if k == 1:
                there = pl.ds(pl.multiple_of(i * step, step), step)
                total += t_chips[0, there].astype(f32) + t_chips[1, there].astype(f32)
            t_own[at] = total.astype(low)

        at = pl.ds(pl.multiple_of(piece * half, half), half)
        t_sent.append(remote(t_own.at[at], t_far.at[at], tsend.at[4 + k], trecv.at[4 + k], far_peer))
        t_sent[-1].start()

    def tokens_gradient():
        pair.wait_recv()

        @pl.loop(0, tokens // step)
        def _(i):
            at = pl.ds(pl.multiple_of(i * step, step), step)
            d = (t_ref[at].astype(f32) + landed[at].astype(f32)) * g_ref[...]
            v = x_ref[at]
            r = lax.rsqrt(jnp.mean(v * v, axis=-1, keepdims=True) + norm_eps)
            n = v * r
            d = r * (d - n * jnp.mean(d * n, axis=-1, keepdims=True))
            grad_low[at] = (dmid_ref[at] + d).astype(low)

        reorder(grad_low, order_ref, grad_ref, True)

    def tokens_output():
        for k in range(2):
            t_sent[2 + k].wait_recv()

        @pl.loop(0, tokens // step)
        def _(i):
            at = pl.ds(pl.multiple_of(i * step, step), step)
            branch = t_own[at].astype(f32) + t_far[at].astype(f32)
            block_low[at] = (mid_ref[at] + branch).astype(low)

        reorder(block_low, order_ref, block_ref, True)

    def products(q):
        top = shift(y, order[q]) * 640
        for side in range(2):

            @pl.when(c == side)
            def _(side=side):
                if side == 0:
                    parts = [(left, right, 0, 0, 768), (left, right, 768, 768, 768)]
                else:
                    parts = [
                        (left, right, 1536, 0, 256),
                        (left_o, right_o, 0, 256, 512),
                        (left_o, right_o, 512, 768, 768),
                    ]

                @pl.loop(0, 5)
                def _(i):
                    at = pl.ds(pl.multiple_of(top + i * 128, 128), 128)
                    for lhs, rhs, source, target, width in parts:
                        sums[at, pl.ds(target, width)] = lax.dot_general(
                            lhs[:, at],
                            rhs[:, pl.ds(source, width)],
                            (((0,), (0,)), ((), ())),
                            preferred_element_type=f32,
                        ).astype(low)

    pieces = [
        SumPiece(h, sums, pl.ds(h * ATTN, ATTN), via.at[h], main.at[h], h * 20) for h in range(2)
    ]
    pieces.append(SumPiece(0, gsums, pl.ds(0, 128), gvia, gmain, 40, 64))

    def add(p, first, size, terms):
        @pl.loop(0, size // step)
        def _(i):
            at = pl.ds(pl.multiple_of(first + i * step, step), step)
            total = p.sums[at, p.columns].astype(f32)
            for ref, index, start in terms:
                total += ref[(*index, pl.ds(pl.multiple_of(start + i * step, step), step))].astype(f32)
            p.sums[at, p.columns] = total.astype(low)

    started = []

    def go(p, ring, slot, src, dst, peer):
        k = p.sems + ring * 4 + slot
        copy = remote(src, dst, send.at[k], recv.at[k], peer)
        copy.start()
        started.append(copy)

    def arrived(p, ring, slot, dst):
        k = p.sems + ring * 4 + slot
        remote(dst, dst, send.at[k], recv.at[k], core).wait_recv()

    def line(p, j):
        i1, peers1, i2, peers2 = around(p.h, y, x)
        if j == 4:
            return lambda k: (k, i2), i1, peers1
        fixed = shift(i1, order[j])
        return lambda k: (fixed, k), i2, peers2

    def out_via(p, ring):
        place, at, (back, ahead) = line(p, ring)
        far = place(shift(at, 2))
        go(p, ring, 0, p.at(*far, 0), p.via.at[ring, 0], ahead)
        go(p, ring, 1, p.at(*far, 1), p.via.at[ring, 1], back)

    def out_main(p, ring):
        place, at, (back, ahead) = line(p, ring)
        small = p.rows // 2
        arrived(p, ring, 0, p.via.at[ring, 0])
        add(p, p.first(*place(shift(at, 1)), 0), small, [(p.via, (ring, 0), 0)])
        go(p, ring, 2, p.at(*place(shift(at, 1))), p.main.at[ring, 0], ahead)
        arrived(p, ring, 1, p.via.at[ring, 1])
        add(p, p.first(*place(shift(at, 3)), 1), small, [(p.via, (ring, 1), 0)])
        go(p, ring, 3, p.at(*place(shift(at, 3))), p.main.at[ring, 1], back)

    def take(p, ring):
        place, at, _ = line(p, ring)
        arrived(p, ring, 2, p.main.at[ring, 0])
        arrived(p, ring, 3, p.main.at[ring, 1])
        add(p, p.first(*place(at)), p.rows, [(p.main, (ring, 0), 0), (p.main, (ring, 1), 0)])

    y_first, x_first, gain = pieces
    for copy in kept:
        copy.wait()
    for copy in shared:
        copy.wait_recv()
    for get in (get_left, get_right, *gets):
        get.wait()
    named = {"x": x_first, "y": y_first, "g": gain}
    acts = {"v": out_via, "m": out_main, "t": take}
    token_acts = {
        "Tc": tokens_to_chips,
        "T0": lambda: tokens_to_far(0),
        "T1": lambda: tokens_to_far(1),
        "Tg": tokens_gradient,
        "To": tokens_output,
    }
    for word in ORDER:
        if word[0] == "P":
            products(int(word[1]))
        elif word[0] == "T":
            token_acts[word]()
        else:
            for name in word[:-2]:
                acts[word[-2]](named[name], int(word[-1]))
    home = (y * 4 + x) * 160
    ghome = pl.ds(pl.multiple_of((y * 4 + x) * 64, 16), 64)
    theirs = pl.ds(pl.multiple_of(home + (1 - zl) * 80, 16), 80)
    across = remote(gsums.at[ghome], gfar, esend.at[0], erecv.at[0], far_peer)
    across.start()
    away = remote(sums.at[theirs], from_chip, esend.at[1], erecv.at[1], chip)
    away.start()
    across.wait()
    both = gsums[ghome].astype(f32) + gfar[...].astype(f32)
    for t in range(4):
        gsum[t] = both[t * 16 : (t + 1) * 16].astype(low)
    finish_gains = send_blocks([gsum], [gall], shere, ssend, srecv)
    away.wait()

    @pl.loop(0, 80 // step)
    def _(i):
        here_at = pl.ds(pl.multiple_of(home + zl * 80 + i * step, step), step)
        at = pl.ds(pl.multiple_of(i * step, step), step)
        attn_low[at] = sums[here_at].astype(f32) + from_chip[at].astype(f32)

    ours = pl.ds(pl.multiple_of(c * 40, 8), 40)
    for_core = pl.ds(pl.multiple_of((1 - c) * 40, 8), 40)
    columns = pl.ds(pl.multiple_of(c * 2 * ATTN, 128), 2 * ATTN)
    last = remote(attn_low.at[for_core], attn_ref.at[:, columns], esend.at[2], erecv.at[2], core)
    keep = pltpu.make_async_copy(attn_low.at[ours], attn_ref.at[:, columns], here.at[0])
    last.start()
    keep.start()
    finish_gains()
    go_ref[...] = (
        gall[0].astype(f32) + gall[1].astype(f32) + gall[2].astype(f32) + gall[3].astype(f32)
    )
    last.wait()
    keep.wait()
    for copy in (*started, *shared, pair, *t_cores, *t_sent):
        copy.wait_send()


def plane_sum(xn, d_q_kv, d_low, mixed, gains, down, d_xn, x, mid, d_mid, gain, order, cid):
    low, dma, f32 = jnp.bfloat16, pltpu.SemaphoreType.DMA, jnp.float32
    rows, width = x.shape
    vmem = pl.BlockSpec(memory_space=pltpu.VMEM)
    return pl.pallas_call(
        plane_sum_kernel,
        out_shape=[
            jax.ShapeDtypeStruct((40, 4 * ATTN), f32),
            jax.ShapeDtypeStruct((16, 128), f32),
            jax.ShapeDtypeStruct(x.shape, low),
            jax.ShapeDtypeStruct(x.shape, low),
        ],
        in_specs=[HBM] * 10 + [vmem, HBM],
        out_specs=[vmem] * 4,
        scratch_shapes=[
            *buffers(xn, mixed, down, d_xn, x, mid, d_mid, order),
            dma((8,)),
            pltpu.VMEM((2 * rows, d_q_kv.shape[1]), low),
            pltpu.VMEM((2 * rows, width), low),
            pltpu.VMEM((2560, 2 * ATTN), low),
            pltpu.VMEM((2, 5, 2, 80, ATTN), low),
            pltpu.VMEM((2, 5, 2, 160, ATTN), low),
            pltpu.VMEM((1024, 128), low),
            pltpu.VMEM((5, 2, 32, 128), low),
            pltpu.VMEM((5, 2, 64, 128), low),
            pltpu.VMEM((80, 2 * ATTN), low),
            pltpu.VMEM((80, 2 * ATTN), f32),
            pltpu.VMEM((64, 128), low),
            pltpu.VMEM((4, 16, 128), low),
            pltpu.VMEM((4, 16, 128), low),
            pltpu.VMEM((2, rows, width), low),
            pltpu.VMEM((rows, width), low),
            pltpu.VMEM((2, rows // 2, width), low),
            pltpu.VMEM((rows, width), low),
            pltpu.VMEM((rows, width), low),
            pltpu.VMEM((rows, width), low),
            pltpu.VMEM((rows, width), low),
            pltpu.VMEM((rows, width), low),
            dma((3,)),
            dma((2,)),
            dma((2,)),
            dma((60,)),
            dma((60,)),
            dma((3,)),
            dma((3,)),
            dma((7,)),
            dma((7,)),
            dma((1,)),
            dma((3,)),
            dma((3,)),
        ],
        compiler_params=pltpu.CompilerParams(
            collective_id=cid, has_side_effects=True, vmem_limit_bytes=60 * 2**20
        ),
    )(xn, d_q_kv, d_low, mixed, gains, down, d_xn, x, mid, d_mid, gain, order)


GELU_IN, GELU_CUBE = math.sqrt(2.0 / math.pi), 0.044715


def feed_kernel(
    xn_in, dy_ref, g_ref, d_ref, h_out, dg_out, o_ref,
    xn_ref, h_ref, dg_ref, in_sem, h_sem, dy, wg, wd, dy_turned, xn_turned, back, out, load_sem, out_sem,
):
    f32, low = jnp.float32, jnp.bfloat16
    units, tile, lines = h_ref.shape[1], 256, out.shape[1]
    get_xn = fetch([(xn_in, xn_ref)], in_sem)[0]
    get_dy = pltpu.make_async_copy(dy_ref, dy, load_sem.at[0])
    get_dy.start()
    loads = []
    for source, target in ((d_ref, wd), (g_ref, wg)):
        for n in range(4):
            some = pl.ds(n * 640, 640)
            loads.append(pltpu.make_async_copy(source.at[some], target.at[some], load_sem.at[1 + len(loads)]))
            loads[-1].start()
    get_xn.wait()
    xn_turned[...] = xn_ref[...].T
    get_dy.wait()
    dy_turned[...] = dy[...].T
    for n in range(4):
        loads[n].wait()
    for k in range(units // tile):
        at = pl.ds(k * tile, tile)
        back[:, at] = jnp.dot(dy[...], wd[:, at], preferred_element_type=f32)
    for n in range(4, 8):
        loads[n].wait()
    for k in range(units // tile):
        at, beside = pl.ds(k * tile, tile), pl.ds(units + k * tile, tile)
        gate = jnp.dot(xn_ref[...], wg[:, at], preferred_element_type=f32)
        up = jnp.dot(xn_ref[...], wg[:, beside], preferred_element_type=f32)
        d = back[:, at]
        square = gate * gate
        t = jnp.tanh(GELU_IN * (gate + GELU_CUBE * gate * square))
        cdf = 0.5 * (1.0 + t)
        slope = cdf + 0.5 * gate * (1.0 - t * t) * (GELU_IN * (1.0 + 3.0 * GELU_CUBE * square))
        gelu = gate * cdf
        h_ref[:, at] = (gelu * up).astype(low)
        dg_ref[:, at] = (d * up * slope).astype(low)
        dg_ref[:, beside] = (d * gelu).astype(low)

    puts = fetch([(h_ref, h_out), (dg_ref, dg_out)], h_sem)

    def put(i):
        slot = lax.rem(i, 2)
        rows = pl.ds(pl.multiple_of(i * lines, lines), lines)
        return pltpu.make_async_copy(out.at[slot], o_ref.at[rows], out_sem.at[slot])

    steps = o_ref.shape[0] // lines

    @pl.loop(0, steps)
    def _(i):
        slot = lax.rem(i, 2)
        pl.when(i >= 2)(lambda: put(i - 2).wait())
        rows = pl.ds(pl.multiple_of(i * lines, lines), lines)
        for left, right, count, first in ((dy_turned, h_ref, 2, 0), (xn_turned, dg_ref, 4, units)):
            for k in range(count):
                out[slot, :, pl.ds(first + k * 512, 512)] = jnp.dot(
                    left[rows], right[:, pl.ds(k * 512, 512)], preferred_element_type=f32
                ).astype(low)
        put(i).start()

    put(steps - 2).wait()
    put(steps - 1).wait()
    for copy in puts:
        copy.wait()


def feed(xn, dy, w_gate_up, w_down):
    depth, width = xn.shape
    units = w_down.shape[1]
    low, dma = jnp.bfloat16, pltpu.SemaphoreType.DMA
    shapes = [
        jax.ShapeDtypeStruct((depth, units), low),
        jax.ShapeDtypeStruct((depth, 2 * units), low),
        jax.ShapeDtypeStruct((width, 3 * units), low),
    ]
    return pl.pallas_call(
        feed_kernel,
        out_shape=shapes,
        in_specs=[HBM] * 4,
        out_specs=[HBM] * 3,
        scratch_shapes=[
            *buffers(xn, *shapes[:2]),
            dma((1,)),
            dma((2,)),
            pltpu.VMEM((depth, width), low),
            pltpu.VMEM((width, 2 * units), low),
            pltpu.VMEM((width, units), low),
            pltpu.VMEM((width, depth), low),
            pltpu.VMEM((width, depth), low),
            pltpu.VMEM((depth, units), jnp.float32),
            pltpu.VMEM((2, 320, 3 * units), low),
            dma((9,)),
            dma((2,)),
        ],
        compiler_params=pltpu.CompilerParams(vmem_limit_bytes=60 * 2**20),
        cost_estimate=pl.CostEstimate(
            flops=12 * depth * width * units,
            bytes_accessed=4 * depth * width + 12 * width * units + 6 * depth * units,
            transcendentals=depth * units,
        ),
    )(xn, dy, w_gate_up, w_down)


def back_kernel(
    dg_in, h_in, w_ref, d_ref, wo_ref, wq_ref,
    x_in, mid_in, dy_in, g2_ref, soft_in, q_in, kv_in, cos_ref, sin_ref,
    down_out, dmid_out, dl_out, dq_out, dx_out, gains_out,
    dg_ref, h_ref, x_ref, mid_ref, dy_ref, soft_ref, q_ref, kv_ref,
    down_ref, dmid_ref, dl_ref, dq_ref, dx_ref, gains_ref, in_sem, out_sem,
    w, wd, wo, part, from_core, other, from_chips, own, from_far, grad, kv_part, kv_far, halved, sums,
    wsem, send, recv, osem, qsem, fsend, frecv,
):
    zl, c, zh = lax.axis_index("zl"), lax.axis_index("c"), lax.axis_index("zh")
    core, far = {"c": 1 - c}, {"zh": 1 - zh}
    chips = [{"zl": 1 - zl, "zh": k} for k in range(2)]
    f32, low = jnp.float32, jnp.bfloat16
    parts, width = w_ref.shape[0] // 640, 640
    rows = x_ref.shape[0]
    half, step = rows // 2, 16
    heads = soft_ref.shape[0]
    get_dg, get_h, *gets = fetch(
        [
            (dg_in, dg_ref), (h_in, h_ref), (x_in, x_ref), (mid_in, mid_ref), (dy_in, dy_ref),
            (soft_in, soft_ref), (q_in, q_ref), (kv_in, kv_ref),
        ],
        in_sem,
    )
    loads = []
    for source, target, first in ((w_ref, w, 0), (d_ref, wd, parts)):
        for n in range(parts):
            some = pl.ds(n * width, width)
            loads.append(pltpu.make_async_copy(source.at[some], target.at[some], wsem.at[first + n]))
            loads[-1].start()
    get_wo = pltpu.make_async_copy(wo_ref, wo, osem)
    get_wo.start()
    wq = w.at[:, pl.ds(0, wq_ref.shape[1])]
    get_wq = pltpu.make_async_copy(wq_ref, wq, qsem)
    greet([core, far, *chips])
    order = [1 - zl, zl]
    started = []

    def go(src, dst, n, out_slot, in_slot, peer):
        copy = remote(src, dst, send.at[n * 6 + out_slot], recv.at[n * 6 + in_slot], peer)
        copy.start()
        started.append(copy)

    def arrived(dst, n, slot):
        remote(dst, dst, send.at[n * 6 + slot], recv.at[n * 6 + slot], core).wait_recv()

    def columns(n):
        return pl.ds(n * width, width)

    def product(left, right, n, target):
        some = pl.ds(n * width, width)
        v = lax.dot_general(
            left[...], right[some], (((1,), (1,)), ((), ())), preferred_element_type=f32
        ).astype(low)
        for t in range(4):
            target[t, :, some] = v[t * rows : (t + 1) * rows]

    def multiply(n):
        loads[n].wait()
        product(dg_ref, w, n, part)
        for i, z in enumerate(order):
            go(part.at[z * 2 + 1 - c, :, columns(n)], from_core.at[i, :, columns(n)], n, i, i, core)

    def down(n):
        loads[parts + n].wait()
        product(h_ref, wd, n, down_ref)

    def to_chips(n):
        arrived(from_core.at[0, :, columns(n)], n, 0)

        @pl.loop(0, rows // step)
        def _(i):
            at = pl.ds(pl.multiple_of(i * step, step), step)
            total = part[(1 - zl) * 2 + c, at, columns(n)].astype(f32) + from_core[0, at, columns(n)].astype(f32)
            other[at, columns(n)] = total.astype(low)

        for k in range(2):
            go(other.at[pl.ds(k * half, half), columns(n)], from_chips.at[zh, :, columns(n)], n, 2 + k, 2 + zh, chips[k])

    def to_far(n, k):
        piece = (1 - zh) if k == 0 else zh
        if k == 0:
            arrived(from_core.at[1, :, columns(n)], n, 1)
        else:
            for i in range(2):
                arrived(from_chips.at[i, :, columns(n)], n, 2 + i)

        @pl.loop(0, half // step)
        def _(i):
            at = pl.ds(pl.multiple_of(piece * half + i * step, step), step)
            total = part[zl * 2 + c, at, columns(n)].astype(f32) + from_core[1, at, columns(n)].astype(f32)
            if k == 1:
                there = pl.ds(pl.multiple_of(i * step, step), step)
                total += from_chips[0, there, columns(n)].astype(f32) + from_chips[1, there, columns(n)].astype(f32)
            own[at, columns(n)] = total.astype(low)

        at = pl.ds(pl.multiple_of(piece * half, half), half)
        go(own.at[at, columns(n)], from_far.at[at, columns(n)], n, 4 + k, 4 + k, far)

    def finish(n):
        for k in range(2):
            arrived(from_far.at[pl.ds(k * half, half), columns(n)], n, 4 + k)

        @pl.loop(0, rows // step)
        def _(i):
            at = pl.ds(pl.multiple_of(i * step, step), step)
            grad[at, columns(n)] = own[at, columns(n)].astype(f32) + from_far[at, columns(n)].astype(f32)

    get_dg.wait()
    multiply(0)
    multiply(1)
    to_chips(0)
    to_far(0, 0)
    multiply(2)
    to_chips(1)
    to_far(1, 0)
    multiply(3)
    get_wq.start()
    to_chips(2)
    to_far(2, 0)
    to_far(0, 1)
    get_h.wait()
    down(0)
    to_chips(3)
    to_far(3, 0)
    to_far(1, 1)
    down(1)
    to_far(2, 1)
    down(2)
    to_far(3, 1)
    down(3)
    for n in range(parts):
        finish(n)
    sums[...] = jnp.zeros_like(sums)
    puts = fetch([(down_ref, down_out)], out_sem)
    for get in gets:
        get.wait()

    @pl.loop(0, rows // step)
    def _(i):
        at = pl.ds(pl.multiple_of(i * step, step), step)
        v, d = mid_ref[at], grad[at]
        r = lax.rsqrt(jnp.mean(v * v, axis=-1, keepdims=True) + norm_eps)
        n = v * r
        sums[1:2] += jnp.sum(d * n, axis=0, keepdims=True) * 0.5
        d = d * g2_ref[...]
        d = dy_ref[at].astype(f32) + r * (d - n * jnp.mean(d * n, axis=-1, keepdims=True))
        dmid_ref[at] = d
        dl_ref[at] = d.astype(low)

    def across(left, right, left_dim, right_dim):
        return lax.dot_general(
            left, right, (((left_dim,), (right_dim,)), ((), ())), preferred_element_type=f32
        )

    def turned_back(u):
        turn = u[:, :ROT]
        turn = turn * cos_ref[...] - pltpu.roll(turn, ROT // 2, 1) * sin_ref[...]
        return jnp.concatenate([turn, u[:, ROT:]], axis=1).astype(low)

    get_wo.wait()
    puts += fetch([(dmid_ref, dmid_out), (dl_ref, dl_out)], out_sem.at[pl.ds(1, 2)])
    keys, values = kv_ref[:, :HEAD_DIM], kv_ref[:, HEAD_DIM:]
    scale = HEAD_DIM**-0.5
    d_keys = jnp.zeros((rows, HEAD_DIM), f32)
    d_values = jnp.zeros((rows, HEAD_DIM), f32)
    for h in range(heads):
        at = pl.ds(h * HEAD_DIM, HEAD_DIM)
        d_mixed = jnp.dot(dl_ref[...], wo[:, at], preferred_element_type=f32).astype(low)
        soft = soft_ref[h]
        d_probs = across(d_mixed, values, 1, 1)
        d_scores = (soft * (d_probs - jnp.sum(soft * d_probs, axis=-1, keepdims=True))).astype(low)
        dq_ref[:, at] = turned_back(jnp.dot(d_scores, keys, preferred_element_type=f32) * scale)
        d_keys += across(d_scores, q_ref[:, at], 0, 0)
        d_values += across(soft.astype(low), d_mixed, 0, 0)
    kv_part[:, :HEAD_DIM] = turned_back(d_keys * scale)
    kv_part[:, HEAD_DIM:] = d_values.astype(low)
    pair = remote(kv_part, kv_far, fsend, frecv, far)
    pair.start()
    pair.wait()
    first_kv = heads * HEAD_DIM
    kv = kv_part[...].astype(f32) + kv_far[...].astype(f32)
    kv = kv.astype(low)
    dq_ref[:, first_kv:] = kv
    halved[:, :first_kv] = dq_ref[:, :first_kv]
    halved[:, first_kv:] = kv * 0.5
    get_wq.wait()
    for k in range(5):
        some = pl.ds(k * 512, 512)
        d = across(halved[...], w[some, : wq_ref.shape[1]], 1, 1)
        grad[:, some] = d
        dx_ref[:, some] = d.astype(low)

    @pl.loop(0, rows // step)
    def _(i):
        at = pl.ds(pl.multiple_of(i * step, step), step)
        v = x_ref[at]
        r = lax.rsqrt(jnp.mean(v * v, axis=-1, keepdims=True) + norm_eps)
        sums[0:1] += jnp.sum(grad[at] * (v * r), axis=0, keepdims=True)

    both = jnp.concatenate([sums[...], jnp.zeros((8, sums.shape[1]), f32)], axis=0)
    for k in range(64):
        tile = jnp.concatenate([both[:, k * 40 : (k + 1) * 40], jnp.zeros((16, 88), f32)], axis=1)
        gains_ref[k * 16 : (k + 1) * 16] = tile.astype(low)
    puts += fetch([(dq_ref, dq_out), (dx_ref, dx_out), (gains_ref, gains_out)], out_sem.at[pl.ds(3, 3)])
    for copy in started:
        copy.wait_send()
    for copy in puts:
        copy.wait()


def feed_back(
    d_gate_up, hidden, w_gate_up, w_down, w_out, w_q_kv,
    x, mid, dy, gain, soft, queries, keys_values, cosine, sine, cid,
):
    dma, low, f32 = pltpu.SemaphoreType.DMA, jnp.bfloat16, jnp.float32
    vmem = pl.BlockSpec(memory_space=pltpu.VMEM)
    rows, width = x.shape
    wide = w_q_kv.shape[1]
    shapes = [
        jax.ShapeDtypeStruct((4, rows, width), low),
        jax.ShapeDtypeStruct((rows, width), f32),
        jax.ShapeDtypeStruct((rows, width), low),
        jax.ShapeDtypeStruct((rows, wide), low),
        jax.ShapeDtypeStruct((rows, width), low),
        jax.ShapeDtypeStruct((1024, 128), low),
    ]
    return pl.pallas_call(
        back_kernel,
        out_shape=shapes,
        in_specs=[HBM] * 9 + [vmem] + [HBM] * 3 + [vmem] * 2,
        out_specs=[HBM] * 6,
        scratch_shapes=[
            *buffers(d_gate_up, hidden, x, mid, dy, soft, queries, keys_values, *shapes),
            dma((8,)),
            dma((6,)),
            pltpu.VMEM(w_gate_up.shape, low),
            pltpu.VMEM(w_down.shape, low),
            pltpu.VMEM(w_out.shape, low),
            pltpu.VMEM((4, rows, width), low),
            pltpu.VMEM((2, rows, width), low),
            pltpu.VMEM((rows, width), low),
            pltpu.VMEM((2, rows // 2, width), low),
            pltpu.VMEM((rows, width), low),
            pltpu.VMEM((rows, width), low),
            pltpu.VMEM((rows, width), f32),
            pltpu.VMEM(keys_values.shape, low),
            pltpu.VMEM(keys_values.shape, low),
            pltpu.VMEM((rows, wide), low),
            pltpu.VMEM((8, width), f32),
            dma((8,)),
            dma((24,)),
            dma((24,)),
            dma,
            dma,
            dma,
            dma,
        ],
        compiler_params=pltpu.CompilerParams(
            collective_id=cid, has_side_effects=True, vmem_limit_bytes=60 * 2**20
        ),
    )(
        d_gate_up, hidden, w_gate_up, w_down, w_out, w_q_kv,
        x, mid, dy, gain, soft, queries, keys_values, cosine, sine,
    )


def tables():
    half_rot = ROT // 2
    rates = jnp.exp(jnp.arange(half_rot, dtype=jnp.float32) * (-2.0 * math.log(10000.0) / ROT))
    angles = jnp.arange(SEQ_LEN, dtype=jnp.float32)[:, None] * rates[None, :]
    return (jnp.cos(angles), jnp.sin(angles))


def padded(weight):
    return jnp.pad(weight.reshape(40, 4, 960), ((0, 0), (0, 0), (0, 64)))


def local(
    tokens,
    attn_gain,
    query_weight,
    kv_weight,
    out_weight,
    mlp_gain,
    gate_weight,
    up_weight,
    down_weight,
    cotangent,
):
    low = jnp.bfloat16
    rows = tokens.shape[0]
    wide = query_weight.shape[1]
    cosine, sine = tables()
    attn = jnp.concatenate([query_weight, kv_weight, out_weight.T], axis=1)
    attn = attn.reshape(40, 2, 2, ATTN).transpose(1, 2, 0, 3)
    attn = jnp.broadcast_to(attn, (2, *attn.shape)).reshape(4, 2, 40, ATTN)
    first = attn.reshape(4, 80, ATTN)
    gains = jnp.pad(jnp.stack([attn_gain, mlp_gain], axis=0), ((0, 14), (0, 88)))
    gains = jnp.broadcast_to(gains, (4, 16, 128))
    down = padded(down_weight.T).reshape(40, 4, 2, FEED).transpose(1, 2, 0, 3).reshape(4, 80, FEED)
    second = jnp.stack([padded(gate_weight), padded(up_weight)], axis=0)
    second = second.transpose(2, 0, 1, 3).reshape(4, 80, 2 * FEED)
    order = jnp.asarray(feature_order(), low)
    first, gains, second, x_in, dy_here = group_exchange(
        first, gains, second, tokens, cotangent, order, 5
    )
    w_gate_up = lax.all_gather(second, PLANE, axis=0, tiled=True)
    w_q_kv, w_out_t, gains, dy, down = attention_gather(first, gains.reshape(64, 128), dy_here, down, 6)
    gains = gains.reshape(64, 16, 128)[:, :2, :40].transpose(1, 0, 2).reshape(2, 2560).astype(jnp.float32)
    dy = dy.reshape(4 * rows, -1)
    gain_one, gain_two = gains[0][None, :], gains[1][None, :]
    cosine = jnp.concatenate([cosine, cosine], axis=1)
    sine = jnp.concatenate([-sine, sine], axis=1)
    x_mid, xn_all, w_down_t, xn_one, mixed_heads, queries, keys_values, soft_rows = middle(
        x_in, gain_one, gain_two, cosine, sine, w_q_kv, w_out_t, down, 2
    )
    xn_all = xn_all.reshape(4 * rows, -1)
    hidden, d_gate_up, sent = feed(xn_all, dy, w_gate_up, w_down_t)
    sent = lax.psum_scatter(sent, PLANE, scatter_dimension=0, tiled=True)
    down_part, d_mid, d_mid_low, d_q_kv, d_xn_one, d_gains = feed_back(
        d_gate_up,
        hidden,
        w_gate_up,
        w_down_t,
        w_out_t,
        w_q_kv,
        x_in,
        x_mid,
        dy_here,
        gain_two,
        soft_rows,
        queries,
        keys_values,
        cosine,
        sine,
        3,
    )
    attn_out, gain_out, block_out, tokens_grad = plane_sum(
        xn_one.reshape(2 * rows, -1),
        d_q_kv,
        d_mid_low,
        mixed_heads.reshape(2 * rows, -1),
        d_gains,
        down_part,
        d_xn_one,
        x_in,
        x_mid,
        d_mid,
        gain_one,
        order,
        7,
    )
    down_out, gate_out, up_out = finish(sent, 8)
    return (
        block_out,
        tokens_grad,
        gain_out[0, :40],
        attn_out[:, :wide],
        attn_out[:, wide : wide + 2 * HEAD_DIM],
        attn_out[:, wide + 2 * HEAD_DIM :].T,
        gain_out[1, :40],
        gate_out,
        up_out,
        down_out.T,
    )


def solution(mesh):
    fine = Mesh(mesh.devices.reshape(4, 2, 4, 2, 2), AXES)
    dp = ("y", "zl", "x", "c")
    in_specs = (
        P(dp, None),
        P(dp),
        P(dp, "zh"),
        P(dp, None),
        P("zh", dp),
        P(dp),
        P(dp, "zh"),
        P(dp, "zh"),
        P("zh", dp),
        P(dp, None),
    )
    out_specs = (
        P(dp, None),
        P(dp, None),
        P(dp),
        P(dp, "zh"),
        P(dp, None),
        P("zh", dp),
        P(dp),
        P(dp, "zh"),
        P(dp, "zh"),
        P("zh", dp),
    )
    return jax.shard_map(local, mesh=fine, in_specs=in_specs, out_specs=out_specs, check_vma=False)
```

```python
import math

import jax
import jax.numpy as jnp
import numpy as np
from jax import lax
from jax.experimental import pallas as pl
from jax.experimental.pallas import tpu as pltpu
from jax.sharding import Mesh
from jax.sharding import PartitionSpec as P

HEAD_DIM = 256
WINDOW = 2048
SEQ_LEN = 128
ROT = 128
AXES = ("y", "zl", "x", "c", "zh")
PLANE = ("y", "x")
GROUP = ("zl", "c")
OWNERS = ("y", "x", "zl", "c")
MESH = pl.DeviceIdType.MESH

norm_eps = 1e-06


def feature_order():
    place = np.arange(640).reshape(2, 4, 80).transpose(1, 0, 2).reshape(640)
    return (np.arange(640)[:, None] == place[None, :]).astype(np.float32)


def reorder(src, order, dst, back):
    for k in range(4):
        group = pl.ds(k * 640, 640)
        dst[:, group] = lax.dot_general(
            src[:, group],
            order[...],
            (((1,), (1 if back else 0,)), ((), ())),
            preferred_element_type=jnp.float32,
        ).astype(dst.dtype)


def greet(peers):
    barrier = pltpu.get_barrier_semaphore()
    for peer in peers:
        pl.semaphore_signal(barrier, inc=1, device_id=peer, device_id_type=MESH)
    pl.semaphore_wait(barrier, len(peers))


def remote(src, dst, send, recv, peer):
    return pltpu.make_async_remote_copy(
        src_ref=src, dst_ref=dst, send_sem=send, recv_sem=recv, device_id=peer, device_id_type=MESH
    )


ATTN, FEED = 768, 512
MAIN, PACKED = 896, 1920


def fetch(pairs, sems):
    copies = [pltpu.make_async_copy(src, dst, sems.at[k]) for k, (src, dst) in enumerate(pairs)]
    for copy in copies:
        copy.start()
    return copies


def buffers(*arrays):
    return [pltpu.VMEM(a.shape, a.dtype) for a in arrays]


HBM = pl.BlockSpec(memory_space=pltpu.HBM)


def ring_of(axis, at):
    return {axis: lax.rem(at + 3, 4)}, {axis: lax.rem(at + 1, 4)}


def send_blocks(ins, outs, here, send, recv):
    zl, c = lax.axis_index("zl"), lax.axis_index("c")
    mine = zl * 2 + c
    peers = [({"zl": 1 - zl, "c": k}, (1 - zl) * 2 + k) for k in range(2)]
    peers.append(({"c": 1 - c}, zl * 2 + 1 - c))
    n = len(ins)
    copies, keeps = [], []
    for i in range(n):
        for k, (peer, block) in enumerate(peers):
            landing = i * 3 + (c if k < 2 else 2)
            copy = remote(ins[i].at[block], outs[i].at[mine], send.at[i * 3 + k], recv.at[landing], peer)
            copy.start()
            copies.append(copy)
    for i in range(n):
        keep = pltpu.make_async_copy(ins[i].at[mine], outs[i].at[mine], here.at[i])
        keep.start()
        keeps.append(keep)

    def finish():
        for keep in keeps:
            keep.wait()
        for i in range(n):
            for k, (peer, block) in enumerate(peers):
                remote(
                    ins[i].at[block], outs[i].at[block], send.at[i * 3 + k], recv.at[i * 3 + k], peer
                ).wait_recv()
        for copy in copies:
            copy.wait_send()

    return finish


def group_peers():
    zl, c = lax.axis_index("zl"), lax.axis_index("c")
    return [{"c": 1 - c}, {"zl": 1 - zl, "c": 0}, {"zl": 1 - zl, "c": 1}]


def exchange_kernel(
    q_ref, kv_ref, wo_ref, g_ref, u_ref, d_ref, gain_ref, tok_ref, cot_ref, order_ref,
    ao_out, go_ref, so_out, do_out, x_out, dy_out,
    a_block, g_block, s_block, d_block, al, sl, ao_ref, so_ref, x_ref, dy_ref, here, send, recv, out_sem,
):
    f32, low = jnp.float32, jnp.bfloat16

    def stacked(v):
        half = v.shape[1] // 2
        return jnp.concatenate([v[:, :half], v[:, half:]], axis=0).astype(low)

    attn = jnp.concatenate([r[...].astype(f32) for r in (q_ref, kv_ref, wo_ref)], axis=1)
    for k in range(2):
        block = stacked(attn[:, k * 2 * ATTN : (k + 1) * 2 * ATTN])
        a_block[k] = block
        a_block[2 + k] = block
    gate, up, down = (r[...].astype(f32) for r in (g_ref, u_ref, d_ref))
    for t in range(4):
        first, tail, end = t * 960, t * 960 + MAIN, (t + 1) * 960
        packed = [gate[:, first:tail], up[:, first:tail], gate[:, tail:end], up[:, tail:end]]
        s_block[t] = stacked(jnp.concatenate([*packed, jnp.zeros((40, 128), f32)], axis=1))
        d_block[t] = stacked(jnp.concatenate([down[:, first:end], jnp.zeros((40, 64), f32)], axis=1))
        g_block[t] = gain_ref[...]
    greet(group_peers())
    finish = send_blocks([a_block, g_block, s_block], [al, go_ref, sl], here, send, recv)
    early = fetch([(d_block, do_out)], out_sem.at[pl.ds(4, 1)])
    reorder(tok_ref, order_ref, x_ref, False)
    reorder(cot_ref, order_ref, dy_ref, False)
    puts = fetch([(x_ref, x_out), (dy_ref, dy_out)], out_sem)
    finish()
    for h in range(2):
        parts = [al[t].astype(f32)[h * 40 : (h + 1) * 40] for t in range(4)]
        ao_ref[h] = jnp.concatenate(parts, axis=0).astype(low)
    for k in range(2):
        parts = [sl[t].astype(f32) for t in (2 * k, 2 * k + 1)]
        parts = [jnp.concatenate([v[:40], v[40:, : PACKED - 2 * FEED]], axis=1) for v in parts]
        so_ref[pl.ds(k * 80, 80)] = jnp.concatenate(parts, axis=0).astype(low)
    last = fetch([(ao_ref, ao_out), (so_ref, so_out)], out_sem.at[pl.ds(2, 2)])
    for put in (*early, *puts, *last):
        put.wait()


def group_exchange(weights, gains, tokens, cotangent, order, cid):
    low, dma = jnp.bfloat16, pltpu.SemaphoreType.DMA
    vmem = pl.BlockSpec(memory_space=pltpu.VMEM)
    shapes = [
        jax.ShapeDtypeStruct((2, 160, ATTN), low),
        jax.ShapeDtypeStruct((4, 16, 128), low),
        jax.ShapeDtypeStruct((160, PACKED), low),
        jax.ShapeDtypeStruct((4, 80, FEED), low),
        jax.ShapeDtypeStruct(tokens.shape, jnp.float32),
        jax.ShapeDtypeStruct(cotangent.shape, low),
    ]
    attn, second = (jax.ShapeDtypeStruct((4, 80, n), low) for n in (ATTN, 2 * FEED))
    return pl.pallas_call(
        exchange_kernel,
        out_shape=shapes,
        in_specs=[vmem] * 10,
        out_specs=[HBM] * 6,
        scratch_shapes=[
            *buffers(attn, shapes[1], second, shapes[3], attn, second),
            *buffers(shapes[0], shapes[2], *shapes[4:]),
            dma((3,)),
            dma((9,)),
            dma((9,)),
            dma((5,)),
        ],
        compiler_params=pltpu.CompilerParams(
            collective_id=cid, has_side_effects=True, vmem_limit_bytes=54 * 2**20
        ),
    )(*weights, gains, tokens, cotangent, order)


def shift(i, by):
    return lax.rem(i + by, 4)


def around(h, y, x):
    if h == 0:
        return x, ring_of("x", x), y, ring_of("y", y)
    return y, ring_of("y", y), x, ring_of("x", x)


class Piece:
    def __init__(self, h, source, target, columns, rows=160):
        self.h, self.source, self.target, self.columns, self.rows = h, source, target, columns, rows

    def own(self):
        return self.source

    def at(self, i1, i2, part=None):
        row, column = (i2, i1) if self.h == 0 else (i1, i2)
        size = self.rows if part is None else self.rows // 2
        first = (row * 4 + column) * self.rows + (0 if part is None else part * size)
        return self.target.at[pl.ds(pl.multiple_of(first, 16), size), self.columns]


def gather_steps(y, x, pieces, send, recv, cross):
    started = []

    def go(src, dst, n, ring, slot, peer):
        k = (n * 5 + ring) * 4 + slot
        copy = remote(src, dst, send.at[k], recv.at[k], peer)
        copy.start()
        started.append(copy)

    def arrived(dst, n, ring, slot):
        k = (n * 5 + ring) * 4 + slot
        remote(dst, dst, send.at[k], recv.at[k], {"c": 1 - lax.axis_index("c")}).wait_recv()

    each = [(n, p, *around(p.h, y, x)) for n, p in enumerate(pieces)]
    firsts = ((1, 0), (2, 3), (3, 1), (4, 2))

    def own_blocks():
        for n, p, i1, (back1, ahead1), i2, _ in each:
            go(p.own(), p.at(i1, i2), n, 0, 0, ahead1)
            go(p.own(), p.at(i1, i2), n, 0, 1, back1)
        for n, p, i1, _, i2, (back2, ahead2) in each:
            go(p.own(), p.at(i1, i2), n, 1, 0, ahead2)
            go(p.own(), p.at(i1, i2), n, 1, 1, back2)
            cross(n, p.own(), p.at(i1, i2), None)

    def first_axis():
        for n, p, i1, (back1, ahead1), i2, (back2, ahead2) in each:
            left, right = p.at(shift(i1, 3), i2), p.at(shift(i1, 1), i2)
            arrived(left, n, 0, 0)
            low = p.at(shift(i1, 3), i2, 0)
            go(low, low, n, 0, 2, ahead1)
            arrived(right, n, 0, 1)
            high = p.at(shift(i1, 1), i2, 1)
            go(high, high, n, 0, 3, back1)
            for ring, ref in ((2, left), (3, right)):
                go(ref, ref, n, ring, 0, ahead2)
                go(ref, ref, n, ring, 1, back2)
                cross(n, ref, ref, (shift(i1, 3 if ring == 2 else 1), i2))
        for n, p, i1, _, i2, (back2, ahead2) in each:
            far = shift(i1, 2)
            arrived(p.at(far, i2, 0), n, 0, 2)
            arrived(p.at(far, i2, 1), n, 0, 3)
            ref = p.at(far, i2)
            go(ref, ref, n, 4, 0, ahead2)
            go(ref, ref, n, 4, 1, back2)
            cross(n, ref, ref, (far, i2))

    def second_axis():
        for ring, by in firsts:
            for n, p, i1, _, i2, (back2, ahead2) in each:
                j = shift(i1, by)
                left, right = p.at(j, shift(i2, 3)), p.at(j, shift(i2, 1))
                arrived(left, n, ring, 0)
                low = p.at(j, shift(i2, 3), 0)
                go(low, low, n, ring, 2, ahead2)
                cross(n, left, left, (j, shift(i2, 3)))
                arrived(right, n, ring, 1)
                high = p.at(j, shift(i2, 1), 1)
                go(high, high, n, ring, 3, back2)
                cross(n, right, right, (j, shift(i2, 1)))

    def last():
        for ring, by in firsts:
            for n, p, i1, _, i2, _ in each:
                j, far = shift(i1, by), shift(i2, 2)
                arrived(p.at(j, far, 0), n, ring, 2)
                arrived(p.at(j, far, 1), n, ring, 3)
                cross(n, p.at(j, far), p.at(j, far), (j, far))

    def finish():
        for copy in started:
            copy.wait_send()

    return own_blocks, first_axis, second_axis, last, finish


def attention_gather_kernel(
    in_hbm, g_hbm, dy_hbm, d_hbm, a_ref, o_ref, go_ref, all_ref, do_out,
    in_ref, g_ref, dy_ref, d_ref, in_sem, dl, do_ref, do_sem, here, send, recv, csend, crecv, zsend, zrecv, dsend, drecv, xhere, xsend, xrecv,
):
    y, x, c = lax.axis_index("y"), lax.axis_index("x"), lax.axis_index("c")
    zl, zh = lax.axis_index("zl"), lax.axis_index("zh")
    core = {"c": 1 - c}
    gets = fetch([(in_hbm, in_ref), (g_hbm, g_ref), (dy_hbm, dy_ref), (d_hbm, d_ref)], in_sem)
    chips = [{"zl": 1 - zl, "zh": k} for k in range(2)]
    greet([*ring_of("x", x), *ring_of("y", y), core, *chips, {"zl": 1 - zl, "c": 1 - c}])
    whole = pl.ds(0, 160)
    for get in gets:
        get.wait()

    chip = {"zl": 1 - zl}
    for side in range(2):

        @pl.when(c == side)
        def _(side=side):
            if side == 0:
                starts = [(a_ref, 0), (a_ref, 256), (a_ref, 512), (a_ref, 768), (a_ref, 1280)]
            else:
                starts = [(a_ref, 1536), (o_ref, 0), (o_ref, 256), (o_ref, 512), (o_ref, 1024)]
            segments = ((0, 0, 256, False), (0, 256, 256, False), (0, 512, 128, True), (1, 0, 512, False), (1, 512, 128, True))
            pieces, others = [], {}
            for n, ((h, source, width, shared), (ref, first)) in enumerate(zip(segments, starts)):
                for part in range(2 if shared else 1):
                    off = pl.multiple_of((zl if part == 0 else 1 - zl) * width, 128) if shared else 0
                    piece = Piece(
                        h, in_ref.at[h, whole, pl.ds(source + off, width)], ref, pl.ds(first + off, width)
                    )
                    if part == 0:
                        pieces.append(piece)
                    else:
                        others[n] = piece
            pieces.append(Piece(0, g_ref, go_ref, pl.ds(0, 128), 64))
            crossed, passed_on, drained = [], [], []

            def to_core(src, dst):
                k = len(crossed)
                copy = remote(src, dst, csend.at[k], crecv.at[k], core)
                copy.start()
                crossed.append(copy)

            def cross(n, src, dst, place):
                if n < 5:
                    to_core(src, dst)
                if n in others and place is not None:
                    k = len(passed_on)
                    copy = remote(dst, dst, zsend.at[k], zrecv.at[k], chip)
                    copy.start()
                    passed_on.append((copy, others[n].at(*place)))

            def drain(count):
                for k in range(len(drained), count):
                    ref = passed_on[k][1]
                    remote(ref, ref, zsend.at[k], zrecv.at[k], chip).wait_recv()
                    to_core(ref, ref)
                    drained.append(k)

            own_blocks, first_axis, second_axis, last, sent = gather_steps(y, x, pieces, send, recv, cross)
            own_blocks()
            keeps = []
            for n, p in enumerate([*pieces, *others.values()]):
                i1, _, i2, _ = around(p.h, y, x)
                keeps.append(pltpu.make_async_copy(p.own(), p.at(i1, i2), here.at[n]))
                keeps[-1].start()
                if n >= len(pieces):
                    to_core(p.own(), p.at(i1, i2))
            finish = send_blocks([d_ref], [dl], xhere, xsend, xrecv)
            half = dy_ref.shape[0] // 2
            mine, other = zl * 2 + c, (1 - zl) * 2 + c
            part = pl.ds(pl.multiple_of(zh * half, half), half)
            away = [
                remote(dy_ref.at[part], all_ref.at[mine, part], dsend.at[k], drecv.at[zh], chips[k])
                for k in range(2)
            ]
            across = remote(dy_ref, all_ref.at[mine], dsend.at[2], drecv.at[2], core)
            for copy in (*away, across):
                copy.start()
            keeps.append(pltpu.make_async_copy(dy_ref, all_ref.at[mine], here.at[8]))
            keeps[-1].start()
            first_axis()
            finish()
            for h in range(2):
                parts = [dl[t].astype(jnp.float32)[h * 40 : (h + 1) * 40] for t in range(4)]
                do_ref[h] = jnp.concatenate(parts, axis=0).astype(jnp.bfloat16)
            puts = fetch([(do_ref, do_out)], do_sem)
            second_axis()
            drain(6)
            passed = []
            for k in range(2):
                rows = pl.ds(k * half, half)
                there = all_ref.at[other, rows]
                remote(dy_ref.at[rows], there, dsend.at[k], drecv.at[k], chips[k]).wait_recv()
                passed.append(remote(there, there, dsend.at[3 + k], drecv.at[3 + k], core))
                passed[-1].start()
            last()
            drain(30)
            sent()
            for copy, _ in passed_on:
                copy.wait_send()
            for copy in (*crossed, *passed, across):
                copy.wait()
            for copy in away:
                copy.wait_send()
            for keep in (*keeps, *puts):
                keep.wait()


def attention_gather(own, gains, dy, down, cid):
    kind, dma = jnp.bfloat16, pltpu.SemaphoreType.DMA
    return pl.pallas_call(
        attention_gather_kernel,
        out_shape=[
            jax.ShapeDtypeStruct((2560, 1792), kind),
            jax.ShapeDtypeStruct((2560, 1280), kind),
            jax.ShapeDtypeStruct((1024, 128), kind),
            jax.ShapeDtypeStruct((4, *dy.shape), kind),
            jax.ShapeDtypeStruct((2, 160, down.shape[2]), kind),
        ],
        in_specs=[HBM] * 4,
        out_specs=[HBM] * 5,
        scratch_shapes=[
            *buffers(own, gains, dy, down),
            dma((4,)),
            pltpu.VMEM(down.shape, kind),
            pltpu.VMEM((2, 160, down.shape[2]), kind),
            dma((1,)),
            dma((9,)),
            dma((120,)),
            dma((120,)),
            dma((112,)),
            dma((112,)),
            dma((30,)),
            dma((30,)),
            dma((5,)),
            dma((5,)),
            dma((1,)),
            dma((3,)),
            dma((3,)),
        ],
        compiler_params=pltpu.CompilerParams(collective_id=cid, has_side_effects=True),
    )(own, gains, dy, down)


def middle_kernel(
    x_in, g_in, cos_ref, sin_ref, wq_ref, wo_ref, d_in,
    mid_out, all_out, w_ref, xn_out, mixed_out, q_out, kv_out, soft_out, rows_out,
    x_ref, g_ref, d_ref, mid_ref, all_ref, xn_ref, mixed_ref, q_ref, kv_ref, soft_ref, rows_ref, in_sem, out_sem,
    wq, wo, p_ref, landed, here, wsem, psend, precv, gsend, grecv, send, recv, csend, crecv,
):
    y, x, c = lax.axis_index("y"), lax.axis_index("x"), lax.axis_index("c")
    zl, zh = lax.axis_index("zl"), lax.axis_index("zh")
    core, far = {"c": 1 - c}, {"zh": 1 - zh}
    chips = [{"zl": 1 - zl, "zh": k} for k in range(2)]
    f32, low = jnp.float32, jnp.bfloat16
    heads = soft_ref.shape[0]
    *gets, get_d = fetch([(x_in, x_ref), (g_in, g_ref), (d_in, d_ref)], in_sem)
    loads = []
    for k in range(heads + 2):
        columns = pl.ds(k * HEAD_DIM, HEAD_DIM)
        loads.append(pltpu.make_async_copy(wq_ref.at[:, columns], wq.at[:, columns], wsem.at[k]))
    for k in range(5):
        some = pl.ds(k * 512, 512)
        loads.append(pltpu.make_async_copy(wo_ref.at[some], wo.at[some], wsem.at[heads + 2 + k]))
    for k in (heads, heads + 1, *range(heads), *range(heads + 2, heads + 7)):
        loads[k].start()
    greet([*ring_of("x", x), *ring_of("y", y), core, far, *chips])
    pieces = [
        Piece(h, d_ref.at[h, pl.ds(0, 160)], w_ref, pl.ds(h * FEED, FEED)) for h in range(2)
    ]
    own_blocks, first_axis, second_axis, last, sent = gather_steps(
        y, x, pieces, send, recv, lambda n, src, dst, place: None
    )
    get_d.wait()
    own_blocks()
    keeps = []
    for n, p in enumerate(pieces):
        i1, _, i2, _ = around(p.h, y, x)
        keeps.append(pltpu.make_async_copy(p.own(), p.at(i1, i2), here.at[n]))
        keeps[-1].start()
    half, step = x_ref.shape[0] // 2, 16
    for get in gets:
        get.wait()
    tiles = [g_ref[k * 16 : (k + 1) * 16].astype(f32)[:8, :40] for k in range(64)]
    rows_ref[...] = jnp.concatenate(tiles, axis=1)

    @pl.loop(0, 2 * half // step)
    def _(i):
        at = pl.ds(pl.multiple_of(i * step, step), step)
        v = x_ref[at]
        r = lax.rsqrt(jnp.mean(v * v, axis=-1, keepdims=True) + norm_eps)
        xn_ref[c, at] = (v * r * rows_ref[0:1]).astype(low)

    shared = [remote(xn_ref.at[c], xn_ref.at[c], csend.at[0], crecv.at[0], core)]
    shared[0].start()

    def projected(k):
        loads[k].wait()
        return jnp.dot(xn_ref[c], wq[:, k * HEAD_DIM : (k + 1) * HEAD_DIM], preferred_element_type=f32)

    def rotated(u):
        turn = u[:, :ROT]
        turn = turn * cos_ref[...] + pltpu.roll(turn, ROT // 2, 1) * sin_ref[...]
        return jnp.concatenate([turn, u[:, ROT:]], axis=1).astype(low)

    kv_ref[:, :HEAD_DIM] = rotated(projected(heads))
    kv_ref[:, HEAD_DIM:] = projected(heads + 1).astype(low)
    rows = lax.broadcasted_iota(jnp.int32, (SEQ_LEN, SEQ_LEN), 0)
    behind = rows - lax.broadcasted_iota(jnp.int32, (SEQ_LEN, SEQ_LEN), 1)
    keep_mask = (behind >= 0) & (behind < WINDOW)
    for h in range(heads):
        columns = pl.ds(h * HEAD_DIM, HEAD_DIM)
        q = rotated(projected(h))
        q_ref[:, columns] = q
        scores = lax.dot_general(
            q, kv_ref[:, :HEAD_DIM], (((1,), (1,)), ((), ())), preferred_element_type=f32
        )
        scores = jnp.where(keep_mask, scores * HEAD_DIM**-0.5, -1e30)
        top = jnp.max(scores, axis=-1, keepdims=True)
        total = top + jnp.log(jnp.sum(jnp.exp(scores - top), axis=-1, keepdims=True))
        soft = jnp.exp(scores - total)
        soft_ref[h] = soft
        mixed_ref[c, :, columns] = jnp.dot(
            soft.astype(low), kv_ref[:, HEAD_DIM:], preferred_element_type=f32
        ).astype(low)
    shared.append(remote(mixed_ref.at[c], mixed_ref.at[c], csend.at[1], crecv.at[1], core))
    shared[1].start()
    puts = fetch([(q_ref, q_out), (kv_ref, kv_out), (soft_ref, soft_out), (rows_ref, rows_out)], out_sem)
    for k in range(5):
        loads[heads + 2 + k].wait()
        some = pl.ds(k * 512, 512)
        p_ref[:, some] = lax.dot_general(
            mixed_ref[c], wo[some], (((1,), (1,)), ((), ())), preferred_element_type=f32
        ).astype(low)
    mine, other = zl * 2 + c, (1 - zl) * 2 + c
    parts = [pl.ds(pl.multiple_of(k * half, half), half) for k in (1 - zh, zh)]
    pair = [
        remote(p_ref.at[part], landed.at[part], psend.at[k], precv.at[k], far)
        for k, part in enumerate(parts)
    ]
    for copy in pair:
        copy.start()
    first_axis()
    away, across = [], []
    for k in range(2):
        part = parts[1 - k]
        pair[k].wait_recv()
        first = (zh if k == 0 else 1 - zh) * half

        @pl.loop(0, half // step)
        def _(i, first=first):
            at = pl.ds(pl.multiple_of(first + i * step, step), step)
            branch = p_ref[at].astype(f32) + landed[at].astype(f32)
            v = x_ref[at] + branch
            mid_ref[at] = v
            r = lax.rsqrt(jnp.mean(v * v, axis=-1, keepdims=True) + norm_eps)
            all_ref[mine, at] = (v * r * rows_ref[1:2]).astype(low)

        ready = all_ref.at[mine, part]
        if k == 0:
            for i in range(2):
                away.append(remote(ready, ready, gsend.at[i], grecv.at[zh], chips[i]))
                away[-1].start()
        across.append(remote(ready, ready, gsend.at[2 + k], grecv.at[2 + k], core))
        across[-1].start()
        if k == 0:
            second_axis()
    passed = []
    for k in range(2):
        there = all_ref.at[other, pl.ds(k * half, half)]
        remote(there, there, gsend.at[k], grecv.at[k], chips[k]).wait_recv()
        passed.append(remote(there, there, gsend.at[4 + k], grecv.at[4 + k], core))
        passed[-1].start()
    last()
    sent()
    for copy in (*across, *passed, *shared):
        copy.wait()
    puts += fetch(
        [(mid_ref, mid_out), (all_ref, all_out), (xn_ref, xn_out), (mixed_ref, mixed_out)],
        out_sem.at[pl.ds(4, 4)],
    )
    for copy in (*away, *pair):
        copy.wait_send()
    for keep in (*keeps, *puts):
        keep.wait()


def middle(x, gains, cosine, sine, w_q_kv, w_out_t, down, cid):
    dma, f32, low = pltpu.SemaphoreType.DMA, jnp.float32, jnp.bfloat16
    vmem = pl.BlockSpec(memory_space=pltpu.VMEM)
    rows, width = x.shape
    wide = w_out_t.shape[1]
    heads = wide // HEAD_DIM
    shapes = [
        jax.ShapeDtypeStruct(x.shape, f32),
        jax.ShapeDtypeStruct((4, *x.shape), low),
        jax.ShapeDtypeStruct((2560, 2 * FEED), low),
        jax.ShapeDtypeStruct((2, rows, width), low),
        jax.ShapeDtypeStruct((2, rows, wide), low),
        jax.ShapeDtypeStruct((rows, wide), low),
        jax.ShapeDtypeStruct((rows, 2 * HEAD_DIM), low),
        jax.ShapeDtypeStruct((heads, rows, rows), f32),
        jax.ShapeDtypeStruct((8, width), f32),
    ]
    return pl.pallas_call(
        middle_kernel,
        out_shape=shapes,
        in_specs=[HBM] * 2 + [vmem] * 2 + [HBM] * 3,
        out_specs=[HBM] * 9,
        scratch_shapes=[
            *buffers(x, gains, down, *shapes[:2], *shapes[3:]),
            dma((3,)),
            dma((8,)),
            pltpu.VMEM(w_q_kv.shape, low),
            pltpu.VMEM(w_out_t.shape, low),
            pltpu.VMEM(x.shape, low),
            pltpu.VMEM(x.shape, low),
            dma((2,)),
            dma((heads + 7,)),
            dma((2,)),
            dma((2,)),
            dma((6,)),
            dma((6,)),
            dma((40,)),
            dma((40,)),
            dma((2,)),
            dma((2,)),
        ],
        compiler_params=pltpu.CompilerParams(
            collective_id=cid, has_side_effects=True, vmem_limit_bytes=60 * 2**20
        ),
    )(x, gains, cosine, sine, w_q_kv, w_out_t, down)


def finish_kernel(s_in, o_ref, s_ref, in_sem, blocks, here, send, recv):
    get = fetch([(s_in, s_ref)], in_sem)[0]
    greet(group_peers())
    get.wait()
    wide = blocks.shape[2]
    for t in range(4):
        first = t * 40 // 16 * 16
        size = (t * 40 + 40 + 15) // 16 * 16 - first
        v = s_ref[pl.ds(first, size)].astype(jnp.float32)[t * 40 - first : t * 40 - first + 40]
        rest = jnp.concatenate([v[:, wide:], jnp.zeros((40, 2 * wide - v.shape[1]), jnp.float32)], axis=1)
        blocks[t] = jnp.concatenate([v[:, :wide], rest], axis=0).astype(jnp.bfloat16)
    send_blocks([blocks], [o_ref], here, send, recv)()


def finish(sent, cid):
    dma = pltpu.SemaphoreType.DMA
    buffer = jax.ShapeDtypeStruct((4, 80, 3 * FEED), sent.dtype)
    return pl.pallas_call(
        finish_kernel,
        out_shape=buffer,
        in_specs=[HBM],
        out_specs=HBM,
        scratch_shapes=[*buffers(sent), dma((1,)), *buffers(buffer), dma((1,)), dma((3,)), dma((3,))],
        compiler_params=pltpu.CompilerParams(
            collective_id=cid, has_side_effects=True, vmem_limit_bytes=60 * 2**20
        ),
    )(sent)


def write_kernel(
    l_in, block_in, grad_in, q_in, kv_in, o_in, g_in,
    block, grad, q, kv, o, g, down_ref, gate_ref, up_ref,
    landed, b1, b2, b3, b4, b5, b6, sem, load_sem,
):
    held = (b1, b2, b3, b4, b5, b6)
    get, *gets = fetch(list(zip((l_in, block_in, grad_in, q_in, kv_in, o_in, g_in), (landed, *held))), load_sem)
    for one in gets:
        one.wait()
    copies = fetch(list(zip(held, (block, grad, q, kv, o, g))), sem)
    get.wait()
    for t in range(4):
        v = landed[t].astype(jnp.float32)
        v = jnp.concatenate([v[:40], v[40:]], axis=1)
        first, tail = t * 960, t * 960 + MAIN
        gate_ref[:, first:tail] = v[:, :MAIN]
        gate_ref[:, tail : tail + 64] = v[:, 2 * MAIN : 2 * MAIN + 64]
        up_ref[:, first:tail] = v[:, MAIN : 2 * MAIN]
        up_ref[:, tail : tail + 64] = v[:, 2 * MAIN + 64 : PACKED]
        down_ref[:, first : first + 960] = v[:, PACKED : PACKED + 960]
    for copy in copies:
        copy.wait()


def written(landed, arrays):
    dma = pltpu.SemaphoreType.DMA
    vmem = pl.BlockSpec(memory_space=pltpu.VMEM)
    return pl.pallas_call(
        write_kernel,
        out_shape=[
            *(jax.ShapeDtypeStruct(a.shape, a.dtype) for a in arrays),
            *[jax.ShapeDtypeStruct((40, 3840), jnp.float32)] * 3,
        ],
        in_specs=[HBM] * 7,
        out_specs=[HBM] * 6 + [vmem] * 3,
        scratch_shapes=[*buffers(landed, *arrays), dma((6,)), dma((7,))],
        compiler_params=pltpu.CompilerParams(vmem_limit_bytes=56 * 2**20),
    )(landed, *arrays)


class SumPiece:
    def __init__(self, h, sums, columns, via, main, sems, rows=160):
        self.h, self.sums, self.columns, self.via, self.main, self.sems, self.rows = (
            h, sums, columns, via, main, sems, rows,
        )

    def first(self, i1, i2, part=0):
        row, column = (i2, i1) if self.h == 0 else (i1, i2)
        return (row * 4 + column) * self.rows + part * (self.rows // 2)

    def at(self, i1, i2, part=None):
        size = self.rows if part is None else self.rows // 2
        return self.sums.at[pl.ds(pl.multiple_of(self.first(i1, i2, part or 0), 16), size), self.columns]


ORDER = (
    "P0", "yv0", "yv1", "yv2", "xv0", "P1", "xv1", "P2", "xv2", "P3", "yxm0", "yxv3", "Tc", "yxm1",
    "T0", "xyt0", "xyv4", "xym2", "gv0", "gv1", "gv2", "gv3", "xyt1", "T1", "xym3", "xyt2", "gm0",
    "gm1", "gm2", "gm3", "xym4", "xyt3", "gt0", "gt1", "gt2", "gt3", "gv4", "Tg", "gm4", "xyt4",
    "gt4", "To",
)


def plane_sum_kernel(
    left_in, dq_ref, dl_ref, right_in, gi_ref, p_in, t_in, x_in, mid_in, dmid_in, g_in, order_in,
    q_out, kv_out, wo_out, go_ref, block_ref, grad_ref,
    left, right_o, p_ref, t_ref, x_ref, mid_ref, dmid_ref, g_ref, order_ref, attn_ref, in_sem,
    right, left_o, sums, via, main, gsums, gvia, gmain, from_chip, attn_low, gfar, gsum, gall,
    t_core, t_other, t_chips, t_own, t_far, landed, block_low, grad_low,
    here, csend, crecv, send, recv, esend, erecv, tsend, trecv, shere, ssend, srecv,
):
    y, x, c, zl, zh = (lax.axis_index(k) for k in ("y", "x", "c", "zl", "zh"))
    core, chip, far_peer = {"c": 1 - c}, {"zl": 1 - zl}, {"zh": 1 - zh}
    chips = [{"zl": 1 - zl, "zh": k} for k in range(2)]
    get_p, get_t, get_left, get_right, *gets = fetch(
        [
            (p_in, p_ref), (t_in, t_ref), (left_in, left), (right_in, right_o), (x_in, x_ref),
            (mid_in, mid_ref), (dmid_in, dmid_ref), (g_in, g_ref), (order_in, order_ref),
        ],
        in_sem,
    )
    greet(
        [*ring_of("x", x), *ring_of("y", y), core, *chips, far_peer, {"zl": 1 - zl, "c": 1 - c}]
    )
    step = 16
    f32, low = jnp.float32, jnp.bfloat16
    order = (2, 1, 3, 0)
    tokens = p_ref.shape[1]
    half = tokens // 2

    inputs = [(dq_ref, right), (dl_ref, left_o)]
    mine = pl.ds(pl.multiple_of(c * tokens, tokens), tokens)
    shared = [
        remote(src, dst.at[mine], csend.at[k], crecv.at[k], core) for k, (src, dst) in enumerate(inputs)
    ]
    kept = [pltpu.make_async_copy(src, dst.at[mine], here.at[k]) for k, (src, dst) in enumerate(inputs)]
    kept.append(pltpu.make_async_copy(gi_ref, gsums, here.at[2]))
    for copy in (*shared, *kept):
        copy.start()
    t_cores = [
        remote(p_ref.at[z * 2 + 1 - c], t_core.at[i], tsend.at[i], trecv.at[i], core)
        for i, z in enumerate((1 - zl, zl))
    ]
    get_p.wait()
    for copy in t_cores:
        copy.start()
    get_t.wait()
    pair = remote(t_ref, landed, tsend.at[6], trecv.at[6], far_peer)
    pair.start()
    t_sent = []

    def tokens_to_chips():
        t_cores[0].wait_recv()

        @pl.loop(0, tokens // step)
        def _(i):
            at = pl.ds(pl.multiple_of(i * step, step), step)
            total = p_ref[(1 - zl) * 2 + c, at].astype(f32) + t_core[0, at].astype(f32)
            t_other[at] = total.astype(low)

        for k in range(2):
            t_sent.append(
                remote(t_other.at[pl.ds(k * half, half)], t_chips.at[zh], tsend.at[2 + k], trecv.at[2 + zh], chips[k])
            )
            t_sent[-1].start()

    def tokens_to_far(k):
        piece = (1 - zh) if k == 0 else zh
        if k == 0:
            t_cores[1].wait_recv()
        else:
            for i in range(2):
                remote(
                    t_other.at[pl.ds(0, half)], t_chips.at[i], tsend.at[2 + i], trecv.at[2 + i], chips[i]
                ).wait_recv()

        @pl.loop(0, half // step)
        def _(i):
            at = pl.ds(pl.multiple_of(piece * half + i * step, step), step)
            total = p_ref[zl * 2 + c, at].astype(f32) + t_core[1, at].astype(f32)
            if k == 1:
                there = pl.ds(pl.multiple_of(i * step, step), step)
                total += t_chips[0, there].astype(f32) + t_chips[1, there].astype(f32)
            t_own[at] = total.astype(low)

        at = pl.ds(pl.multiple_of(piece * half, half), half)
        t_sent.append(remote(t_own.at[at], t_far.at[at], tsend.at[4 + k], trecv.at[4 + k], far_peer))
        t_sent[-1].start()

    def tokens_gradient():
        pair.wait_recv()

        @pl.loop(0, tokens // step)
        def _(i):
            at = pl.ds(pl.multiple_of(i * step, step), step)
            d = (t_ref[at].astype(f32) + landed[at].astype(f32)) * g_ref[0:1]
            v = x_ref[at]
            r = lax.rsqrt(jnp.mean(v * v, axis=-1, keepdims=True) + norm_eps)
            n = v * r
            d = r * (d - n * jnp.mean(d * n, axis=-1, keepdims=True))
            grad_low[at] = (dmid_ref[at] + d).astype(low)

        reorder(grad_low, order_ref, grad_ref, True)

    def tokens_output():
        for k in range(2):
            t_sent[2 + k].wait_recv()

        @pl.loop(0, tokens // step)
        def _(i):
            at = pl.ds(pl.multiple_of(i * step, step), step)
            branch = t_own[at].astype(f32) + t_far[at].astype(f32)
            block_low[at] = (mid_ref[at] + branch).astype(low)

        reorder(block_low, order_ref, block_ref, True)

    def products(q):
        top = shift(y, order[q]) * 640
        for side in range(2):

            @pl.when(c == side)
            def _(side=side):
                if side == 0:
                    parts = [(left, right, 0, 0, 768), (left, right, 768, 768, 768)]
                else:
                    parts = [
                        (left, right, 1536, 0, 256),
                        (left_o, right_o, 0, 256, 512),
                        (left_o, right_o, 512, 768, 768),
                    ]

                @pl.loop(0, 5)
                def _(i):
                    at = pl.ds(pl.multiple_of(top + i * 128, 128), 128)
                    for lhs, rhs, source, target, width in parts:
                        sums[at, pl.ds(target, width)] = lax.dot_general(
                            lhs[:, at],
                            rhs[:, pl.ds(source, width)],
                            (((0,), (0,)), ((), ())),
                            preferred_element_type=f32,
                        ).astype(low)

    pieces = [
        SumPiece(h, sums, pl.ds(h * ATTN, ATTN), via.at[h], main.at[h], h * 20) for h in range(2)
    ]
    pieces.append(SumPiece(0, gsums, pl.ds(0, 128), gvia, gmain, 40, 64))

    def add(p, first, size, terms):
        @pl.loop(0, size // step)
        def _(i):
            at = pl.ds(pl.multiple_of(first + i * step, step), step)
            total = p.sums[at, p.columns].astype(f32)
            for ref, index, start in terms:
                total += ref[(*index, pl.ds(pl.multiple_of(start + i * step, step), step))].astype(f32)
            p.sums[at, p.columns] = total.astype(low)

    started = []

    def go(p, ring, slot, src, dst, peer):
        k = p.sems + ring * 4 + slot
        copy = remote(src, dst, send.at[k], recv.at[k], peer)
        copy.start()
        started.append(copy)

    def arrived(p, ring, slot, dst):
        k = p.sems + ring * 4 + slot
        remote(dst, dst, send.at[k], recv.at[k], core).wait_recv()

    def line(p, j):
        i1, peers1, i2, peers2 = around(p.h, y, x)
        if j == 4:
            return lambda k: (k, i2), i1, peers1
        fixed = shift(i1, order[j])
        return lambda k: (fixed, k), i2, peers2

    def out_via(p, ring):
        place, at, (back, ahead) = line(p, ring)
        far = place(shift(at, 2))
        go(p, ring, 0, p.at(*far, 0), p.via.at[ring, 0], ahead)
        go(p, ring, 1, p.at(*far, 1), p.via.at[ring, 1], back)

    def out_main(p, ring):
        place, at, (back, ahead) = line(p, ring)
        small = p.rows // 2
        arrived(p, ring, 0, p.via.at[ring, 0])
        add(p, p.first(*place(shift(at, 1)), 0), small, [(p.via, (ring, 0), 0)])
        go(p, ring, 2, p.at(*place(shift(at, 1))), p.main.at[ring, 0], ahead)
        arrived(p, ring, 1, p.via.at[ring, 1])
        add(p, p.first(*place(shift(at, 3)), 1), small, [(p.via, (ring, 1), 0)])
        go(p, ring, 3, p.at(*place(shift(at, 3))), p.main.at[ring, 1], back)

    def take(p, ring):
        place, at, _ = line(p, ring)
        arrived(p, ring, 2, p.main.at[ring, 0])
        arrived(p, ring, 3, p.main.at[ring, 1])
        add(p, p.first(*place(at)), p.rows, [(p.main, (ring, 0), 0), (p.main, (ring, 1), 0)])

    y_first, x_first, gain = pieces
    for copy in kept:
        copy.wait()
    for copy in shared:
        copy.wait_recv()
    for get in (get_left, get_right, *gets):
        get.wait()
    named = {"x": x_first, "y": y_first, "g": gain}
    acts = {"v": out_via, "m": out_main, "t": take}
    token_acts = {
        "Tc": tokens_to_chips,
        "T0": lambda: tokens_to_far(0),
        "T1": lambda: tokens_to_far(1),
        "Tg": tokens_gradient,
        "To": tokens_output,
    }
    for word in ORDER:
        if word[0] == "P":
            products(int(word[1]))
        elif word[0] == "T":
            token_acts[word]()
        else:
            for name in word[:-2]:
                acts[word[-2]](named[name], int(word[-1]))
    home = (y * 4 + x) * 160
    ghome = pl.ds(pl.multiple_of((y * 4 + x) * 64, 16), 64)
    theirs = pl.ds(pl.multiple_of(home + (1 - zl) * 80, 16), 80)
    across = remote(gsums.at[ghome], gfar, esend.at[0], erecv.at[0], far_peer)
    across.start()
    away = remote(sums.at[theirs], from_chip, esend.at[1], erecv.at[1], chip)
    away.start()
    across.wait()
    both = gsums[ghome].astype(f32) + gfar[...].astype(f32)
    for t in range(4):
        gsum[t] = both[t * 16 : (t + 1) * 16].astype(low)
    finish_gains = send_blocks([gsum], [gall], shere, ssend, srecv)
    away.wait()

    @pl.loop(0, 80 // step)
    def _(i):
        here_at = pl.ds(pl.multiple_of(home + zl * 80 + i * step, step), step)
        at = pl.ds(pl.multiple_of(i * step, step), step)
        attn_low[at] = sums[here_at].astype(f32) + from_chip[at].astype(f32)

    ours = pl.ds(pl.multiple_of(c * 40, 8), 40)
    for_core = pl.ds(pl.multiple_of((1 - c) * 40, 8), 40)
    columns = pl.ds(pl.multiple_of(c * 2 * ATTN, 128), 2 * ATTN)
    last = remote(attn_low.at[for_core], attn_ref.at[:, columns], esend.at[2], erecv.at[2], core)
    keep = pltpu.make_async_copy(attn_low.at[ours], attn_ref.at[:, columns], here.at[0])
    last.start()
    keep.start()
    finish_gains()
    go_ref[...] = (
        gall[0].astype(f32) + gall[1].astype(f32) + gall[2].astype(f32) + gall[3].astype(f32)
    )
    last.wait()
    keep.wait()
    first = 0
    for out in (q_out, kv_out, wo_out):
        out[...] = attn_ref[:, first : first + out.shape[1]]
        first += out.shape[1]
    for copy in (*started, *shared, pair, *t_cores, *t_sent):
        copy.wait_send()


def plane_sum(xn, d_q_kv, d_low, mixed, gains, down, d_xn, x, mid, d_mid, gains_row, order, cid):
    low, dma, f32 = jnp.bfloat16, pltpu.SemaphoreType.DMA, jnp.float32
    rows, width = x.shape
    vmem = pl.BlockSpec(memory_space=pltpu.VMEM)
    return pl.pallas_call(
        plane_sum_kernel,
        out_shape=[
            *(jax.ShapeDtypeStruct((40, n), f32) for n in (1280, 512, 1280)),
            jax.ShapeDtypeStruct((16, 128), f32),
            jax.ShapeDtypeStruct(x.shape, low),
            jax.ShapeDtypeStruct(x.shape, low),
        ],
        in_specs=[HBM] * 12,
        out_specs=[vmem] * 6,
        scratch_shapes=[
            *buffers(xn, mixed, down, d_xn, x, mid, d_mid, gains_row, order),
            pltpu.VMEM((40, 4 * ATTN), f32),
            dma((9,)),
            pltpu.VMEM((2 * rows, d_q_kv.shape[1]), low),
            pltpu.VMEM((2 * rows, width), low),
            pltpu.VMEM((2560, 2 * ATTN), low),
            pltpu.VMEM((2, 5, 2, 80, ATTN), low),
            pltpu.VMEM((2, 5, 2, 160, ATTN), low),
            pltpu.VMEM((1024, 128), low),
            pltpu.VMEM((5, 2, 32, 128), low),
            pltpu.VMEM((5, 2, 64, 128), low),
            pltpu.VMEM((80, 2 * ATTN), low),
            pltpu.VMEM((80, 2 * ATTN), f32),
            pltpu.VMEM((64, 128), low),
            pltpu.VMEM((4, 16, 128), low),
            pltpu.VMEM((4, 16, 128), low),
            pltpu.VMEM((2, rows, width), low),
            pltpu.VMEM((rows, width), low),
            pltpu.VMEM((2, rows // 2, width), low),
            pltpu.VMEM((rows, width), low),
            pltpu.VMEM((rows, width), low),
            pltpu.VMEM((rows, width), low),
            pltpu.VMEM((rows, width), low),
            pltpu.VMEM((rows, width), low),
            dma((3,)),
            dma((2,)),
            dma((2,)),
            dma((60,)),
            dma((60,)),
            dma((3,)),
            dma((3,)),
            dma((7,)),
            dma((7,)),
            dma((1,)),
            dma((3,)),
            dma((3,)),
        ],
        compiler_params=pltpu.CompilerParams(
            collective_id=cid, has_side_effects=True, vmem_limit_bytes=60 * 2**20
        ),
    )(xn, d_q_kv, d_low, mixed, gains, down, d_xn, x, mid, d_mid, gains_row, order)


GELU_IN, GELU_CUBE = math.sqrt(2.0 / math.pi), 0.044715


def feed_kernel(
    xn_in, dy_ref, g_ref, d_ref, h_out, dg_out, o_ref,
    xn_ref, h_ref, dg_ref, in_sem, h_sem, dy, wg, wd, dy_turned, xn_turned, back, out, load_sem, out_sem,
):
    f32, low = jnp.float32, jnp.bfloat16
    units, lines = h_ref.shape[1], out.shape[1]
    lanes = lax.broadcasted_iota(jnp.int32, (1, 128), 1)
    get_xn = fetch([(xn_in, xn_ref)], in_sem)[0]
    get_dy = pltpu.make_async_copy(dy_ref, dy, load_sem.at[0])
    get_dy.start()
    loads = []
    for source, target in ((d_ref, wd), (g_ref, wg)):
        for n in range(4):
            some = pl.ds(n * 640, 640)
            loads.append(pltpu.make_async_copy(source.at[some], target.at[some], load_sem.at[1 + len(loads)]))
            loads[-1].start()
    get_xn.wait()
    xn_turned[...] = xn_ref[...].T
    get_dy.wait()
    dy_turned[...] = dy[...].T
    for n in range(4):
        loads[n].wait()
    for k in range(units // 256):
        at = pl.ds(k * 256, 256)
        back[:, at] = jnp.dot(dy[...], wd[:, at], preferred_element_type=f32)
    for n in range(4, 8):
        loads[n].wait()
    def act(gate, up, d):
        square = gate * gate
        t = jnp.tanh(GELU_IN * (gate + GELU_CUBE * gate * square))
        cdf = 0.5 * (1.0 + t)
        slope = cdf + 0.5 * gate * (1.0 - t * t) * (GELU_IN * (1.0 + 3.0 * GELU_CUBE * square))
        gelu = gate * cdf
        return gelu * up, d * up * slope, d * gelu

    for first, size in ((0, 256), (256, 256), (512, 256), (768, 128)):
        at, beside = pl.ds(first, size), pl.ds(MAIN + first, size)
        gate = jnp.dot(xn_ref[...], wg[:, at], preferred_element_type=f32)
        up = jnp.dot(xn_ref[...], wg[:, beside], preferred_element_type=f32)
        hidden, d_gate, d_up = act(gate, up, back[:, at])
        h_ref[:, at] = hidden.astype(low)
        dg_ref[:, at] = d_gate.astype(low)
        dg_ref[:, beside] = d_up.astype(low)
    at, both = pl.ds(MAIN, 128), pl.ds(2 * MAIN, 128)
    gate = jnp.dot(xn_ref[...], wg[:, both], preferred_element_type=f32)
    hidden, d_gate, d_up = act(gate, pltpu.roll(gate, 64, 1), back[:, at])
    h_ref[:, at] = jnp.where(lanes < 64, hidden, 0.0).astype(low)
    dg_ref[:, both] = jnp.where(lanes < 64, d_gate, pltpu.roll(d_up, 64, 1)).astype(low)
    puts = fetch([(h_ref, h_out), (dg_ref, dg_out)], h_sem)

    def put(i):
        slot = lax.rem(i, 2)
        rows = pl.ds(pl.multiple_of(i * lines, lines), lines)
        return pltpu.make_async_copy(out.at[slot], o_ref.at[rows], out_sem.at[slot])

    steps = o_ref.shape[0] // lines

    @pl.loop(0, steps)
    def _(i):
        slot = lax.rem(i, 2)
        pl.when(i >= 2)(lambda: put(i - 2).wait())
        rows = pl.ds(pl.multiple_of(i * lines, lines), lines)
        for left, right, first, total in ((xn_turned, dg_ref, 0, PACKED), (dy_turned, h_ref, PACKED, 960)):
            for k in range(0, total, 512):
                size = min(512, right.shape[1] - k)
                kept = min(size, total - k)
                v = jnp.dot(left[rows], right[:, pl.ds(k, size)], preferred_element_type=f32)
                out[slot, :, pl.ds(first + k, kept)] = v[:, :kept].astype(low)
        put(i).start()

    put(steps - 2).wait()
    put(steps - 1).wait()
    for copy in puts:
        copy.wait()


def feed(xn, dy, w_gate_up, w_down):
    depth, width = xn.shape
    units = w_down.shape[1]
    low, dma = jnp.bfloat16, pltpu.SemaphoreType.DMA
    shapes = [
        jax.ShapeDtypeStruct((depth, units), low),
        jax.ShapeDtypeStruct((depth, PACKED), low),
        jax.ShapeDtypeStruct((width, PACKED + 960), low),
    ]
    return pl.pallas_call(
        feed_kernel,
        out_shape=shapes,
        in_specs=[HBM] * 4,
        out_specs=[HBM] * 3,
        scratch_shapes=[
            *buffers(xn, *shapes[:2]),
            dma((1,)),
            dma((2,)),
            pltpu.VMEM((depth, width), low),
            pltpu.VMEM((width, PACKED), low),
            pltpu.VMEM((width, units), low),
            pltpu.VMEM((width, depth), low),
            pltpu.VMEM((width, depth), low),
            pltpu.VMEM((depth, units), jnp.float32),
            pltpu.VMEM((2, 640, PACKED + 960), low),
            dma((9,)),
            dma((2,)),
        ],
        compiler_params=pltpu.CompilerParams(vmem_limit_bytes=60 * 2**20),
        cost_estimate=pl.CostEstimate(
            flops=12 * depth * width * units,
            bytes_accessed=4 * depth * width + 12 * width * units + 6 * depth * units,
            transcendentals=depth * units,
        ),
    )(xn, dy, w_gate_up, w_down)


def back_kernel(
    dg_in, h_in, w_ref, d_ref, wo_ref, wq_ref,
    x_in, mid_in, dy_in, g_in, soft_in, q_in, kv_in, cos_ref, sin_ref,
    down_out, dmid_out, dl_out, dq_out, dx_out, gains_out,
    dg_ref, h_ref, x_ref, mid_ref, dy_ref, g_ref, soft_ref, q_ref, kv_ref,
    down_ref, dmid_ref, dl_ref, dq_ref, dx_ref, gains_ref, in_sem, out_sem,
    w, wd, wo, part, from_core, other, from_chips, own, from_far, grad, kv_part, kv_far, halved, sums,
    wsem, send, recv, osem, qsem, fsend, frecv,
):
    zl, c, zh = lax.axis_index("zl"), lax.axis_index("c"), lax.axis_index("zh")
    core, far = {"c": 1 - c}, {"zh": 1 - zh}
    chips = [{"zl": 1 - zl, "zh": k} for k in range(2)]
    f32, low = jnp.float32, jnp.bfloat16
    parts, width = w_ref.shape[0] // 640, 640
    rows = x_ref.shape[0]
    half, step = rows // 2, 16
    heads = soft_ref.shape[0]
    get_dg, get_h, *gets = fetch(
        [
            (dg_in, dg_ref), (h_in, h_ref), (x_in, x_ref), (mid_in, mid_ref), (dy_in, dy_ref),
            (g_in, g_ref), (soft_in, soft_ref), (q_in, q_ref), (kv_in, kv_ref),
        ],
        in_sem,
    )
    loads = []
    for source, target, first in ((w_ref, w, 0), (d_ref, wd, parts)):
        for n in range(parts):
            some = pl.ds(n * width, width)
            loads.append(pltpu.make_async_copy(source.at[some], target.at[some], wsem.at[first + n]))
            loads[-1].start()
    get_wo = pltpu.make_async_copy(wo_ref, wo, osem)
    get_wo.start()
    wq = w.at[:, pl.ds(0, wq_ref.shape[1])]
    get_wq = pltpu.make_async_copy(wq_ref, wq, qsem)
    greet([core, far, *chips])
    order = [1 - zl, zl]
    started = []

    def go(src, dst, n, out_slot, in_slot, peer):
        copy = remote(src, dst, send.at[n * 6 + out_slot], recv.at[n * 6 + in_slot], peer)
        copy.start()
        started.append(copy)

    def arrived(dst, n, slot):
        remote(dst, dst, send.at[n * 6 + slot], recv.at[n * 6 + slot], core).wait_recv()

    def columns(n):
        return pl.ds(n * width, width)

    def product(left, right, n, target):
        some = pl.ds(n * width, width)
        v = lax.dot_general(
            left[...], right[some], (((1,), (1,)), ((), ())), preferred_element_type=f32
        ).astype(low)
        for t in range(4):
            target[t, :, some] = v[t * rows : (t + 1) * rows]

    def multiply(n):
        loads[n].wait()
        product(dg_ref, w, n, part)
        for i, z in enumerate(order):
            go(part.at[z * 2 + 1 - c, :, columns(n)], from_core.at[i, :, columns(n)], n, i, i, core)

    def down(n):
        loads[parts + n].wait()
        product(h_ref, wd, n, down_ref)

    def to_chips(n):
        arrived(from_core.at[0, :, columns(n)], n, 0)

        @pl.loop(0, rows // step)
        def _(i):
            at = pl.ds(pl.multiple_of(i * step, step), step)
            total = part[(1 - zl) * 2 + c, at, columns(n)].astype(f32) + from_core[0, at, columns(n)].astype(f32)
            other[at, columns(n)] = total.astype(low)

        for k in range(2):
            go(other.at[pl.ds(k * half, half), columns(n)], from_chips.at[zh, :, columns(n)], n, 2 + k, 2 + zh, chips[k])

    def to_far(n, k):
        piece = (1 - zh) if k == 0 else zh
        if k == 0:
            arrived(from_core.at[1, :, columns(n)], n, 1)
        else:
            for i in range(2):
                arrived(from_chips.at[i, :, columns(n)], n, 2 + i)

        @pl.loop(0, half // step)
        def _(i):
            at = pl.ds(pl.multiple_of(piece * half + i * step, step), step)
            total = part[zl * 2 + c, at, columns(n)].astype(f32) + from_core[1, at, columns(n)].astype(f32)
            if k == 1:
                there = pl.ds(pl.multiple_of(i * step, step), step)
                total += from_chips[0, there, columns(n)].astype(f32) + from_chips[1, there, columns(n)].astype(f32)
            own[at, columns(n)] = total.astype(low)

        at = pl.ds(pl.multiple_of(piece * half, half), half)
        go(own.at[at, columns(n)], from_far.at[at, columns(n)], n, 4 + k, 4 + k, far)

    def finish(n):
        for k in range(2):
            arrived(from_far.at[pl.ds(k * half, half), columns(n)], n, 4 + k)

        @pl.loop(0, rows // step)
        def _(i):
            at = pl.ds(pl.multiple_of(i * step, step), step)
            grad[at, columns(n)] = own[at, columns(n)].astype(f32) + from_far[at, columns(n)].astype(f32)

    get_dg.wait()
    multiply(0)
    multiply(1)
    to_chips(0)
    to_far(0, 0)
    multiply(2)
    to_chips(1)
    to_far(1, 0)
    multiply(3)
    get_wq.start()
    to_chips(2)
    to_far(2, 0)
    to_far(0, 1)
    get_h.wait()
    down(0)
    to_chips(3)
    to_far(3, 0)
    to_far(1, 1)
    down(1)
    to_far(2, 1)
    down(2)
    to_far(3, 1)
    down(3)
    for n in range(parts):
        finish(n)
    sums[...] = jnp.zeros_like(sums)
    puts = fetch([(down_ref, down_out)], out_sem)
    for get in gets:
        get.wait()

    @pl.loop(0, rows // step)
    def _(i):
        at = pl.ds(pl.multiple_of(i * step, step), step)
        v, d = mid_ref[at], grad[at]
        r = lax.rsqrt(jnp.mean(v * v, axis=-1, keepdims=True) + norm_eps)
        n = v * r
        sums[1:2] += jnp.sum(d * n, axis=0, keepdims=True) * 0.5
        d = d * g_ref[1:2]
        d = dy_ref[at].astype(f32) + r * (d - n * jnp.mean(d * n, axis=-1, keepdims=True))
        dmid_ref[at] = d
        dl_ref[at] = d.astype(low)

    def across(left, right, left_dim, right_dim):
        return lax.dot_general(
            left, right, (((left_dim,), (right_dim,)), ((), ())), preferred_element_type=f32
        )

    def turned_back(u):
        turn = u[:, :ROT]
        turn = turn * cos_ref[...] - pltpu.roll(turn, ROT // 2, 1) * sin_ref[...]
        return jnp.concatenate([turn, u[:, ROT:]], axis=1).astype(low)

    get_wo.wait()
    puts += fetch([(dmid_ref, dmid_out), (dl_ref, dl_out)], out_sem.at[pl.ds(1, 2)])
    keys, values = kv_ref[:, :HEAD_DIM], kv_ref[:, HEAD_DIM:]
    scale = HEAD_DIM**-0.5
    d_keys = jnp.zeros((rows, HEAD_DIM), f32)
    d_values = jnp.zeros((rows, HEAD_DIM), f32)
    for h in range(heads):
        at = pl.ds(h * HEAD_DIM, HEAD_DIM)
        d_mixed = jnp.dot(dl_ref[...], wo[:, at], preferred_element_type=f32).astype(low)
        soft = soft_ref[h]
        d_probs = across(d_mixed, values, 1, 1)
        d_scores = (soft * (d_probs - jnp.sum(soft * d_probs, axis=-1, keepdims=True))).astype(low)
        dq_ref[:, at] = turned_back(jnp.dot(d_scores, keys, preferred_element_type=f32) * scale)
        d_keys += across(d_scores, q_ref[:, at], 0, 0)
        d_values += across(soft.astype(low), d_mixed, 0, 0)
    kv_part[:, :HEAD_DIM] = turned_back(d_keys * scale)
    kv_part[:, HEAD_DIM:] = d_values.astype(low)
    pair = remote(kv_part, kv_far, fsend, frecv, far)
    pair.start()
    pair.wait()
    first_kv = heads * HEAD_DIM
    kv = kv_part[...].astype(f32) + kv_far[...].astype(f32)
    kv = kv.astype(low)
    dq_ref[:, first_kv:] = kv
    halved[:, :first_kv] = dq_ref[:, :first_kv]
    halved[:, first_kv:] = kv * 0.5
    get_wq.wait()
    for k in range(5):
        some = pl.ds(k * 512, 512)
        d = across(halved[...], w[some, : wq_ref.shape[1]], 1, 1)
        grad[:, some] = d
        dx_ref[:, some] = d.astype(low)

    @pl.loop(0, rows // step)
    def _(i):
        at = pl.ds(pl.multiple_of(i * step, step), step)
        v = x_ref[at]
        r = lax.rsqrt(jnp.mean(v * v, axis=-1, keepdims=True) + norm_eps)
        sums[0:1] += jnp.sum(grad[at] * (v * r), axis=0, keepdims=True)

    both = jnp.concatenate([sums[...], jnp.zeros((8, sums.shape[1]), f32)], axis=0)
    for k in range(64):
        tile = jnp.concatenate([both[:, k * 40 : (k + 1) * 40], jnp.zeros((16, 88), f32)], axis=1)
        gains_ref[k * 16 : (k + 1) * 16] = tile.astype(low)
    puts += fetch([(dq_ref, dq_out), (dx_ref, dx_out), (gains_ref, gains_out)], out_sem.at[pl.ds(3, 3)])
    for copy in started:
        copy.wait_send()
    for copy in puts:
        copy.wait()


def feed_back(
    d_gate_up, hidden, w_gate_up, w_down, w_out, w_q_kv,
    x, mid, dy, gains, soft, queries, keys_values, cosine, sine, cid,
):
    dma, low, f32 = pltpu.SemaphoreType.DMA, jnp.bfloat16, jnp.float32
    vmem = pl.BlockSpec(memory_space=pltpu.VMEM)
    rows, width = x.shape
    wide = w_q_kv.shape[1]
    shapes = [
        jax.ShapeDtypeStruct((4, rows, width), low),
        jax.ShapeDtypeStruct((rows, width), f32),
        jax.ShapeDtypeStruct((rows, width), low),
        jax.ShapeDtypeStruct((rows, wide), low),
        jax.ShapeDtypeStruct((rows, width), low),
        jax.ShapeDtypeStruct((1024, 128), low),
    ]
    return pl.pallas_call(
        back_kernel,
        out_shape=shapes,
        in_specs=[HBM] * 13 + [vmem] * 2,
        out_specs=[HBM] * 6,
        scratch_shapes=[
            *buffers(d_gate_up, hidden, x, mid, dy, gains, soft, queries, keys_values, *shapes),
            dma((9,)),
            dma((6,)),
            pltpu.VMEM(w_gate_up.shape, low),
            pltpu.VMEM(w_down.shape, low),
            pltpu.VMEM(w_out.shape, low),
            pltpu.VMEM((4, rows, width), low),
            pltpu.VMEM((2, rows, width), low),
            pltpu.VMEM((rows, width), low),
            pltpu.VMEM((2, rows // 2, width), low),
            pltpu.VMEM((rows, width), low),
            pltpu.VMEM((rows, width), low),
            pltpu.VMEM((rows, width), f32),
            pltpu.VMEM(keys_values.shape, low),
            pltpu.VMEM(keys_values.shape, low),
            pltpu.VMEM((rows, wide), low),
            pltpu.VMEM((8, width), f32),
            dma((8,)),
            dma((24,)),
            dma((24,)),
            dma,
            dma,
            dma,
            dma,
        ],
        compiler_params=pltpu.CompilerParams(
            collective_id=cid, has_side_effects=True, vmem_limit_bytes=60 * 2**20
        ),
    )(
        d_gate_up, hidden, w_gate_up, w_down, w_out, w_q_kv,
        x, mid, dy, gains, soft, queries, keys_values, cosine, sine,
    )


def tables():
    half = ROT // 2
    rates = np.exp(np.arange(half, dtype=np.float32) * np.float32(-2.0 * math.log(10000.0) / ROT))
    angles = np.arange(SEQ_LEN, dtype=np.float32)[:, None] * rates[None, :]
    cosine, sine = np.cos(angles), np.sin(angles)
    return np.concatenate([cosine, cosine], axis=1), np.concatenate([-sine, sine], axis=1)


def local(
    tokens,
    attn_gain,
    query_weight,
    kv_weight,
    out_weight,
    mlp_gain,
    gate_weight,
    up_weight,
    down_weight,
    cotangent,
):
    low = jnp.bfloat16
    rows = tokens.shape[0]
    gains = jnp.pad(jnp.stack([attn_gain, mlp_gain], axis=0), ((0, 14), (0, 88)))
    order = jnp.asarray(feature_order(), low)
    weights = (query_weight, kv_weight, out_weight.T, gate_weight, up_weight, down_weight.T)
    first, gains, second, down, x_in, dy_here = group_exchange(
        weights, gains, tokens, cotangent, order, 5
    )
    w_gate_up = lax.all_gather(second, PLANE, axis=0, tiled=True)
    w_q_kv, w_out_t, gains, dy, down = attention_gather(first, gains.reshape(64, 128), dy_here, down, 6)
    dy = dy.reshape(4 * rows, -1)
    cosine, sine = (jnp.asarray(t) for t in tables())
    x_mid, xn_all, w_down_t, xn_one, mixed_heads, queries, keys_values, soft_rows, gains = middle(
        x_in, gains, cosine, sine, w_q_kv, w_out_t, down, 2
    )
    xn_all = xn_all.reshape(4 * rows, -1)
    hidden, d_gate_up, sent = feed(xn_all, dy, w_gate_up, w_down_t)
    sent = lax.psum_scatter(sent, PLANE, scatter_dimension=0, tiled=True)
    down_part, d_mid, d_mid_low, d_q_kv, d_xn_one, d_gains = feed_back(
        d_gate_up,
        hidden,
        w_gate_up,
        w_down_t,
        w_out_t,
        w_q_kv,
        x_in,
        x_mid,
        dy_here,
        gains,
        soft_rows,
        queries,
        keys_values,
        cosine,
        sine,
        3,
    )
    query_out, kv_out, out_out, gain_out, block_out, tokens_grad = plane_sum(
        xn_one.reshape(2 * rows, -1),
        d_q_kv,
        d_mid_low,
        mixed_heads.reshape(2 * rows, -1),
        d_gains,
        down_part,
        d_xn_one,
        x_in,
        x_mid,
        d_mid,
        gains,
        order,
        7,
    )
    block_out, tokens_grad, query_out, kv_out, out_out, gain_out, down_out, gate_out, up_out = written(
        finish(sent, 8), (block_out, tokens_grad, query_out, kv_out, out_out, gain_out)
    )
    return (
        block_out,
        tokens_grad,
        gain_out[0, :40],
        query_out,
        kv_out,
        out_out.T,
        gain_out[1, :40],
        gate_out,
        up_out,
        down_out.T,
    )


def solution(mesh):
    fine = Mesh(mesh.devices.reshape(4, 2, 4, 2, 2), AXES)
    dp = ("y", "zl", "x", "c")
    in_specs = (
        P(dp, None),
        P(dp),
        P(dp, "zh"),
        P(dp, None),
        P("zh", dp),
        P(dp),
        P(dp, "zh"),
        P(dp, "zh"),
        P("zh", dp),
        P(dp, None),
    )
    out_specs = (
        P(dp, None),
        P(dp, None),
        P(dp),
        P(dp, "zh"),
        P(dp, None),
        P("zh", dp),
        P(dp),
        P(dp, "zh"),
        P(dp, "zh"),
        P("zh", dp),
    )
    return jax.shard_map(local, mesh=fine, in_specs=in_specs, out_specs=out_specs, check_vma=False)
```

```python
import math

import jax
import jax.numpy as jnp
import numpy as np
from jax import lax
from jax.experimental import pallas as pl
from jax.experimental.pallas import tpu as pltpu
from jax.sharding import Mesh
from jax.sharding import PartitionSpec as P

HEAD_DIM = 256
WINDOW = 2048
SEQ_LEN = 128
ROT = 128
AXES = ("y", "zl", "x", "c", "zh")
PLANE = ("y", "x")
GROUP = ("zl", "c")
OWNERS = ("y", "x", "zl", "c")
MESH = pl.DeviceIdType.MESH

norm_eps = 1e-06


def feature_order():
    place = np.arange(640).reshape(2, 4, 80).transpose(1, 0, 2).reshape(640)
    return (np.arange(640)[:, None] == place[None, :]).astype(np.float32)


def reorder(src, order, dst, back):
    for k in range(4):
        group = pl.ds(k * 640, 640)
        dst[:, group] = lax.dot_general(
            src[:, group],
            order[...],
            (((1,), (1 if back else 0,)), ((), ())),
            preferred_element_type=jnp.float32,
        ).astype(dst.dtype)


def greet(peers):
    barrier = pltpu.get_barrier_semaphore()
    for peer in peers:
        pl.semaphore_signal(barrier, inc=1, device_id=peer, device_id_type=MESH)
    pl.semaphore_wait(barrier, len(peers))


def remote(src, dst, send, recv, peer):
    return pltpu.make_async_remote_copy(
        src_ref=src, dst_ref=dst, send_sem=send, recv_sem=recv, device_id=peer, device_id_type=MESH
    )


ATTN, FEED = 768, 512
MAIN, PACKED = 896, 1920


def fetch(pairs, sems):
    copies = [pltpu.make_async_copy(src, dst, sems.at[k]) for k, (src, dst) in enumerate(pairs)]
    for copy in copies:
        copy.start()
    return copies


def buffers(*arrays):
    return [pltpu.VMEM(a.shape, a.dtype) for a in arrays]


HBM = pl.BlockSpec(memory_space=pltpu.HBM)


def ring_of(axis, at):
    return {axis: lax.rem(at + 3, 4)}, {axis: lax.rem(at + 1, 4)}


def send_blocks(ins, outs, here, send, recv):
    zl, c = lax.axis_index("zl"), lax.axis_index("c")
    mine = zl * 2 + c
    peers = [({"zl": 1 - zl, "c": k}, (1 - zl) * 2 + k) for k in range(2)]
    peers.append(({"c": 1 - c}, zl * 2 + 1 - c))
    n = len(ins)
    copies, keeps = [], []
    for i in range(n):
        for k, (peer, block) in enumerate(peers):
            landing = i * 3 + (c if k < 2 else 2)
            copy = remote(ins[i].at[block], outs[i].at[mine], send.at[i * 3 + k], recv.at[landing], peer)
            copy.start()
            copies.append(copy)
    for i in range(n):
        keep = pltpu.make_async_copy(ins[i].at[mine], outs[i].at[mine], here.at[i])
        keep.start()
        keeps.append(keep)

    def finish():
        for keep in keeps:
            keep.wait()
        for i in range(n):
            for k, (peer, block) in enumerate(peers):
                remote(
                    ins[i].at[block], outs[i].at[block], send.at[i * 3 + k], recv.at[i * 3 + k], peer
                ).wait_recv()
        for copy in copies:
            copy.wait_send()

    return finish


def group_peers():
    zl, c = lax.axis_index("zl"), lax.axis_index("c")
    return [{"c": 1 - c}, {"zl": 1 - zl, "c": 0}, {"zl": 1 - zl, "c": 1}]


def exchange_kernel(
    q_ref, kv_ref, wo_ref, g_ref, u_ref, d_ref, gain_ref, tok_ref, cot_ref, order_ref,
    ao_out, go_ref, so_out, do_out, x_out, dy_out,
    a_block, g_block, s_block, d_block, al, sl, ao_ref, so_ref, x_ref, dy_ref, here, send, recv, out_sem,
):
    f32, low = jnp.float32, jnp.bfloat16

    def stacked(v):
        half = v.shape[1] // 2
        return jnp.concatenate([v[:, :half], v[:, half:]], axis=0).astype(low)

    attn = jnp.concatenate([r[...].astype(f32) for r in (q_ref, kv_ref, wo_ref)], axis=1)
    for k in range(2):
        block = stacked(attn[:, k * 2 * ATTN : (k + 1) * 2 * ATTN])
        a_block[k] = block
        a_block[2 + k] = block
    gate, up, down = (r[...].astype(f32) for r in (g_ref, u_ref, d_ref))
    for t in range(4):
        first, tail, end = t * 960, t * 960 + MAIN, (t + 1) * 960
        packed = [gate[:, first:tail], up[:, first:tail], gate[:, tail:end], up[:, tail:end]]
        s_block[t] = stacked(jnp.concatenate([*packed, jnp.zeros((40, 128), f32)], axis=1))
        d_block[t] = stacked(jnp.concatenate([down[:, first:end], jnp.zeros((40, 64), f32)], axis=1))
        g_block[t] = gain_ref[...]
    greet(group_peers())
    finish = send_blocks([a_block, g_block, s_block], [al, go_ref, sl], here, send, recv)
    early = fetch([(d_block, do_out)], out_sem.at[pl.ds(4, 1)])
    reorder(tok_ref, order_ref, x_ref, False)
    reorder(cot_ref, order_ref, dy_ref, False)
    puts = fetch([(x_ref, x_out), (dy_ref, dy_out)], out_sem)
    finish()
    for h in range(2):
        parts = [al[t].astype(f32)[h * 40 : (h + 1) * 40] for t in range(4)]
        ao_ref[h] = jnp.concatenate(parts, axis=0).astype(low)
    for k in range(2):
        parts = [sl[t].astype(f32) for t in (2 * k, 2 * k + 1)]
        parts = [jnp.concatenate([v[:40], v[40:, : PACKED - 2 * FEED]], axis=1) for v in parts]
        so_ref[pl.ds(k * 80, 80)] = jnp.concatenate(parts, axis=0).astype(low)
    last = fetch([(ao_ref, ao_out), (so_ref, so_out)], out_sem.at[pl.ds(2, 2)])
    for put in (*early, *puts, *last):
        put.wait()


def group_exchange(weights, gains, tokens, cotangent, order, cid):
    low, dma = jnp.bfloat16, pltpu.SemaphoreType.DMA
    vmem = pl.BlockSpec(memory_space=pltpu.VMEM)
    shapes = [
        jax.ShapeDtypeStruct((2, 160, ATTN), low),
        jax.ShapeDtypeStruct((4, 16, 128), low),
        jax.ShapeDtypeStruct((160, PACKED), low),
        jax.ShapeDtypeStruct((4, 80, FEED), low),
        jax.ShapeDtypeStruct(tokens.shape, jnp.float32),
        jax.ShapeDtypeStruct(cotangent.shape, low),
    ]
    attn, second = (jax.ShapeDtypeStruct((4, 80, n), low) for n in (ATTN, 2 * FEED))
    return pl.pallas_call(
        exchange_kernel,
        out_shape=shapes,
        in_specs=[vmem] * 10,
        out_specs=[HBM] * 6,
        scratch_shapes=[
            *buffers(attn, shapes[1], second, shapes[3], attn, second),
            *buffers(shapes[0], shapes[2], *shapes[4:]),
            dma((3,)),
            dma((9,)),
            dma((9,)),
            dma((5,)),
        ],
        compiler_params=pltpu.CompilerParams(
            collective_id=cid, has_side_effects=True, vmem_limit_bytes=54 * 2**20
        ),
    )(*weights, gains, tokens, cotangent, order)


def shift(i, by):
    return lax.rem(i + by, 4)


def around(h, y, x):
    if h == 0:
        return x, ring_of("x", x), y, ring_of("y", y)
    return y, ring_of("y", y), x, ring_of("x", x)


class Piece:
    def __init__(self, h, source, target, columns, rows=160):
        self.h, self.source, self.target, self.columns, self.rows = h, source, target, columns, rows

    def own(self):
        return self.source

    def at(self, i1, i2, part=None):
        row, column = (i2, i1) if self.h == 0 else (i1, i2)
        size = self.rows if part is None else self.rows // 2
        first = (row * 4 + column) * self.rows + (0 if part is None else part * size)
        return self.target.at[pl.ds(pl.multiple_of(first, 16), size), self.columns]


def gather_steps(y, x, pieces, send, recv, cross):
    started = []

    def go(src, dst, n, ring, slot, peer):
        k = (n * 5 + ring) * 4 + slot
        copy = remote(src, dst, send.at[k], recv.at[k], peer)
        copy.start()
        started.append(copy)

    def arrived(dst, n, ring, slot):
        k = (n * 5 + ring) * 4 + slot
        remote(dst, dst, send.at[k], recv.at[k], {"c": 1 - lax.axis_index("c")}).wait_recv()

    each = [(n, p, *around(p.h, y, x)) for n, p in enumerate(pieces)]
    firsts = ((1, 0), (2, 3), (3, 1), (4, 2))

    def own_blocks():
        for n, p, i1, (back1, ahead1), i2, _ in each:
            go(p.own(), p.at(i1, i2), n, 0, 0, ahead1)
            go(p.own(), p.at(i1, i2), n, 0, 1, back1)
        for n, p, i1, _, i2, (back2, ahead2) in each:
            go(p.own(), p.at(i1, i2), n, 1, 0, ahead2)
            go(p.own(), p.at(i1, i2), n, 1, 1, back2)
            cross(n, p.own(), p.at(i1, i2), None)

    def first_axis():
        for n, p, i1, (back1, ahead1), i2, (back2, ahead2) in each:
            left, right = p.at(shift(i1, 3), i2), p.at(shift(i1, 1), i2)
            arrived(left, n, 0, 0)
            low = p.at(shift(i1, 3), i2, 0)
            go(low, low, n, 0, 2, ahead1)
            arrived(right, n, 0, 1)
            high = p.at(shift(i1, 1), i2, 1)
            go(high, high, n, 0, 3, back1)
            for ring, ref in ((2, left), (3, right)):
                go(ref, ref, n, ring, 0, ahead2)
                go(ref, ref, n, ring, 1, back2)
                cross(n, ref, ref, (shift(i1, 3 if ring == 2 else 1), i2))
        for n, p, i1, _, i2, (back2, ahead2) in each:
            far = shift(i1, 2)
            arrived(p.at(far, i2, 0), n, 0, 2)
            arrived(p.at(far, i2, 1), n, 0, 3)
            ref = p.at(far, i2)
            go(ref, ref, n, 4, 0, ahead2)
            go(ref, ref, n, 4, 1, back2)
            cross(n, ref, ref, (far, i2))

    def second_axis():
        for ring, by in firsts:
            for n, p, i1, _, i2, (back2, ahead2) in each:
                j = shift(i1, by)
                left, right = p.at(j, shift(i2, 3)), p.at(j, shift(i2, 1))
                arrived(left, n, ring, 0)
                low = p.at(j, shift(i2, 3), 0)
                go(low, low, n, ring, 2, ahead2)
                cross(n, left, left, (j, shift(i2, 3)))
                arrived(right, n, ring, 1)
                high = p.at(j, shift(i2, 1), 1)
                go(high, high, n, ring, 3, back2)
                cross(n, right, right, (j, shift(i2, 1)))

    def last():
        for ring, by in firsts:
            for n, p, i1, _, i2, _ in each:
                j, far = shift(i1, by), shift(i2, 2)
                arrived(p.at(j, far, 0), n, ring, 2)
                arrived(p.at(j, far, 1), n, ring, 3)
                cross(n, p.at(j, far), p.at(j, far), (j, far))

    def finish():
        for copy in started:
            copy.wait_send()

    return own_blocks, first_axis, second_axis, last, finish


def attention_gather_kernel(
    in_hbm, g_hbm, dy_hbm, d_hbm, a_ref, o_ref, go_ref, all_ref, do_out,
    in_ref, g_ref, dy_ref, d_ref, in_sem, dl, do_ref, do_sem, here, send, recv, csend, crecv, zsend, zrecv, dsend, drecv, xhere, xsend, xrecv,
):
    y, x, c = lax.axis_index("y"), lax.axis_index("x"), lax.axis_index("c")
    zl, zh = lax.axis_index("zl"), lax.axis_index("zh")
    core = {"c": 1 - c}
    gets = fetch([(in_hbm, in_ref), (g_hbm, g_ref), (dy_hbm, dy_ref), (d_hbm, d_ref)], in_sem)
    chips = [{"zl": 1 - zl, "zh": k} for k in range(2)]
    greet([*ring_of("x", x), *ring_of("y", y), core, *chips, {"zl": 1 - zl, "c": 1 - c}])
    whole = pl.ds(0, 160)
    for get in gets:
        get.wait()

    chip = {"zl": 1 - zl}
    for side in range(2):

        @pl.when(c == side)
        def _(side=side):
            if side == 0:
                starts = [(a_ref, 512), (a_ref, 1024), (a_ref, 0), (a_ref, 256), (a_ref, 768)]
            else:
                starts = [(o_ref, 256), (o_ref, 768), (a_ref, 1536), (o_ref, 0), (o_ref, 512)]
            segments = ((0, 512, 128, True), (1, 256, 256, True), (0, 0, 256, False), (0, 256, 256, False), (1, 0, 256, False))
            pieces, others = [], {}
            for n, ((h, source, width, shared), (ref, first)) in enumerate(zip(segments, starts)):
                for part in range(2 if shared else 1):
                    off = pl.multiple_of((zl if part == 0 else 1 - zl) * width, 128) if shared else 0
                    piece = Piece(
                        h, in_ref.at[h, whole, pl.ds(source + off, width)], ref, pl.ds(first + off, width)
                    )
                    if part == 0:
                        pieces.append(piece)
                    else:
                        others[n] = piece
            pieces.append(Piece(0, g_ref, go_ref, pl.ds(0, 128), 64))
            crossed, passed_on, drained = [], [], []

            def to_core(src, dst):
                k = len(crossed)
                copy = remote(src, dst, csend.at[k], crecv.at[k], core)
                copy.start()
                crossed.append(copy)

            def cross(n, src, dst, place):
                if n < 5:
                    to_core(src, dst)
                if n in others and place is not None:
                    k = len(passed_on)
                    copy = remote(dst, dst, zsend.at[k], zrecv.at[k], chip)
                    copy.start()
                    passed_on.append((copy, others[n].at(*place)))

            def drain(count):
                for k in range(len(drained), count):
                    ref = passed_on[k][1]
                    remote(ref, ref, zsend.at[k], zrecv.at[k], chip).wait_recv()
                    to_core(ref, ref)
                    drained.append(k)

            own_blocks, first_axis, second_axis, last, sent = gather_steps(y, x, pieces, send, recv, cross)
            own_blocks()
            keeps = []
            for n, p in enumerate([*pieces, *others.values()]):
                i1, _, i2, _ = around(p.h, y, x)
                keeps.append(pltpu.make_async_copy(p.own(), p.at(i1, i2), here.at[n]))
                keeps[-1].start()
                if n >= len(pieces):
                    to_core(p.own(), p.at(i1, i2))
            finish = send_blocks([d_ref], [dl], xhere, xsend, xrecv)
            half = dy_ref.shape[0] // 2
            mine, other = zl * 2 + c, (1 - zl) * 2 + c
            part = pl.ds(pl.multiple_of(zh * half, half), half)
            away = [
                remote(dy_ref.at[part], all_ref.at[mine, part], dsend.at[k], drecv.at[zh], chips[k])
                for k in range(2)
            ]
            across = remote(dy_ref, all_ref.at[mine], dsend.at[2], drecv.at[2], core)
            for copy in (*away, across):
                copy.start()
            keeps.append(pltpu.make_async_copy(dy_ref, all_ref.at[mine], here.at[8]))
            keeps[-1].start()
            first_axis()
            finish()
            for h in range(2):
                parts = [dl[t].astype(jnp.float32)[h * 40 : (h + 1) * 40] for t in range(4)]
                do_ref[h] = jnp.concatenate(parts, axis=0).astype(jnp.bfloat16)
            puts = fetch([(do_ref, do_out)], do_sem)
            second_axis()
            drain(6)
            passed = []
            for k in range(2):
                rows = pl.ds(k * half, half)
                there = all_ref.at[other, rows]
                remote(dy_ref.at[rows], there, dsend.at[k], drecv.at[k], chips[k]).wait_recv()
                passed.append(remote(there, there, dsend.at[3 + k], drecv.at[3 + k], core))
                passed[-1].start()
            last()
            drain(30)
            sent()
            for copy, _ in passed_on:
                copy.wait_send()
            for copy in (*crossed, *passed, across):
                copy.wait()
            for copy in away:
                copy.wait_send()
            for keep in (*keeps, *puts):
                keep.wait()


def attention_gather(own, gains, dy, down, cid):
    kind, dma = jnp.bfloat16, pltpu.SemaphoreType.DMA
    return pl.pallas_call(
        attention_gather_kernel,
        out_shape=[
            jax.ShapeDtypeStruct((2560, 1792), kind),
            jax.ShapeDtypeStruct((2560, 1280), kind),
            jax.ShapeDtypeStruct((1024, 128), kind),
            jax.ShapeDtypeStruct((4, *dy.shape), kind),
            jax.ShapeDtypeStruct((2, 160, down.shape[2]), kind),
        ],
        in_specs=[HBM] * 4,
        out_specs=[HBM] * 5,
        scratch_shapes=[
            *buffers(own, gains, dy, down),
            dma((4,)),
            pltpu.VMEM(down.shape, kind),
            pltpu.VMEM((2, 160, down.shape[2]), kind),
            dma((1,)),
            dma((9,)),
            dma((120,)),
            dma((120,)),
            dma((112,)),
            dma((112,)),
            dma((30,)),
            dma((30,)),
            dma((5,)),
            dma((5,)),
            dma((1,)),
            dma((3,)),
            dma((3,)),
        ],
        compiler_params=pltpu.CompilerParams(collective_id=cid, has_side_effects=True),
    )(own, gains, dy, down)


def middle_kernel(
    x_in, g_in, cos_ref, sin_ref, wq_ref, wo_ref, d_in,
    mid_out, all_out, w_ref, xn_out, mixed_out, q_out, kv_out, soft_out, rows_out,
    x_ref, g_ref, d_ref, mid_ref, all_ref, xn_ref, mixed_ref, q_ref, kv_ref, soft_ref, rows_ref, in_sem, out_sem,
    wq, wo, p_ref, landed, here, wsem, psend, precv, gsend, grecv, send, recv, csend, crecv,
):
    y, x, c = lax.axis_index("y"), lax.axis_index("x"), lax.axis_index("c")
    zl, zh = lax.axis_index("zl"), lax.axis_index("zh")
    core, far = {"c": 1 - c}, {"zh": 1 - zh}
    chips = [{"zl": 1 - zl, "zh": k} for k in range(2)]
    f32, low = jnp.float32, jnp.bfloat16
    heads = soft_ref.shape[0]
    *gets, get_d = fetch([(x_in, x_ref), (g_in, g_ref), (d_in, d_ref)], in_sem)
    loads = []
    for k in range(heads + 2):
        columns = pl.ds(k * HEAD_DIM, HEAD_DIM)
        loads.append(pltpu.make_async_copy(wq_ref.at[:, columns], wq.at[:, columns], wsem.at[k]))
    for k in range(5):
        some = pl.ds(k * 512, 512)
        loads.append(pltpu.make_async_copy(wo_ref.at[some], wo.at[some], wsem.at[heads + 2 + k]))
    for k in (heads, heads + 1, *range(heads), *range(heads + 2, heads + 7)):
        loads[k].start()
    greet([*ring_of("x", x), *ring_of("y", y), core, far, *chips])
    pieces = [
        Piece(h, d_ref.at[h, pl.ds(0, 160)], w_ref, pl.ds(h * FEED, FEED)) for h in range(2)
    ]
    own_blocks, first_axis, second_axis, last, sent = gather_steps(
        y, x, pieces, send, recv, lambda n, src, dst, place: None
    )
    get_d.wait()
    own_blocks()
    keeps = []
    for n, p in enumerate(pieces):
        i1, _, i2, _ = around(p.h, y, x)
        keeps.append(pltpu.make_async_copy(p.own(), p.at(i1, i2), here.at[n]))
        keeps[-1].start()
    half, step = x_ref.shape[0] // 2, 16
    for get in gets:
        get.wait()
    tiles = [g_ref[k * 16 : (k + 1) * 16].astype(f32)[:8, :40] for k in range(64)]
    rows_ref[...] = jnp.concatenate(tiles, axis=1)

    @pl.loop(0, 2 * half // step)
    def _(i):
        at = pl.ds(pl.multiple_of(i * step, step), step)
        v = x_ref[at]
        r = lax.rsqrt(jnp.mean(v * v, axis=-1, keepdims=True) + norm_eps)
        xn_ref[c, at] = (v * r * rows_ref[0:1]).astype(low)

    shared = [remote(xn_ref.at[c], xn_ref.at[c], csend.at[0], crecv.at[0], core)]
    shared[0].start()

    def projected(k):
        loads[k].wait()
        return jnp.dot(xn_ref[c], wq[:, k * HEAD_DIM : (k + 1) * HEAD_DIM], preferred_element_type=f32)

    def rotated(u):
        turn = u[:, :ROT]
        turn = turn * cos_ref[...] + pltpu.roll(turn, ROT // 2, 1) * sin_ref[...]
        return jnp.concatenate([turn, u[:, ROT:]], axis=1).astype(low)

    kv_ref[:, :HEAD_DIM] = rotated(projected(heads))
    kv_ref[:, HEAD_DIM:] = projected(heads + 1).astype(low)
    rows = lax.broadcasted_iota(jnp.int32, (SEQ_LEN, SEQ_LEN), 0)
    behind = rows - lax.broadcasted_iota(jnp.int32, (SEQ_LEN, SEQ_LEN), 1)
    keep_mask = (behind >= 0) & (behind < WINDOW)
    for h in range(heads):
        columns = pl.ds(h * HEAD_DIM, HEAD_DIM)
        q = rotated(projected(h))
        q_ref[:, columns] = q
        scores = lax.dot_general(
            q, kv_ref[:, :HEAD_DIM], (((1,), (1,)), ((), ())), preferred_element_type=f32
        )
        scores = jnp.where(keep_mask, scores * HEAD_DIM**-0.5, -1e30)
        top = jnp.max(scores, axis=-1, keepdims=True)
        total = top + jnp.log(jnp.sum(jnp.exp(scores - top), axis=-1, keepdims=True))
        soft = jnp.exp(scores - total)
        soft_ref[h] = soft
        mixed_ref[c, :, columns] = jnp.dot(
            soft.astype(low), kv_ref[:, HEAD_DIM:], preferred_element_type=f32
        ).astype(low)
    shared.append(remote(mixed_ref.at[c], mixed_ref.at[c], csend.at[1], crecv.at[1], core))
    shared[1].start()
    puts = fetch([(q_ref, q_out), (kv_ref, kv_out), (soft_ref, soft_out), (rows_ref, rows_out)], out_sem)
    mine, other = zl * 2 + c, (1 - zl) * 2 + c
    parts = [pl.ds(pl.multiple_of(k * half, half), half) for k in (1 - zh, zh)]
    chunks = [pl.ds(k * 512, 512) for k in range(5)]
    pair = [
        [
            remote(p_ref.at[part, some], landed.at[part, some], psend.at[5 * k + n], precv.at[5 * k + n], far)
            for n, some in enumerate(chunks)
        ]
        for k, part in enumerate(parts)
    ]
    for n, some in enumerate(chunks):
        loads[heads + 2 + n].wait()
        p_ref[:, some] = lax.dot_general(
            mixed_ref[c], wo[some], (((1,), (1,)), ((), ())), preferred_element_type=f32
        ).astype(low)
        pair[0][n].start()
    for copy in pair[1]:
        copy.start()
    first_axis()
    away, across = [], []
    for k in range(2):
        part = parts[1 - k]
        for copy in pair[k]:
            copy.wait_recv()
        first = (zh if k == 0 else 1 - zh) * half

        @pl.loop(0, half // step)
        def _(i, first=first):
            at = pl.ds(pl.multiple_of(first + i * step, step), step)
            branch = p_ref[at].astype(f32) + landed[at].astype(f32)
            v = x_ref[at] + branch
            mid_ref[at] = v
            r = lax.rsqrt(jnp.mean(v * v, axis=-1, keepdims=True) + norm_eps)
            all_ref[mine, at] = (v * r * rows_ref[1:2]).astype(low)

        ready = all_ref.at[mine, part]
        if k == 0:
            for i in range(2):
                away.append(remote(ready, ready, gsend.at[i], grecv.at[zh], chips[i]))
                away[-1].start()
        across.append(remote(ready, ready, gsend.at[2 + k], grecv.at[2 + k], core))
        across[-1].start()
        if k == 0:
            second_axis()
    passed = []
    for k in range(2):
        there = all_ref.at[other, pl.ds(k * half, half)]
        remote(there, there, gsend.at[k], grecv.at[k], chips[k]).wait_recv()
        passed.append(remote(there, there, gsend.at[4 + k], grecv.at[4 + k], core))
        passed[-1].start()
    last()
    sent()
    for copy in (*across, *passed, *shared):
        copy.wait()
    puts += fetch(
        [(mid_ref, mid_out), (all_ref, all_out), (xn_ref, xn_out), (mixed_ref, mixed_out)],
        out_sem.at[pl.ds(4, 4)],
    )
    for copy in (*away, *pair[0], *pair[1]):
        copy.wait_send()
    for keep in (*keeps, *puts):
        keep.wait()


def middle(x, gains, cosine, sine, w_q_kv, w_out_t, down, cid):
    dma, f32, low = pltpu.SemaphoreType.DMA, jnp.float32, jnp.bfloat16
    vmem = pl.BlockSpec(memory_space=pltpu.VMEM)
    rows, width = x.shape
    wide = w_out_t.shape[1]
    heads = wide // HEAD_DIM
    shapes = [
        jax.ShapeDtypeStruct(x.shape, f32),
        jax.ShapeDtypeStruct((4, *x.shape), low),
        jax.ShapeDtypeStruct((2560, 2 * FEED), low),
        jax.ShapeDtypeStruct((2, rows, width), low),
        jax.ShapeDtypeStruct((2, rows, wide), low),
        jax.ShapeDtypeStruct((rows, wide), low),
        jax.ShapeDtypeStruct((rows, 2 * HEAD_DIM), low),
        jax.ShapeDtypeStruct((heads, rows, rows), f32),
        jax.ShapeDtypeStruct((8, width), f32),
    ]
    return pl.pallas_call(
        middle_kernel,
        out_shape=shapes,
        in_specs=[HBM] * 2 + [vmem] * 2 + [HBM] * 3,
        out_specs=[HBM] * 9,
        scratch_shapes=[
            *buffers(x, gains, down, *shapes[:2], *shapes[3:]),
            dma((3,)),
            dma((8,)),
            pltpu.VMEM(w_q_kv.shape, low),
            pltpu.VMEM(w_out_t.shape, low),
            pltpu.VMEM(x.shape, low),
            pltpu.VMEM(x.shape, low),
            dma((2,)),
            dma((heads + 7,)),
            dma((10,)),
            dma((10,)),
            dma((6,)),
            dma((6,)),
            dma((40,)),
            dma((40,)),
            dma((2,)),
            dma((2,)),
        ],
        compiler_params=pltpu.CompilerParams(
            collective_id=cid, has_side_effects=True, vmem_limit_bytes=60 * 2**20
        ),
    )(x, gains, cosine, sine, w_q_kv, w_out_t, down)


def finish_kernel(s_in, o_ref, s_ref, in_sem, blocks, here, send, recv):
    get = fetch([(s_in, s_ref)], in_sem)[0]
    greet(group_peers())
    get.wait()
    wide = blocks.shape[2]
    for t in range(4):
        first = t * 40 // 16 * 16
        size = (t * 40 + 40 + 15) // 16 * 16 - first
        v = s_ref[pl.ds(first, size)].astype(jnp.float32)[t * 40 - first : t * 40 - first + 40]
        rest = jnp.concatenate([v[:, wide:], jnp.zeros((40, 2 * wide - v.shape[1]), jnp.float32)], axis=1)
        blocks[t] = jnp.concatenate([v[:, :wide], rest], axis=0).astype(jnp.bfloat16)
    send_blocks([blocks], [o_ref], here, send, recv)()


def finish(sent, cid):
    dma = pltpu.SemaphoreType.DMA
    buffer = jax.ShapeDtypeStruct((4, 80, 3 * FEED), sent.dtype)
    return pl.pallas_call(
        finish_kernel,
        out_shape=buffer,
        in_specs=[HBM],
        out_specs=HBM,
        scratch_shapes=[*buffers(sent), dma((1,)), *buffers(buffer), dma((1,)), dma((3,)), dma((3,))],
        compiler_params=pltpu.CompilerParams(
            collective_id=cid, has_side_effects=True, vmem_limit_bytes=60 * 2**20
        ),
    )(sent)


def write_kernel(
    l_in, block_in, grad_in, q_in, kv_in, o_in, g_in,
    block, grad, q, kv, o, g, down_ref, gate_ref, up_ref,
    landed, b1, b2, b3, b4, b5, b6, sem, load_sem,
):
    held = (b1, b2, b3, b4, b5, b6)
    get, *gets = fetch(list(zip((l_in, block_in, grad_in, q_in, kv_in, o_in, g_in), (landed, *held))), load_sem)
    for one in gets:
        one.wait()
    copies = fetch(list(zip(held, (block, grad, q, kv, o, g))), sem)
    get.wait()
    for t in range(4):
        v = landed[t].astype(jnp.float32)
        v = jnp.concatenate([v[:40], v[40:]], axis=1)
        first, tail = t * 960, t * 960 + MAIN
        gate_ref[:, first:tail] = v[:, :MAIN]
        gate_ref[:, tail : tail + 64] = v[:, 2 * MAIN : 2 * MAIN + 64]
        up_ref[:, first:tail] = v[:, MAIN : 2 * MAIN]
        up_ref[:, tail : tail + 64] = v[:, 2 * MAIN + 64 : PACKED]
        down_ref[:, first : first + 960] = v[:, PACKED : PACKED + 960]
    for copy in copies:
        copy.wait()


def written(landed, arrays):
    dma = pltpu.SemaphoreType.DMA
    vmem = pl.BlockSpec(memory_space=pltpu.VMEM)
    return pl.pallas_call(
        write_kernel,
        out_shape=[
            *(jax.ShapeDtypeStruct(a.shape, a.dtype) for a in arrays),
            *[jax.ShapeDtypeStruct((40, 3840), jnp.float32)] * 3,
        ],
        in_specs=[HBM] * 7,
        out_specs=[HBM] * 6 + [vmem] * 3,
        scratch_shapes=[*buffers(landed, *arrays), dma((6,)), dma((7,))],
        compiler_params=pltpu.CompilerParams(vmem_limit_bytes=56 * 2**20),
    )(landed, *arrays)


class SumPiece:
    def __init__(self, h, sums, columns, via, main, sems, rows=160):
        self.h, self.sums, self.columns, self.via, self.main, self.sems, self.rows = (
            h, sums, columns, via, main, sems, rows,
        )

    def first(self, i1, i2, part=0):
        row, column = (i2, i1) if self.h == 0 else (i1, i2)
        return (row * 4 + column) * self.rows + part * (self.rows // 2)

    def at(self, i1, i2, part=None):
        size = self.rows if part is None else self.rows // 2
        return self.sums.at[pl.ds(pl.multiple_of(self.first(i1, i2, part or 0), 16), size), self.columns]


ORDER = (
    "P0", "yv0", "xv0", "yv2", "P1", "P2", "xv2", "Tc", "gv0", "gv1", "gv2", "gv3", "xm0", "T0",
    "yv1", "gm0", "gm1", "gm2", "gm3", "xv1", "ym0", "P3", "ym2", "xv3", "xm1", "xt0", "yv3", "xm2",
    "ym1", "yt2", "gt0", "gt1", "gt2", "gt3", "gv4", "gm4", "yt0", "xt1", "xm3", "gt4", "ym3",
    "xv4", "yv4", "T1", "xt2", "Tg", "yt1", "xm4", "ym4", "To", "yt3", "xt3", "yt4", "xt4",
)


def plane_sum_kernel(
    left_in, dq_ref, dl_ref, right_in, gi_ref, p_in, t_in, x_in, mid_in, dmid_in, g_in, order_in,
    q_out, kv_out, wo_out, go_ref, block_ref, grad_ref,
    left, right_o, p_ref, t_ref, x_ref, mid_ref, dmid_ref, g_ref, order_ref, attn_ref, in_sem,
    right, left_o, sums, via, main, gsums, gvia, gmain, from_chip, attn_low, gfar, gsum, gall,
    t_core, t_other, t_chips, t_own, t_far, landed, block_low, grad_low,
    here, csend, crecv, send, recv, esend, erecv, tsend, trecv, shere, ssend, srecv,
):
    y, x, c, zl, zh = (lax.axis_index(k) for k in ("y", "x", "c", "zl", "zh"))
    core, chip, far_peer = {"c": 1 - c}, {"zl": 1 - zl}, {"zh": 1 - zh}
    chips = [{"zl": 1 - zl, "zh": k} for k in range(2)]
    get_p, get_t, get_left, get_right, *gets = fetch(
        [
            (p_in, p_ref), (t_in, t_ref), (left_in, left), (right_in, right_o), (x_in, x_ref),
            (mid_in, mid_ref), (dmid_in, dmid_ref), (g_in, g_ref), (order_in, order_ref),
        ],
        in_sem,
    )
    greet(
        [*ring_of("x", x), *ring_of("y", y), core, *chips, far_peer, {"zl": 1 - zl, "c": 1 - c}]
    )
    step = 16
    f32, low = jnp.float32, jnp.bfloat16
    order = (2, 1, 3, 0)
    tokens = p_ref.shape[1]
    half = tokens // 2

    inputs = [(dq_ref, right), (dl_ref, left_o)]
    mine = pl.ds(pl.multiple_of(c * tokens, tokens), tokens)
    shared = [
        remote(src, dst.at[mine], csend.at[k], crecv.at[k], core) for k, (src, dst) in enumerate(inputs)
    ]
    kept = [pltpu.make_async_copy(src, dst.at[mine], here.at[k]) for k, (src, dst) in enumerate(inputs)]
    kept.append(pltpu.make_async_copy(gi_ref, gsums, here.at[2]))
    for copy in (*shared, *kept):
        copy.start()
    t_cores = [
        remote(p_ref.at[z * 2 + 1 - c], t_core.at[i], tsend.at[i], trecv.at[i], core)
        for i, z in enumerate((1 - zl, zl))
    ]
    get_p.wait()
    for copy in t_cores:
        copy.start()
    get_t.wait()
    pair = remote(t_ref, landed, tsend.at[6], trecv.at[6], far_peer)
    pair.start()
    t_sent = []

    def tokens_to_chips():
        t_cores[0].wait_recv()

        @pl.loop(0, tokens // step)
        def _(i):
            at = pl.ds(pl.multiple_of(i * step, step), step)
            total = p_ref[(1 - zl) * 2 + c, at].astype(f32) + t_core[0, at].astype(f32)
            t_other[at] = total.astype(low)

        for k in range(2):
            t_sent.append(
                remote(t_other.at[pl.ds(k * half, half)], t_chips.at[zh], tsend.at[2 + k], trecv.at[2 + zh], chips[k])
            )
            t_sent[-1].start()

    def tokens_to_far(k):
        piece = (1 - zh) if k == 0 else zh
        if k == 0:
            t_cores[1].wait_recv()
        else:
            for i in range(2):
                remote(
                    t_other.at[pl.ds(0, half)], t_chips.at[i], tsend.at[2 + i], trecv.at[2 + i], chips[i]
                ).wait_recv()

        @pl.loop(0, half // step)
        def _(i):
            at = pl.ds(pl.multiple_of(piece * half + i * step, step), step)
            total = p_ref[zl * 2 + c, at].astype(f32) + t_core[1, at].astype(f32)
            if k == 1:
                there = pl.ds(pl.multiple_of(i * step, step), step)
                total += t_chips[0, there].astype(f32) + t_chips[1, there].astype(f32)
            t_own[at] = total.astype(low)

        at = pl.ds(pl.multiple_of(piece * half, half), half)
        t_sent.append(remote(t_own.at[at], t_far.at[at], tsend.at[4 + k], trecv.at[4 + k], far_peer))
        t_sent[-1].start()

    def tokens_gradient():
        pair.wait_recv()

        @pl.loop(0, tokens // step)
        def _(i):
            at = pl.ds(pl.multiple_of(i * step, step), step)
            d = (t_ref[at].astype(f32) + landed[at].astype(f32)) * g_ref[0:1]
            v = x_ref[at]
            r = lax.rsqrt(jnp.mean(v * v, axis=-1, keepdims=True) + norm_eps)
            n = v * r
            d = r * (d - n * jnp.mean(d * n, axis=-1, keepdims=True))
            grad_low[at] = (dmid_ref[at] + d).astype(low)

        reorder(grad_low, order_ref, grad_ref, True)

    def tokens_output():
        for k in range(2):
            t_sent[2 + k].wait_recv()

        @pl.loop(0, tokens // step)
        def _(i):
            at = pl.ds(pl.multiple_of(i * step, step), step)
            branch = t_own[at].astype(f32) + t_far[at].astype(f32)
            block_low[at] = (mid_ref[at] + branch).astype(low)

        reorder(block_low, order_ref, block_ref, True)

    def products(q):
        top = shift(y, order[q]) * 640
        for side in range(2):

            @pl.when(c == side)
            def _(side=side):
                if side == 0:
                    parts = [(left, right, 0, 0, 768), (left, right, 768, 768, 768)]
                else:
                    parts = [
                        (left, right, 1536, 0, 256),
                        (left_o, right_o, 0, 256, 512),
                        (left_o, right_o, 512, 768, 768),
                    ]

                @pl.loop(0, 5)
                def _(i):
                    at = pl.ds(pl.multiple_of(top + i * 128, 128), 128)
                    for lhs, rhs, source, target, width in parts:
                        sums[at, pl.ds(target, width)] = lax.dot_general(
                            lhs[:, at],
                            rhs[:, pl.ds(source, width)],
                            (((0,), (0,)), ((), ())),
                            preferred_element_type=f32,
                        ).astype(low)

    pieces = [
        SumPiece(h, sums, pl.ds(h * ATTN, ATTN), via.at[h], main.at[h], h * 20) for h in range(2)
    ]
    pieces.append(SumPiece(0, gsums, pl.ds(0, 128), gvia, gmain, 40, 64))

    def add(p, first, size, terms):
        @pl.loop(0, size // step)
        def _(i):
            at = pl.ds(pl.multiple_of(first + i * step, step), step)
            total = p.sums[at, p.columns].astype(f32)
            for ref, index, start in terms:
                total += ref[(*index, pl.ds(pl.multiple_of(start + i * step, step), step))].astype(f32)
            p.sums[at, p.columns] = total.astype(low)

    started = []

    def go(p, ring, slot, src, dst, peer):
        k = p.sems + ring * 4 + slot
        copy = remote(src, dst, send.at[k], recv.at[k], peer)
        copy.start()
        started.append(copy)

    def arrived(p, ring, slot, dst):
        k = p.sems + ring * 4 + slot
        remote(dst, dst, send.at[k], recv.at[k], core).wait_recv()

    def line(p, j):
        i1, peers1, i2, peers2 = around(p.h, y, x)
        if j == 4:
            return lambda k: (k, i2), i1, peers1
        fixed = shift(i1, order[j])
        return lambda k: (fixed, k), i2, peers2

    def out_via(p, ring):
        place, at, (back, ahead) = line(p, ring)
        far = place(shift(at, 2))
        go(p, ring, 0, p.at(*far, 0), p.via.at[ring, 0], ahead)
        go(p, ring, 1, p.at(*far, 1), p.via.at[ring, 1], back)

    def out_main(p, ring):
        place, at, (back, ahead) = line(p, ring)
        small = p.rows // 2
        arrived(p, ring, 0, p.via.at[ring, 0])
        add(p, p.first(*place(shift(at, 1)), 0), small, [(p.via, (ring, 0), 0)])
        go(p, ring, 2, p.at(*place(shift(at, 1))), p.main.at[ring, 0], ahead)
        arrived(p, ring, 1, p.via.at[ring, 1])
        add(p, p.first(*place(shift(at, 3)), 1), small, [(p.via, (ring, 1), 0)])
        go(p, ring, 3, p.at(*place(shift(at, 3))), p.main.at[ring, 1], back)

    def take(p, ring):
        place, at, _ = line(p, ring)
        arrived(p, ring, 2, p.main.at[ring, 0])
        arrived(p, ring, 3, p.main.at[ring, 1])
        add(p, p.first(*place(at)), p.rows, [(p.main, (ring, 0), 0), (p.main, (ring, 1), 0)])

    y_first, x_first, gain = pieces
    for copy in kept:
        copy.wait()
    for copy in shared:
        copy.wait_recv()
    for get in (get_left, get_right, *gets):
        get.wait()
    named = {"x": x_first, "y": y_first, "g": gain}
    acts = {"v": out_via, "m": out_main, "t": take}
    token_acts = {
        "Tc": tokens_to_chips,
        "T0": lambda: tokens_to_far(0),
        "T1": lambda: tokens_to_far(1),
        "Tg": tokens_gradient,
        "To": tokens_output,
    }
    for word in ORDER:
        if word[0] == "P":
            products(int(word[1]))
        elif word[0] == "T":
            token_acts[word]()
        else:
            for name in word[:-2]:
                acts[word[-2]](named[name], int(word[-1]))
    home = (y * 4 + x) * 160
    ghome = pl.ds(pl.multiple_of((y * 4 + x) * 64, 16), 64)
    theirs = pl.ds(pl.multiple_of(home + (1 - zl) * 80, 16), 80)
    across = remote(gsums.at[ghome], gfar, esend.at[0], erecv.at[0], far_peer)
    across.start()
    away = remote(sums.at[theirs], from_chip, esend.at[1], erecv.at[1], chip)
    away.start()
    across.wait()
    both = gsums[ghome].astype(f32) + gfar[...].astype(f32)
    for t in range(4):
        gsum[t] = both[t * 16 : (t + 1) * 16].astype(low)
    finish_gains = send_blocks([gsum], [gall], shere, ssend, srecv)
    away.wait()

    @pl.loop(0, 80 // step)
    def _(i):
        here_at = pl.ds(pl.multiple_of(home + zl * 80 + i * step, step), step)
        at = pl.ds(pl.multiple_of(i * step, step), step)
        attn_low[at] = sums[here_at].astype(f32) + from_chip[at].astype(f32)

    ours = pl.ds(pl.multiple_of(c * 40, 8), 40)
    for_core = pl.ds(pl.multiple_of((1 - c) * 40, 8), 40)
    columns = pl.ds(pl.multiple_of(c * 2 * ATTN, 128), 2 * ATTN)
    last = remote(attn_low.at[for_core], attn_ref.at[:, columns], esend.at[2], erecv.at[2], core)
    keep = pltpu.make_async_copy(attn_low.at[ours], attn_ref.at[:, columns], here.at[0])
    last.start()
    keep.start()
    finish_gains()
    go_ref[...] = (
        gall[0].astype(f32) + gall[1].astype(f32) + gall[2].astype(f32) + gall[3].astype(f32)
    )
    last.wait()
    keep.wait()
    first = 0
    for out in (q_out, kv_out, wo_out):
        out[...] = attn_ref[:, first : first + out.shape[1]]
        first += out.shape[1]
    for copy in (*started, *shared, pair, *t_cores, *t_sent):
        copy.wait_send()


def plane_sum(xn, d_q_kv, d_low, mixed, gains, down, d_xn, x, mid, d_mid, gains_row, order, cid):
    low, dma, f32 = jnp.bfloat16, pltpu.SemaphoreType.DMA, jnp.float32
    rows, width = x.shape
    vmem = pl.BlockSpec(memory_space=pltpu.VMEM)
    return pl.pallas_call(
        plane_sum_kernel,
        out_shape=[
            *(jax.ShapeDtypeStruct((40, n), f32) for n in (1280, 512, 1280)),
            jax.ShapeDtypeStruct((16, 128), f32),
            jax.ShapeDtypeStruct(x.shape, low),
            jax.ShapeDtypeStruct(x.shape, low),
        ],
        in_specs=[HBM] * 12,
        out_specs=[vmem] * 6,
        scratch_shapes=[
            *buffers(xn, mixed, down, d_xn, x, mid, d_mid, gains_row, order),
            pltpu.VMEM((40, 4 * ATTN), f32),
            dma((9,)),
            pltpu.VMEM((2 * rows, d_q_kv.shape[1]), low),
            pltpu.VMEM((2 * rows, width), low),
            pltpu.VMEM((2560, 2 * ATTN), low),
            pltpu.VMEM((2, 5, 2, 80, ATTN), low),
            pltpu.VMEM((2, 5, 2, 160, ATTN), low),
            pltpu.VMEM((1024, 128), low),
            pltpu.VMEM((5, 2, 32, 128), low),
            pltpu.VMEM((5, 2, 64, 128), low),
            pltpu.VMEM((80, 2 * ATTN), low),
            pltpu.VMEM((80, 2 * ATTN), f32),
            pltpu.VMEM((64, 128), low),
            pltpu.VMEM((4, 16, 128), low),
            pltpu.VMEM((4, 16, 128), low),
            pltpu.VMEM((2, rows, width), low),
            pltpu.VMEM((rows, width), low),
            pltpu.VMEM((2, rows // 2, width), low),
            pltpu.VMEM((rows, width), low),
            pltpu.VMEM((rows, width), low),
            pltpu.VMEM((rows, width), low),
            pltpu.VMEM((rows, width), low),
            pltpu.VMEM((rows, width), low),
            dma((3,)),
            dma((2,)),
            dma((2,)),
            dma((60,)),
            dma((60,)),
            dma((3,)),
            dma((3,)),
            dma((7,)),
            dma((7,)),
            dma((1,)),
            dma((3,)),
            dma((3,)),
        ],
        compiler_params=pltpu.CompilerParams(
            collective_id=cid, has_side_effects=True, vmem_limit_bytes=60 * 2**20
        ),
    )(xn, d_q_kv, d_low, mixed, gains, down, d_xn, x, mid, d_mid, gains_row, order)


GELU_IN, GELU_CUBE = math.sqrt(2.0 / math.pi), 0.044715


def feed_kernel(
    xn_in, dy_ref, g_ref, d_ref, h_out, dg_out, o_ref,
    xn_ref, h_ref, dg_ref, in_sem, h_sem, dy, wg, wd, dy_turned, xn_turned, back, out, load_sem, out_sem,
):
    f32, low = jnp.float32, jnp.bfloat16
    units, lines = h_ref.shape[1], out.shape[1]
    lanes = lax.broadcasted_iota(jnp.int32, (1, 128), 1)
    get_xn = fetch([(xn_in, xn_ref)], in_sem)[0]
    get_dy = pltpu.make_async_copy(dy_ref, dy, load_sem.at[0])
    get_dy.start()
    loads = []
    for source, target in ((d_ref, wd), (g_ref, wg)):
        for n in range(4):
            some = pl.ds(n * 640, 640)
            loads.append(pltpu.make_async_copy(source.at[some], target.at[some], load_sem.at[1 + len(loads)]))
    for n in range(4):
        loads[n].start()
    get_xn.wait()
    xn_turned[...] = xn_ref[...].T
    get_dy.wait()
    dy_turned[...] = dy[...].T
    for n in range(4):
        loads[n].wait()
    for n in range(4, 8):
        loads[n].start()
    for k in range(units // 256):
        at = pl.ds(k * 256, 256)
        back[:, at] = jnp.dot(dy[...], wd[:, at], preferred_element_type=f32)
    for n in range(4, 8):
        loads[n].wait()
    def act(gate, up, d):
        square = gate * gate
        t = jnp.tanh(GELU_IN * (gate + GELU_CUBE * gate * square))
        cdf = 0.5 * (1.0 + t)
        slope = cdf + 0.5 * gate * (1.0 - t * t) * (GELU_IN * (1.0 + 3.0 * GELU_CUBE * square))
        gelu = gate * cdf
        return gelu * up, d * up * slope, d * gelu

    for first, size in ((0, 256), (256, 256), (512, 256), (768, 128)):
        at, beside = pl.ds(first, size), pl.ds(MAIN + first, size)
        gate = jnp.dot(xn_ref[...], wg[:, at], preferred_element_type=f32)
        up = jnp.dot(xn_ref[...], wg[:, beside], preferred_element_type=f32)
        hidden, d_gate, d_up = act(gate, up, back[:, at])
        h_ref[:, at] = hidden.astype(low)
        dg_ref[:, at] = d_gate.astype(low)
        dg_ref[:, beside] = d_up.astype(low)
    at, both = pl.ds(MAIN, 128), pl.ds(2 * MAIN, 128)
    gate = jnp.dot(xn_ref[...], wg[:, both], preferred_element_type=f32)
    hidden, d_gate, d_up = act(gate, pltpu.roll(gate, 64, 1), back[:, at])
    h_ref[:, at] = jnp.where(lanes < 64, hidden, 0.0).astype(low)
    dg_ref[:, both] = jnp.where(lanes < 64, d_gate, pltpu.roll(d_up, 64, 1)).astype(low)
    puts = fetch([(h_ref, h_out), (dg_ref, dg_out)], h_sem)

    def put(i):
        slot = lax.rem(i, 2)
        rows = pl.ds(pl.multiple_of(i * lines, lines), lines)
        return pltpu.make_async_copy(out.at[slot], o_ref.at[rows], out_sem.at[slot])

    steps = o_ref.shape[0] // lines

    @pl.loop(0, steps)
    def _(i):
        slot = lax.rem(i, 2)
        pl.when(i >= 2)(lambda: put(i - 2).wait())
        rows = pl.ds(pl.multiple_of(i * lines, lines), lines)
        for left, right, first, total in ((xn_turned, dg_ref, 0, PACKED), (dy_turned, h_ref, PACKED, 960)):
            for k in range(0, total, 512):
                size = min(512, right.shape[1] - k)
                kept = min(size, total - k)
                v = jnp.dot(left[rows], right[:, pl.ds(k, size)], preferred_element_type=f32)
                out[slot, :, pl.ds(first + k, kept)] = v[:, :kept].astype(low)
        put(i).start()

    put(steps - 2).wait()
    put(steps - 1).wait()
    for copy in puts:
        copy.wait()


def feed(xn, dy, w_gate_up, w_down):
    depth, width = xn.shape
    units = w_down.shape[1]
    low, dma = jnp.bfloat16, pltpu.SemaphoreType.DMA
    shapes = [
        jax.ShapeDtypeStruct((depth, units), low),
        jax.ShapeDtypeStruct((depth, PACKED), low),
        jax.ShapeDtypeStruct((width, PACKED + 960), low),
    ]
    return pl.pallas_call(
        feed_kernel,
        out_shape=shapes,
        in_specs=[HBM] * 4,
        out_specs=[HBM] * 3,
        scratch_shapes=[
            *buffers(xn, *shapes[:2]),
            dma((1,)),
            dma((2,)),
            pltpu.VMEM((depth, width), low),
            pltpu.VMEM((width, PACKED), low),
            pltpu.VMEM((width, units), low),
            pltpu.VMEM((width, depth), low),
            pltpu.VMEM((width, depth), low),
            pltpu.VMEM((depth, units), jnp.float32),
            pltpu.VMEM((2, 640, PACKED + 960), low),
            dma((9,)),
            dma((2,)),
        ],
        compiler_params=pltpu.CompilerParams(vmem_limit_bytes=60 * 2**20),
        cost_estimate=pl.CostEstimate(
            flops=12 * depth * width * units,
            bytes_accessed=4 * depth * width + 12 * width * units + 6 * depth * units,
            transcendentals=depth * units,
        ),
    )(xn, dy, w_gate_up, w_down)


def back_kernel(
    dg_in, h_in, w_ref, d_ref, wo_ref, wq_ref,
    x_in, mid_in, dy_in, g_in, soft_in, q_in, kv_in, cos_ref, sin_ref,
    down_out, dmid_out, dl_out, dq_out, dx_out, gains_out,
    dg_ref, h_ref, x_ref, mid_ref, dy_ref, g_ref, soft_ref, q_ref, kv_ref,
    down_ref, dmid_ref, dl_ref, dq_ref, dx_ref, gains_ref, in_sem, out_sem,
    w, wd, wo, part, from_core, other, from_chips, own, from_far, grad, kv_part, kv_far, halved, sums,
    wsem, send, recv, osem, qsem, fsend, frecv,
):
    zl, c, zh = lax.axis_index("zl"), lax.axis_index("c"), lax.axis_index("zh")
    core, far = {"c": 1 - c}, {"zh": 1 - zh}
    chips = [{"zl": 1 - zl, "zh": k} for k in range(2)]
    f32, low = jnp.float32, jnp.bfloat16
    parts, width = w_ref.shape[0] // 640, 640
    rows = x_ref.shape[0]
    half, step = rows // 2, 16
    heads = soft_ref.shape[0]
    get_dg = fetch([(dg_in, dg_ref)], in_sem)[0]
    loads = []
    for source, target, first in ((w_ref, w, 0), (d_ref, wd, parts)):
        for n in range(parts):
            some = pl.ds(n * width, width)
            loads.append(pltpu.make_async_copy(source.at[some], target.at[some], wsem.at[first + n]))
    for n in range(2):
        loads[n].start()
    get_wo = pltpu.make_async_copy(wo_ref, wo, osem)
    wq = w.at[:, pl.ds(0, wq_ref.shape[1])]
    get_wq = pltpu.make_async_copy(wq_ref, wq, qsem)
    greet([core, far, *chips])
    order = [1 - zl, zl]
    started = []

    def go(src, dst, n, out_slot, in_slot, peer):
        copy = remote(src, dst, send.at[n * 6 + out_slot], recv.at[n * 6 + in_slot], peer)
        copy.start()
        started.append(copy)

    def arrived(dst, n, slot):
        remote(dst, dst, send.at[n * 6 + slot], recv.at[n * 6 + slot], core).wait_recv()

    def columns(n):
        return pl.ds(n * width, width)

    def product(left, right, n, target):
        some = pl.ds(n * width, width)
        v = lax.dot_general(
            left[...], right[some], (((1,), (1,)), ((), ())), preferred_element_type=f32
        ).astype(low)
        for t in range(4):
            target[t, :, some] = v[t * rows : (t + 1) * rows]

    def multiply(n):
        loads[n].wait()
        product(dg_ref, w, n, part)
        for i, z in enumerate(order):
            go(part.at[z * 2 + 1 - c, :, columns(n)], from_core.at[i, :, columns(n)], n, i, i, core)

    def down(n):
        loads[parts + n].wait()
        product(h_ref, wd, n, down_ref)

    def to_chips(n):
        arrived(from_core.at[0, :, columns(n)], n, 0)

        @pl.loop(0, rows // step)
        def _(i):
            at = pl.ds(pl.multiple_of(i * step, step), step)
            total = part[(1 - zl) * 2 + c, at, columns(n)].astype(f32) + from_core[0, at, columns(n)].astype(f32)
            other[at, columns(n)] = total.astype(low)

        for k in range(2):
            go(other.at[pl.ds(k * half, half), columns(n)], from_chips.at[zh, :, columns(n)], n, 2 + k, 2 + zh, chips[k])

    def to_far(n, k):
        piece = (1 - zh) if k == 0 else zh
        if k == 0:
            arrived(from_core.at[1, :, columns(n)], n, 1)
        else:
            for i in range(2):
                arrived(from_chips.at[i, :, columns(n)], n, 2 + i)

        @pl.loop(0, half // step)
        def _(i):
            at = pl.ds(pl.multiple_of(piece * half + i * step, step), step)
            total = part[zl * 2 + c, at, columns(n)].astype(f32) + from_core[1, at, columns(n)].astype(f32)
            if k == 1:
                there = pl.ds(pl.multiple_of(i * step, step), step)
                total += from_chips[0, there, columns(n)].astype(f32) + from_chips[1, there, columns(n)].astype(f32)
            own[at, columns(n)] = total.astype(low)

        at = pl.ds(pl.multiple_of(piece * half, half), half)
        go(own.at[at, columns(n)], from_far.at[at, columns(n)], n, 4 + k, 4 + k, far)

    def finish(n):
        for k in range(2):
            arrived(from_far.at[pl.ds(k * half, half), columns(n)], n, 4 + k)

        @pl.loop(0, rows // step)
        def _(i):
            at = pl.ds(pl.multiple_of(i * step, step), step)
            grad[at, columns(n)] = own[at, columns(n)].astype(f32) + from_far[at, columns(n)].astype(f32)

    get_dg.wait()
    loads[2].start()
    multiply(0)
    loads[3].start()
    multiply(1)
    get_h, *gets = fetch(
        [
            (h_in, h_ref), (x_in, x_ref), (mid_in, mid_ref), (dy_in, dy_ref),
            (g_in, g_ref), (soft_in, soft_ref), (q_in, q_ref), (kv_in, kv_ref),
        ],
        in_sem.at[pl.ds(1, 8)],
    )
    for n in range(parts, 2 * parts):
        loads[n].start()
    to_chips(0)
    to_far(0, 0)
    multiply(2)
    to_chips(1)
    to_far(1, 0)
    multiply(3)
    get_wo.start()
    get_wq.start()
    to_chips(2)
    to_far(2, 0)
    to_far(0, 1)
    get_h.wait()
    down(0)
    to_chips(3)
    to_far(3, 0)
    to_far(1, 1)
    down(1)
    to_far(2, 1)
    down(2)
    to_far(3, 1)
    down(3)
    for n in range(parts):
        finish(n)
    sums[...] = jnp.zeros_like(sums)
    puts = fetch([(down_ref, down_out)], out_sem)
    for get in gets:
        get.wait()

    @pl.loop(0, rows // step)
    def _(i):
        at = pl.ds(pl.multiple_of(i * step, step), step)
        v, d = mid_ref[at], grad[at]
        r = lax.rsqrt(jnp.mean(v * v, axis=-1, keepdims=True) + norm_eps)
        n = v * r
        sums[1:2] += jnp.sum(d * n, axis=0, keepdims=True) * 0.5
        d = d * g_ref[1:2]
        d = dy_ref[at].astype(f32) + r * (d - n * jnp.mean(d * n, axis=-1, keepdims=True))
        dmid_ref[at] = d
        dl_ref[at] = d.astype(low)

    def across(left, right, left_dim, right_dim):
        return lax.dot_general(
            left, right, (((left_dim,), (right_dim,)), ((), ())), preferred_element_type=f32
        )

    def turned_back(u):
        turn = u[:, :ROT]
        turn = turn * cos_ref[...] - pltpu.roll(turn, ROT // 2, 1) * sin_ref[...]
        return jnp.concatenate([turn, u[:, ROT:]], axis=1).astype(low)

    get_wo.wait()
    puts += fetch([(dmid_ref, dmid_out), (dl_ref, dl_out)], out_sem.at[pl.ds(1, 2)])
    keys, values = kv_ref[:, :HEAD_DIM], kv_ref[:, HEAD_DIM:]
    scale = HEAD_DIM**-0.5
    d_keys = jnp.zeros((rows, HEAD_DIM), f32)
    d_values = jnp.zeros((rows, HEAD_DIM), f32)
    for h in range(heads):
        at = pl.ds(h * HEAD_DIM, HEAD_DIM)
        d_mixed = jnp.dot(dl_ref[...], wo[:, at], preferred_element_type=f32).astype(low)
        soft = soft_ref[h]
        d_probs = across(d_mixed, values, 1, 1)
        d_scores = (soft * (d_probs - jnp.sum(soft * d_probs, axis=-1, keepdims=True))).astype(low)
        dq_ref[:, at] = turned_back(jnp.dot(d_scores, keys, preferred_element_type=f32) * scale)
        d_keys += across(d_scores, q_ref[:, at], 0, 0)
        d_values += across(soft.astype(low), d_mixed, 0, 0)
    kv_part[:, :HEAD_DIM] = turned_back(d_keys * scale)
    kv_part[:, HEAD_DIM:] = d_values.astype(low)
    pair = remote(kv_part, kv_far, fsend, frecv, far)
    pair.start()
    first_kv = heads * HEAD_DIM
    get_wq.wait()
    for k in range(5):
        some = pl.ds(k * 512, 512)
        grad[:, some] = across(dq_ref[:, :first_kv], w[some, :first_kv], 1, 1)
    pair.wait()
    kv = kv_part[...].astype(f32) + kv_far[...].astype(f32)
    kv = kv.astype(low)
    dq_ref[:, first_kv:] = kv
    halved[...] = kv * 0.5
    for k in range(5):
        some = pl.ds(k * 512, 512)
        d = grad[:, some] + across(halved[...], w[some, first_kv : wq_ref.shape[1]], 1, 1)
        grad[:, some] = d
        dx_ref[:, some] = d.astype(low)

    @pl.loop(0, rows // step)
    def _(i):
        at = pl.ds(pl.multiple_of(i * step, step), step)
        v = x_ref[at]
        r = lax.rsqrt(jnp.mean(v * v, axis=-1, keepdims=True) + norm_eps)
        sums[0:1] += jnp.sum(grad[at] * (v * r), axis=0, keepdims=True)

    both = jnp.concatenate([sums[...], jnp.zeros((8, sums.shape[1]), f32)], axis=0)
    for k in range(64):
        tile = jnp.concatenate([both[:, k * 40 : (k + 1) * 40], jnp.zeros((16, 88), f32)], axis=1)
        gains_ref[k * 16 : (k + 1) * 16] = tile.astype(low)
    puts += fetch([(dq_ref, dq_out), (dx_ref, dx_out), (gains_ref, gains_out)], out_sem.at[pl.ds(3, 3)])
    for copy in started:
        copy.wait_send()
    for copy in puts:
        copy.wait()


def feed_back(
    d_gate_up, hidden, w_gate_up, w_down, w_out, w_q_kv,
    x, mid, dy, gains, soft, queries, keys_values, cosine, sine, cid,
):
    dma, low, f32 = pltpu.SemaphoreType.DMA, jnp.bfloat16, jnp.float32
    vmem = pl.BlockSpec(memory_space=pltpu.VMEM)
    rows, width = x.shape
    wide = w_q_kv.shape[1]
    shapes = [
        jax.ShapeDtypeStruct((4, rows, width), low),
        jax.ShapeDtypeStruct((rows, width), f32),
        jax.ShapeDtypeStruct((rows, width), low),
        jax.ShapeDtypeStruct((rows, wide), low),
        jax.ShapeDtypeStruct((rows, width), low),
        jax.ShapeDtypeStruct((1024, 128), low),
    ]
    return pl.pallas_call(
        back_kernel,
        out_shape=shapes,
        in_specs=[HBM] * 13 + [vmem] * 2,
        out_specs=[HBM] * 6,
        scratch_shapes=[
            *buffers(d_gate_up, hidden, x, mid, dy, gains, soft, queries, keys_values, *shapes),
            dma((9,)),
            dma((6,)),
            pltpu.VMEM(w_gate_up.shape, low),
            pltpu.VMEM(w_down.shape, low),
            pltpu.VMEM(w_out.shape, low),
            pltpu.VMEM((4, rows, width), low),
            pltpu.VMEM((2, rows, width), low),
            pltpu.VMEM((rows, width), low),
            pltpu.VMEM((2, rows // 2, width), low),
            pltpu.VMEM((rows, width), low),
            pltpu.VMEM((rows, width), low),
            pltpu.VMEM((rows, width), f32),
            pltpu.VMEM(keys_values.shape, low),
            pltpu.VMEM(keys_values.shape, low),
            pltpu.VMEM(keys_values.shape, low),
            pltpu.VMEM((8, width), f32),
            dma((8,)),
            dma((24,)),
            dma((24,)),
            dma,
            dma,
            dma,
            dma,
        ],
        compiler_params=pltpu.CompilerParams(
            collective_id=cid, has_side_effects=True, vmem_limit_bytes=60 * 2**20
        ),
    )(
        d_gate_up, hidden, w_gate_up, w_down, w_out, w_q_kv,
        x, mid, dy, gains, soft, queries, keys_values, cosine, sine,
    )


def tables():
    half = ROT // 2
    rates = np.exp(np.arange(half, dtype=np.float32) * np.float32(-2.0 * math.log(10000.0) / ROT))
    angles = np.arange(SEQ_LEN, dtype=np.float32)[:, None] * rates[None, :]
    cosine, sine = np.cos(angles), np.sin(angles)
    return np.concatenate([cosine, cosine], axis=1), np.concatenate([-sine, sine], axis=1)


def local(
    tokens,
    attn_gain,
    query_weight,
    kv_weight,
    out_weight,
    mlp_gain,
    gate_weight,
    up_weight,
    down_weight,
    cotangent,
):
    low = jnp.bfloat16
    rows = tokens.shape[0]
    gains = jnp.pad(jnp.stack([attn_gain, mlp_gain], axis=0), ((0, 14), (0, 88)))
    order = jnp.asarray(feature_order(), low)
    weights = (query_weight, kv_weight, out_weight.T, gate_weight, up_weight, down_weight.T)
    first, gains, second, down, x_in, dy_here = group_exchange(
        weights, gains, tokens, cotangent, order, 5
    )
    w_gate_up = lax.all_gather(second, PLANE, axis=0, tiled=True)
    w_q_kv, w_out_t, gains, dy, down = attention_gather(first, gains.reshape(64, 128), dy_here, down, 6)
    dy = dy.reshape(4 * rows, -1)
    cosine, sine = (jnp.asarray(t) for t in tables())
    x_mid, xn_all, w_down_t, xn_one, mixed_heads, queries, keys_values, soft_rows, gains = middle(
        x_in, gains, cosine, sine, w_q_kv, w_out_t, down, 2
    )
    xn_all = xn_all.reshape(4 * rows, -1)
    hidden, d_gate_up, sent = feed(xn_all, dy, w_gate_up, w_down_t)
    sent = lax.psum_scatter(sent, PLANE, scatter_dimension=0, tiled=True)
    down_part, d_mid, d_mid_low, d_q_kv, d_xn_one, d_gains = feed_back(
        d_gate_up,
        hidden,
        w_gate_up,
        w_down_t,
        w_out_t,
        w_q_kv,
        x_in,
        x_mid,
        dy_here,
        gains,
        soft_rows,
        queries,
        keys_values,
        cosine,
        sine,
        3,
    )
    query_out, kv_out, out_out, gain_out, block_out, tokens_grad = plane_sum(
        xn_one.reshape(2 * rows, -1),
        d_q_kv,
        d_mid_low,
        mixed_heads.reshape(2 * rows, -1),
        d_gains,
        down_part,
        d_xn_one,
        x_in,
        x_mid,
        d_mid,
        gains,
        order,
        7,
    )
    block_out, tokens_grad, query_out, kv_out, out_out, gain_out, down_out, gate_out, up_out = written(
        finish(sent, 8), (block_out, tokens_grad, query_out, kv_out, out_out, gain_out)
    )
    return (
        block_out,
        tokens_grad,
        gain_out[0, :40],
        query_out,
        kv_out,
        out_out.T,
        gain_out[1, :40],
        gate_out,
        up_out,
        down_out.T,
    )


def solution(mesh):
    fine = Mesh(mesh.devices.reshape(4, 2, 4, 2, 2), AXES)
    dp = ("y", "zl", "x", "c")
    in_specs = (
        P(dp, None),
        P(dp),
        P(dp, "zh"),
        P(dp, None),
        P("zh", dp),
        P(dp),
        P(dp, "zh"),
        P(dp, "zh"),
        P("zh", dp),
        P(dp, None),
    )
    out_specs = (
        P(dp, None),
        P(dp, None),
        P(dp),
        P(dp, "zh"),
        P(dp, None),
        P("zh", dp),
        P(dp),
        P(dp, "zh"),
        P(dp, "zh"),
        P("zh", dp),
    )
    return jax.shard_map(local, mesh=fine, in_specs=in_specs, out_specs=out_specs, check_vma=False)
```

```python
import math

import jax
import jax.numpy as jnp
import numpy as np
from jax import lax
from jax.experimental import pallas as pl
from jax.experimental.pallas import tpu as pltpu
from jax.sharding import Mesh
from jax.sharding import PartitionSpec as P

HEAD_DIM = 256
WINDOW = 2048
SEQ_LEN = 128
ROT = 128
AXES = ("y", "zl", "x", "c", "zh")
PLANE = ("y", "x")
GROUP = ("zl", "c")
OWNERS = ("y", "x", "zl", "c")
MESH = pl.DeviceIdType.MESH

norm_eps = 1e-06


def feature_order():
    place = np.arange(640).reshape(2, 4, 80).transpose(1, 0, 2).reshape(640)
    return (np.arange(640)[:, None] == place[None, :]).astype(np.float32)


def reorder(src, order, dst, back):
    for k in range(4):
        group = pl.ds(k * 640, 640)
        dst[:, group] = lax.dot_general(
            src[:, group],
            order[...],
            (((1,), (1 if back else 0,)), ((), ())),
            preferred_element_type=jnp.float32,
        ).astype(dst.dtype)


def greet(peers):
    barrier = pltpu.get_barrier_semaphore()
    for peer in peers:
        pl.semaphore_signal(barrier, inc=1, device_id=peer, device_id_type=MESH)
    pl.semaphore_wait(barrier, len(peers))


def remote(src, dst, send, recv, peer):
    return pltpu.make_async_remote_copy(
        src_ref=src, dst_ref=dst, send_sem=send, recv_sem=recv, device_id=peer, device_id_type=MESH
    )


ATTN, FEED = 768, 512
MAIN, PACKED = 896, 1920


def fetch(pairs, sems):
    copies = [pltpu.make_async_copy(src, dst, sems.at[k]) for k, (src, dst) in enumerate(pairs)]
    for copy in copies:
        copy.start()
    return copies


def buffers(*arrays):
    return [pltpu.VMEM(a.shape, a.dtype) for a in arrays]


HBM = pl.BlockSpec(memory_space=pltpu.HBM)


def ring_of(axis, at):
    return {axis: lax.rem(at + 3, 4)}, {axis: lax.rem(at + 1, 4)}


def send_blocks(ins, outs, here, send, recv):
    zl, c = lax.axis_index("zl"), lax.axis_index("c")
    mine = zl * 2 + c
    peers = [({"zl": 1 - zl, "c": k}, (1 - zl) * 2 + k) for k in range(2)]
    peers.append(({"c": 1 - c}, zl * 2 + 1 - c))
    n = len(ins)
    copies, keeps = [], []
    for i in range(n):
        for k, (peer, block) in enumerate(peers):
            landing = i * 3 + (c if k < 2 else 2)
            copy = remote(ins[i].at[block], outs[i].at[mine], send.at[i * 3 + k], recv.at[landing], peer)
            copy.start()
            copies.append(copy)
    for i in range(n):
        keep = pltpu.make_async_copy(ins[i].at[mine], outs[i].at[mine], here.at[i])
        keep.start()
        keeps.append(keep)

    def finish():
        for keep in keeps:
            keep.wait()
        for i in range(n):
            for k, (peer, block) in enumerate(peers):
                remote(
                    ins[i].at[block], outs[i].at[block], send.at[i * 3 + k], recv.at[i * 3 + k], peer
                ).wait_recv()
        for copy in copies:
            copy.wait_send()

    return finish


def group_peers():
    zl, c = lax.axis_index("zl"), lax.axis_index("c")
    return [{"c": 1 - c}, {"zl": 1 - zl, "c": 0}, {"zl": 1 - zl, "c": 1}]


def exchange_kernel(
    q_ref, kv_ref, wo_ref, g_ref, u_ref, d_ref, gain_ref, tok_ref, cot_ref, order_ref,
    ao_out, go_ref, so_out, do_out, x_out, dy_out,
    a_block, g_block, s_block, d_block, al, sl, ao_ref, so_ref, x_ref, dy_ref, here, send, recv, out_sem,
):
    f32, low = jnp.float32, jnp.bfloat16

    def stacked(v):
        half = v.shape[1] // 2
        return jnp.concatenate([v[:, :half], v[:, half:]], axis=0).astype(low)

    attn = jnp.concatenate([r[...].astype(f32) for r in (q_ref, kv_ref, wo_ref)], axis=1)
    for k in range(2):
        block = stacked(attn[:, k * 2 * ATTN : (k + 1) * 2 * ATTN])
        a_block[k] = block
        a_block[2 + k] = block
    gate, up, down = (r[...].astype(f32) for r in (g_ref, u_ref, d_ref))
    for t in range(4):
        first, tail, end = t * 960, t * 960 + MAIN, (t + 1) * 960
        packed = [gate[:, first:tail], up[:, first:tail], gate[:, tail:end], up[:, tail:end]]
        s_block[t] = stacked(jnp.concatenate([*packed, jnp.zeros((40, 128), f32)], axis=1))
        d_block[t] = stacked(jnp.concatenate([down[:, first:end], jnp.zeros((40, 64), f32)], axis=1))
        g_block[t] = gain_ref[...]
    greet(group_peers())
    finish = send_blocks([a_block, g_block, s_block], [al, go_ref, sl], here, send, recv)
    early = fetch([(d_block, do_out)], out_sem.at[pl.ds(4, 1)])
    reorder(tok_ref, order_ref, x_ref, False)
    reorder(cot_ref, order_ref, dy_ref, False)
    puts = fetch([(x_ref, x_out), (dy_ref, dy_out)], out_sem)
    finish()
    for h in range(2):
        parts = [al[t].astype(f32)[h * 40 : (h + 1) * 40] for t in range(4)]
        ao_ref[h] = jnp.concatenate(parts, axis=0).astype(low)
    for k in range(2):
        parts = [sl[t].astype(f32) for t in (2 * k, 2 * k + 1)]
        parts = [jnp.concatenate([v[:40], v[40:, : PACKED - 2 * FEED]], axis=1) for v in parts]
        so_ref[pl.ds(k * 80, 80)] = jnp.concatenate(parts, axis=0).astype(low)
    last = fetch([(ao_ref, ao_out), (so_ref, so_out)], out_sem.at[pl.ds(2, 2)])
    for put in (*early, *puts, *last):
        put.wait()


def group_exchange(weights, gains, tokens, cotangent, order, cid):
    low, dma = jnp.bfloat16, pltpu.SemaphoreType.DMA
    vmem = pl.BlockSpec(memory_space=pltpu.VMEM)
    shapes = [
        jax.ShapeDtypeStruct((2, 160, ATTN), low),
        jax.ShapeDtypeStruct((4, 16, 128), low),
        jax.ShapeDtypeStruct((160, PACKED), low),
        jax.ShapeDtypeStruct((4, 80, FEED), low),
        jax.ShapeDtypeStruct(tokens.shape, jnp.float32),
        jax.ShapeDtypeStruct(cotangent.shape, low),
    ]
    attn, second = (jax.ShapeDtypeStruct((4, 80, n), low) for n in (ATTN, 2 * FEED))
    return pl.pallas_call(
        exchange_kernel,
        out_shape=shapes,
        in_specs=[vmem] * 10,
        out_specs=[HBM] * 6,
        scratch_shapes=[
            *buffers(attn, shapes[1], second, shapes[3], attn, second),
            *buffers(shapes[0], shapes[2], *shapes[4:]),
            dma((3,)),
            dma((9,)),
            dma((9,)),
            dma((5,)),
        ],
        compiler_params=pltpu.CompilerParams(
            collective_id=cid, has_side_effects=True, vmem_limit_bytes=54 * 2**20
        ),
    )(*weights, gains, tokens, cotangent, order)


def shift(i, by):
    return lax.rem(i + by, 4)


def around(h, y, x):
    if h == 0:
        return x, ring_of("x", x), y, ring_of("y", y)
    return y, ring_of("y", y), x, ring_of("x", x)


class Piece:
    def __init__(self, h, source, target, columns, rows=160):
        self.h, self.source, self.target, self.columns, self.rows = h, source, target, columns, rows

    def own(self):
        return self.source

    def at(self, i1, i2, part=None):
        row, column = (i2, i1) if self.h == 0 else (i1, i2)
        size = self.rows if part is None else self.rows // 2
        first = (row * 4 + column) * self.rows + (0 if part is None else part * size)
        return self.target.at[pl.ds(pl.multiple_of(first, 16), size), self.columns]


def gather_steps(y, x, pieces, send, recv, cross):
    started = []

    def go(src, dst, n, ring, slot, peer):
        k = (n * 5 + ring) * 4 + slot
        copy = remote(src, dst, send.at[k], recv.at[k], peer)
        copy.start()
        started.append(copy)

    def arrived(dst, n, ring, slot):
        k = (n * 5 + ring) * 4 + slot
        remote(dst, dst, send.at[k], recv.at[k], {"c": 1 - lax.axis_index("c")}).wait_recv()

    each = [(n, p, *around(p.h, y, x)) for n, p in enumerate(pieces)]
    firsts = ((1, 0), (2, 3), (3, 1), (4, 2))

    def own_blocks():
        for n, p, i1, (back1, ahead1), i2, _ in each:
            go(p.own(), p.at(i1, i2), n, 0, 0, ahead1)
            go(p.own(), p.at(i1, i2), n, 0, 1, back1)
        for n, p, i1, _, i2, (back2, ahead2) in each:
            go(p.own(), p.at(i1, i2), n, 1, 0, ahead2)
            go(p.own(), p.at(i1, i2), n, 1, 1, back2)
            cross(n, p.own(), p.at(i1, i2), None)

    def first_axis():
        for n, p, i1, (back1, ahead1), i2, (back2, ahead2) in each:
            left, right = p.at(shift(i1, 3), i2), p.at(shift(i1, 1), i2)
            arrived(left, n, 0, 0)
            low = p.at(shift(i1, 3), i2, 0)
            go(low, low, n, 0, 2, ahead1)
            arrived(right, n, 0, 1)
            high = p.at(shift(i1, 1), i2, 1)
            go(high, high, n, 0, 3, back1)
            for ring, ref in ((2, left), (3, right)):
                go(ref, ref, n, ring, 0, ahead2)
                go(ref, ref, n, ring, 1, back2)
                cross(n, ref, ref, (shift(i1, 3 if ring == 2 else 1), i2))
        for n, p, i1, _, i2, (back2, ahead2) in each:
            far = shift(i1, 2)
            arrived(p.at(far, i2, 0), n, 0, 2)
            arrived(p.at(far, i2, 1), n, 0, 3)
            ref = p.at(far, i2)
            go(ref, ref, n, 4, 0, ahead2)
            go(ref, ref, n, 4, 1, back2)
            cross(n, ref, ref, (far, i2))

    def second_axis():
        for ring, by in firsts:
            for n, p, i1, _, i2, (back2, ahead2) in each:
                j = shift(i1, by)
                left, right = p.at(j, shift(i2, 3)), p.at(j, shift(i2, 1))
                arrived(left, n, ring, 0)
                low = p.at(j, shift(i2, 3), 0)
                go(low, low, n, ring, 2, ahead2)
                cross(n, left, left, (j, shift(i2, 3)))
                arrived(right, n, ring, 1)
                high = p.at(j, shift(i2, 1), 1)
                go(high, high, n, ring, 3, back2)
                cross(n, right, right, (j, shift(i2, 1)))

    def last():
        for ring, by in firsts:
            for n, p, i1, _, i2, _ in each:
                j, far = shift(i1, by), shift(i2, 2)
                arrived(p.at(j, far, 0), n, ring, 2)
                arrived(p.at(j, far, 1), n, ring, 3)
                cross(n, p.at(j, far), p.at(j, far), (j, far))

    def finish():
        for copy in started:
            copy.wait_send()

    return own_blocks, first_axis, second_axis, last, finish


def attention_gather_kernel(
    in_hbm, g_hbm, dy_hbm, d_hbm, a_ref, o_ref, go_ref, all_ref, do_out,
    in_ref, g_ref, dy_ref, d_ref, in_sem, dl, do_ref, do_sem, here, send, recv, csend, crecv, zsend, zrecv, dsend, drecv, xhere, xsend, xrecv,
):
    y, x, c = lax.axis_index("y"), lax.axis_index("x"), lax.axis_index("c")
    zl, zh = lax.axis_index("zl"), lax.axis_index("zh")
    core = {"c": 1 - c}
    gets = fetch([(in_hbm, in_ref), (g_hbm, g_ref), (dy_hbm, dy_ref), (d_hbm, d_ref)], in_sem)
    chips = [{"zl": 1 - zl, "zh": k} for k in range(2)]
    greet([*ring_of("x", x), *ring_of("y", y), core, *chips, {"zl": 1 - zl, "c": 1 - c}])
    whole = pl.ds(0, 160)
    for get in gets:
        get.wait()

    chip = {"zl": 1 - zl}
    for side in range(2):

        @pl.when(c == side)
        def _(side=side):
            if side == 0:
                starts = [(a_ref, 512), (a_ref, 1024), (a_ref, 0), (a_ref, 256), (a_ref, 768)]
            else:
                starts = [(o_ref, 256), (o_ref, 768), (a_ref, 1536), (o_ref, 0), (o_ref, 512)]
            segments = ((0, 512, 128, True), (1, 256, 256, True), (0, 0, 256, False), (0, 256, 256, False), (1, 0, 256, False))
            pieces, others = [], {}
            for n, ((h, source, width, shared), (ref, first)) in enumerate(zip(segments, starts)):
                for part in range(2 if shared else 1):
                    off = pl.multiple_of((zl if part == 0 else 1 - zl) * width, 128) if shared else 0
                    piece = Piece(
                        h, in_ref.at[h, whole, pl.ds(source + off, width)], ref, pl.ds(first + off, width)
                    )
                    if part == 0:
                        pieces.append(piece)
                    else:
                        others[n] = piece
            pieces.append(Piece(0, g_ref, go_ref, pl.ds(0, 128), 64))
            crossed, passed_on, drained = [], [], []

            def to_core(src, dst):
                k = len(crossed)
                copy = remote(src, dst, csend.at[k], crecv.at[k], core)
                copy.start()
                crossed.append(copy)

            def cross(n, src, dst, place):
                if n < 5:
                    to_core(src, dst)
                if n in others and place is not None:
                    k = len(passed_on)
                    copy = remote(dst, dst, zsend.at[k], zrecv.at[k], chip)
                    copy.start()
                    passed_on.append((copy, others[n].at(*place)))

            def drain(count):
                for k in range(len(drained), count):
                    ref = passed_on[k][1]
                    remote(ref, ref, zsend.at[k], zrecv.at[k], chip).wait_recv()
                    to_core(ref, ref)
                    drained.append(k)

            own_blocks, first_axis, second_axis, last, sent = gather_steps(y, x, pieces, send, recv, cross)
            own_blocks()
            keeps = []
            for n, p in enumerate([*pieces, *others.values()]):
                i1, _, i2, _ = around(p.h, y, x)
                keeps.append(pltpu.make_async_copy(p.own(), p.at(i1, i2), here.at[n]))
                keeps[-1].start()
                if n >= len(pieces):
                    to_core(p.own(), p.at(i1, i2))
            finish = send_blocks([d_ref], [dl], xhere, xsend, xrecv)
            half = dy_ref.shape[0] // 2
            mine, other = zl * 2 + c, (1 - zl) * 2 + c
            part = pl.ds(pl.multiple_of(zh * half, half), half)
            away = [
                remote(dy_ref.at[part], all_ref.at[mine, part], dsend.at[k], drecv.at[zh], chips[k])
                for k in range(2)
            ]
            across = remote(dy_ref, all_ref.at[mine], dsend.at[2], drecv.at[2], core)
            for copy in (*away, across):
                copy.start()
            keeps.append(pltpu.make_async_copy(dy_ref, all_ref.at[mine], here.at[8]))
            keeps[-1].start()
            first_axis()
            finish()
            for h in range(2):
                parts = [dl[t].astype(jnp.float32)[h * 40 : (h + 1) * 40] for t in range(4)]
                do_ref[h] = jnp.concatenate(parts, axis=0).astype(jnp.bfloat16)
            puts = fetch([(do_ref, do_out)], do_sem)
            second_axis()
            drain(6)
            passed = []
            for k in range(2):
                rows = pl.ds(k * half, half)
                there = all_ref.at[other, rows]
                remote(dy_ref.at[rows], there, dsend.at[k], drecv.at[k], chips[k]).wait_recv()
                passed.append(remote(there, there, dsend.at[3 + k], drecv.at[3 + k], core))
                passed[-1].start()
            last()
            drain(30)
            sent()
            for copy, _ in passed_on:
                copy.wait_send()
            for copy in (*crossed, *passed, across):
                copy.wait()
            for copy in away:
                copy.wait_send()
            for keep in (*keeps, *puts):
                keep.wait()


def attention_gather(own, gains, dy, down, cid):
    kind, dma = jnp.bfloat16, pltpu.SemaphoreType.DMA
    return pl.pallas_call(
        attention_gather_kernel,
        out_shape=[
            jax.ShapeDtypeStruct((2560, 1792), kind),
            jax.ShapeDtypeStruct((2560, 1280), kind),
            jax.ShapeDtypeStruct((1024, 128), kind),
            jax.ShapeDtypeStruct((4, *dy.shape), kind),
            jax.ShapeDtypeStruct((2, 160, down.shape[2]), kind),
        ],
        in_specs=[HBM] * 4,
        out_specs=[HBM] * 5,
        scratch_shapes=[
            *buffers(own, gains, dy, down),
            dma((4,)),
            pltpu.VMEM(down.shape, kind),
            pltpu.VMEM((2, 160, down.shape[2]), kind),
            dma((1,)),
            dma((9,)),
            dma((120,)),
            dma((120,)),
            dma((112,)),
            dma((112,)),
            dma((30,)),
            dma((30,)),
            dma((5,)),
            dma((5,)),
            dma((1,)),
            dma((3,)),
            dma((3,)),
        ],
        compiler_params=pltpu.CompilerParams(collective_id=cid, has_side_effects=True),
    )(own, gains, dy, down)


def middle_kernel(
    x_in, g_in, cos_ref, sin_ref, wq_ref, wo_ref, d_in,
    mid_out, all_out, w_ref, xn_out, mixed_out, q_out, kv_out, soft_out, rows_out,
    x_ref, g_ref, d_ref, mid_ref, all_ref, xn_ref, mixed_ref, q_ref, kv_ref, soft_ref, rows_ref, in_sem, out_sem,
    wq, wo, p_ref, landed, here, wsem, psend, precv, gsend, grecv, send, recv, csend, crecv,
):
    y, x, c = lax.axis_index("y"), lax.axis_index("x"), lax.axis_index("c")
    zl, zh = lax.axis_index("zl"), lax.axis_index("zh")
    core, far = {"c": 1 - c}, {"zh": 1 - zh}
    chips = [{"zl": 1 - zl, "zh": k} for k in range(2)]
    f32, low = jnp.float32, jnp.bfloat16
    heads = soft_ref.shape[0]
    *gets, get_d = fetch([(x_in, x_ref), (g_in, g_ref), (d_in, d_ref)], in_sem)
    loads = []
    for k in range(heads + 2):
        columns = pl.ds(k * HEAD_DIM, HEAD_DIM)
        loads.append(pltpu.make_async_copy(wq_ref.at[:, columns], wq.at[:, columns], wsem.at[k]))
    for k in range(5):
        some = pl.ds(k * 512, 512)
        loads.append(pltpu.make_async_copy(wo_ref.at[some], wo.at[some], wsem.at[heads + 2 + k]))
    for k in (heads, heads + 1, *range(heads), *range(heads + 2, heads + 7)):
        loads[k].start()
    greet([*ring_of("x", x), *ring_of("y", y), core, far, *chips])
    pieces = [
        Piece(h, d_ref.at[h, pl.ds(0, 160)], w_ref, pl.ds(h * FEED, FEED)) for h in range(2)
    ]
    own_blocks, first_axis, second_axis, last, sent = gather_steps(
        y, x, pieces, send, recv, lambda n, src, dst, place: None
    )
    get_d.wait()
    own_blocks()
    keeps = []
    for n, p in enumerate(pieces):
        i1, _, i2, _ = around(p.h, y, x)
        keeps.append(pltpu.make_async_copy(p.own(), p.at(i1, i2), here.at[n]))
        keeps[-1].start()
    half, step = x_ref.shape[0] // 2, 16
    for get in gets:
        get.wait()
    tiles = [g_ref[k * 16 : (k + 1) * 16].astype(f32)[:8, :40] for k in range(64)]
    rows_ref[...] = jnp.concatenate(tiles, axis=1)

    @pl.loop(0, 2 * half // step)
    def _(i):
        at = pl.ds(pl.multiple_of(i * step, step), step)
        v = x_ref[at]
        r = lax.rsqrt(jnp.mean(v * v, axis=-1, keepdims=True) + norm_eps)
        xn_ref[c, at] = (v * r * rows_ref[0:1]).astype(low)

    shared = [remote(xn_ref.at[c], xn_ref.at[c], csend.at[0], crecv.at[0], core)]
    shared[0].start()

    def projected(k):
        loads[k].wait()
        return jnp.dot(xn_ref[c], wq[:, k * HEAD_DIM : (k + 1) * HEAD_DIM], preferred_element_type=f32)

    def rotated(u):
        turn = u[:, :ROT]
        turn = turn * cos_ref[...] + pltpu.roll(turn, ROT // 2, 1) * sin_ref[...]
        return jnp.concatenate([turn, u[:, ROT:]], axis=1).astype(low)

    kv_ref[:, :HEAD_DIM] = rotated(projected(heads))
    kv_ref[:, HEAD_DIM:] = projected(heads + 1).astype(low)
    rows = lax.broadcasted_iota(jnp.int32, (SEQ_LEN, SEQ_LEN), 0)
    behind = rows - lax.broadcasted_iota(jnp.int32, (SEQ_LEN, SEQ_LEN), 1)
    keep_mask = (behind >= 0) & (behind < WINDOW)
    for h in range(heads):
        columns = pl.ds(h * HEAD_DIM, HEAD_DIM)
        q = rotated(projected(h))
        q_ref[:, columns] = q
        scores = lax.dot_general(
            q, kv_ref[:, :HEAD_DIM], (((1,), (1,)), ((), ())), preferred_element_type=f32
        )
        scores = jnp.where(keep_mask, scores * HEAD_DIM**-0.5, -1e30)
        top = jnp.max(scores, axis=-1, keepdims=True)
        total = top + jnp.log(jnp.sum(jnp.exp(scores - top), axis=-1, keepdims=True))
        soft = jnp.exp(scores - total)
        soft_ref[h] = soft
        mixed_ref[c, :, columns] = jnp.dot(
            soft.astype(low), kv_ref[:, HEAD_DIM:], preferred_element_type=f32
        ).astype(low)
    shared.append(remote(mixed_ref.at[c], mixed_ref.at[c], csend.at[1], crecv.at[1], core))
    shared[1].start()
    puts = fetch([(q_ref, q_out), (kv_ref, kv_out), (soft_ref, soft_out), (rows_ref, rows_out)], out_sem)
    mine, other = zl * 2 + c, (1 - zl) * 2 + c
    parts = [pl.ds(pl.multiple_of(k * half, half), half) for k in (1 - zh, zh)]
    chunks = [pl.ds(k * 512, 512) for k in range(5)]
    pair = [
        [
            remote(p_ref.at[part, some], landed.at[part, some], psend.at[5 * k + n], precv.at[5 * k + n], far)
            for n, some in enumerate(chunks)
        ]
        for k, part in enumerate(parts)
    ]
    for n, some in enumerate(chunks):
        loads[heads + 2 + n].wait()
        p_ref[:, some] = lax.dot_general(
            mixed_ref[c], wo[some], (((1,), (1,)), ((), ())), preferred_element_type=f32
        ).astype(low)
        pair[0][n].start()
    for copy in pair[1]:
        copy.start()
    first_axis()
    away, across = [], []
    for k in range(2):
        part = parts[1 - k]
        for copy in pair[k]:
            copy.wait_recv()
        first = (zh if k == 0 else 1 - zh) * half

        @pl.loop(0, half // step)
        def _(i, first=first):
            at = pl.ds(pl.multiple_of(first + i * step, step), step)
            branch = p_ref[at].astype(f32) + landed[at].astype(f32)
            v = x_ref[at] + branch
            mid_ref[at] = v
            r = lax.rsqrt(jnp.mean(v * v, axis=-1, keepdims=True) + norm_eps)
            all_ref[mine, at] = (v * r * rows_ref[1:2]).astype(low)

        ready = all_ref.at[mine, part]
        if k == 0:
            for i in range(2):
                away.append(remote(ready, ready, gsend.at[i], grecv.at[zh], chips[i]))
                away[-1].start()
        across.append(remote(ready, ready, gsend.at[2 + k], grecv.at[2 + k], core))
        across[-1].start()
        if k == 0:
            second_axis()
    passed = []
    for k in range(2):
        there = all_ref.at[other, pl.ds(k * half, half)]
        remote(there, there, gsend.at[k], grecv.at[k], chips[k]).wait_recv()
        passed.append(remote(there, there, gsend.at[4 + k], grecv.at[4 + k], core))
        passed[-1].start()
    last()
    sent()
    for copy in (*across, *passed, *shared):
        copy.wait()
    puts += fetch(
        [(mid_ref, mid_out), (all_ref, all_out), (xn_ref, xn_out), (mixed_ref, mixed_out)],
        out_sem.at[pl.ds(4, 4)],
    )
    for copy in (*away, *pair[0], *pair[1]):
        copy.wait_send()
    for keep in (*keeps, *puts):
        keep.wait()


def middle(x, gains, cosine, sine, w_q_kv, w_out_t, down, cid):
    dma, f32, low = pltpu.SemaphoreType.DMA, jnp.float32, jnp.bfloat16
    vmem = pl.BlockSpec(memory_space=pltpu.VMEM)
    rows, width = x.shape
    wide = w_out_t.shape[1]
    heads = wide // HEAD_DIM
    shapes = [
        jax.ShapeDtypeStruct(x.shape, f32),
        jax.ShapeDtypeStruct((4, *x.shape), low),
        jax.ShapeDtypeStruct((2560, 2 * FEED), low),
        jax.ShapeDtypeStruct((2, rows, width), low),
        jax.ShapeDtypeStruct((2, rows, wide), low),
        jax.ShapeDtypeStruct((rows, wide), low),
        jax.ShapeDtypeStruct((rows, 2 * HEAD_DIM), low),
        jax.ShapeDtypeStruct((heads, rows, rows), f32),
        jax.ShapeDtypeStruct((8, width), f32),
    ]
    return pl.pallas_call(
        middle_kernel,
        out_shape=shapes,
        in_specs=[HBM] * 2 + [vmem] * 2 + [HBM] * 3,
        out_specs=[HBM] * 9,
        scratch_shapes=[
            *buffers(x, gains, down, *shapes[:2], *shapes[3:]),
            dma((3,)),
            dma((8,)),
            pltpu.VMEM(w_q_kv.shape, low),
            pltpu.VMEM(w_out_t.shape, low),
            pltpu.VMEM(x.shape, low),
            pltpu.VMEM(x.shape, low),
            dma((2,)),
            dma((heads + 7,)),
            dma((10,)),
            dma((10,)),
            dma((6,)),
            dma((6,)),
            dma((40,)),
            dma((40,)),
            dma((2,)),
            dma((2,)),
        ],
        compiler_params=pltpu.CompilerParams(
            collective_id=cid, has_side_effects=True, vmem_limit_bytes=60 * 2**20
        ),
    )(x, gains, cosine, sine, w_q_kv, w_out_t, down)


def finish_kernel(s_in, o_ref, s_ref, in_sem, blocks, here, send, recv):
    get = fetch([(s_in, s_ref)], in_sem)[0]
    greet(group_peers())
    get.wait()
    wide = blocks.shape[2]
    for t in range(4):
        first = t * 40 // 16 * 16
        size = (t * 40 + 40 + 15) // 16 * 16 - first
        v = s_ref[pl.ds(first, size)].astype(jnp.float32)[t * 40 - first : t * 40 - first + 40]
        rest = jnp.concatenate([v[:, wide:], jnp.zeros((40, 2 * wide - v.shape[1]), jnp.float32)], axis=1)
        blocks[t] = jnp.concatenate([v[:, :wide], rest], axis=0).astype(jnp.bfloat16)
    send_blocks([blocks], [o_ref], here, send, recv)()


def finish(sent, cid):
    dma = pltpu.SemaphoreType.DMA
    buffer = jax.ShapeDtypeStruct((4, 80, 3 * FEED), sent.dtype)
    return pl.pallas_call(
        finish_kernel,
        out_shape=buffer,
        in_specs=[HBM],
        out_specs=HBM,
        scratch_shapes=[*buffers(sent), dma((1,)), *buffers(buffer), dma((1,)), dma((3,)), dma((3,))],
        compiler_params=pltpu.CompilerParams(
            collective_id=cid, has_side_effects=True, vmem_limit_bytes=60 * 2**20
        ),
    )(sent)


def write_kernel(
    l_in, block_in, grad_in, q_in, kv_in, o_in, g_in,
    block, grad, q, kv, o, g, down_ref, gate_ref, up_ref,
    landed, b1, b2, b3, b4, b5, b6, sem, load_sem,
):
    held = (b1, b2, b3, b4, b5, b6)
    get, *gets = fetch(list(zip((l_in, block_in, grad_in, q_in, kv_in, o_in, g_in), (landed, *held))), load_sem)
    for one in gets:
        one.wait()
    copies = fetch(list(zip(held, (block, grad, q, kv, o, g))), sem)
    get.wait()
    for t in range(4):
        v = landed[t].astype(jnp.float32)
        v = jnp.concatenate([v[:40], v[40:]], axis=1)
        first, tail = t * 960, t * 960 + MAIN
        gate_ref[:, first:tail] = v[:, :MAIN]
        gate_ref[:, tail : tail + 64] = v[:, 2 * MAIN : 2 * MAIN + 64]
        up_ref[:, first:tail] = v[:, MAIN : 2 * MAIN]
        up_ref[:, tail : tail + 64] = v[:, 2 * MAIN + 64 : PACKED]
        down_ref[:, first : first + 960] = v[:, PACKED : PACKED + 960]
    for copy in copies:
        copy.wait()


def written(landed, arrays):
    dma = pltpu.SemaphoreType.DMA
    vmem = pl.BlockSpec(memory_space=pltpu.VMEM)
    return pl.pallas_call(
        write_kernel,
        out_shape=[
            *(jax.ShapeDtypeStruct(a.shape, a.dtype) for a in arrays),
            *[jax.ShapeDtypeStruct((40, 3840), jnp.float32)] * 3,
        ],
        in_specs=[HBM] * 7,
        out_specs=[HBM] * 6 + [vmem] * 3,
        scratch_shapes=[*buffers(landed, *arrays), dma((6,)), dma((7,))],
        compiler_params=pltpu.CompilerParams(vmem_limit_bytes=56 * 2**20),
    )(landed, *arrays)


class SumPiece:
    def __init__(self, h, sums, columns, via, main, sems, rows=160):
        self.h, self.sums, self.columns, self.via, self.main, self.sems, self.rows = (
            h, sums, columns, via, main, sems, rows,
        )

    def first(self, i1, i2, part=0):
        row, column = (i2, i1) if self.h == 0 else (i1, i2)
        return (row * 4 + column) * self.rows + part * (self.rows // 2)

    def at(self, i1, i2, part=None):
        size = self.rows if part is None else self.rows // 2
        return self.sums.at[pl.ds(pl.multiple_of(self.first(i1, i2, part or 0), 16), size), self.columns]


ORDER = (
    "P0", "yv0", "xv0", "yv2", "P1", "P2", "xv2", "Tc", "gv0", "gv1", "gv2", "gv3", "xm0", "T0",
    "yv1", "gm0", "gm1", "gm2", "gm3", "xv1", "ym0", "P3", "ym2", "xv3", "xm1", "xt0", "yv3", "xm2",
    "ym1", "yt2", "gt0", "gt1", "gt2", "gt3", "gv4", "gm4", "yt0", "xt1", "xm3", "gt4", "ym3",
    "xv4", "yv4", "T1", "xt2", "Tg", "yt1", "xm4", "ym4", "To", "yt3", "xt3", "yt4", "xt4",
)


def plane_sum_kernel(
    left_in, dq_ref, dl_ref, right_in, gi_ref, p_in, t_in, x_in, mid_in, dmid_in, g_in, order_in,
    q_out, kv_out, wo_out, go_ref, block_ref, grad_ref,
    left, right_o, p_ref, t_ref, x_ref, mid_ref, dmid_ref, g_ref, order_ref, attn_ref, in_sem,
    right, left_o, sums, via, main, gsums, gvia, gmain, from_chip, attn_low, gfar, gsum, gall,
    t_core, t_other, t_chips, t_own, t_far, landed, block_low, grad_low,
    here, csend, crecv, send, recv, esend, erecv, tsend, trecv, shere, ssend, srecv,
):
    y, x, c, zl, zh = (lax.axis_index(k) for k in ("y", "x", "c", "zl", "zh"))
    core, chip, far_peer = {"c": 1 - c}, {"zl": 1 - zl}, {"zh": 1 - zh}
    chips = [{"zl": 1 - zl, "zh": k} for k in range(2)]
    get_left, get_right, get_p, get_t, *gets = fetch(
        [
            (left_in, left), (right_in, right_o), (p_in, p_ref), (t_in, t_ref), (x_in, x_ref),
            (mid_in, mid_ref), (dmid_in, dmid_ref), (g_in, g_ref), (order_in, order_ref),
        ],
        in_sem,
    )
    greet(
        [*ring_of("x", x), *ring_of("y", y), core, *chips, far_peer, {"zl": 1 - zl, "c": 1 - c}]
    )
    step = 16
    f32, low = jnp.float32, jnp.bfloat16
    order = (2, 1, 3, 0)
    tokens = p_ref.shape[1]
    half = tokens // 2

    inputs = [(dq_ref, right), (dl_ref, left_o)]
    mine = pl.ds(pl.multiple_of(c * tokens, tokens), tokens)
    shared = [
        remote(src, dst.at[mine], csend.at[k], crecv.at[k], core) for k, (src, dst) in enumerate(inputs)
    ]
    kept = [pltpu.make_async_copy(src, dst.at[mine], here.at[k]) for k, (src, dst) in enumerate(inputs)]
    kept.append(pltpu.make_async_copy(gi_ref, gsums, here.at[2]))
    for copy in (*shared, *kept):
        copy.start()
    t_cores = [
        remote(p_ref.at[z * 2 + 1 - c], t_core.at[i], tsend.at[i], trecv.at[i], core)
        for i, z in enumerate((1 - zl, zl))
    ]
    get_p.wait()
    for copy in t_cores:
        copy.start()
    get_t.wait()
    pair = remote(t_ref, landed, tsend.at[6], trecv.at[6], far_peer)
    pair.start()
    t_sent = []

    def tokens_to_chips():
        t_cores[0].wait_recv()

        @pl.loop(0, tokens // step)
        def _(i):
            at = pl.ds(pl.multiple_of(i * step, step), step)
            total = p_ref[(1 - zl) * 2 + c, at].astype(f32) + t_core[0, at].astype(f32)
            t_other[at] = total.astype(low)

        for k in range(2):
            t_sent.append(
                remote(t_other.at[pl.ds(k * half, half)], t_chips.at[zh], tsend.at[2 + k], trecv.at[2 + zh], chips[k])
            )
            t_sent[-1].start()

    def tokens_to_far(k):
        piece = (1 - zh) if k == 0 else zh
        if k == 0:
            t_cores[1].wait_recv()
        else:
            for i in range(2):
                remote(
                    t_other.at[pl.ds(0, half)], t_chips.at[i], tsend.at[2 + i], trecv.at[2 + i], chips[i]
                ).wait_recv()

        @pl.loop(0, half // step)
        def _(i):
            at = pl.ds(pl.multiple_of(piece * half + i * step, step), step)
            total = p_ref[zl * 2 + c, at].astype(f32) + t_core[1, at].astype(f32)
            if k == 1:
                there = pl.ds(pl.multiple_of(i * step, step), step)
                total += t_chips[0, there].astype(f32) + t_chips[1, there].astype(f32)
            t_own[at] = total.astype(low)

        at = pl.ds(pl.multiple_of(piece * half, half), half)
        t_sent.append(remote(t_own.at[at], t_far.at[at], tsend.at[4 + k], trecv.at[4 + k], far_peer))
        t_sent[-1].start()

    def tokens_gradient():
        pair.wait_recv()

        @pl.loop(0, tokens // step)
        def _(i):
            at = pl.ds(pl.multiple_of(i * step, step), step)
            d = (t_ref[at].astype(f32) + landed[at].astype(f32)) * g_ref[0:1]
            v = x_ref[at]
            r = lax.rsqrt(jnp.mean(v * v, axis=-1, keepdims=True) + norm_eps)
            n = v * r
            d = r * (d - n * jnp.mean(d * n, axis=-1, keepdims=True))
            grad_low[at] = (dmid_ref[at] + d).astype(low)

        reorder(grad_low, order_ref, grad_ref, True)

    def tokens_output():
        for k in range(2):
            t_sent[2 + k].wait_recv()

        @pl.loop(0, tokens // step)
        def _(i):
            at = pl.ds(pl.multiple_of(i * step, step), step)
            branch = t_own[at].astype(f32) + t_far[at].astype(f32)
            block_low[at] = (mid_ref[at] + branch).astype(low)

        reorder(block_low, order_ref, block_ref, True)

    def products(q):
        top = shift(y, order[q]) * 640
        for side in range(2):

            @pl.when(c == side)
            def _(side=side):
                if side == 0:
                    parts = [(left, right, 0, 0, 768), (left, right, 768, 768, 768)]
                else:
                    parts = [
                        (left, right, 1536, 0, 256),
                        (left_o, right_o, 0, 256, 512),
                        (left_o, right_o, 512, 768, 768),
                    ]

                @pl.loop(0, 5)
                def _(i):
                    at = pl.ds(pl.multiple_of(top + i * 128, 128), 128)
                    for lhs, rhs, source, target, width in parts:
                        sums[at, pl.ds(target, width)] = lax.dot_general(
                            lhs[:, at],
                            rhs[:, pl.ds(source, width)],
                            (((0,), (0,)), ((), ())),
                            preferred_element_type=f32,
                        ).astype(low)

    pieces = [
        SumPiece(h, sums, pl.ds(h * ATTN, ATTN), via.at[h], main.at[h], h * 20) for h in range(2)
    ]
    pieces.append(SumPiece(0, gsums, pl.ds(0, 128), gvia, gmain, 40, 64))

    def add(p, first, size, terms):
        @pl.loop(0, size // step)
        def _(i):
            at = pl.ds(pl.multiple_of(first + i * step, step), step)
            total = p.sums[at, p.columns].astype(f32)
            for ref, index, start in terms:
                total += ref[(*index, pl.ds(pl.multiple_of(start + i * step, step), step))].astype(f32)
            p.sums[at, p.columns] = total.astype(low)

    started = []

    def go(p, ring, slot, src, dst, peer):
        k = p.sems + ring * 4 + slot
        copy = remote(src, dst, send.at[k], recv.at[k], peer)
        copy.start()
        started.append(copy)

    def arrived(p, ring, slot, dst):
        k = p.sems + ring * 4 + slot
        remote(dst, dst, send.at[k], recv.at[k], core).wait_recv()

    def line(p, j):
        i1, peers1, i2, peers2 = around(p.h, y, x)
        if j == 4:
            return lambda k: (k, i2), i1, peers1
        fixed = shift(i1, order[j])
        return lambda k: (fixed, k), i2, peers2

    def out_via(p, ring):
        place, at, (back, ahead) = line(p, ring)
        far = place(shift(at, 2))
        go(p, ring, 0, p.at(*far, 0), p.via.at[ring, 0], ahead)
        go(p, ring, 1, p.at(*far, 1), p.via.at[ring, 1], back)

    def out_main(p, ring):
        place, at, (back, ahead) = line(p, ring)
        small = p.rows // 2
        arrived(p, ring, 0, p.via.at[ring, 0])
        add(p, p.first(*place(shift(at, 1)), 0), small, [(p.via, (ring, 0), 0)])
        go(p, ring, 2, p.at(*place(shift(at, 1))), p.main.at[ring, 0], ahead)
        arrived(p, ring, 1, p.via.at[ring, 1])
        add(p, p.first(*place(shift(at, 3)), 1), small, [(p.via, (ring, 1), 0)])
        go(p, ring, 3, p.at(*place(shift(at, 3))), p.main.at[ring, 1], back)

    def take(p, ring):
        place, at, _ = line(p, ring)
        arrived(p, ring, 2, p.main.at[ring, 0])
        arrived(p, ring, 3, p.main.at[ring, 1])
        add(p, p.first(*place(at)), p.rows, [(p.main, (ring, 0), 0), (p.main, (ring, 1), 0)])

    y_first, x_first, gain = pieces
    for copy in kept:
        copy.wait()
    for copy in shared:
        copy.wait_recv()
    get_left.wait()
    get_right.wait()
    named = {"x": x_first, "y": y_first, "g": gain}
    acts = {"v": out_via, "m": out_main, "t": take}
    token_acts = {
        "Tc": tokens_to_chips,
        "T0": lambda: tokens_to_far(0),
        "T1": lambda: tokens_to_far(1),
        "Tg": tokens_gradient,
        "To": tokens_output,
    }
    for word in ORDER:
        if word[0] == "P":
            products(int(word[1]))
        elif word[0] == "T":
            while gets:
                gets.pop().wait()
            token_acts[word]()
        else:
            for name in word[:-2]:
                acts[word[-2]](named[name], int(word[-1]))
    home = (y * 4 + x) * 160
    ghome = pl.ds(pl.multiple_of((y * 4 + x) * 64, 16), 64)
    theirs = pl.ds(pl.multiple_of(home + (1 - zl) * 80, 16), 80)
    across = remote(gsums.at[ghome], gfar, esend.at[0], erecv.at[0], far_peer)
    across.start()
    away = remote(sums.at[theirs], from_chip, esend.at[1], erecv.at[1], chip)
    away.start()
    across.wait()
    both = gsums[ghome].astype(f32) + gfar[...].astype(f32)
    for t in range(4):
        gsum[t] = both[t * 16 : (t + 1) * 16].astype(low)
    finish_gains = send_blocks([gsum], [gall], shere, ssend, srecv)
    away.wait()

    @pl.loop(0, 80 // step)
    def _(i):
        here_at = pl.ds(pl.multiple_of(home + zl * 80 + i * step, step), step)
        at = pl.ds(pl.multiple_of(i * step, step), step)
        attn_low[at] = sums[here_at].astype(f32) + from_chip[at].astype(f32)

    ours = pl.ds(pl.multiple_of(c * 40, 8), 40)
    for_core = pl.ds(pl.multiple_of((1 - c) * 40, 8), 40)
    columns = pl.ds(pl.multiple_of(c * 2 * ATTN, 128), 2 * ATTN)
    last = remote(attn_low.at[for_core], attn_ref.at[:, columns], esend.at[2], erecv.at[2], core)
    keep = pltpu.make_async_copy(attn_low.at[ours], attn_ref.at[:, columns], here.at[0])
    last.start()
    keep.start()
    finish_gains()
    go_ref[...] = (
        gall[0].astype(f32) + gall[1].astype(f32) + gall[2].astype(f32) + gall[3].astype(f32)
    )
    last.wait()
    keep.wait()
    first = 0
    for out in (q_out, kv_out, wo_out):
        out[...] = attn_ref[:, first : first + out.shape[1]]
        first += out.shape[1]
    for copy in (*started, *shared, pair, *t_cores, *t_sent):
        copy.wait_send()


def plane_sum(xn, d_q_kv, d_low, mixed, gains, down, d_xn, x, mid, d_mid, gains_row, order, cid):
    low, dma, f32 = jnp.bfloat16, pltpu.SemaphoreType.DMA, jnp.float32
    rows, width = x.shape
    vmem = pl.BlockSpec(memory_space=pltpu.VMEM)
    return pl.pallas_call(
        plane_sum_kernel,
        out_shape=[
            *(jax.ShapeDtypeStruct((40, n), f32) for n in (1280, 512, 1280)),
            jax.ShapeDtypeStruct((16, 128), f32),
            jax.ShapeDtypeStruct(x.shape, low),
            jax.ShapeDtypeStruct(x.shape, low),
        ],
        in_specs=[HBM] * 12,
        out_specs=[vmem] * 6,
        scratch_shapes=[
            *buffers(xn, mixed, down, d_xn, x, mid, d_mid, gains_row, order),
            pltpu.VMEM((40, 4 * ATTN), f32),
            dma((9,)),
            pltpu.VMEM((2 * rows, d_q_kv.shape[1]), low),
            pltpu.VMEM((2 * rows, width), low),
            pltpu.VMEM((2560, 2 * ATTN), low),
            pltpu.VMEM((2, 5, 2, 80, ATTN), low),
            pltpu.VMEM((2, 5, 2, 160, ATTN), low),
            pltpu.VMEM((1024, 128), low),
            pltpu.VMEM((5, 2, 32, 128), low),
            pltpu.VMEM((5, 2, 64, 128), low),
            pltpu.VMEM((80, 2 * ATTN), low),
            pltpu.VMEM((80, 2 * ATTN), f32),
            pltpu.VMEM((64, 128), low),
            pltpu.VMEM((4, 16, 128), low),
            pltpu.VMEM((4, 16, 128), low),
            pltpu.VMEM((2, rows, width), low),
            pltpu.VMEM((rows, width), low),
            pltpu.VMEM((2, rows // 2, width), low),
            pltpu.VMEM((rows, width), low),
            pltpu.VMEM((rows, width), low),
            pltpu.VMEM((rows, width), low),
            pltpu.VMEM((rows, width), low),
            pltpu.VMEM((rows, width), low),
            dma((3,)),
            dma((2,)),
            dma((2,)),
            dma((60,)),
            dma((60,)),
            dma((3,)),
            dma((3,)),
            dma((7,)),
            dma((7,)),
            dma((1,)),
            dma((3,)),
            dma((3,)),
        ],
        compiler_params=pltpu.CompilerParams(
            collective_id=cid, has_side_effects=True, vmem_limit_bytes=60 * 2**20
        ),
    )(xn, d_q_kv, d_low, mixed, gains, down, d_xn, x, mid, d_mid, gains_row, order)


GELU_IN, GELU_CUBE = math.sqrt(2.0 / math.pi), 0.044715


def feed_kernel(
    xn_in, dy_ref, g_ref, d_ref, h_out, dg_out, o_ref,
    xn_ref, h_ref, dg_ref, in_sem, h_sem, dy, wg, wd, dy_turned, xn_turned, back, out, load_sem, out_sem,
):
    f32, low = jnp.float32, jnp.bfloat16
    units, lines = h_ref.shape[1], out.shape[1]
    lanes = lax.broadcasted_iota(jnp.int32, (1, 128), 1)
    get_xn = fetch([(xn_in, xn_ref)], in_sem)[0]
    get_dy = pltpu.make_async_copy(dy_ref, dy, load_sem.at[0])
    get_dy.start()
    loads = []
    for source, target in ((d_ref, wd), (g_ref, wg)):
        for n in range(4):
            some = pl.ds(n * 640, 640)
            loads.append(pltpu.make_async_copy(source.at[some], target.at[some], load_sem.at[1 + len(loads)]))
    for n in range(4):
        loads[n].start()
    get_xn.wait()
    xn_turned[...] = xn_ref[...].T
    get_dy.wait()
    dy_turned[...] = dy[...].T
    for n in range(4):
        loads[n].wait()
    for n in range(4, 8):
        loads[n].start()
    for k in range(units // 256):
        at = pl.ds(k * 256, 256)
        back[:, at] = jnp.dot(dy[...], wd[:, at], preferred_element_type=f32)
    for n in range(4, 8):
        loads[n].wait()
    def act(gate, up, d):
        square = gate * gate
        t = jnp.tanh(GELU_IN * (gate + GELU_CUBE * gate * square))
        cdf = 0.5 * (1.0 + t)
        slope = cdf + 0.5 * gate * (1.0 - t * t) * (GELU_IN * (1.0 + 3.0 * GELU_CUBE * square))
        gelu = gate * cdf
        return gelu * up, d * up * slope, d * gelu

    for first, size in ((0, 256), (256, 256), (512, 256), (768, 128)):
        at, beside = pl.ds(first, size), pl.ds(MAIN + first, size)
        gate = jnp.dot(xn_ref[...], wg[:, at], preferred_element_type=f32)
        up = jnp.dot(xn_ref[...], wg[:, beside], preferred_element_type=f32)
        hidden, d_gate, d_up = act(gate, up, back[:, at])
        h_ref[:, at] = hidden.astype(low)
        dg_ref[:, at] = d_gate.astype(low)
        dg_ref[:, beside] = d_up.astype(low)
    at, both = pl.ds(MAIN, 128), pl.ds(2 * MAIN, 128)
    gate = jnp.dot(xn_ref[...], wg[:, both], preferred_element_type=f32)
    hidden, d_gate, d_up = act(gate, pltpu.roll(gate, 64, 1), back[:, at])
    h_ref[:, at] = jnp.where(lanes < 64, hidden, 0.0).astype(low)
    dg_ref[:, both] = jnp.where(lanes < 64, d_gate, pltpu.roll(d_up, 64, 1)).astype(low)
    puts = fetch([(h_ref, h_out), (dg_ref, dg_out)], h_sem)

    def put(i):
        slot = lax.rem(i, 2)
        rows = pl.ds(pl.multiple_of(i * lines, lines), lines)
        return pltpu.make_async_copy(out.at[slot], o_ref.at[rows], out_sem.at[slot])

    steps = o_ref.shape[0] // lines

    @pl.loop(0, steps)
    def _(i):
        slot = lax.rem(i, 2)
        pl.when(i >= 2)(lambda: put(i - 2).wait())
        rows = pl.ds(pl.multiple_of(i * lines, lines), lines)
        for left, right, first, total in ((xn_turned, dg_ref, 0, PACKED), (dy_turned, h_ref, PACKED, 960)):
            for k in range(0, total, 512):
                size = min(512, right.shape[1] - k)
                kept = min(size, total - k)
                v = jnp.dot(left[rows], right[:, pl.ds(k, size)], preferred_element_type=f32)
                out[slot, :, pl.ds(first + k, kept)] = v[:, :kept].astype(low)
        put(i).start()

    put(steps - 2).wait()
    put(steps - 1).wait()
    for copy in puts:
        copy.wait()


def feed(xn, dy, w_gate_up, w_down):
    depth, width = xn.shape
    units = w_down.shape[1]
    low, dma = jnp.bfloat16, pltpu.SemaphoreType.DMA
    shapes = [
        jax.ShapeDtypeStruct((depth, units), low),
        jax.ShapeDtypeStruct((depth, PACKED), low),
        jax.ShapeDtypeStruct((width, PACKED + 960), low),
    ]
    return pl.pallas_call(
        feed_kernel,
        out_shape=shapes,
        in_specs=[HBM] * 4,
        out_specs=[HBM] * 3,
        scratch_shapes=[
            *buffers(xn, *shapes[:2]),
            dma((1,)),
            dma((2,)),
            pltpu.VMEM((depth, width), low),
            pltpu.VMEM((width, PACKED), low),
            pltpu.VMEM((width, units), low),
            pltpu.VMEM((width, depth), low),
            pltpu.VMEM((width, depth), low),
            pltpu.VMEM((depth, units), jnp.float32),
            pltpu.VMEM((2, 640, PACKED + 960), low),
            dma((9,)),
            dma((2,)),
        ],
        compiler_params=pltpu.CompilerParams(vmem_limit_bytes=60 * 2**20),
        cost_estimate=pl.CostEstimate(
            flops=12 * depth * width * units,
            bytes_accessed=4 * depth * width + 12 * width * units + 6 * depth * units,
            transcendentals=depth * units,
        ),
    )(xn, dy, w_gate_up, w_down)


def back_kernel(
    dg_in, h_in, w_ref, d_ref, wo_ref, wq_ref,
    x_in, mid_in, dy_in, g_in, soft_in, q_in, kv_in, cos_ref, sin_ref,
    down_out, dmid_out, dl_out, dq_out, dx_out, gains_out,
    dg_ref, h_ref, x_ref, mid_ref, dy_ref, g_ref, soft_ref, q_ref, kv_ref,
    down_ref, dmid_ref, dl_ref, dq_ref, dx_ref, gains_ref, in_sem, out_sem,
    w, wd, wo, part, from_core, other, from_chips, own, from_far, grad, kv_part, kv_far, halved, sums,
    wsem, send, recv, osem, qsem, fsend, frecv,
):
    zl, c, zh = lax.axis_index("zl"), lax.axis_index("c"), lax.axis_index("zh")
    core, far = {"c": 1 - c}, {"zh": 1 - zh}
    chips = [{"zl": 1 - zl, "zh": k} for k in range(2)]
    f32, low = jnp.float32, jnp.bfloat16
    parts, width = w_ref.shape[0] // 640, 640
    rows = x_ref.shape[0]
    half, step = rows // 2, 16
    heads = soft_ref.shape[0]
    get_dg = fetch([(dg_in, dg_ref)], in_sem)[0]
    loads = []
    for source, target, first in ((w_ref, w, 0), (d_ref, wd, parts)):
        for n in range(parts):
            some = pl.ds(n * width, width)
            loads.append(pltpu.make_async_copy(source.at[some], target.at[some], wsem.at[first + n]))
    for n in range(2):
        loads[n].start()
    get_wo = pltpu.make_async_copy(wo_ref, wo, osem)
    wq = w.at[:, pl.ds(0, wq_ref.shape[1])]
    get_wq = pltpu.make_async_copy(wq_ref, wq, qsem)
    greet([core, far, *chips])
    order = [1 - zl, zl]
    started = []

    def go(src, dst, n, out_slot, in_slot, peer):
        copy = remote(src, dst, send.at[n * 6 + out_slot], recv.at[n * 6 + in_slot], peer)
        copy.start()
        started.append(copy)

    def arrived(dst, n, slot):
        remote(dst, dst, send.at[n * 6 + slot], recv.at[n * 6 + slot], core).wait_recv()

    def columns(n):
        return pl.ds(n * width, width)

    def product(left, right, n, target):
        some = pl.ds(n * width, width)
        v = lax.dot_general(
            left[...], right[some], (((1,), (1,)), ((), ())), preferred_element_type=f32
        ).astype(low)
        for t in range(4):
            target[t, :, some] = v[t * rows : (t + 1) * rows]

    def multiply(n):
        loads[n].wait()
        product(dg_ref, w, n, part)
        for i, z in enumerate(order):
            go(part.at[z * 2 + 1 - c, :, columns(n)], from_core.at[i, :, columns(n)], n, i, i, core)

    def down(n):
        loads[parts + n].wait()
        product(h_ref, wd, n, down_ref)

    def to_chips(n):
        arrived(from_core.at[0, :, columns(n)], n, 0)

        @pl.loop(0, rows // step)
        def _(i):
            at = pl.ds(pl.multiple_of(i * step, step), step)
            total = part[(1 - zl) * 2 + c, at, columns(n)].astype(f32) + from_core[0, at, columns(n)].astype(f32)
            other[at, columns(n)] = total.astype(low)

        for k in range(2):
            go(other.at[pl.ds(k * half, half), columns(n)], from_chips.at[zh, :, columns(n)], n, 2 + k, 2 + zh, chips[k])

    def to_far(n, k):
        piece = (1 - zh) if k == 0 else zh
        if k == 0:
            arrived(from_core.at[1, :, columns(n)], n, 1)
        else:
            for i in range(2):
                arrived(from_chips.at[i, :, columns(n)], n, 2 + i)

        @pl.loop(0, half // step)
        def _(i):
            at = pl.ds(pl.multiple_of(piece * half + i * step, step), step)
            total = part[zl * 2 + c, at, columns(n)].astype(f32) + from_core[1, at, columns(n)].astype(f32)
            if k == 1:
                there = pl.ds(pl.multiple_of(i * step, step), step)
                total += from_chips[0, there, columns(n)].astype(f32) + from_chips[1, there, columns(n)].astype(f32)
            own[at, columns(n)] = total.astype(low)

        at = pl.ds(pl.multiple_of(piece * half, half), half)
        go(own.at[at, columns(n)], from_far.at[at, columns(n)], n, 4 + k, 4 + k, far)

    def finish(n):
        for k in range(2):
            arrived(from_far.at[pl.ds(k * half, half), columns(n)], n, 4 + k)

        @pl.loop(0, rows // step)
        def _(i):
            at = pl.ds(pl.multiple_of(i * step, step), step)
            grad[at, columns(n)] = own[at, columns(n)].astype(f32) + from_far[at, columns(n)].astype(f32)

    get_dg.wait()
    loads[2].start()
    multiply(0)
    loads[3].start()
    multiply(1)
    get_h, *gets = fetch(
        [
            (h_in, h_ref), (x_in, x_ref), (mid_in, mid_ref), (dy_in, dy_ref),
            (g_in, g_ref), (soft_in, soft_ref), (q_in, q_ref), (kv_in, kv_ref),
        ],
        in_sem.at[pl.ds(1, 8)],
    )
    for n in range(parts, 2 * parts):
        loads[n].start()
    to_chips(0)
    to_far(0, 0)
    multiply(2)
    to_chips(1)
    to_far(1, 0)
    multiply(3)
    get_wo.start()
    get_wq.start()
    to_chips(2)
    to_far(2, 0)
    to_far(0, 1)
    get_h.wait()
    down(0)
    to_chips(3)
    to_far(3, 0)
    to_far(1, 1)
    down(1)
    to_far(2, 1)
    down(2)
    to_far(3, 1)
    down(3)
    for n in range(parts):
        finish(n)
    sums[...] = jnp.zeros_like(sums)
    puts = fetch([(down_ref, down_out)], out_sem)
    for get in gets:
        get.wait()

    @pl.loop(0, rows // step)
    def _(i):
        at = pl.ds(pl.multiple_of(i * step, step), step)
        v, d = mid_ref[at], grad[at]
        r = lax.rsqrt(jnp.mean(v * v, axis=-1, keepdims=True) + norm_eps)
        n = v * r
        sums[1:2] += jnp.sum(d * n, axis=0, keepdims=True) * 0.5
        d = d * g_ref[1:2]
        d = dy_ref[at].astype(f32) + r * (d - n * jnp.mean(d * n, axis=-1, keepdims=True))
        dmid_ref[at] = d
        dl_ref[at] = d.astype(low)

    def across(left, right, left_dim, right_dim):
        return lax.dot_general(
            left, right, (((left_dim,), (right_dim,)), ((), ())), preferred_element_type=f32
        )

    def turned_back(u):
        turn = u[:, :ROT]
        turn = turn * cos_ref[...] - pltpu.roll(turn, ROT // 2, 1) * sin_ref[...]
        return jnp.concatenate([turn, u[:, ROT:]], axis=1).astype(low)

    get_wo.wait()
    puts += fetch([(dmid_ref, dmid_out), (dl_ref, dl_out)], out_sem.at[pl.ds(1, 2)])
    keys, values = kv_ref[:, :HEAD_DIM], kv_ref[:, HEAD_DIM:]
    scale = HEAD_DIM**-0.5
    d_keys = jnp.zeros((rows, HEAD_DIM), f32)
    d_values = jnp.zeros((rows, HEAD_DIM), f32)
    for h in range(heads):
        at = pl.ds(h * HEAD_DIM, HEAD_DIM)
        d_mixed = jnp.dot(dl_ref[...], wo[:, at], preferred_element_type=f32).astype(low)
        soft = soft_ref[h]
        d_probs = across(d_mixed, values, 1, 1)
        d_scores = (soft * (d_probs - jnp.sum(soft * d_probs, axis=-1, keepdims=True))).astype(low)
        dq_ref[:, at] = turned_back(jnp.dot(d_scores, keys, preferred_element_type=f32) * scale)
        d_keys += across(d_scores, q_ref[:, at], 0, 0)
        d_values += across(soft.astype(low), d_mixed, 0, 0)
    kv_part[:, :HEAD_DIM] = turned_back(d_keys * scale)
    kv_part[:, HEAD_DIM:] = d_values.astype(low)
    pair = remote(kv_part, kv_far, fsend, frecv, far)
    pair.start()
    first_kv = heads * HEAD_DIM
    get_wq.wait()
    for k in range(5):
        some = pl.ds(k * 512, 512)
        grad[:, some] = across(dq_ref[:, :first_kv], w[some, :first_kv], 1, 1)
    pair.wait()
    kv = kv_part[...].astype(f32) + kv_far[...].astype(f32)
    kv = kv.astype(low)
    dq_ref[:, first_kv:] = kv
    halved[...] = kv * 0.5
    for k in range(5):
        some = pl.ds(k * 512, 512)
        d = grad[:, some] + across(halved[...], w[some, first_kv : wq_ref.shape[1]], 1, 1)
        grad[:, some] = d
        dx_ref[:, some] = d.astype(low)

    @pl.loop(0, rows // step)
    def _(i):
        at = pl.ds(pl.multiple_of(i * step, step), step)
        v = x_ref[at]
        r = lax.rsqrt(jnp.mean(v * v, axis=-1, keepdims=True) + norm_eps)
        sums[0:1] += jnp.sum(grad[at] * (v * r), axis=0, keepdims=True)

    both = jnp.concatenate([sums[...], jnp.zeros((8, sums.shape[1]), f32)], axis=0)
    for k in range(64):
        tile = jnp.concatenate([both[:, k * 40 : (k + 1) * 40], jnp.zeros((16, 88), f32)], axis=1)
        gains_ref[k * 16 : (k + 1) * 16] = tile.astype(low)
    puts += fetch([(dq_ref, dq_out), (dx_ref, dx_out), (gains_ref, gains_out)], out_sem.at[pl.ds(3, 3)])
    for copy in started:
        copy.wait_send()
    for copy in puts:
        copy.wait()


def feed_back(
    d_gate_up, hidden, w_gate_up, w_down, w_out, w_q_kv,
    x, mid, dy, gains, soft, queries, keys_values, cosine, sine, cid,
):
    dma, low, f32 = pltpu.SemaphoreType.DMA, jnp.bfloat16, jnp.float32
    vmem = pl.BlockSpec(memory_space=pltpu.VMEM)
    rows, width = x.shape
    wide = w_q_kv.shape[1]
    shapes = [
        jax.ShapeDtypeStruct((4, rows, width), low),
        jax.ShapeDtypeStruct((rows, width), f32),
        jax.ShapeDtypeStruct((rows, width), low),
        jax.ShapeDtypeStruct((rows, wide), low),
        jax.ShapeDtypeStruct((rows, width), low),
        jax.ShapeDtypeStruct((1024, 128), low),
    ]
    return pl.pallas_call(
        back_kernel,
        out_shape=shapes,
        in_specs=[HBM] * 13 + [vmem] * 2,
        out_specs=[HBM] * 6,
        scratch_shapes=[
            *buffers(d_gate_up, hidden, x, mid, dy, gains, soft, queries, keys_values, *shapes),
            dma((9,)),
            dma((6,)),
            pltpu.VMEM(w_gate_up.shape, low),
            pltpu.VMEM(w_down.shape, low),
            pltpu.VMEM(w_out.shape, low),
            pltpu.VMEM((4, rows, width), low),
            pltpu.VMEM((2, rows, width), low),
            pltpu.VMEM((rows, width), low),
            pltpu.VMEM((2, rows // 2, width), low),
            pltpu.VMEM((rows, width), low),
            pltpu.VMEM((rows, width), low),
            pltpu.VMEM((rows, width), f32),
            pltpu.VMEM(keys_values.shape, low),
            pltpu.VMEM(keys_values.shape, low),
            pltpu.VMEM(keys_values.shape, low),
            pltpu.VMEM((8, width), f32),
            dma((8,)),
            dma((24,)),
            dma((24,)),
            dma,
            dma,
            dma,
            dma,
        ],
        compiler_params=pltpu.CompilerParams(
            collective_id=cid, has_side_effects=True, vmem_limit_bytes=60 * 2**20
        ),
    )(
        d_gate_up, hidden, w_gate_up, w_down, w_out, w_q_kv,
        x, mid, dy, gains, soft, queries, keys_values, cosine, sine,
    )


def tables():
    half = ROT // 2
    rates = np.exp(np.arange(half, dtype=np.float32) * np.float32(-2.0 * math.log(10000.0) / ROT))
    angles = np.arange(SEQ_LEN, dtype=np.float32)[:, None] * rates[None, :]
    cosine, sine = np.cos(angles), np.sin(angles)
    return np.concatenate([cosine, cosine], axis=1), np.concatenate([-sine, sine], axis=1)


def local(
    tokens,
    attn_gain,
    query_weight,
    kv_weight,
    out_weight,
    mlp_gain,
    gate_weight,
    up_weight,
    down_weight,
    cotangent,
):
    low = jnp.bfloat16
    rows = tokens.shape[0]
    gains = jnp.pad(jnp.stack([attn_gain, mlp_gain], axis=0), ((0, 14), (0, 88)))
    order = jnp.asarray(feature_order(), low)
    weights = (query_weight, kv_weight, out_weight.T, gate_weight, up_weight, down_weight.T)
    first, gains, second, down, x_in, dy_here = group_exchange(
        weights, gains, tokens, cotangent, order, 5
    )
    w_gate_up = lax.all_gather(second, PLANE, axis=0, tiled=True)
    w_q_kv, w_out_t, gains, dy, down = attention_gather(first, gains.reshape(64, 128), dy_here, down, 6)
    dy = dy.reshape(4 * rows, -1)
    cosine, sine = (jnp.asarray(t) for t in tables())
    x_mid, xn_all, w_down_t, xn_one, mixed_heads, queries, keys_values, soft_rows, gains = middle(
        x_in, gains, cosine, sine, w_q_kv, w_out_t, down, 2
    )
    xn_all = xn_all.reshape(4 * rows, -1)
    hidden, d_gate_up, sent = feed(xn_all, dy, w_gate_up, w_down_t)
    sent = lax.psum_scatter(sent, PLANE, scatter_dimension=0, tiled=True)
    down_part, d_mid, d_mid_low, d_q_kv, d_xn_one, d_gains = feed_back(
        d_gate_up,
        hidden,
        w_gate_up,
        w_down_t,
        w_out_t,
        w_q_kv,
        x_in,
        x_mid,
        dy_here,
        gains,
        soft_rows,
        queries,
        keys_values,
        cosine,
        sine,
        3,
    )
    query_out, kv_out, out_out, gain_out, block_out, tokens_grad = plane_sum(
        xn_one.reshape(2 * rows, -1),
        d_q_kv,
        d_mid_low,
        mixed_heads.reshape(2 * rows, -1),
        d_gains,
        down_part,
        d_xn_one,
        x_in,
        x_mid,
        d_mid,
        gains,
        order,
        7,
    )
    block_out, tokens_grad, query_out, kv_out, out_out, gain_out, down_out, gate_out, up_out = written(
        finish(sent, 8), (block_out, tokens_grad, query_out, kv_out, out_out, gain_out)
    )
    return (
        block_out,
        tokens_grad,
        gain_out[0, :40],
        query_out,
        kv_out,
        out_out.T,
        gain_out[1, :40],
        gate_out,
        up_out,
        down_out.T,
    )


def solution(mesh):
    fine = Mesh(mesh.devices.reshape(4, 2, 4, 2, 2), AXES)
    dp = ("y", "zl", "x", "c")
    in_specs = (
        P(dp, None),
        P(dp),
        P(dp, "zh"),
        P(dp, None),
        P("zh", dp),
        P(dp),
        P(dp, "zh"),
        P(dp, "zh"),
        P("zh", dp),
        P(dp, None),
    )
    out_specs = (
        P(dp, None),
        P(dp, None),
        P(dp),
        P(dp, "zh"),
        P(dp, None),
        P("zh", dp),
        P(dp),
        P(dp, "zh"),
        P(dp, "zh"),
        P("zh", dp),
    )
    return jax.shard_map(local, mesh=fine, in_specs=in_specs, out_specs=out_specs, check_vma=False)
```
